128 devices in a mesh: ctx: 16 (over x, y), wa: 8 (over z, core).
Axes of the slice: x: 4, y: 4, z: 4, core: 2. Of those that a mesh axis runs over, the one named last changes fastest.
Arguments:
- layer_input: bfloat16 [8, 2048, 896], P('wa', 'ctx'), may hold values from -6 to 6
- positions: int32 [8, 2048], P('wa', 'ctx'), may hold values from 0 to 2047, as said below
- attention_gain: bfloat16 [896], P('wa'), may hold values from 0.5 to 1.5
- projection: bfloat16 [896, 1152], P('wa'), may hold values from -0.1875 to 0.1875
- projection_biases: bfloat16 [1152], P('wa'), may hold values from -3 to 3
- output_matrix: bfloat16 [896, 896], P('wa'), may hold values from -3.5 to 3.5
- feed_gain: bfloat16 [896], P('wa'), may hold values from 0.5 to 1.5
- gate_up_matrix: bfloat16 [896, 9728], P('wa'), may hold values from -0.1875 to 0.1875
- down_matrix: bfloat16 [4864, 896], P('wa'), may hold values from -0.078125 to 0.078125
- cotangent: bfloat16 [8, 2048, 896], P('wa', 'ctx'), may hold values from -6 to 6
Outputs:
- layer_output: bfloat16 [8, 2048, 896], P('wa', 'ctx')
- input_grad: float32 [8, 2048, 896], P('wa', 'ctx')
- attention_gain_grad: float32 [896], P('wa')
- projection_grad: float32 [896, 1152], P('wa')
- projection_bias_grad: float32 [1152], P('wa')
- output_weight_grad: float32 [896, 896], P('wa')
- feed_gain_grad: float32 [896], P('wa')
- gate_up_grad: float32 [896, 9728], P('wa')
- down_grad: float32 [4864, 896], P('wa')
The draws below stay inside these ranges and needn't reach their ends.
Inputs may be any that keep to these rules, and one draw needn't show every extreme that they name: `positions`: each sequence is a run of documents: the first token of a sequence has position 0, and every later token has position 0 (it opens a document) or one more than the token before. The first sequence is one document over all 2048 tokens.
All inputs are finite; a program needn't handle non-finite values.
Results may differ from the reference program's by a relative error of at most 0.024.
Values may be sent and summed in bfloat16 or wider, within the bound.
No kernel may reach another device: no remote copies, remote signals or barrier semaphores. Data moves between devices by JAX's collectives and lax.ppermute only.
A program may use at most 128 MiB of HBM per device.

```python
import math
import jax
import jax.numpy as jnp
from jax import lax

D = 896
QUERY_HEADS = 14
KEY_VALUE_HEADS = 2
HEAD_SIZE = 64
FF = 4864
TOK_DEV = 128
QD = 896
E = 1152
SEQUENCE_LENGTH = 2048
SEQUENCE_COUNT = 8


def draw_positions(key, part):
    key = jax.random.fold_in(key, 7)
    first_key, second_key = jax.random.split(key)
    opening = jax.random.randint(first_key, (SEQUENCE_COUNT, 1), 0, TOK_DEV // 2 + 1)
    closing = jax.random.randint(second_key, (SEQUENCE_COUNT, 1), SEQUENCE_LENGTH - TOK_DEV // 2, SEQUENCE_LENGTH + 1)
    leading = jnp.arange(SEQUENCE_COUNT, dtype=jnp.int32)[:, None] == 0
    opening = jnp.where(leading, 0, opening)
    closing = jnp.where(leading, SEQUENCE_LENGTH, closing)
    places = jnp.arange(SEQUENCE_LENGTH, dtype=jnp.int32)[None, :]
    inside = jnp.where(places < closing, places - opening, places - closing)
    return jnp.where(places < opening, places, inside).astype(jnp.int32)


def spiked(entries, rng, source, target, parts, factor):
    owner, partner = [(jnp.arange(entries.shape[position]) // (entries.shape[position] // parts)).reshape([-1 if axis == position else 1 for axis in range(entries.ndim)]) for position in (source, target)]
    chosen = jax.random.permutation(rng, parts)[partner]
    strong = (owner == chosen) | (owner == (partner + parts // 2) % parts)
    return jnp.where(strong, factor * entries, entries)


def block_scale(key, dims, cuts, least, top_value):
    def one(axis_at, blocks):
        draws = jax.random.uniform(jax.random.fold_in(jax.random.fold_in(key, 6), axis_at), (blocks,), jnp.float32, least / len(cuts), top_value / len(cuts))
        return jnp.repeat(jnp.exp(draws), dims[axis_at] // blocks).reshape((-1,) + (1,) * (len(dims) - axis_at - 1))

    loudness = one(*cuts[0])
    for cut in cuts[1:]:
        loudness = loudness * one(*cut)
    return loudness


def gaussian(rng, shape, deviation, most, pieces=(), kind=jnp.bfloat16):
    drawn = deviation * jax.random.normal(rng, shape, jnp.float32)
    if pieces:
        drawn = drawn * block_scale(rng, shape, pieces, -0.22, 0.18)
    return jnp.clip(drawn, -most, most).astype(kind)


def heavy_noise(stream_key, dims, spread, most, cuts, heavy, held_as=jnp.bfloat16):
    values = spread * jax.random.normal(stream_key, dims, jnp.float32)
    if cuts:
        values = values * block_scale(stream_key, dims, cuts, -0.22, 0.18)
    return jnp.clip(spiked(values, jax.random.fold_in(stream_key, 3), *heavy), -most, most).astype(held_as)


def setup_inputs(seed: int = 0) -> dict:
    seeds = jax.random.split(jax.random.key(seed), 11)
    return {
        "layer_input": heavy_noise(seeds[0], (SEQUENCE_COUNT, SEQUENCE_LENGTH, D), 1.0, 6.0, ((0, 8), (1, 16)), (1, 2, 16, 2.0)),
        "positions": draw_positions(jax.random.fold_in(seeds[10], 71), 0),
        "attention_gain": jnp.clip(1.0 + 0.1 * jax.random.normal(seeds[2], (D,), jnp.float32), 0.5, 1.5).astype(jnp.bfloat16),
        "projection": gaussian(seeds[3], (D, E), D ** -0.5, 0.1875, ((0, 8),)),
        "projection_biases": gaussian(seeds[4], (E,), 0.5, 3.0, ((0, 8),)),
        "output_matrix": gaussian(seeds[5], (QD, D), (max(QD // 256, 1)) ** -0.5, 3.5, ((0, 8),)),
        "feed_gain": jnp.clip(1.0 + 0.1 * jax.random.normal(seeds[6], (D,), jnp.float32), 0.5, 1.5).astype(jnp.bfloat16),
        "gate_up_matrix": gaussian(seeds[7], (D, 2 * FF), D ** -0.5, 0.1875, ((0, 8),)),
        "down_matrix": gaussian(seeds[8], (FF, D), FF ** -0.5, 0.078125, ((0, 8),)),
        "cotangent": gaussian(seeds[9], (SEQUENCE_COUNT, SEQUENCE_LENGTH, D), 1.0, 6.0, ((0, 8), (1, 16))),
    }


EPS = 1e-06
THETA = 1000000.0
NEG = -1e+30
HIGH_PRECISION = lax.Precision.HIGHEST

@jax.custom_vjp
def low(v):
    return lax.optimization_barrier(v.astype(jnp.bfloat16)).astype(jnp.float32)

@jax.custom_vjp
def lower_restored(v):
    return v

def low_keep(v):
    return (low(v), None)

def low_pass(kept, grad):
    return (grad,)

def back_keep(v):
    return (v, None)

def back_low(kept, grad):
    return (low(grad),)
low.defvjp(low_keep, low_pass)
lower_restored.defvjp(back_keep, back_low)

def norm_rows(value, gain):
    return value * lax.rsqrt(lax.optimization_barrier(jnp.mean(value * value, axis=-1, keepdims=True)) + EPS) * gain

def rotate(tensor, cosine_table, sine_table):
    half = tensor.shape[-1] // 2
    first = tensor[..., :half]
    second = tensor[..., half:]
    return jnp.concatenate([first * cosine_table - second * sine_table, second * cosine_table + first * sine_table], axis=-1)

def angles(positions):
    half = HEAD_SIZE // 2
    inverse = THETA ** (-(jnp.arange(half) * 2.0 / HEAD_SIZE))
    turned = positions.astype(jnp.float32)[..., None] * inverse.astype(jnp.float32)
    return (jnp.cos(turned), jnp.sin(turned))

def query_block(query_rows, seq_keys, seq_values, query_pos, block_start):
    block_count = query_rows.shape[0]
    grouped_queries = query_rows.reshape(block_count, KEY_VALUE_HEADS, QUERY_HEADS // KEY_VALUE_HEADS, HEAD_SIZE)
    raw = jnp.einsum('cmxz,omz->mxco', grouped_queries, seq_keys, precision=HIGH_PRECISION) * HEAD_SIZE ** (-0.5)
    scores = lower_restored(raw)
    gap = (block_start + jnp.arange(block_count))[:, None] - jnp.arange(seq_keys.shape[0])[None, :]
    seen = (gap >= 0) & (gap <= query_pos[:, None])
    masked = jnp.where(seen, scores, NEG)
    peak = lax.optimization_barrier(jnp.max(masked, axis=-1, keepdims=True))
    lifted = jnp.where(seen, jnp.exp(masked - peak), 0.0)
    probs = low(lifted / lax.optimization_barrier(jnp.sum(lifted, axis=-1, keepdims=True)))
    mixed = jnp.einsum('kgts,skd->tkgd', probs, seq_values, precision=HIGH_PRECISION)
    return mixed.reshape(block_count, QUERY_HEADS * HEAD_SIZE)

def attend(query_rows, key_rows, value_rows, positions):
    token_block = math.gcd(512, SEQUENCE_LENGTH)
    block_count = SEQUENCE_LENGTH // token_block
    starts = jnp.arange(block_count) * token_block

    def one_sequence(packed):
        seq_queries, seq_keys, seq_values, seq_pos = packed

        def one_block(inner):
            return jax.checkpoint(query_block)(inner[0], seq_keys, seq_values, inner[1], inner[2])
        mixed = lax.map(one_block, (seq_queries.reshape(block_count, token_block, QUERY_HEADS * HEAD_SIZE), seq_pos.reshape(block_count, token_block), starts))
        return mixed.reshape(SEQUENCE_LENGTH, QUERY_HEADS * HEAD_SIZE)
    return lax.map(jax.checkpoint(one_sequence), (query_rows, key_rows, value_rows, positions))

def forward(decoder_layer, attention_gain, projection, projection_biases, output_matrix, feed_gain, gate_up_matrix, down_matrix, positions):
    query_total_width = QUERY_HEADS * HEAD_SIZE
    key_total_width = KEY_VALUE_HEADS * HEAD_SIZE
    first_normed = low(norm_rows(decoder_layer, attention_gain))
    projected_rows = lower_restored(jnp.einsum('kwt,to->kwo', first_normed, projection, precision=HIGH_PRECISION) + projection_biases)
    cosine_table, sine_table = angles(positions)
    cosine_table = cosine_table[:, :, None, :]
    sine_table = sine_table[:, :, None, :]
    query_rows = projected_rows[..., :query_total_width].reshape(SEQUENCE_COUNT, SEQUENCE_LENGTH, QUERY_HEADS, HEAD_SIZE)
    key_rows = projected_rows[..., query_total_width:query_total_width + key_total_width].reshape(SEQUENCE_COUNT, SEQUENCE_LENGTH, KEY_VALUE_HEADS, HEAD_SIZE)
    value_rows = projected_rows[..., query_total_width + key_total_width:].reshape(SEQUENCE_COUNT, SEQUENCE_LENGTH, KEY_VALUE_HEADS, HEAD_SIZE)
    query_rows = low(rotate(query_rows, cosine_table, sine_table))
    key_rows = low(rotate(key_rows, cosine_table, sine_table))
    value_rows = low(value_rows)
    mixed = attend(query_rows.reshape(SEQUENCE_COUNT, SEQUENCE_LENGTH, query_total_width), key_rows, value_rows, positions)
    attention_output = low(lower_restored(mixed))
    middle_state = decoder_layer + lower_restored(jnp.einsum('ipw,wo->ipo', attention_output, output_matrix, precision=HIGH_PRECISION))
    second_normed = low(norm_rows(middle_state, feed_gain))
    joined_heads = lower_restored(jnp.einsum('qix,xg->qig', second_normed, gate_up_matrix, precision=HIGH_PRECISION))
    hidden_state = low(jax.nn.silu(joined_heads[..., :FF]) * joined_heads[..., FF:])
    return middle_state + lower_restored(jnp.einsum('xuq,qy->xuy', hidden_state, down_matrix, precision=HIGH_PRECISION))

def reference(layer_input, positions, attention_gain, projection, projection_biases, output_matrix, feed_gain, gate_up_matrix, down_matrix, cotangent):
    params = (attention_gain, projection, projection_biases, output_matrix, feed_gain, gate_up_matrix, down_matrix)
    params = tuple((item.astype(jnp.float32) for item in params))

    def wrapped(decoder_layer, gain_one, proj, bias, out_weight, gain_two, gate_up, down):
        return forward(decoder_layer, gain_one, proj, bias, out_weight, gain_two, gate_up, down, positions)
    result, pull = jax.vjp(wrapped, layer_input.astype(jnp.float32), *params)
    grads = pull(cotangent.astype(jnp.float32))
    return (result.astype(jnp.bfloat16), grads[0], grads[1], grads[2], grads[3], grads[4], grads[5], grads[6], grads[7])
```

```python
import math

import jax
import jax.numpy as jnp
from jax import lax
from jax.sharding import PartitionSpec as P

QUERY_HEADS = 14
KEY_VALUE_HEADS = 2
HEAD_SIZE = 64
FF = 4864


EPS = 1e-06
THETA = 1000000.0
NEG = -1e30


def rows_product(left, right):
    return lax.dot_general(
        left, right, (((0,), (0,)), ((), ())), preferred_element_type=jnp.float32
    )


def column_product(left, right):
    return lax.dot_general(
        left, right, (((1,), (1,)), ((), ())), preferred_element_type=jnp.float32
    )


def norm_rows(value, gain):
    return value * lax.rsqrt(jnp.mean(value * value, axis=-1, keepdims=True) + EPS) * gain


def rotate(tensor, cosine_table, sine_table):
    half = tensor.shape[-1] // 2
    first = tensor[..., :half]
    second = tensor[..., half:]
    return jnp.concatenate(
        [first * cosine_table - second * sine_table, second * cosine_table + first * sine_table],
        axis=-1,
    )


def inverse_rotate(tensor, cosine_table, sine_table):
    half = tensor.shape[-1] // 2
    first = tensor[..., :half]
    second = tensor[..., half:]
    return jnp.concatenate(
        [first * cosine_table + second * sine_table, second * cosine_table - first * sine_table],
        axis=-1,
    )


def angles(positions):
    half = HEAD_SIZE // 2
    inverse = THETA ** (-(jnp.arange(half) * 2.0 / HEAD_SIZE))
    turned = positions.astype(jnp.float32)[:, None] * inverse.astype(jnp.float32)
    return (jnp.cos(turned), jnp.sin(turned))


def swiglu(joined_heads):
    return jax.nn.silu(joined_heads[:, :FF]) * joined_heads[:, FF:]


def block_scores(grouped_queries, key_rows, block_start, query_index, query_pos):
    block_count = key_rows.shape[0]
    raw = jnp.einsum(
        "cmxz,omz->mxco",
        grouped_queries,
        key_rows.reshape(block_count, KEY_VALUE_HEADS, HEAD_SIZE),
        preferred_element_type=jnp.float32,
    ) * HEAD_SIZE ** (-0.5)
    gap = query_index[:, None] - (block_start + jnp.arange(block_count))[None, :]
    seen = (gap >= 0) & (gap <= query_pos[:, None])
    return (jnp.where(seen, raw, NEG), seen)


def keep_carry(carry):
    return carry


def key_stats(grouped_queries, key_rows, query_index, query_pos, token_block):
    array_shape = (KEY_VALUE_HEADS, QUERY_HEADS // KEY_VALUE_HEADS, grouped_queries.shape[0])

    def visit(which, carry):
        block_start = which * token_block

        def update(state):
            peak, total = state
            token_piece = lax.dynamic_slice_in_dim(key_rows, block_start, token_block, 0)
            masked, seen = block_scores(
                grouped_queries, token_piece, block_start, query_index, query_pos
            )
            raised = jnp.maximum(peak, jnp.max(masked, axis=-1))
            added = jnp.sum(jnp.where(seen, jnp.exp(masked - raised[..., None]), 0.0), axis=-1)
            return (raised, total * jnp.exp(peak - raised) + added)

        return lax.cond(block_start <= query_index[-1], update, keep_carry, carry)

    start_state = (jnp.full(array_shape, NEG, jnp.float32), jnp.zeros(array_shape, jnp.float32))
    return lax.fori_loop(0, key_rows.shape[0] // token_block, visit, start_state)


def key_mix(
    grouped_queries, key_rows, value_rows, query_index, query_pos, peak, total, token_block
):
    array_shape = (
        grouped_queries.shape[0],
        KEY_VALUE_HEADS,
        QUERY_HEADS // KEY_VALUE_HEADS,
        HEAD_SIZE,
    )

    def visit(which, carry):
        block_start = which * token_block

        def update(mixed):
            token_piece = lax.dynamic_slice_in_dim(key_rows, block_start, token_block, 0)
            value_segment = lax.dynamic_slice_in_dim(
                value_rows, block_start, token_block, 0
            ).reshape(token_block, KEY_VALUE_HEADS, HEAD_SIZE)
            masked, seen = block_scores(
                grouped_queries, token_piece, block_start, query_index, query_pos
            )
            probs = jnp.where(seen, jnp.exp(masked - peak[..., None]) / total[..., None], 0.0)
            return mixed + jnp.einsum(
                "kgts,skd->tkgd",
                probs.astype(jnp.bfloat16),
                value_segment,
                preferred_element_type=jnp.float32,
            )

        return lax.cond(block_start <= query_index[-1], update, keep_carry, carry)

    return lax.fori_loop(
        0, key_rows.shape[0] // token_block, visit, jnp.zeros(array_shape, jnp.float32)
    )


def key_grads(
    grouped_queries,
    key_rows,
    value_rows,
    mix_grad,
    delta,
    query_index,
    query_pos,
    peak,
    total,
    token_block,
):
    length = key_rows.shape[0]
    model_width = KEY_VALUE_HEADS * HEAD_SIZE

    def visit(which, carry):
        block_start = which * token_block

        def update(state):
            query_grad, key_grad, value_grad = state
            token_piece = lax.dynamic_slice_in_dim(key_rows, block_start, token_block, 0)
            value_segment = lax.dynamic_slice_in_dim(
                value_rows, block_start, token_block, 0
            ).reshape(token_block, KEY_VALUE_HEADS, HEAD_SIZE)
            masked, seen = block_scores(
                grouped_queries, token_piece, block_start, query_index, query_pos
            )
            probs = jnp.where(seen, jnp.exp(masked - peak[..., None]) / total[..., None], 0.0)
            prob_grad = jnp.einsum(
                "cmxz,omz->mxco", mix_grad, value_segment, preferred_element_type=jnp.float32
            )
            score_grad = (probs * (prob_grad - delta[..., None])).astype(jnp.bfloat16)
            query_grad = query_grad + jnp.einsum(
                "kgts,skd->tkgd",
                score_grad,
                token_piece.reshape(token_block, KEY_VALUE_HEADS, HEAD_SIZE),
                preferred_element_type=jnp.float32,
            )
            key_part = jnp.einsum(
                "kgts,tkgd->skd", score_grad, grouped_queries, preferred_element_type=jnp.float32
            ).reshape(token_block, model_width)
            value_part = jnp.einsum(
                "kgts,tkgd->skd",
                probs.astype(jnp.bfloat16),
                mix_grad,
                preferred_element_type=jnp.float32,
            ).reshape(token_block, model_width)
            key_grad = lax.dynamic_update_slice_in_dim(key_grad, key_part, block_start, 0)
            value_grad = lax.dynamic_update_slice_in_dim(value_grad, value_part, block_start, 0)
            return (query_grad, key_grad, value_grad)

        return lax.cond(block_start <= query_index[-1], update, keep_carry, carry)

    start_state = (
        jnp.zeros(grouped_queries.shape, jnp.float32),
        jnp.zeros((length, model_width), jnp.float32),
        jnp.zeros((length, model_width), jnp.float32),
    )
    return lax.fori_loop(0, length // token_block, visit, start_state)


def core_swap(value):
    return lax.ppermute(value, "wa", [(i, i ^ 1) for i in range(8)])


Z_GROUPS = [[0, 2, 4, 6], [1, 3, 5, 7]]


def z_exchange(value):
    return lax.all_to_all(value, "wa", 0, 0, tiled=True, axis_index_groups=Z_GROUPS)


def z_gather(value):
    return z_exchange(jnp.broadcast_to(value[None], (4,) + value.shape))


def ctx_exchange(value):
    return lax.all_to_all(value, "ctx", 0, 0, tiled=True)


def core_order(own, other, core, axis):
    first = jnp.where(core == 0, own, other)
    second = jnp.where(core == 0, other, own)
    return jnp.stack([first, second], axis=axis)


def gather_rows(value, core):
    own = z_gather(value)
    return core_order(own, core_swap(own), core, 1).reshape((8,) + value.shape)


def gather_tokens(value):
    own = z_gather(value)
    return jnp.concatenate([own, core_swap(own)], axis=0)


def reduce_tokens(partial):
    sent = core_swap(partial[4:].astype(jnp.bfloat16))
    mine = (partial[:4] + sent.astype(jnp.float32)).astype(jnp.bfloat16)
    return jnp.sum(z_exchange(mine).astype(jnp.float32), axis=0)


def reduce_rows(partial, core):
    pairs = partial.reshape((4, 2) + partial.shape[1:])
    kept = jnp.where(core == 0, pairs[:, 0], pairs[:, 1])
    sent = jnp.where(core == 0, pairs[:, 1], pairs[:, 0])
    mine = (kept.astype(jnp.float32) + core_swap(sent).astype(jnp.float32)).astype(jnp.bfloat16)
    return jnp.sum(z_exchange(mine).astype(jnp.float32), axis=0)


def on_device(
    layer_input,
    positions,
    attention_gain,
    projection,
    projection_biases,
    output_matrix,
    feed_gain,
    gate_up_matrix,
    down_matrix,
    cotangent,
):
    core = lax.axis_index("wa") % 2
    rows = projection.shape[0]
    tokens = layer_input.shape[1]
    head_group = QUERY_HEADS // KEY_VALUE_HEADS
    query_width = QUERY_HEADS * HEAD_SIZE
    key_width = KEY_VALUE_HEADS * HEAD_SIZE
    width = layer_input.shape[2]
    proj_width = projection.shape[1]
    bias_rows = projection_biases.shape[0]
    slice_width = down_matrix.shape[0]
    lanes = -(-slice_width // 128) * 128
    pad_rows = 16

    small = jnp.concatenate([projection_biases, attention_gain, feed_gain])
    small = jnp.pad(small[None], ((0, pad_rows - 1), (0, proj_width - small.shape[0])))
    packed = gather_rows(jnp.concatenate([projection, small], axis=0), core)
    full_proj = packed[:, :rows].reshape(width, proj_width)
    vectors = packed[:, rows].astype(jnp.float32)
    full_bias = vectors[:, :bias_rows].reshape(proj_width)
    gain_one = vectors[:, bias_rows : bias_rows + rows].reshape(width)
    gain_two = vectors[:, bias_rows + rows : bias_rows + 2 * rows].reshape(width)
    complete_output = lax.all_gather(output_matrix, "wa", axis=0, tiled=True)

    by_core = gate_up_matrix.reshape(rows, 2, 4, 2, slice_width)
    kept = jnp.where(core == 0, by_core[:, :, :, 0], by_core[:, :, :, 1])
    sent = jnp.where(core == 0, by_core[:, :, :, 1], by_core[:, :, :, 0])
    widen = ((0, 0), (0, 0), (0, 0), (0, lanes - slice_width))
    kept = jnp.pad(kept, widen).transpose(2, 0, 1, 3).reshape(4, rows, 2 * lanes)
    sent = jnp.pad(sent, widen).transpose(2, 0, 1, 3).reshape(4, rows, 2 * lanes)
    gate_up = z_exchange(core_order(kept, core_swap(sent), core, 1).reshape(4, 2 * rows, 2 * lanes))
    gate_up = gate_up.reshape(width, 2 * lanes)
    down = jnp.pad(down_matrix, ((0, lanes - slice_width), (0, 0)))

    out_grad = cotangent[0]
    all_out_grad = gather_tokens(out_grad).reshape(8 * tokens, width)

    decoder_layer = layer_input[0].astype(jnp.float32)
    query_pos = positions[0]
    query_index = lax.axis_index("ctx") * tokens + jnp.arange(tokens, dtype=jnp.int32)
    first_normed = norm_rows(decoder_layer, gain_one).astype(jnp.bfloat16)
    projected_rows = jnp.dot(first_normed, full_proj, preferred_element_type=jnp.float32) + full_bias
    cosine_table, sine_table = angles(query_pos)
    cosine_table = cosine_table[:, None, :]
    sine_table = sine_table[:, None, :]
    query_rows = rotate(
        projected_rows[:, :query_width].reshape(tokens, QUERY_HEADS, HEAD_SIZE),
        cosine_table,
        sine_table,
    ).astype(jnp.bfloat16)
    key_rows = rotate(
        projected_rows[:, query_width : query_width + key_width].reshape(
            tokens, KEY_VALUE_HEADS, HEAD_SIZE
        ),
        cosine_table,
        sine_table,
    )
    key_rows = key_rows.astype(jnp.bfloat16).reshape(tokens, key_width)
    value_rows = projected_rows[:, query_width + key_width :].astype(jnp.bfloat16)
    pair = jnp.concatenate([key_rows, value_rows], axis=1)
    pairs = ctx_exchange(jnp.broadcast_to(pair[None], (16,) + pair.shape))
    pairs = pairs.reshape(16 * tokens, 2 * key_width)
    all_keys, all_values = pairs[:, :key_width], pairs[:, key_width:]
    token_block = math.gcd(512, all_keys.shape[0])
    grouped_queries = query_rows.reshape(tokens, KEY_VALUE_HEADS, head_group, HEAD_SIZE)
    peak, total = key_stats(grouped_queries, all_keys, query_index, query_pos, token_block)
    mixed = key_mix(
        grouped_queries, all_keys, all_values, query_index, query_pos, peak, total, token_block
    )
    attention_output = mixed.reshape(tokens, query_width).astype(jnp.bfloat16)
    middle_state = decoder_layer + jnp.dot(
        attention_output, complete_output, preferred_element_type=jnp.float32
    )
    second_normed = norm_rows(middle_state, gain_two).astype(jnp.bfloat16)

    all_normed = gather_tokens(second_normed).reshape(8 * tokens, width)
    joined = jnp.dot(all_normed, gate_up, preferred_element_type=jnp.float32)
    gate, up = joined[:, :lanes], joined[:, lanes:]
    hidden_grad = column_product(all_out_grad, down)
    sg = jax.nn.sigmoid(gate)
    act = gate * sg
    hidden_state = (act * up).astype(jnp.bfloat16)
    gate_grad = hidden_grad * up * sg * (1.0 + gate * (1.0 - sg))
    up_grad = hidden_grad * act
    joined_grad = jnp.concatenate([gate_grad, up_grad], axis=1).astype(jnp.bfloat16)
    normed_two_grad = reduce_tokens(column_product(joined_grad, gate_up).reshape(8, tokens, width))
    feed_out = reduce_tokens(
        jnp.dot(hidden_state, down, preferred_element_type=jnp.float32).reshape(8, tokens, width)
    )
    result = (middle_state + feed_out).astype(jnp.bfloat16)
    down_local = rows_product(hidden_state, all_out_grad)[:slice_width].astype(jnp.bfloat16)
    gate_up_local = rows_product(all_normed, joined_grad).astype(jnp.bfloat16)
    by_rows = gate_up_local.reshape(4, 2, rows, 2 * lanes)
    kept = jnp.where(core == 0, by_rows[:, 0], by_rows[:, 1])
    sent = jnp.where(core == 0, by_rows[:, 1], by_rows[:, 0])
    gate_up_rows = z_exchange(
        core_order(kept, core_swap(sent), core, 1).reshape(4, 2 * rows, 2 * lanes)
    )
    gate_up_rows = gate_up_rows.reshape(4, 2, rows, 2, lanes)[..., :slice_width]
    gate_up_rows = gate_up_rows.transpose(2, 3, 0, 1, 4).reshape(rows, 16 * slice_width)
    gate_up_total, down_total = lax.psum((gate_up_rows, down_local), "ctx")

    _, norm_two_pull = jax.vjp(norm_rows, middle_state, gain_two)
    middle_part, gain_two_local = norm_two_pull(normed_two_grad)
    middle_grad = out_grad.astype(jnp.float32) + middle_part
    middle_lower = middle_grad.astype(jnp.bfloat16)
    out_weight_local = rows_product(attention_output, middle_lower).astype(jnp.bfloat16)
    out_weight_rows = lax.psum_scatter(out_weight_local, "wa", scatter_dimension=0, tiled=True)
    mix_grad = (
        column_product(middle_lower, complete_output)
        .astype(jnp.bfloat16)
        .reshape(tokens, KEY_VALUE_HEADS, head_group, HEAD_SIZE)
    )
    delta = jnp.einsum("tkgd,tkgd->kgt", mix_grad.astype(jnp.float32), mixed)
    query_grad, key_grad, value_grad = key_grads(
        grouped_queries,
        all_keys,
        all_values,
        mix_grad,
        delta,
        query_index,
        query_pos,
        peak,
        total,
        token_block,
    )
    pair_grad = jnp.concatenate([key_grad, value_grad], axis=1).astype(jnp.bfloat16)
    pair_grad = jnp.sum(
        ctx_exchange(pair_grad.reshape(16, tokens, 2 * key_width)).astype(jnp.float32), axis=0
    )
    score_scale = HEAD_SIZE ** (-0.5)
    query_back = inverse_rotate(
        (query_grad * score_scale).reshape(tokens, QUERY_HEADS, HEAD_SIZE),
        cosine_table,
        sine_table,
    ).reshape(tokens, query_width)
    key_restored = inverse_rotate(
        (pair_grad[:, :key_width] * score_scale).reshape(tokens, KEY_VALUE_HEADS, HEAD_SIZE),
        cosine_table,
        sine_table,
    ).reshape(tokens, key_width)
    projected_grad = jnp.concatenate(
        [query_back, key_restored, pair_grad[:, key_width:]], axis=1
    ).astype(jnp.bfloat16)
    proj_local = rows_product(first_normed, projected_grad).astype(jnp.bfloat16)
    bias_local = jnp.sum(projected_grad.astype(jnp.float32), axis=0)
    normed_one_grad = column_product(projected_grad, full_proj)
    _, norm_one_pull = jax.vjp(norm_rows, decoder_layer, gain_one)
    layer_part, gain_one_local = norm_one_pull(normed_one_grad)
    input_grad = middle_grad + layer_part

    small = jnp.concatenate(
        [
            bias_local.reshape(8, bias_rows),
            gain_one_local.reshape(8, rows),
            gain_two_local.reshape(8, rows),
        ],
        axis=1,
    ).astype(jnp.bfloat16)
    small = jnp.pad(small[:, None], ((0, 0), (0, pad_rows - 1), (0, proj_width - small.shape[1])))
    mine = reduce_rows(
        jnp.concatenate([proj_local.reshape(8, rows, proj_width), small], axis=1), core
    ).astype(jnp.bfloat16)
    out_weight_rows = jnp.pad(out_weight_rows, ((0, pad_rows), (0, 0)))
    mine = jnp.concatenate([mine, out_weight_rows], axis=1)
    columns = mine.shape[1] // 16
    mine = mine.reshape(rows + pad_rows, 16, columns).transpose(1, 0, 2)
    mine = jnp.sum(ctx_exchange(mine).astype(jnp.float32), axis=0).astype(jnp.bfloat16)
    mine = ctx_exchange(jnp.broadcast_to(mine[None], (16,) + mine.shape))
    mine = mine.transpose(1, 0, 2).reshape(rows + pad_rows, 16 * columns).astype(jnp.float32)
    vectors = mine[rows]
    return (
        result[None],
        input_grad[None],
        vectors[bias_rows : bias_rows + rows],
        mine[:rows, :proj_width],
        vectors[:bias_rows],
        mine[:rows, proj_width:],
        vectors[bias_rows + rows : bias_rows + 2 * rows],
        gate_up_total.astype(jnp.float32),
        down_total.astype(jnp.float32),
    )


def solution(mesh):
    placed = (
        P("wa", "ctx", None),
        P("wa", "ctx"),
        P("wa"),
        P("wa", None),
        P("wa"),
        P("wa", None),
        P("wa"),
        P("wa", None),
        P("wa", None),
        P("wa", "ctx", None),
    )
    return jax.shard_map(
        on_device,
        mesh=mesh,
        in_specs=placed,
        out_specs=(
            P("wa", "ctx", None),
            P("wa", "ctx", None),
            P("wa"),
            P("wa", None),
            P("wa"),
            P("wa", None),
            P("wa"),
            P("wa", None),
            P("wa", None),
        ),
        check_vma=False,
    )
```

```python
import math

import jax
import jax.numpy as jnp
from jax import lax
from jax.experimental import pallas as pl
from jax.experimental.pallas import tpu as pltpu
from jax.sharding import PartitionSpec as P

QUERY_HEADS = 14
KEY_VALUE_HEADS = 2
HEAD_SIZE = 64
FF = 4864


EPS = 1e-06
THETA = 1000000.0
NEG = -1e30
BLOCK = 512


def rows_product(left, right):
    return lax.dot_general(
        left, right, (((0,), (0,)), ((), ())), preferred_element_type=jnp.float32
    )


def column_product(left, right):
    return lax.dot_general(
        left, right, (((1,), (1,)), ((), ())), preferred_element_type=jnp.float32
    )


def norm_rows(value, gain):
    return value * lax.rsqrt(jnp.mean(value * value, axis=-1, keepdims=True) + EPS) * gain


def rotate(tensor, cosine_table, sine_table):
    half = tensor.shape[-1] // 2
    first = tensor[..., :half]
    second = tensor[..., half:]
    return jnp.concatenate(
        [first * cosine_table - second * sine_table, second * cosine_table + first * sine_table],
        axis=-1,
    )


def inverse_rotate(tensor, cosine_table, sine_table):
    half = tensor.shape[-1] // 2
    first = tensor[..., :half]
    second = tensor[..., half:]
    return jnp.concatenate(
        [first * cosine_table + second * sine_table, second * cosine_table - first * sine_table],
        axis=-1,
    )


def angles(positions):
    half = HEAD_SIZE // 2
    inverse = THETA ** (-(jnp.arange(half) * 2.0 / HEAD_SIZE))
    turned = positions.astype(jnp.float32)[:, None] * inverse.astype(jnp.float32)
    return (jnp.cos(turned), jnp.sin(turned))


def key_bias(low_ref, block_start, block, first_index):
    tokens = low_ref.shape[1]
    keys = block_start + lax.broadcasted_iota(jnp.int32, (block, tokens), 0)
    index = first_index + lax.broadcasted_iota(jnp.int32, (block, tokens), 1)
    return jnp.where((keys <= index) & (keys >= low_ref[...]), 0.0, NEG)


def head_places(tokens):
    group = QUERY_HEADS // KEY_VALUE_HEADS
    for h in range(QUERY_HEADS):
        g, i = divmod(h, group)
        yield g, slice(h * HEAD_SIZE, (h + 1) * HEAD_SIZE), slice(i * tokens, (i + 1) * tokens)


def attend_kernel(
    start_ref, q_ref, kv_ref, low_ref, mixed_ref, lse_ref, qt, s_ref, p_ref, bias_ref, m_ref, l_ref, acc_ref
):
    tokens = q_ref.shape[0]
    block, rows = s_ref.shape
    turned = (q_ref[...].astype(jnp.float32) * HEAD_SIZE ** (-0.5)).T.astype(jnp.bfloat16)
    for g, lanes, at in head_places(tokens):
        qt[g, :, at] = turned[lanes, :]
    m_ref[...] = jnp.full_like(m_ref, NEG)
    l_ref[...] = jnp.zeros_like(l_ref)
    acc_ref[...] = jnp.zeros_like(acc_ref)

    def visit(which, carry):
        block_start = pl.multiple_of(which * block, block)
        here = pl.ds(block_start, block)
        bias_ref[...] = key_bias(low_ref, block_start, block, start_ref[0])
        key_width = KEY_VALUE_HEADS * HEAD_SIZE
        values = kv_ref[here, key_width:].astype(jnp.float32).T.astype(jnp.bfloat16)
        for g in range(KEY_VALUE_HEADS):
            lanes = slice(g * HEAD_SIZE, (g + 1) * HEAD_SIZE)
            s_ref[...] = jnp.dot(kv_ref[here, lanes], qt[g], preferred_element_type=jnp.float32)
            for i in range(rows // tokens):
                at = slice(i * tokens, (i + 1) * tokens)
                s = s_ref[:, at] + bias_ref[...]
                old = m_ref[g, :, at]
                peak = jnp.maximum(old, jnp.max(s, axis=0, keepdims=True))
                e = jnp.exp(s - peak)
                scale = jnp.exp(old - peak)
                m_ref[g, :, at] = peak
                l_ref[g, :, at] = l_ref[g, :, at] * scale + jnp.sum(e, axis=0, keepdims=True)
                acc_ref[g, :, at] = acc_ref[g, :, at] * scale
                p_ref[:, at] = e.astype(jnp.bfloat16)
            acc_ref[g] += jnp.dot(values[lanes, :], p_ref[...], preferred_element_type=jnp.float32)
        return carry

    lax.fori_loop(start_ref[1], start_ref[2], visit, 0)
    mixed = [acc_ref[g, :, at] / l_ref[g, :, at] for g, _, at in head_places(tokens)]
    mixed_ref[...] = jnp.concatenate(mixed, axis=0).T
    lse_ref[...] = m_ref[...] + jnp.log(l_ref[...])


def attend_back_kernel(
    start_ref, q_ref, kv_ref, low_ref, dmix_ref, mixed_ref, lse_ref, dq_ref, dkv_ref,
    qs, qt, ms, mt, delta_ref, s_ref, dp_ref, p_ref, g_ref, bias_ref, acc_ref,
):
    tokens = q_ref.shape[0]
    block, rows = s_ref.shape
    key_width = KEY_VALUE_HEADS * HEAD_SIZE
    q = q_ref[...].astype(jnp.float32) * HEAD_SIZE ** (-0.5)
    dmix = dmix_ref[...].astype(jnp.float32)
    q_turned = q.T.astype(jnp.bfloat16)
    dmix_turned = dmix.T
    weighed = (dmix * mixed_ref[...]).T
    q = q.astype(jnp.bfloat16)
    for g, lanes, at in head_places(tokens):
        qs[g, at, :] = q[:, lanes]
        ms[g, at, :] = dmix_ref[:, lanes]
        qt[g, :, at] = q_turned[lanes, :]
        mt[g, :, at] = dmix_turned[lanes, :].astype(jnp.bfloat16)
        delta_ref[g, :, at] = jnp.sum(weighed[lanes, :], axis=0, keepdims=True)
    acc_ref[...] = jnp.zeros_like(acc_ref)
    dkv_ref[...] = jnp.zeros_like(dkv_ref)

    def visit(which, carry):
        block_start = pl.multiple_of(which * block, block)
        here = pl.ds(block_start, block)
        bias_ref[...] = key_bias(low_ref, block_start, block, start_ref[0])
        keys_turned = kv_ref[here, :key_width].astype(jnp.float32).T.astype(jnp.bfloat16)
        grads = [None] * (2 * KEY_VALUE_HEADS)
        for g in range(KEY_VALUE_HEADS):
            lanes = slice(g * HEAD_SIZE, (g + 1) * HEAD_SIZE)
            s_ref[...] = jnp.dot(kv_ref[here, lanes], qt[g], preferred_element_type=jnp.float32)
            values = kv_ref[here, key_width + g * HEAD_SIZE : key_width + (g + 1) * HEAD_SIZE]
            dp_ref[...] = jnp.dot(values, mt[g], preferred_element_type=jnp.float32)
            for i in range(rows // tokens):
                at = slice(i * tokens, (i + 1) * tokens)
                p = jnp.exp(s_ref[:, at] + bias_ref[...] - lse_ref[g, :, at])
                p_ref[:, at] = p.astype(jnp.bfloat16)
                g_ref[:, at] = (p * (dp_ref[:, at] - delta_ref[g, :, at])).astype(jnp.bfloat16)
            acc_ref[g] += jnp.dot(keys_turned[lanes, :], g_ref[...], preferred_element_type=jnp.float32)
            grads[g] = jnp.dot(g_ref[...], qs[g], preferred_element_type=jnp.float32)
            grads[KEY_VALUE_HEADS + g] = jnp.dot(
                p_ref[...], ms[g], preferred_element_type=jnp.float32
            )
        dkv_ref[here, :] = jnp.concatenate(grads, axis=1).astype(jnp.bfloat16)
        return carry

    lax.fori_loop(start_ref[1], start_ref[2], visit, 0)
    dq = [acc_ref[g, :, at] for g, _, at in head_places(tokens)]
    dq_ref[...] = jnp.concatenate(dq, axis=0).T * HEAD_SIZE ** (-0.5)


def in_vmem():
    return pl.BlockSpec(memory_space=pltpu.VMEM)


def attend(start, queries, pairs, low):
    tokens, width = queries.shape
    rows = QUERY_HEADS // KEY_VALUE_HEADS * tokens
    block = math.gcd(BLOCK, pairs.shape[0])
    heads = KEY_VALUE_HEADS
    return pl.pallas_call(
        attend_kernel,
        out_shape=(
            jax.ShapeDtypeStruct((tokens, width), jnp.float32),
            jax.ShapeDtypeStruct((heads, 1, rows), jnp.float32),
        ),
        in_specs=[pl.BlockSpec(memory_space=pltpu.SMEM)] + [in_vmem()] * 3,
        out_specs=(in_vmem(), in_vmem()),
        scratch_shapes=[
            pltpu.VMEM((heads, HEAD_SIZE, rows), jnp.bfloat16),
            pltpu.VMEM((block, rows), jnp.float32),
            pltpu.VMEM((block, rows), jnp.bfloat16),
            pltpu.VMEM((block, tokens), jnp.float32),
            pltpu.VMEM((heads, 1, rows), jnp.float32),
            pltpu.VMEM((heads, 1, rows), jnp.float32),
            pltpu.VMEM((heads, HEAD_SIZE, rows), jnp.float32),
        ],
        compiler_params=pltpu.CompilerParams(vmem_limit_bytes=32 * 2**20),
        cost_estimate=pl.CostEstimate(
            flops=16 * tokens * width * pairs.shape[0], bytes_accessed=2 * 2**20, transcendentals=0
        ),
        name="attend",
    )(start, queries, pairs, low)


def attend_back(start, queries, pairs, low, mix_grad, mixed, lse):
    tokens, width = queries.shape
    rows = QUERY_HEADS // KEY_VALUE_HEADS * tokens
    block = math.gcd(BLOCK, pairs.shape[0])
    heads = KEY_VALUE_HEADS
    return pl.pallas_call(
        attend_back_kernel,
        out_shape=(
            jax.ShapeDtypeStruct((tokens, width), jnp.float32),
            jax.ShapeDtypeStruct(pairs.shape, jnp.bfloat16),
        ),
        in_specs=[pl.BlockSpec(memory_space=pltpu.SMEM)] + [in_vmem()] * 6,
        out_specs=(in_vmem(), in_vmem()),
        scratch_shapes=[
            pltpu.VMEM((heads, rows, HEAD_SIZE), jnp.bfloat16),
            pltpu.VMEM((heads, HEAD_SIZE, rows), jnp.bfloat16),
            pltpu.VMEM((heads, rows, HEAD_SIZE), jnp.bfloat16),
            pltpu.VMEM((heads, HEAD_SIZE, rows), jnp.bfloat16),
            pltpu.VMEM((heads, 1, rows), jnp.float32),
            pltpu.VMEM((block, rows), jnp.float32),
            pltpu.VMEM((block, rows), jnp.float32),
            pltpu.VMEM((block, rows), jnp.bfloat16),
            pltpu.VMEM((block, rows), jnp.bfloat16),
            pltpu.VMEM((block, tokens), jnp.float32),
            pltpu.VMEM((heads, HEAD_SIZE, rows), jnp.float32),
        ],
        compiler_params=pltpu.CompilerParams(vmem_limit_bytes=40 * 2**20),
        cost_estimate=pl.CostEstimate(
            flops=40 * tokens * width * pairs.shape[0], bytes_accessed=4 * 2**20, transcendentals=0
        ),
        name="attend_back",
    )(start, queries, pairs, low, mix_grad, mixed, lse)


def split_kernel(place_ref, matrix_ref, kept_ref, sent_ref):
    z, core = place_ref[0], place_ref[1]
    width, lanes = matrix_ref.shape[1] // 16, kept_ref.shape[2] // 2
    for owner in range(8):
        at = lax.rem(owner // 2 - z + 4, 4)
        gate = matrix_ref[:, owner * width : (owner + 1) * width].astype(jnp.float32)
        up = matrix_ref[:, (8 + owner) * width : (9 + owner) * width].astype(jnp.float32)
        blank = jnp.zeros((gate.shape[0], lanes - width), jnp.float32)
        both = jnp.concatenate([gate, blank, up, blank], axis=1).astype(jnp.bfloat16)

        @pl.when(core == owner % 2)
        def _(both=both, at=at):
            kept_ref[at] = both

        @pl.when(core != owner % 2)
        def _(both=both, at=at):
            sent_ref[at] = both


def split_columns(place, matrix, lanes):
    rows = matrix.shape[0]
    out = jax.ShapeDtypeStruct((4, rows, 2 * lanes), matrix.dtype)
    return pl.pallas_call(
        split_kernel,
        out_shape=(out, out),
        in_specs=[pl.BlockSpec(memory_space=pltpu.SMEM), in_vmem()],
        out_specs=(in_vmem(), in_vmem()),
        compiler_params=pltpu.CompilerParams(vmem_limit_bytes=32 * 2**20),
        name="split_columns",
    )(place, matrix)


def place_kernel(at_ref, *refs):
    pieces, out_ref = refs[:-1], refs[-1]
    rows = pieces[0].shape[0]
    for n, piece in enumerate(pieces):
        out_ref[pl.ds(pl.multiple_of(at_ref[n] * rows, 16), rows), :] = piece[...]


def place_rows(at, pieces):
    rows, width = pieces[0].shape
    return pl.pallas_call(
        place_kernel,
        out_shape=jax.ShapeDtypeStruct((len(pieces) * rows, width), pieces[0].dtype),
        in_specs=[pl.BlockSpec(memory_space=pltpu.SMEM)] + [in_vmem()] * len(pieces),
        out_specs=in_vmem(),
        compiler_params=pltpu.CompilerParams(vmem_limit_bytes=32 * 2**20),
        name="place_rows",
    )(at, *pieces)


def join_kernel(parts_ref, gate_up_ref, down_ref, stage_ref):
    lanes = parts_ref.shape[2]
    width = gate_up_ref.shape[1] // 16
    tile = 16
    for part in range(2 * gate_up_ref.shape[0] // tile):
        r, half = divmod(part, 2)
        columns = [
            parts_ref[part, k * tile : (k + 1) * tile, :].astype(jnp.float32)[:, :width]
            for k in range(8)
        ]
        gate_up_ref[r * tile : (r + 1) * tile, half * 8 * width : (half + 1) * 8 * width] = (
            jnp.concatenate(columns, axis=1)
        )
    rows = stage_ref.shape[0] // 16
    for part in range(16):
        stage_ref[part * rows : (part + 1) * rows, :] = parts_ref[part, 8 * tile :, :].astype(
            jnp.float32
        )[:rows]
    for block in range(stage_ref.shape[0] // 128):
        at = slice(block * 128, (block + 1) * 128)
        down_ref[:, at] = stage_ref[at, :].T[:width]


def join_columns(parts, rows, width, model_width):
    return pl.pallas_call(
        join_kernel,
        out_shape=(
            jax.ShapeDtypeStruct((rows, 16 * width), jnp.float32),
            jax.ShapeDtypeStruct((width, model_width), jnp.float32),
        ),
        in_specs=[in_vmem()],
        out_specs=(in_vmem(), in_vmem()),
        scratch_shapes=[pltpu.VMEM((model_width, parts.shape[2]), jnp.float32)],
        compiler_params=pltpu.CompilerParams(vmem_limit_bytes=40 * 2**20),
        name="join_columns",
    )(parts)


def core_swap(value):
    return lax.ppermute(value, "wa", [(i, i ^ 1) for i in range(8)])


def z_shift(value, step):
    return lax.ppermute(value, "wa", [(i, (i + 2 * step) % 8) for i in range(8)])


def ctx_exchange(value):
    return lax.all_to_all(value, "ctx", 0, 0, tiled=True)


def ctx_gather(value):
    return ctx_exchange(jnp.broadcast_to(value[None], (16,) + value.shape))


STEPS = (0, 1, 3, 2)


def gather_tokens(value):
    pieces = [z_shift(value, step) if step else value for step in STEPS]
    return [jnp.concatenate([piece, core_swap(piece)], axis=0) for piece in pieces]


def reduce_tokens(partials):
    total = 0.0
    for step, partial in zip(STEPS, partials):
        rows = partial.shape[0] // 2
        other = core_swap(partial[rows:].astype(jnp.bfloat16)).astype(jnp.float32)
        if step:
            mine = z_shift((partial[:rows] + other).astype(jnp.bfloat16), -step).astype(jnp.float32)
        else:
            mine = partial[:rows] + other
        total = total + mine
    return total


def reduce_rows(partial, z, core):
    pairs = partial.reshape((4, 2) + partial.shape[1:])
    other = core_swap(jnp.where(core == 0, pairs[:, 1], pairs[:, 0]))
    total = 0.0
    for step in STEPS:
        at = (z + step) % 4
        mine = lax.dynamic_index_in_dim(partial, 2 * at + core, 0, keepdims=False)
        mine = mine.astype(jnp.float32) + lax.dynamic_index_in_dim(
            other, at, 0, keepdims=False
        ).astype(jnp.float32)
        if step:
            mine = z_shift(mine.astype(jnp.bfloat16), step).astype(jnp.float32)
        total = total + mine
    return total


def on_device(
    layer_input,
    positions,
    attention_gain,
    projection,
    projection_biases,
    output_matrix,
    feed_gain,
    gate_up_matrix,
    down_matrix,
    cotangent,
):
    place = lax.axis_index("wa").astype(jnp.int32)
    z, core = place // 2, place % 2
    ctx = lax.axis_index("ctx").astype(jnp.int32)
    rows = projection.shape[0]
    tokens = layer_input.shape[1]
    query_width = QUERY_HEADS * HEAD_SIZE
    key_width = KEY_VALUE_HEADS * HEAD_SIZE
    width = layer_input.shape[2]
    proj_width = projection.shape[1]
    bias_rows = projection_biases.shape[0]
    slice_width = down_matrix.shape[0]
    lanes = -(-slice_width // 128) * 128
    tile = 16
    sources = [(z + 4 - step) % 4 for step in STEPS]

    small = jnp.concatenate([projection_biases, attention_gain, feed_gain])
    small = jnp.pad(small[None], ((0, tile - 1), (0, proj_width - small.shape[0])))
    packed = jnp.concatenate([projection, small], axis=0)
    own = [z_shift(packed, step) if step else packed for step in STEPS]
    others = [core_swap(piece) for piece in own]
    places = jnp.stack([2 * s + core for s in sources] + [2 * s + 1 - core for s in sources])
    packed = place_rows(places, own + others).reshape(8, rows + tile, proj_width)
    full_proj = packed[:, :rows].reshape(width, proj_width)
    vectors = packed[:, rows].astype(jnp.float32)
    full_bias = vectors[:, :bias_rows].reshape(proj_width)
    gain_one = vectors[:, bias_rows : bias_rows + rows].reshape(width)
    gain_two = vectors[:, bias_rows + rows : bias_rows + 2 * rows].reshape(width)
    complete_output = lax.all_gather(output_matrix, "wa", axis=0, tiled=True)

    decoder_layer = layer_input[0].astype(jnp.float32)
    query_pos = positions[0]
    first_normed = norm_rows(decoder_layer, gain_one).astype(jnp.bfloat16)
    projected_rows = jnp.dot(first_normed, full_proj, preferred_element_type=jnp.float32) + full_bias
    cosine_table, sine_table = angles(query_pos)
    cosine_table = cosine_table[:, None, :]
    sine_table = sine_table[:, None, :]
    queries = rotate(
        projected_rows[:, :query_width].reshape(tokens, QUERY_HEADS, HEAD_SIZE),
        cosine_table,
        sine_table,
    )
    queries = queries.astype(jnp.bfloat16).reshape(tokens, query_width)
    key_rows = rotate(
        projected_rows[:, query_width : query_width + key_width].reshape(
            tokens, KEY_VALUE_HEADS, HEAD_SIZE
        ),
        cosine_table,
        sine_table,
    )
    pair = jnp.concatenate(
        [key_rows.reshape(tokens, key_width), projected_rows[:, query_width + key_width :]], axis=1
    ).astype(jnp.bfloat16)

    gate_up_matrix, out_grad, packed = lax.optimization_barrier(
        (gate_up_matrix, cotangent[0], packed)
    )
    kept, sent = split_columns(jnp.stack([z, core]), gate_up_matrix, lanes)
    other = core_swap(sent)
    pieces = []
    for step in STEPS:
        if step:
            both = z_shift(jnp.concatenate([kept[step], other[step]], axis=0), step)
            pieces += [both[:rows], both[rows:]]
        else:
            pieces += [kept[0], other[0]]
    places = jnp.stack([p for s in sources for p in (2 * s + core, 2 * s + 1 - core)])
    gate_up = place_rows(places, pieces)
    down = jnp.pad(down_matrix, ((0, lanes - slice_width), (0, 0)))
    grad_pieces = gather_tokens(out_grad)

    pairs = ctx_gather(pair).reshape(16 * tokens, 2 * key_width)
    low = ctx * tokens + jnp.arange(tokens, dtype=jnp.int32) - query_pos
    block = math.gcd(BLOCK, pairs.shape[0])
    start = jnp.stack(
        [
            ctx * tokens,
            jnp.maximum(jnp.min(low), 0) // block,
            (ctx * tokens + tokens + block - 1) // block,
        ]
    ).astype(jnp.int32)
    low = low[None]
    mixed, lse = attend(start, queries, pairs, low)
    attention_output = mixed.astype(jnp.bfloat16)
    middle_state = decoder_layer + jnp.dot(
        attention_output, complete_output, preferred_element_type=jnp.float32
    )
    second_normed = norm_rows(middle_state, gain_two).astype(jnp.bfloat16)

    normed_pieces = gather_tokens(second_normed)
    hidden_pieces, joined_pieces, normed_grads, feed_outs = [], [], [], []
    for normed_piece, grad_piece in zip(normed_pieces, grad_pieces):
        joined = jnp.dot(normed_piece, gate_up, preferred_element_type=jnp.float32)
        gate, up = joined[:, :lanes], joined[:, lanes:]
        hidden_grad = column_product(grad_piece, down)
        sg = jax.nn.sigmoid(gate)
        act = gate * sg
        hidden = (act * up).astype(jnp.bfloat16)
        gate_grad = hidden_grad * up * sg * (1.0 + gate * (1.0 - sg))
        up_grad = hidden_grad * act
        joined_grad = jnp.concatenate([gate_grad, up_grad], axis=1).astype(jnp.bfloat16)
        hidden_pieces.append(hidden)
        joined_pieces.append(joined_grad)
        normed_grads.append(column_product(joined_grad, gate_up))
        feed_outs.append(jnp.dot(hidden, down, preferred_element_type=jnp.float32))
    normed_two_grad = reduce_tokens(normed_grads)
    feed_out = reduce_tokens(feed_outs)
    result = (middle_state + feed_out).astype(jnp.bfloat16)

    down_local = rows_product(jnp.concatenate(grad_pieces), jnp.concatenate(hidden_pieces))
    down_local = down_local.astype(jnp.bfloat16).reshape(16, width // 16, lanes)
    down_rows = -(-width // 16 // tile) * tile
    down_local = jnp.pad(down_local, ((0, 0), (0, down_rows - width // 16), (0, 0)))
    gate_up_local = rows_product(jnp.concatenate(normed_pieces), jnp.concatenate(joined_pieces))
    gate_up_local = gate_up_local.astype(jnp.bfloat16).reshape(8, rows // tile, tile, 2, lanes)
    gate_up_local = gate_up_local.transpose(1, 3, 0, 2, 4).reshape(2 * rows // tile, 8 * tile, lanes)
    gate_up_local = jnp.pad(gate_up_local, ((0, 16 - 2 * rows // tile), (0, 0), (0, 0)))
    parts = ctx_exchange(jnp.concatenate([gate_up_local, down_local], axis=1))
    parts = jnp.sum(parts.astype(jnp.float32), axis=0).astype(jnp.bfloat16)
    gate_up_part = lax.all_to_all(parts[: 8 * tile], "wa", 0, 0, tiled=True)
    parts = jnp.concatenate([gate_up_part, parts[8 * tile :]], axis=0)
    parts = lax.all_gather(parts, "ctx", axis=0)
    gate_up_total, down_total = join_columns(parts, rows, slice_width, width)

    _, norm_two_pull = jax.vjp(norm_rows, middle_state, gain_two)
    middle_part, gain_two_local = norm_two_pull(normed_two_grad)
    middle_grad = out_grad.astype(jnp.float32) + middle_part
    middle_lower = middle_grad.astype(jnp.bfloat16)
    mix_grad = column_product(middle_lower, complete_output).astype(jnp.bfloat16)
    query_grad, pair_grad = attend_back(start, queries, pairs, low, mix_grad, mixed, lse)
    pair_grad = ctx_exchange(pair_grad.reshape(16, tokens, 2 * key_width))
    query_back = inverse_rotate(
        query_grad.reshape(tokens, QUERY_HEADS, HEAD_SIZE), cosine_table, sine_table
    )
    query_back = query_back.reshape(tokens, query_width).astype(jnp.bfloat16)
    early = jnp.concatenate(
        [rows_product(attention_output, middle_lower), rows_product(first_normed, query_back)],
        axis=1,
    ).astype(jnp.bfloat16)
    early = reduce_rows(early.reshape(8, rows, width + query_width), z, core)

    pair_grad = jnp.sum(pair_grad.astype(jnp.float32), axis=0)
    key_back = inverse_rotate(
        pair_grad[:, :key_width].reshape(tokens, KEY_VALUE_HEADS, HEAD_SIZE),
        cosine_table,
        sine_table,
    ).reshape(tokens, key_width)
    pair_back = jnp.concatenate([key_back, pair_grad[:, key_width:]], axis=1).astype(jnp.bfloat16)
    projected_grad = jnp.concatenate([query_back, pair_back], axis=1)
    bias_local = jnp.sum(projected_grad.astype(jnp.float32), axis=0)
    normed_one_grad = column_product(projected_grad, full_proj)
    _, norm_one_pull = jax.vjp(norm_rows, decoder_layer, gain_one)
    layer_part, gain_one_local = norm_one_pull(normed_one_grad)
    input_grad = middle_grad + layer_part

    small = jnp.concatenate(
        [
            bias_local.reshape(8, bias_rows),
            gain_one_local.reshape(8, rows),
            gain_two_local.reshape(8, rows),
        ],
        axis=1,
    ).astype(jnp.bfloat16)
    late = rows_product(first_normed, pair_back).astype(jnp.bfloat16).reshape(8, rows, 2 * key_width)
    small = jnp.pad(small, ((0, 0), (0, 2 * 2 * key_width - small.shape[1])))
    small = jnp.pad(small.reshape(8, 2, 2 * key_width), ((0, 0), (0, tile - 2), (0, 0)))
    late = reduce_rows(jnp.concatenate([late, small], axis=1), z, core)
    mine = jnp.concatenate([jnp.pad(early, ((0, tile), (0, 0))), late], axis=1).astype(jnp.bfloat16)
    columns = mine.shape[1] // 16
    mine = mine.reshape(rows + tile, 16, columns).transpose(1, 0, 2)
    mine = jnp.sum(ctx_exchange(mine).astype(jnp.float32), axis=0).astype(jnp.bfloat16)
    mine = ctx_gather(mine).transpose(1, 0, 2).reshape(rows + tile, 16 * columns)
    mine = mine.astype(jnp.float32)
    vectors = mine[rows : rows + 2, width + query_width :].reshape(2 * 2 * key_width)
    return (
        result[None],
        input_grad[None],
        vectors[bias_rows : bias_rows + rows],
        mine[:rows, width:],
        vectors[:bias_rows],
        mine[:rows, :width],
        vectors[bias_rows + rows : bias_rows + 2 * rows],
        gate_up_total,
        down_total,
    )


def solution(mesh):
    placed = (
        P("wa", "ctx", None),
        P("wa", "ctx"),
        P("wa"),
        P("wa", None),
        P("wa"),
        P("wa", None),
        P("wa"),
        P("wa", None),
        P("wa", None),
        P("wa", "ctx", None),
    )
    return jax.shard_map(
        on_device,
        mesh=mesh,
        in_specs=placed,
        out_specs=(
            P("wa", "ctx", None),
            P("wa", "ctx", None),
            P("wa"),
            P("wa", None),
            P("wa"),
            P("wa", None),
            P("wa"),
            P("wa", None),
            P("wa", None),
        ),
        check_vma=False,
    )
```

```python
import math

import jax
import jax.numpy as jnp
from jax import lax
from jax.experimental import pallas as pl
from jax.experimental.pallas import tpu as pltpu
from jax.sharding import PartitionSpec as P

QUERY_HEADS = 14
KEY_VALUE_HEADS = 2
HEAD_SIZE = 64
FF = 4864


EPS = 1e-06
THETA = 1000000.0
NEG = -1e30


def rows_product(left, right):
    return lax.dot_general(
        left, right, (((0,), (0,)), ((), ())), preferred_element_type=jnp.float32
    )


def column_product(left, right):
    return lax.dot_general(
        left, right, (((1,), (1,)), ((), ())), preferred_element_type=jnp.float32
    )


def norm_rows(value, gain):
    return value * lax.rsqrt(jnp.mean(value * value, axis=-1, keepdims=True) + EPS) * gain


def rotate(tensor, cosine_table, sine_table):
    half = tensor.shape[-1] // 2
    first = tensor[..., :half]
    second = tensor[..., half:]
    return jnp.concatenate(
        [first * cosine_table - second * sine_table, second * cosine_table + first * sine_table],
        axis=-1,
    )


def inverse_rotate(tensor, cosine_table, sine_table):
    half = tensor.shape[-1] // 2
    first = tensor[..., :half]
    second = tensor[..., half:]
    return jnp.concatenate(
        [first * cosine_table + second * sine_table, second * cosine_table - first * sine_table],
        axis=-1,
    )


def angles(positions):
    half = HEAD_SIZE // 2
    inverse = THETA ** (-(jnp.arange(half) * 2.0 / HEAD_SIZE))
    turned = positions.astype(jnp.float32)[:, None] * inverse.astype(jnp.float32)
    return (jnp.cos(turned), jnp.sin(turned))


def turn_heads(value, cosine, sine):
    width = value.shape[1]
    lane = lax.broadcasted_iota(jnp.int32, value.shape, 1)
    half = HEAD_SIZE // 2
    partner = jnp.where(
        lane % HEAD_SIZE < half, pltpu.roll(value, width - half, 1), pltpu.roll(value, half, 1)
    )
    repeats = width // cosine.shape[1]
    return value * jnp.tile(cosine, (1, repeats)) + partner * jnp.tile(sine, (1, repeats))


def project_kernel(x_ref, gain_ref, proj_ref, bias_ref, cos_ref, sin_ref, normed_ref, q_ref, pairs_ref):
    x = x_ref[...].astype(jnp.float32)
    scale = lax.rsqrt(jnp.mean(x * x, axis=-1, keepdims=True) + EPS)
    normed = (x * scale * gain_ref[...]).astype(jnp.bfloat16)
    normed_ref[...] = normed
    width = q_ref.shape[1]
    turned = width + KEY_VALUE_HEADS * HEAD_SIZE
    projected = jnp.dot(normed, proj_ref[...], preferred_element_type=jnp.float32) + bias_ref[...]
    rotated = turn_heads(projected[:, :turned], cos_ref[...], sin_ref[...])
    q_ref[...] = rotated[:, :width].astype(jnp.bfloat16)
    pair = jnp.concatenate([rotated[:, width:], projected[:, turned:]], axis=1).astype(jnp.bfloat16)
    for n in range(pairs_ref.shape[0]):
        pairs_ref[n] = pair


def project(x, gain, proj, bias, cosine, sine):
    tokens, width = x.shape
    return pl.pallas_call(
        project_kernel,
        out_shape=(
            jax.ShapeDtypeStruct((tokens, width), jnp.bfloat16),
            jax.ShapeDtypeStruct((tokens, QUERY_HEADS * HEAD_SIZE), jnp.bfloat16),
            jax.ShapeDtypeStruct((16, tokens, 2 * KEY_VALUE_HEADS * HEAD_SIZE), jnp.bfloat16),
        ),
        in_specs=[in_vmem()] * 6,
        out_specs=(in_vmem(),) * 3,
        compiler_params=pltpu.CompilerParams(vmem_limit_bytes=32 * 2**20),
        name="project",
    )(x, gain, proj, bias, cosine, sine)


def project_back_kernel(
    place_ref, x_ref, gain_ref, proj_ref, cos_ref, sin_ref, normed_ref, dq_ref, grad_ref, gain_two_ref,
    *refs,
):
    pieces, (input_grad_ref, kept_ref, sent_ref, stage_ref) = refs[:-4], refs[-4:]
    z, core = place_ref[0], place_ref[1]
    key_width = KEY_VALUE_HEADS * HEAD_SIZE
    pair = pieces[0][...].astype(jnp.float32)
    for piece in pieces[1:]:
        pair = pair + piece[...].astype(jnp.float32)
    keys = turn_heads(pair[:, :key_width], cos_ref[...], -sin_ref[...])
    pair = jnp.concatenate([keys, pair[:, key_width:]], axis=1).astype(jnp.bfloat16)
    turned = normed_ref[...].astype(jnp.float32).T.astype(jnp.bfloat16)
    stage_ref[...] = jnp.dot(turned, pair, preferred_element_type=jnp.float32)
    bias = jnp.concatenate(
        [
            jnp.sum(dq_ref[...].astype(jnp.float32), axis=0, keepdims=True),
            jnp.sum(pair.astype(jnp.float32), axis=0, keepdims=True),
        ],
        axis=1,
    )
    x = x_ref[...].astype(jnp.float32)
    scale = lax.rsqrt(jnp.mean(x * x, axis=-1, keepdims=True) + EPS)
    grad = lax.dot_general(
        jnp.concatenate([dq_ref[...], pair], axis=1),
        proj_ref[...],
        (((1,), (1,)), ((), ())),
        preferred_element_type=jnp.float32,
    )
    gain_one = jnp.sum(grad * x * scale, axis=0, keepdims=True)
    gained = grad * gain_ref[...]
    mean = jnp.mean(gained * x, axis=-1, keepdims=True)
    input_grad_ref[...] = grad_ref[...] + scale * gained - x * (scale * scale * scale * mean)

    rows = stage_ref.shape[0] // 8
    bias_rows = bias.shape[1] // 8
    blank = jnp.zeros((kept_ref.shape[1] - rows - 2, stage_ref.shape[1]), jnp.float32)
    for owner in range(8):
        at = lax.rem(owner // 2 - z + 4, 4)
        here = slice(owner * rows, (owner + 1) * rows)
        gain_two = gain_two_ref[:, here]
        first = jnp.concatenate(
            [bias[:, owner * bias_rows : (owner + 1) * bias_rows], gain_one[:, here]], axis=1
        )
        second = jnp.concatenate(
            [gain_two, jnp.zeros((1, stage_ref.shape[1] - rows), jnp.float32)], axis=1
        )
        both = jnp.concatenate([stage_ref[here, :], first, second, blank], axis=0).astype(jnp.bfloat16)

        @pl.when(core == owner % 2)
        def _(both=both, at=at):
            kept_ref[at] = both

        @pl.when(core != owner % 2)
        def _(both=both, at=at):
            sent_ref[at] = both


def project_back(place, x, gain, proj, cosine, sine, normed, dq, grad, gain_two, pieces):
    tokens, width = x.shape
    pair_width = pieces[0].shape[1]
    out = jax.ShapeDtypeStruct((4, width // 8 + 16, pair_width), jnp.bfloat16)
    return pl.pallas_call(
        project_back_kernel,
        out_shape=(jax.ShapeDtypeStruct((tokens, width), jnp.float32), out, out),
        in_specs=[pl.BlockSpec(memory_space=pltpu.SMEM)] + [in_vmem()] * (9 + len(pieces)),
        out_specs=(in_vmem(),) * 3,
        scratch_shapes=[pltpu.VMEM((width, pair_width), jnp.float32)],
        compiler_params=pltpu.CompilerParams(vmem_limit_bytes=32 * 2**20),
        name="project_back",
    )(place, x, gain, proj, cosine, sine, normed, dq, grad, gain_two, *pieces)


def key_bias(low_ref, block_start, block, first_index):
    tokens = low_ref.shape[1]
    keys = block_start + lax.broadcasted_iota(jnp.int32, (block, tokens), 0)
    index = first_index + lax.broadcasted_iota(jnp.int32, (block, tokens), 1)
    return jnp.where((keys <= index) & (keys >= low_ref[...]), 0.0, NEG)


def head_places(tokens):
    group = QUERY_HEADS // KEY_VALUE_HEADS
    for h in range(QUERY_HEADS):
        g, i = divmod(h, group)
        yield g, slice(h * HEAD_SIZE, (h + 1) * HEAD_SIZE), slice(i * tokens, (i + 1) * tokens)


def attend_kernel(
    start_ref, q_ref, kv_ref, low_ref, mixed_ref, lse_ref, qt, s_ref, p_ref, bias_ref, m_ref, l_ref, acc_ref
):
    tokens = q_ref.shape[0]
    block, rows = s_ref.shape
    turned = (q_ref[...].astype(jnp.float32) * HEAD_SIZE ** (-0.5)).T.astype(jnp.bfloat16)
    for g, lanes, at in head_places(tokens):
        qt[g, :, at] = turned[lanes, :]
    m_ref[...] = jnp.full_like(m_ref, NEG)
    l_ref[...] = jnp.zeros_like(l_ref)
    acc_ref[...] = jnp.zeros_like(acc_ref)

    def visit(which, carry):
        block_start = pl.multiple_of(which * block, block)
        here = pl.ds(block_start, block)
        bias_ref[...] = key_bias(low_ref, block_start, block, start_ref[0])
        key_width = KEY_VALUE_HEADS * HEAD_SIZE
        values = kv_ref[here, key_width:].astype(jnp.float32).T.astype(jnp.bfloat16)
        for g in range(KEY_VALUE_HEADS):
            lanes = slice(g * HEAD_SIZE, (g + 1) * HEAD_SIZE)
            s_ref[...] = jnp.dot(kv_ref[here, lanes], qt[g], preferred_element_type=jnp.float32)
            for i in range(rows // tokens):
                at = slice(i * tokens, (i + 1) * tokens)
                s = s_ref[:, at] + bias_ref[...]
                old = m_ref[g, :, at]
                peak = jnp.maximum(old, jnp.max(s, axis=0, keepdims=True))
                e = jnp.exp(s - peak)
                scale = jnp.exp(old - peak)
                m_ref[g, :, at] = peak
                l_ref[g, :, at] = l_ref[g, :, at] * scale + jnp.sum(e, axis=0, keepdims=True)
                acc_ref[g, :, at] = acc_ref[g, :, at] * scale
                p_ref[:, at] = e.astype(jnp.bfloat16)
            acc_ref[g] += jnp.dot(values[lanes, :], p_ref[...], preferred_element_type=jnp.float32)
        return carry

    lax.fori_loop(start_ref[1], start_ref[2], visit, 0)
    mixed = [acc_ref[g, :, at] / l_ref[g, :, at] for g, _, at in head_places(tokens)]
    mixed_ref[...] = jnp.concatenate(mixed, axis=0).T
    lse_ref[...] = m_ref[...] + jnp.log(l_ref[...])


def attend_back_kernel(
    start_ref, q_ref, kv_ref, low_ref, dmix_ref, mixed_ref, lse_ref, cos_ref, sin_ref, dq_ref, dkv_ref,
    qs, qt, ms, mt, delta_ref, s_ref, dp_ref, p_ref, g_ref, bias_ref, acc_ref,
):
    tokens = q_ref.shape[0]
    block, rows = s_ref.shape
    key_width = KEY_VALUE_HEADS * HEAD_SIZE
    q = q_ref[...].astype(jnp.float32) * HEAD_SIZE ** (-0.5)
    dmix = dmix_ref[...].astype(jnp.float32)
    q_turned = q.T.astype(jnp.bfloat16)
    dmix_turned = dmix.T
    weighed = (dmix * mixed_ref[...]).T
    q = q.astype(jnp.bfloat16)
    for g, lanes, at in head_places(tokens):
        qs[g, at, :] = q[:, lanes]
        ms[g, at, :] = dmix_ref[:, lanes]
        qt[g, :, at] = q_turned[lanes, :]
        mt[g, :, at] = dmix_turned[lanes, :].astype(jnp.bfloat16)
        delta_ref[g, :, at] = jnp.sum(weighed[lanes, :], axis=0, keepdims=True)
    acc_ref[...] = jnp.zeros_like(acc_ref)
    dkv_ref[...] = jnp.zeros_like(dkv_ref)

    def visit(which, carry):
        block_start = pl.multiple_of(which * block, block)
        here = pl.ds(block_start, block)
        bias_ref[...] = key_bias(low_ref, block_start, block, start_ref[0])
        keys_turned = kv_ref[here, :key_width].astype(jnp.float32).T.astype(jnp.bfloat16)
        grads = [None] * (2 * KEY_VALUE_HEADS)
        for g in range(KEY_VALUE_HEADS):
            lanes = slice(g * HEAD_SIZE, (g + 1) * HEAD_SIZE)
            s_ref[...] = jnp.dot(kv_ref[here, lanes], qt[g], preferred_element_type=jnp.float32)
            values = kv_ref[here, key_width + g * HEAD_SIZE : key_width + (g + 1) * HEAD_SIZE]
            dp_ref[...] = jnp.dot(values, mt[g], preferred_element_type=jnp.float32)
            for i in range(rows // tokens):
                at = slice(i * tokens, (i + 1) * tokens)
                p = jnp.exp(s_ref[:, at] + bias_ref[...] - lse_ref[g, :, at])
                p_ref[:, at] = p.astype(jnp.bfloat16)
                g_ref[:, at] = (p * (dp_ref[:, at] - delta_ref[g, :, at])).astype(jnp.bfloat16)
            acc_ref[g] += jnp.dot(keys_turned[lanes, :], g_ref[...], preferred_element_type=jnp.float32)
            grads[g] = jnp.dot(g_ref[...], qs[g], preferred_element_type=jnp.float32)
            grads[KEY_VALUE_HEADS + g] = jnp.dot(
                p_ref[...], ms[g], preferred_element_type=jnp.float32
            )
        grads = jnp.concatenate(grads, axis=1).astype(jnp.bfloat16)
        x_step = lax.rem(which - start_ref[3] + 4, 4)
        for y in range(4):
            y_step = lax.rem(y - start_ref[4] + 4, 4)
            dkv_ref[y_step, x_step] = grads[y * tokens : (y + 1) * tokens, :]
        return carry

    lax.fori_loop(start_ref[1], start_ref[2], visit, 0)
    dq = [acc_ref[g, :, at] for g, _, at in head_places(tokens)]
    dq = jnp.concatenate(dq, axis=0).T * HEAD_SIZE ** (-0.5)
    dq_ref[...] = turn_heads(dq, cos_ref[...], -sin_ref[...]).astype(jnp.bfloat16)


def in_vmem():
    return pl.BlockSpec(memory_space=pltpu.VMEM)


def attend(start, queries, pairs, low):
    tokens, width = queries.shape
    rows = QUERY_HEADS // KEY_VALUE_HEADS * tokens
    block = 4 * tokens
    heads = KEY_VALUE_HEADS
    return pl.pallas_call(
        attend_kernel,
        out_shape=(
            jax.ShapeDtypeStruct((tokens, width), jnp.float32),
            jax.ShapeDtypeStruct((heads, 1, rows), jnp.float32),
        ),
        in_specs=[pl.BlockSpec(memory_space=pltpu.SMEM)] + [in_vmem()] * 3,
        out_specs=(in_vmem(), in_vmem()),
        scratch_shapes=[
            pltpu.VMEM((heads, HEAD_SIZE, rows), jnp.bfloat16),
            pltpu.VMEM((block, rows), jnp.float32),
            pltpu.VMEM((block, rows), jnp.bfloat16),
            pltpu.VMEM((block, tokens), jnp.float32),
            pltpu.VMEM((heads, 1, rows), jnp.float32),
            pltpu.VMEM((heads, 1, rows), jnp.float32),
            pltpu.VMEM((heads, HEAD_SIZE, rows), jnp.float32),
        ],
        compiler_params=pltpu.CompilerParams(vmem_limit_bytes=32 * 2**20),
        cost_estimate=pl.CostEstimate(
            flops=16 * tokens * width * pairs.shape[0], bytes_accessed=2 * 2**20, transcendentals=0
        ),
        name="attend",
    )(start, queries, pairs, low)


def attend_back(start, queries, pairs, low, mix_grad, mixed, lse, cosine, sine):
    tokens, width = queries.shape
    rows = QUERY_HEADS // KEY_VALUE_HEADS * tokens
    block = 4 * tokens
    heads = KEY_VALUE_HEADS
    return pl.pallas_call(
        attend_back_kernel,
        out_shape=(
            jax.ShapeDtypeStruct((tokens, width), jnp.bfloat16),
            jax.ShapeDtypeStruct((4, 4, tokens, pairs.shape[1]), jnp.bfloat16),
        ),
        in_specs=[pl.BlockSpec(memory_space=pltpu.SMEM)] + [in_vmem()] * 8,
        out_specs=(in_vmem(), in_vmem()),
        scratch_shapes=[
            pltpu.VMEM((heads, rows, HEAD_SIZE), jnp.bfloat16),
            pltpu.VMEM((heads, HEAD_SIZE, rows), jnp.bfloat16),
            pltpu.VMEM((heads, rows, HEAD_SIZE), jnp.bfloat16),
            pltpu.VMEM((heads, HEAD_SIZE, rows), jnp.bfloat16),
            pltpu.VMEM((heads, 1, rows), jnp.float32),
            pltpu.VMEM((block, rows), jnp.float32),
            pltpu.VMEM((block, rows), jnp.float32),
            pltpu.VMEM((block, rows), jnp.bfloat16),
            pltpu.VMEM((block, rows), jnp.bfloat16),
            pltpu.VMEM((block, tokens), jnp.float32),
            pltpu.VMEM((heads, HEAD_SIZE, rows), jnp.float32),
        ],
        compiler_params=pltpu.CompilerParams(vmem_limit_bytes=40 * 2**20),
        cost_estimate=pl.CostEstimate(
            flops=40 * tokens * width * pairs.shape[0], bytes_accessed=4 * 2**20, transcendentals=0
        ),
        name="attend_back",
    )(start, queries, pairs, low, mix_grad, mixed, lse, cosine, sine)


def split_kernel(place_ref, matrix_ref, kept_ref, sent_ref):
    z, core = place_ref[0], place_ref[1]
    width, lanes = matrix_ref.shape[1] // 16, kept_ref.shape[2] // 2
    for owner in range(8):
        at = lax.rem(owner // 2 - z + 4, 4)
        gate = matrix_ref[:, owner * width : (owner + 1) * width].astype(jnp.float32)
        up = matrix_ref[:, (8 + owner) * width : (9 + owner) * width].astype(jnp.float32)
        blank = jnp.zeros((gate.shape[0], lanes - width), jnp.float32)
        both = jnp.concatenate([gate, blank, up, blank], axis=1).astype(jnp.bfloat16)

        @pl.when(core == owner % 2)
        def _(both=both, at=at):
            kept_ref[at] = both

        @pl.when(core != owner % 2)
        def _(both=both, at=at):
            sent_ref[at] = both


def split_columns(place, matrix, lanes):
    rows = matrix.shape[0]
    out = jax.ShapeDtypeStruct((4, rows, 2 * lanes), matrix.dtype)
    return pl.pallas_call(
        split_kernel,
        out_shape=(out, out),
        in_specs=[pl.BlockSpec(memory_space=pltpu.SMEM), in_vmem()],
        out_specs=(in_vmem(), in_vmem()),
        compiler_params=pltpu.CompilerParams(vmem_limit_bytes=32 * 2**20),
        name="split_columns",
    )(place, matrix)


def place_kernel(at_ref, *refs):
    pieces, out_ref, rest_ref = refs[:-2], refs[-2], refs[-1]
    rows = out_ref.shape[0] // len(pieces)
    for n, piece in enumerate(pieces):
        out_ref[pl.ds(pl.multiple_of(at_ref[n] * rows, 16), rows), :] = piece[:rows, :]
        if piece.shape[0] > rows:
            rest_ref[at_ref[n]] = piece[rows:, :]
        else:
            rest_ref[...] = jnp.zeros_like(rest_ref)


def place_rows(at, pieces, rows):
    height, width = pieces[0].shape
    count = len(pieces)
    rest = (count, height - rows, width) if height > rows else (1, 8, 128)
    return pl.pallas_call(
        place_kernel,
        out_shape=(
            jax.ShapeDtypeStruct((count * rows, width), pieces[0].dtype),
            jax.ShapeDtypeStruct(rest, pieces[0].dtype if height > rows else jnp.float32),
        ),
        in_specs=[pl.BlockSpec(memory_space=pltpu.SMEM)] + [in_vmem()] * count,
        out_specs=(in_vmem(), in_vmem()),
        compiler_params=pltpu.CompilerParams(vmem_limit_bytes=32 * 2**20),
        name="place_rows",
    )(at, *pieces)


def feed_grads_kernel(*refs):
    ins, (out_ref, down_ref, left_ref, right_ref, stage_ref) = refs[:16], refs[-5:]
    normed, grads, joined, hidden = ins[:4], ins[4:8], ins[8:12], ins[12:]
    lanes = stage_ref.shape[1]
    tile = 16
    rows = stage_ref.shape[0] // 8
    step = normed[0].shape[0]

    def load(left, right, at):
        for n in range(4):
            here = slice(n * step, (n + 1) * step)
            if left is not None:
                left_ref[:, here] = left[n][...].astype(jnp.float32).T.astype(jnp.bfloat16)
            right_ref[here, :] = right[n][:, at]
        stage_ref[...] = jnp.dot(left_ref[...], right_ref[...], preferred_element_type=jnp.float32)

    for half in range(2):
        load(None if half else normed, joined, slice(half * lanes, (half + 1) * lanes))
        for r in range(rows // tile):
            for k in range(8):
                first = k * rows + r * tile
                out_ref[2 * r + half, k] = stage_ref[
                    first : first + tile, :
                ].astype(jnp.bfloat16)
    for part in range(2 * rows // tile, 16):
        out_ref[part] = jnp.zeros((8, tile, lanes), jnp.bfloat16)
    load(grads, hidden, slice(0, lanes))
    rows = stage_ref.shape[0] // 16
    blank = jnp.zeros((down_ref.shape[1] - rows, lanes), jnp.float32)
    for part in range(16):
        piece = jnp.concatenate([stage_ref[part * rows : (part + 1) * rows, :], blank], axis=0)
        down_ref[part] = piece.astype(jnp.bfloat16)


def feed_grads(normed, grads, joined, hidden, earlier):
    step, width = normed[0].shape
    lanes = hidden[0].shape[1]
    part = -(-width // 16 // 16) * 16
    return pl.pallas_call(
        feed_grads_kernel,
        out_shape=(
            jax.ShapeDtypeStruct((16, 8, 16, lanes), jnp.bfloat16),
            jax.ShapeDtypeStruct((16, part, lanes), jnp.bfloat16),
        ),
        in_specs=[in_vmem()] * 16 + [pl.BlockSpec(memory_space=pl.ANY)] * len(earlier),
        out_specs=(in_vmem(), in_vmem()),
        scratch_shapes=[
            pltpu.VMEM((width, 4 * step), jnp.bfloat16),
            pltpu.VMEM((4 * step, lanes), jnp.bfloat16),
            pltpu.VMEM((width, lanes), jnp.float32),
        ],
        compiler_params=pltpu.CompilerParams(vmem_limit_bytes=40 * 2**20),
        cost_estimate=pl.CostEstimate(
            flops=24 * step * width * lanes, bytes_accessed=12 * 2**20, transcendentals=0
        ),
        name="feed_grads",
    )(*normed, *grads, *joined, *hidden, *earlier)


def rows_grads_kernel(place_ref, *refs):
    kept_ref, sent_ref, stage_ref = refs[-3:]
    pairs = (len(refs) - 3) // 2
    rest_ref = refs[2 * pairs] if (len(refs) - 3) % 2 else None
    z, core = place_ref[0], place_ref[1]
    rows = stage_ref.shape[0] // 8
    first = 0
    for n in range(pairs):
        left, right = refs[2 * n], refs[2 * n + 1]
        turned = left[...].astype(jnp.float32).T.astype(jnp.bfloat16)
        stage_ref[:, first : first + right.shape[1]] = jnp.dot(
            turned, right[...], preferred_element_type=jnp.float32
        )
        first += right.shape[1]
    for owner in range(8):
        at = lax.rem(owner // 2 - z + 4, 4)

        @pl.when(core == owner % 2)
        def _(owner=owner, at=at):
            kept_ref[at, :rows, :] = stage_ref[owner * rows : (owner + 1) * rows, :].astype(jnp.bfloat16)
            if rest_ref is not None:
                kept_ref[at, rows:, :] = rest_ref[owner]

        @pl.when(core != owner % 2)
        def _(owner=owner, at=at):
            sent_ref[at, :rows, :] = stage_ref[owner * rows : (owner + 1) * rows, :].astype(jnp.bfloat16)
            if rest_ref is not None:
                sent_ref[at, rows:, :] = rest_ref[owner]


def rows_grads(place, pairs, rest=None):
    height = pairs[0][0].shape[1]
    width = sum(right.shape[1] for _, right in pairs)
    rows = height // 8 + (0 if rest is None else rest.shape[1])
    arrays = [array for pair in pairs for array in pair] + ([] if rest is None else [rest])
    out = jax.ShapeDtypeStruct((4, rows, width), jnp.bfloat16)
    return pl.pallas_call(
        rows_grads_kernel,
        out_shape=(out, out),
        in_specs=[pl.BlockSpec(memory_space=pltpu.SMEM)] + [in_vmem()] * len(arrays),
        out_specs=(in_vmem(), in_vmem()),
        scratch_shapes=[pltpu.VMEM((height, width), jnp.float32)],
        compiler_params=pltpu.CompilerParams(vmem_limit_bytes=32 * 2**20),
        cost_estimate=pl.CostEstimate(
            flops=2 * 128 * height * width, bytes_accessed=4 * 2**20, transcendentals=0
        ),
        name="rows_grads",
    )(place, *arrays)


def join_kernel(parts_ref, gate_up_ref, down_ref, stage_ref):
    lanes = parts_ref.shape[2]
    width = gate_up_ref.shape[1] // 16
    tile = 16
    for part in range(2 * gate_up_ref.shape[0] // tile):
        r, half = divmod(part, 2)
        columns = [
            parts_ref[part, k * tile : (k + 1) * tile, :].astype(jnp.float32)[:, :width]
            for k in range(8)
        ]
        gate_up_ref[r * tile : (r + 1) * tile, half * 8 * width : (half + 1) * 8 * width] = (
            jnp.concatenate(columns, axis=1)
        )
    rows = stage_ref.shape[0] // 16
    for part in range(16):
        stage_ref[part * rows : (part + 1) * rows, :] = parts_ref[part, 8 * tile :, :].astype(
            jnp.float32
        )[:rows]
    for block in range(stage_ref.shape[0] // 128):
        at = slice(block * 128, (block + 1) * 128)
        down_ref[:, at] = stage_ref[at, :].T[:width]


def join_columns(parts, rows, width, model_width):
    return pl.pallas_call(
        join_kernel,
        out_shape=(
            jax.ShapeDtypeStruct((rows, 16 * width), jnp.float32),
            jax.ShapeDtypeStruct((width, model_width), jnp.float32),
        ),
        in_specs=[in_vmem()],
        out_specs=(in_vmem(), in_vmem()),
        scratch_shapes=[pltpu.VMEM((model_width, parts.shape[2]), jnp.float32)],
        compiler_params=pltpu.CompilerParams(vmem_limit_bytes=40 * 2**20),
        name="join_columns",
    )(parts)


def core_swap(value):
    return lax.ppermute(value, "wa", [(i, i ^ 1) for i in range(8)])


def z_shift(value, step):
    return lax.ppermute(value, "wa", [(i, (i + 2 * step) % 8) for i in range(8)])


def y_shift(value, step):
    pairs = [(i, i // 4 * 4 + (i + step) % 4) for i in range(16)]
    return lax.ppermute(value, "ctx", pairs)


def x_shift(value, step):
    return lax.ppermute(value, "ctx", [(i, (i + 4 * step) % 16) for i in range(16)])


def ctx_exchange(value):
    return lax.all_to_all(value, "ctx", 0, 0, tiled=True)


def ctx_gather(value):
    return ctx_exchange(jnp.broadcast_to(value[None], (16,) + value.shape))


STEPS = (0, 1, 3, 2)


def gather_tokens(value):
    pieces = [z_shift(value, step) if step else value for step in STEPS]
    return [jnp.concatenate([piece, core_swap(piece)], axis=0) for piece in pieces]


def pair_tokens(partials):
    paired = []
    for step, partial in zip(STEPS, partials):
        rows = partial.shape[0] // 2
        other = core_swap(partial[rows:].astype(jnp.bfloat16)).astype(jnp.float32)
        mine = partial[:rows] + other
        paired.append(mine.astype(jnp.bfloat16) if step else mine)
    return paired


def reduce_tokens(paired):
    total = 0.0
    for step, mine in zip(STEPS, paired):
        total = total + (z_shift(mine, -step).astype(jnp.float32) if step else mine)
    return total


def reduce_rows(kept, sent):
    other = core_swap(sent)
    total = 0.0
    for step in STEPS:
        mine = kept[step].astype(jnp.float32) + other[step].astype(jnp.float32)
        if step:
            mine = z_shift(mine.astype(jnp.bfloat16), step).astype(jnp.float32)
        total = total + mine
    return total


def after(value, *others):
    held = sum(other[(0,) * other.ndim].astype(jnp.float32) for other in others) * 0.0
    return value + held.astype(value.dtype)


def spread_kernel(at_ref, *refs):
    pieces, (left_ref, right_ref, small_ref, stage_ref) = refs[:-4], refs[-4:]
    columns = pieces[0].shape[2]
    for n, piece in enumerate(pieces):
        for m in range(piece.shape[0]):
            start = pl.multiple_of(at_ref[n * piece.shape[0] + m] * columns, columns)
            stage_ref[:, pl.ds(start, columns)] = piece[m].astype(jnp.float32)
    rows, width = left_ref.shape
    left_ref[...] = stage_ref[:rows, :width]
    right_ref[...] = stage_ref[:rows, width:]
    small_ref[...] = stage_ref[rows : rows + 8, stage_ref.shape[1] - small_ref.shape[1] :]


def spread_columns(at, pieces, rows, width, small_width):
    count, height, columns = pieces[0].shape
    total = len(pieces) * count * columns
    return pl.pallas_call(
        spread_kernel,
        out_shape=(
            jax.ShapeDtypeStruct((rows, width), jnp.float32),
            jax.ShapeDtypeStruct((rows, total - width), jnp.float32),
            jax.ShapeDtypeStruct((8, small_width), jnp.float32),
        ),
        in_specs=[pl.BlockSpec(memory_space=pltpu.SMEM)] + [in_vmem()] * len(pieces),
        out_specs=(in_vmem(),) * 3,
        scratch_shapes=[pltpu.VMEM((height, total), jnp.float32)],
        compiler_params=pltpu.CompilerParams(vmem_limit_bytes=32 * 2**20),
        name="spread_columns",
    )(at, *pieces)


def on_device(
    layer_input,
    positions,
    attention_gain,
    projection,
    projection_biases,
    output_matrix,
    feed_gain,
    gate_up_matrix,
    down_matrix,
    cotangent,
):
    place = lax.axis_index("wa").astype(jnp.int32)
    z, core = place // 2, place % 2
    ctx = lax.axis_index("ctx").astype(jnp.int32)
    rows = projection.shape[0]
    tokens = layer_input.shape[1]
    query_width = QUERY_HEADS * HEAD_SIZE
    key_width = KEY_VALUE_HEADS * HEAD_SIZE
    width = layer_input.shape[2]
    proj_width = projection.shape[1]
    bias_rows = projection_biases.shape[0]
    slice_width = down_matrix.shape[0]
    lanes = -(-slice_width // 128) * 128
    tile = 16
    sources = [(z + 4 - step) % 4 for step in STEPS]

    small = jnp.concatenate([projection_biases, attention_gain, feed_gain])
    small = jnp.pad(small[None], ((0, tile - 1), (0, proj_width - small.shape[0])))
    packed = jnp.concatenate([projection, small], axis=0)
    own = [z_shift(packed, step) if step else packed for step in STEPS]
    others = [core_swap(piece) for piece in own]
    places = jnp.stack([2 * s + core for s in sources] + [2 * s + 1 - core for s in sources])
    full_proj, vectors = place_rows(places, own + others, rows)
    vectors = vectors[:, 0].astype(jnp.float32)
    full_bias = vectors[:, :bias_rows].reshape(1, proj_width)
    gain_one = vectors[:, bias_rows : bias_rows + rows].reshape(1, width)
    gain_two = vectors[:, bias_rows + rows : bias_rows + 2 * rows].reshape(width)

    spot = jnp.stack([z, core])
    kept, sent = split_columns(spot, gate_up_matrix, lanes)
    other = core_swap(sent)
    pieces = []
    for step in STEPS:
        if step:
            both = jnp.concatenate([kept[step], other[step]], axis=0)
            both = z_shift(after(both, *own[1:]), step)
            pieces += [both[:rows], both[rows:]]
        else:
            pieces += [kept[0], other[0]]
    places = jnp.stack([p for s in sources for p in (2 * s + core, 2 * s + 1 - core)])
    gate_up, _ = place_rows(places, pieces, rows)
    down = jnp.pad(down_matrix, ((0, lanes - slice_width), (0, 0)))

    layer_rows = layer_input[0]
    decoder_layer = layer_rows.astype(jnp.float32)
    query_pos = positions[0]
    cosine, sine = angles(query_pos)
    cosine = jnp.tile(cosine, (1, 4))
    sine = jnp.tile(jnp.concatenate([-sine, sine], axis=1), (1, 2))
    first_normed, queries, pair = project(layer_rows, gain_one, full_proj, full_bias, cosine, sine)
    complete_output = lax.all_gather(after(output_matrix, pair), "wa", axis=0, tiled=True)
    out_grad = cotangent[0]
    grad_pieces = gather_tokens(after(out_grad, pieces[2]))

    pairs = ctx_exchange(pair).reshape(16 * tokens, 2 * key_width)
    low = ctx * tokens + jnp.arange(tokens, dtype=jnp.int32) - query_pos
    block = 4 * tokens
    start = jnp.stack(
        [
            ctx * tokens,
            jnp.maximum(jnp.min(low), 0) // block,
            (ctx * tokens + tokens + block - 1) // block,
            ctx // 4,
            ctx % 4,
        ]
    ).astype(jnp.int32)
    low = low[None]
    mixed, lse = attend(start, queries, pairs, low)
    attention_output = mixed.astype(jnp.bfloat16)
    middle_state = decoder_layer + jnp.dot(
        attention_output, complete_output, preferred_element_type=jnp.float32
    )
    second_normed = norm_rows(middle_state, gain_two).astype(jnp.bfloat16)

    normed_pieces = gather_tokens(second_normed)
    hidden_pieces, joined_pieces, normed_grads = [], [], []
    for normed_piece, grad_piece in zip(normed_pieces, grad_pieces):
        joined = jnp.dot(normed_piece, gate_up, preferred_element_type=jnp.float32)
        gate, up = joined[:, :lanes], joined[:, lanes:]
        hidden_grad = column_product(grad_piece, down)
        sg = jax.nn.sigmoid(gate)
        act = gate * sg
        hidden = (act * up).astype(jnp.bfloat16)
        gate_grad = hidden_grad * up * sg * (1.0 + gate * (1.0 - sg))
        up_grad = hidden_grad * act
        joined_grad = jnp.concatenate([gate_grad, up_grad], axis=1).astype(jnp.bfloat16)
        hidden_pieces.append(hidden)
        joined_pieces.append(joined_grad)
        normed_grads.append(column_product(joined_grad, gate_up))
    paired = pair_tokens(normed_grads)

    local_parts = feed_grads(normed_pieces, grad_pieces, joined_pieces, hidden_pieces, paired)
    normed_two_grad = after(reduce_tokens(paired), local_parts[0])
    gate_up_part = lax.all_to_all(
        local_parts[0].reshape(16 * 8, tile, lanes), ("ctx", "wa"), 0, 0, tiled=True
    )
    gate_up_part = jnp.sum(gate_up_part.reshape(16, 8 * tile, lanes).astype(jnp.float32), axis=0)
    down_part = jnp.sum(ctx_exchange(local_parts[1]).astype(jnp.float32), axis=0)
    parts = ctx_gather(jnp.concatenate([gate_up_part, down_part], axis=0).astype(jnp.bfloat16))
    gate_up_total, down_total = join_columns(parts, rows, slice_width, width)

    feed_outs = [
        jnp.dot(hidden, down, preferred_element_type=jnp.float32) for hidden in hidden_pieces
    ]
    feed_out = reduce_tokens(pair_tokens(feed_outs))
    result = (middle_state + feed_out).astype(jnp.bfloat16)

    _, norm_two_pull = jax.vjp(norm_rows, middle_state, gain_two)
    middle_part, gain_two_local = norm_two_pull(normed_two_grad)
    middle_grad = out_grad.astype(jnp.float32) + middle_part
    middle_lower = middle_grad.astype(jnp.bfloat16)
    mix_grad = column_product(middle_lower, complete_output).astype(jnp.bfloat16)
    query_back, pair_grad = attend_back(
        start, queries, pairs, low, mix_grad, mixed, lse, cosine, sine
    )
    early = reduce_rows(
        *rows_grads(spot, [(attention_output, middle_lower), (first_normed, query_back)])
    )

    summed = 0.0
    for step in STEPS:
        piece = y_shift(pair_grad[step], step) if step else pair_grad[0]
        summed = summed + piece.astype(jnp.float32)
    summed = summed.astype(jnp.bfloat16)
    pieces = [x_shift(summed[step], step) if step else summed[0] for step in STEPS]
    input_grad, kept, sent = project_back(
        spot,
        layer_rows,
        gain_one,
        full_proj,
        cosine,
        sine,
        first_normed,
        query_back,
        middle_grad,
        gain_two_local[None],
        pieces,
    )
    late = reduce_rows(kept, sent)

    mine = jnp.concatenate([jnp.pad(early, ((0, tile), (0, 0))), late], axis=1).astype(jnp.bfloat16)
    columns = mine.shape[1] // 16
    mine = mine.reshape(rows + tile, 4, 4, columns).transpose(1, 2, 0, 3)
    x, y = ctx // 4, ctx % 4
    summed = 0.0
    for step in STEPS:
        piece = lax.dynamic_index_in_dim(mine, (y + step) % 4, 0, keepdims=False)
        summed = summed + (y_shift(piece, step) if step else piece).astype(jnp.float32)
    mine = summed.astype(jnp.bfloat16)
    summed = 0.0
    for step in STEPS:
        piece = lax.dynamic_index_in_dim(mine, (x + step) % 4, 0, keepdims=False)
        summed = summed + (x_shift(piece, step) if step else piece).astype(jnp.float32)
    mine = summed.astype(jnp.bfloat16)
    mine = jnp.stack([x_shift(mine, step) if step else mine for step in STEPS])
    pieces = [y_shift(mine, step) if step else mine for step in STEPS]
    places = jnp.stack(
        [(y + 4 - y_step) % 4 * 4 + (x + 4 - x_step) % 4 for y_step in STEPS for x_step in STEPS]
    )
    output_total, projection_total, vectors = spread_columns(
        places, pieces, rows, width, 2 * key_width
    )
    return (
        result[None],
        input_grad[None],
        vectors[0, bias_rows : bias_rows + rows],
        projection_total,
        vectors[0, :bias_rows],
        output_total,
        vectors[1, :rows],
        gate_up_total,
        down_total,
    )


def solution(mesh):
    placed = (
        P("wa", "ctx", None),
        P("wa", "ctx"),
        P("wa"),
        P("wa", None),
        P("wa"),
        P("wa", None),
        P("wa"),
        P("wa", None),
        P("wa", None),
        P("wa", "ctx", None),
    )
    return jax.shard_map(
        on_device,
        mesh=mesh,
        in_specs=placed,
        out_specs=(
            P("wa", "ctx", None),
            P("wa", "ctx", None),
            P("wa"),
            P("wa", None),
            P("wa"),
            P("wa", None),
            P("wa"),
            P("wa", None),
            P("wa", None),
        ),
        check_vma=False,
    )
```

```python
import math

import jax
import jax.numpy as jnp
from jax import lax
from jax.experimental import pallas as pl
from jax.experimental.pallas import tpu as pltpu
from jax.sharding import PartitionSpec as P

QUERY_HEADS = 14
KEY_VALUE_HEADS = 2
HEAD_SIZE = 64
FF = 4864


EPS = 1e-06
THETA = 1000000.0
NEG = -1e30


def rows_product(left, right):
    return lax.dot_general(
        left, right, (((0,), (0,)), ((), ())), preferred_element_type=jnp.float32
    )


def column_product(left, right):
    return lax.dot_general(
        left, right, (((1,), (1,)), ((), ())), preferred_element_type=jnp.float32
    )


def norm_rows(value, gain):
    return value * lax.rsqrt(jnp.mean(value * value, axis=-1, keepdims=True) + EPS) * gain


def rotate(tensor, cosine_table, sine_table):
    half = tensor.shape[-1] // 2
    first = tensor[..., :half]
    second = tensor[..., half:]
    return jnp.concatenate(
        [first * cosine_table - second * sine_table, second * cosine_table + first * sine_table],
        axis=-1,
    )


def inverse_rotate(tensor, cosine_table, sine_table):
    half = tensor.shape[-1] // 2
    first = tensor[..., :half]
    second = tensor[..., half:]
    return jnp.concatenate(
        [first * cosine_table + second * sine_table, second * cosine_table - first * sine_table],
        axis=-1,
    )


def angles(positions):
    half = HEAD_SIZE // 2
    inverse = THETA ** (-(jnp.arange(half) * 2.0 / HEAD_SIZE))
    turned = positions.astype(jnp.float32)[:, None] * inverse.astype(jnp.float32)
    return (jnp.cos(turned), jnp.sin(turned))


def turn_heads(value, cosine, sine):
    width = value.shape[1]
    lane = lax.broadcasted_iota(jnp.int32, value.shape, 1)
    half = HEAD_SIZE // 2
    partner = jnp.where(
        lane % HEAD_SIZE < half, pltpu.roll(value, width - half, 1), pltpu.roll(value, half, 1)
    )
    repeats = width // cosine.shape[1]
    return value * jnp.tile(cosine, (1, repeats)) + partner * jnp.tile(sine, (1, repeats))


def project_kernel(x_ref, gain_ref, proj_ref, bias_ref, cos_ref, sin_ref, normed_ref, q_ref, pairs_ref):
    x = x_ref[...].astype(jnp.float32)
    scale = lax.rsqrt(jnp.mean(x * x, axis=-1, keepdims=True) + EPS)
    normed = (x * scale * gain_ref[...]).astype(jnp.bfloat16)
    normed_ref[...] = normed
    width = q_ref.shape[1]
    turned = width + KEY_VALUE_HEADS * HEAD_SIZE
    projected = jnp.dot(normed, proj_ref[...], preferred_element_type=jnp.float32) + bias_ref[...]
    rotated = turn_heads(projected[:, :turned], cos_ref[...], sin_ref[...])
    q_ref[...] = rotated[:, :width].astype(jnp.bfloat16)
    pair = jnp.concatenate([rotated[:, width:], projected[:, turned:]], axis=1).astype(jnp.bfloat16)
    for n in range(pairs_ref.shape[0]):
        pairs_ref[n] = pair


def project(x, gain, proj, bias, cosine, sine):
    tokens, width = x.shape
    return pl.pallas_call(
        project_kernel,
        out_shape=(
            jax.ShapeDtypeStruct((tokens, width), jnp.bfloat16),
            jax.ShapeDtypeStruct((tokens, QUERY_HEADS * HEAD_SIZE), jnp.bfloat16),
            jax.ShapeDtypeStruct((16, tokens, 2 * KEY_VALUE_HEADS * HEAD_SIZE), jnp.bfloat16),
        ),
        in_specs=[in_vmem()] * 6,
        out_specs=(in_vmem(),) * 3,
        compiler_params=pltpu.CompilerParams(vmem_limit_bytes=12 * 2**20),
        name="project",
    )(x, gain, proj, bias, cosine, sine)


def project_back_kernel(
    place_ref, x_ref, gain_ref, proj_ref, cos_ref, sin_ref, normed_ref, dq_ref, grad_ref, gain_two_ref,
    pieces_ref, input_grad_ref, kept_ref, sent_ref, stage_ref,
):
    z, core = place_ref[0], place_ref[1]
    key_width = KEY_VALUE_HEADS * HEAD_SIZE
    pair = pieces_ref[0].astype(jnp.float32)
    for n in range(1, pieces_ref.shape[0]):
        pair = pair + pieces_ref[n].astype(jnp.float32)
    keys = turn_heads(pair[:, :key_width], cos_ref[...], -sin_ref[...])
    pair = jnp.concatenate([keys, pair[:, key_width:]], axis=1).astype(jnp.bfloat16)
    turned = normed_ref[...].astype(jnp.float32).T.astype(jnp.bfloat16)
    stage_ref[...] = jnp.dot(turned, pair, preferred_element_type=jnp.float32)
    bias = jnp.concatenate(
        [
            jnp.sum(dq_ref[...].astype(jnp.float32), axis=0, keepdims=True),
            jnp.sum(pair.astype(jnp.float32), axis=0, keepdims=True),
        ],
        axis=1,
    )
    x = x_ref[...].astype(jnp.float32)
    scale = lax.rsqrt(jnp.mean(x * x, axis=-1, keepdims=True) + EPS)
    grad = lax.dot_general(
        jnp.concatenate([dq_ref[...], pair], axis=1),
        proj_ref[...],
        (((1,), (1,)), ((), ())),
        preferred_element_type=jnp.float32,
    )
    gain_one = jnp.sum(grad * x * scale, axis=0, keepdims=True)
    gained = grad * gain_ref[...]
    mean = jnp.mean(gained * x, axis=-1, keepdims=True)
    input_grad_ref[...] = grad_ref[...] + scale * gained - x * (scale * scale * scale * mean)

    rows = stage_ref.shape[0] // 8
    bias_rows = bias.shape[1] // 8
    blank = jnp.zeros((kept_ref.shape[1] - rows - 2, stage_ref.shape[1]), jnp.float32)
    for owner in range(8):
        at = lax.rem(owner // 2 - z + 4, 4)
        here = slice(owner * rows, (owner + 1) * rows)
        gain_two = gain_two_ref[:, here]
        first = jnp.concatenate(
            [bias[:, owner * bias_rows : (owner + 1) * bias_rows], gain_one[:, here]], axis=1
        )
        second = jnp.concatenate(
            [gain_two, jnp.zeros((1, stage_ref.shape[1] - rows), jnp.float32)], axis=1
        )
        both = jnp.concatenate([stage_ref[here, :], first, second, blank], axis=0).astype(jnp.bfloat16)

        @pl.when(core == owner % 2)
        def _(both=both, at=at):
            kept_ref[at] = both

        @pl.when(core != owner % 2)
        def _(both=both, at=at):
            sent_ref[at] = both


def project_back(place, x, gain, proj, cosine, sine, normed, dq, grad, gain_two, pieces):
    tokens, width = x.shape
    pair_width = pieces.shape[2]
    out = jax.ShapeDtypeStruct((4, width // 8 + 16, pair_width), jnp.bfloat16)
    return pl.pallas_call(
        project_back_kernel,
        out_shape=(jax.ShapeDtypeStruct((tokens, width), jnp.float32), out, out),
        in_specs=[pl.BlockSpec(memory_space=pltpu.SMEM)] + [in_vmem()] * 10,
        out_specs=(in_vmem(),) * 3,
        scratch_shapes=[pltpu.VMEM((width, pair_width), jnp.float32)],
        compiler_params=pltpu.CompilerParams(vmem_limit_bytes=16 * 2**20),
        name="project_back",
    )(place, x, gain, proj, cosine, sine, normed, dq, grad, gain_two, pieces)


def key_bias(low_ref, block_start, block, first_index):
    tokens = low_ref.shape[1]
    keys = block_start + lax.broadcasted_iota(jnp.int32, (block, tokens), 0)
    index = first_index + lax.broadcasted_iota(jnp.int32, (block, tokens), 1)
    return jnp.where((keys <= index) & (keys >= low_ref[...]), 0.0, NEG)


def head_places(tokens):
    group = QUERY_HEADS // KEY_VALUE_HEADS
    for h in range(QUERY_HEADS):
        g, i = divmod(h, group)
        yield g, slice(h * HEAD_SIZE, (h + 1) * HEAD_SIZE), slice(i * tokens, (i + 1) * tokens)


def attend_kernel(
    start_ref, q_ref, kv_ref, low_ref, x_ref, out_ref, gain_ref, mixed_ref, lse_ref, attended_ref, middle_ref, normed_ref,
    qt, s_ref, p_ref, bias_ref, m_ref, l_ref, acc_ref,
):
    tokens = q_ref.shape[0]
    block, rows = s_ref.shape
    turned = (q_ref[...].astype(jnp.float32) * HEAD_SIZE ** (-0.5)).T.astype(jnp.bfloat16)
    for g, lanes, at in head_places(tokens):
        qt[g, :, at] = turned[lanes, :]
    m_ref[...] = jnp.full_like(m_ref, NEG)
    l_ref[...] = jnp.zeros_like(l_ref)
    acc_ref[...] = jnp.zeros_like(acc_ref)

    def visit(which, carry):
        block_start = pl.multiple_of(which * block, block)
        here = pl.ds(block_start, block)
        bias_ref[...] = key_bias(low_ref, block_start, block, start_ref[0])
        key_width = KEY_VALUE_HEADS * HEAD_SIZE
        values = kv_ref[here, key_width:].astype(jnp.float32).T.astype(jnp.bfloat16)
        for g in range(KEY_VALUE_HEADS):
            lanes = slice(g * HEAD_SIZE, (g + 1) * HEAD_SIZE)
            s_ref[...] = jnp.dot(kv_ref[here, lanes], qt[g], preferred_element_type=jnp.float32)
            for i in range(rows // tokens):
                at = slice(i * tokens, (i + 1) * tokens)
                s = s_ref[:, at] + bias_ref[...]
                old = m_ref[g, :, at]
                peak = jnp.maximum(old, jnp.max(s, axis=0, keepdims=True))
                e = jnp.exp(s - peak)
                scale = jnp.exp(old - peak)
                m_ref[g, :, at] = peak
                l_ref[g, :, at] = l_ref[g, :, at] * scale + jnp.sum(e, axis=0, keepdims=True)
                acc_ref[g, :, at] = acc_ref[g, :, at] * scale
                p_ref[:, at] = e.astype(jnp.bfloat16)
            acc_ref[g] += jnp.dot(values[lanes, :], p_ref[...], preferred_element_type=jnp.float32)
        return carry

    lax.fori_loop(start_ref[1], start_ref[2], visit, 0)
    mixed = [acc_ref[g, :, at] / l_ref[g, :, at] for g, _, at in head_places(tokens)]
    mixed = jnp.concatenate(mixed, axis=0).T
    mixed_ref[...] = mixed
    lse_ref[...] = m_ref[...] + jnp.log(l_ref[...])
    attended = mixed.astype(jnp.bfloat16)
    attended_ref[...] = attended
    middle = x_ref[...].astype(jnp.float32) + jnp.dot(
        attended, out_ref[...], preferred_element_type=jnp.float32
    )
    middle_ref[...] = middle
    scale = lax.rsqrt(jnp.mean(middle * middle, axis=-1, keepdims=True) + EPS)
    normed_ref[...] = (middle * scale * gain_ref[...]).astype(jnp.bfloat16)


def attend_back_kernel(
    start_ref, q_ref, kv_ref, low_ref, dmix_ref, mixed_ref, lse_ref, cos_ref, sin_ref, dq_ref, dkv_ref,
    qs, qt, ms, mt, delta_ref, s_ref, dp_ref, p_ref, g_ref, bias_ref, acc_ref,
):
    tokens = q_ref.shape[0]
    block, rows = s_ref.shape
    key_width = KEY_VALUE_HEADS * HEAD_SIZE
    q = q_ref[...].astype(jnp.float32) * HEAD_SIZE ** (-0.5)
    dmix = dmix_ref[...].astype(jnp.float32)
    q_turned = q.T.astype(jnp.bfloat16)
    dmix_turned = dmix.T
    weighed = (dmix * mixed_ref[...]).T
    q = q.astype(jnp.bfloat16)
    for g, lanes, at in head_places(tokens):
        qs[g, at, :] = q[:, lanes]
        ms[g, at, :] = dmix_ref[:, lanes]
        qt[g, :, at] = q_turned[lanes, :]
        mt[g, :, at] = dmix_turned[lanes, :].astype(jnp.bfloat16)
        delta_ref[g, :, at] = jnp.sum(weighed[lanes, :], axis=0, keepdims=True)
    acc_ref[...] = jnp.zeros_like(acc_ref)
    dkv_ref[...] = jnp.zeros_like(dkv_ref)

    def visit(which, carry):
        block_start = pl.multiple_of(which * block, block)
        here = pl.ds(block_start, block)
        bias_ref[...] = key_bias(low_ref, block_start, block, start_ref[0])
        keys_turned = kv_ref[here, :key_width].astype(jnp.float32).T.astype(jnp.bfloat16)
        grads = [None] * (2 * KEY_VALUE_HEADS)
        for g in range(KEY_VALUE_HEADS):
            lanes = slice(g * HEAD_SIZE, (g + 1) * HEAD_SIZE)
            s_ref[...] = jnp.dot(kv_ref[here, lanes], qt[g], preferred_element_type=jnp.float32)
            values = kv_ref[here, key_width + g * HEAD_SIZE : key_width + (g + 1) * HEAD_SIZE]
            dp_ref[...] = jnp.dot(values, mt[g], preferred_element_type=jnp.float32)
            for i in range(rows // tokens):
                at = slice(i * tokens, (i + 1) * tokens)
                p = jnp.exp(s_ref[:, at] + bias_ref[...] - lse_ref[g, :, at])
                p_ref[:, at] = p.astype(jnp.bfloat16)
                g_ref[:, at] = (p * (dp_ref[:, at] - delta_ref[g, :, at])).astype(jnp.bfloat16)
            acc_ref[g] += jnp.dot(keys_turned[lanes, :], g_ref[...], preferred_element_type=jnp.float32)
            grads[g] = jnp.dot(g_ref[...], qs[g], preferred_element_type=jnp.float32)
            grads[KEY_VALUE_HEADS + g] = jnp.dot(
                p_ref[...], ms[g], preferred_element_type=jnp.float32
            )
        grads = jnp.concatenate(grads, axis=1).astype(jnp.bfloat16)
        for n in range(block // tokens):
            dkv_ref[which * (block // tokens) + n] = grads[n * tokens : (n + 1) * tokens, :]
        return carry

    lax.fori_loop(start_ref[1], start_ref[2], visit, 0)
    dq = [acc_ref[g, :, at] for g, _, at in head_places(tokens)]
    dq = jnp.concatenate(dq, axis=0).T * HEAD_SIZE ** (-0.5)
    dq_ref[...] = turn_heads(dq, cos_ref[...], -sin_ref[...]).astype(jnp.bfloat16)


def in_vmem():
    return pl.BlockSpec(memory_space=pltpu.VMEM)


def attend(start, queries, pairs, low, x, out_matrix, gain):
    tokens, width = queries.shape
    rows = QUERY_HEADS // KEY_VALUE_HEADS * tokens
    block = 4 * tokens
    heads = KEY_VALUE_HEADS
    return pl.pallas_call(
        attend_kernel,
        out_shape=(
            jax.ShapeDtypeStruct((tokens, width), jnp.float32),
            jax.ShapeDtypeStruct((heads, 1, rows), jnp.float32),
            jax.ShapeDtypeStruct((tokens, width), jnp.bfloat16),
            jax.ShapeDtypeStruct(x.shape, jnp.float32),
            jax.ShapeDtypeStruct(x.shape, jnp.bfloat16),
        ),
        in_specs=[pl.BlockSpec(memory_space=pltpu.SMEM)] + [in_vmem()] * 6,
        out_specs=(in_vmem(),) * 5,
        scratch_shapes=[
            pltpu.VMEM((heads, HEAD_SIZE, rows), jnp.bfloat16),
            pltpu.VMEM((block, rows), jnp.float32),
            pltpu.VMEM((block, rows), jnp.bfloat16),
            pltpu.VMEM((block, tokens), jnp.float32),
            pltpu.VMEM((heads, 1, rows), jnp.float32),
            pltpu.VMEM((heads, 1, rows), jnp.float32),
            pltpu.VMEM((heads, HEAD_SIZE, rows), jnp.float32),
        ],
        compiler_params=pltpu.CompilerParams(vmem_limit_bytes=16 * 2**20),
        cost_estimate=pl.CostEstimate(
            flops=16 * tokens * width * pairs.shape[0], bytes_accessed=2 * 2**20, transcendentals=0
        ),
        name="attend",
    )(start, queries, pairs, low, x, out_matrix, gain)


def attend_back(start, queries, pairs, low, mix_grad, mixed, lse, cosine, sine):
    tokens, width = queries.shape
    rows = QUERY_HEADS // KEY_VALUE_HEADS * tokens
    block = 4 * tokens
    heads = KEY_VALUE_HEADS
    return pl.pallas_call(
        attend_back_kernel,
        out_shape=(
            jax.ShapeDtypeStruct((tokens, width), jnp.bfloat16),
            jax.ShapeDtypeStruct((pairs.shape[0] // tokens, tokens, pairs.shape[1]), jnp.bfloat16),
        ),
        in_specs=[pl.BlockSpec(memory_space=pltpu.SMEM)] + [in_vmem()] * 8,
        out_specs=(in_vmem(), in_vmem()),
        scratch_shapes=[
            pltpu.VMEM((heads, rows, HEAD_SIZE), jnp.bfloat16),
            pltpu.VMEM((heads, HEAD_SIZE, rows), jnp.bfloat16),
            pltpu.VMEM((heads, rows, HEAD_SIZE), jnp.bfloat16),
            pltpu.VMEM((heads, HEAD_SIZE, rows), jnp.bfloat16),
            pltpu.VMEM((heads, 1, rows), jnp.float32),
            pltpu.VMEM((block, rows), jnp.float32),
            pltpu.VMEM((block, rows), jnp.float32),
            pltpu.VMEM((block, rows), jnp.bfloat16),
            pltpu.VMEM((block, rows), jnp.bfloat16),
            pltpu.VMEM((block, tokens), jnp.float32),
            pltpu.VMEM((heads, HEAD_SIZE, rows), jnp.float32),
        ],
        compiler_params=pltpu.CompilerParams(vmem_limit_bytes=24 * 2**20),
        cost_estimate=pl.CostEstimate(
            flops=40 * tokens * width * pairs.shape[0], bytes_accessed=4 * 2**20, transcendentals=0
        ),
        name="attend_back",
    )(start, queries, pairs, low, mix_grad, mixed, lse, cosine, sine)


def split_kernel(place_ref, matrix_ref, kept_ref, sent_ref):
    z, core = place_ref[0], place_ref[1]
    width, lanes = matrix_ref.shape[1] // 16, kept_ref.shape[2] // 2
    for owner in range(8):
        at = lax.rem(owner // 2 - z + 4, 4)
        gate = matrix_ref[:, owner * width : (owner + 1) * width].astype(jnp.float32)
        up = matrix_ref[:, (8 + owner) * width : (9 + owner) * width].astype(jnp.float32)
        blank = jnp.zeros((gate.shape[0], lanes - width), jnp.float32)
        both = jnp.concatenate([gate, blank, up, blank], axis=1).astype(jnp.bfloat16)

        @pl.when(core == owner % 2)
        def _(both=both, at=at):
            kept_ref[at] = both

        @pl.when(core != owner % 2)
        def _(both=both, at=at):
            sent_ref[at] = both


def split_columns(place, matrix, lanes):
    rows = matrix.shape[0]
    out = jax.ShapeDtypeStruct((4, rows, 2 * lanes), matrix.dtype)
    return pl.pallas_call(
        split_kernel,
        out_shape=(out, out),
        in_specs=[pl.BlockSpec(memory_space=pltpu.SMEM), in_vmem()],
        out_specs=(in_vmem(), in_vmem()),
        compiler_params=pltpu.CompilerParams(vmem_limit_bytes=16 * 2**20),
        name="split_columns",
    )(place, matrix)


def place_kernel(at_ref, *refs):
    pieces, out_ref, rest_ref = refs[:-2], refs[-2], refs[-1]
    rows = out_ref.shape[0] // len(pieces)
    for n, piece in enumerate(pieces):
        out_ref[pl.ds(pl.multiple_of(at_ref[n] * rows, 16), rows), :] = piece[:rows, :]
        if piece.shape[0] > rows:
            rest_ref[at_ref[n]] = piece[rows:, :]
        else:
            rest_ref[...] = jnp.zeros_like(rest_ref)


def place_rows(at, pieces, rows):
    height, width = pieces[0].shape
    count = len(pieces)
    rest = (count, height - rows, width) if height > rows else (1, 8, 128)
    return pl.pallas_call(
        place_kernel,
        out_shape=(
            jax.ShapeDtypeStruct((count * rows, width), pieces[0].dtype),
            jax.ShapeDtypeStruct(rest, pieces[0].dtype if height > rows else jnp.float32),
        ),
        in_specs=[pl.BlockSpec(memory_space=pltpu.SMEM)] + [in_vmem()] * count,
        out_specs=(in_vmem(), in_vmem()),
        compiler_params=pltpu.CompilerParams(vmem_limit_bytes=12 * 2**20),
        name="place_rows",
    )(at, *pieces)


def feed_kernel(left_ref, right_ref, left_grad_ref, right_grad_ref, gate_up_ref, down_ref, hidden_ref, joined_ref, own_ref, other_ref):
    lanes = hidden_ref.shape[1]
    tokens = left_ref.shape[0]
    normed = jnp.concatenate([left_ref[...], right_ref[...]], axis=0)
    grad = jnp.concatenate([left_grad_ref[...], right_grad_ref[...]], axis=0)
    gate = jnp.dot(normed, gate_up_ref[:, :lanes], preferred_element_type=jnp.float32)
    up = jnp.dot(normed, gate_up_ref[:, lanes:], preferred_element_type=jnp.float32)
    hidden_grad = lax.dot_general(
        grad, down_ref[...], (((1,), (1,)), ((), ())), preferred_element_type=jnp.float32
    )
    sg = 1.0 / (1.0 + jnp.exp(-gate))
    act = gate * sg
    hidden_ref[...] = (act * up).astype(jnp.bfloat16)
    joined_ref[:, :lanes] = (hidden_grad * up * sg * (1.0 + gate * (1.0 - sg))).astype(jnp.bfloat16)
    joined_ref[:, lanes:] = (hidden_grad * act).astype(jnp.bfloat16)
    back = lax.dot_general(
        joined_ref[...], gate_up_ref[...], (((1,), (1,)), ((), ())), preferred_element_type=jnp.float32
    )
    own_ref[...] = back[:tokens]
    other_ref[...] = back[tokens:].astype(jnp.bfloat16)


def feed(normed, grads, gate_up, down):
    tokens, width = normed[0].shape
    lanes = down.shape[0]
    return pl.pallas_call(
        feed_kernel,
        out_shape=(
            jax.ShapeDtypeStruct((2 * tokens, lanes), jnp.bfloat16),
            jax.ShapeDtypeStruct((2 * tokens, 2 * lanes), jnp.bfloat16),
            jax.ShapeDtypeStruct((tokens, width), jnp.float32),
            jax.ShapeDtypeStruct((tokens, width), jnp.bfloat16),
        ),
        in_specs=[in_vmem()] * 6,
        out_specs=(in_vmem(),) * 4,
        compiler_params=pltpu.CompilerParams(vmem_limit_bytes=20 * 2**20),
        cost_estimate=pl.CostEstimate(
            flops=20 * tokens * width * lanes, bytes_accessed=6 * 2**20, transcendentals=0
        ),
        name="feed",
    )(*normed, *grads, gate_up, down)


def feed_grads_kernel(*refs):
    normed, grads, joined, hidden = refs[:8], refs[8:16], refs[16:20], refs[20:24]
    out_ref, down_ref, left_ref, right_ref, grads_ref, stage_ref, down_stage_ref = refs[-7:]
    lanes = hidden[0].shape[1]
    tile = 16
    rows = stage_ref.shape[0] // 8
    tokens = normed[0].shape[0]
    step = 2 * tokens
    for n in range(8):
        here = slice(n * tokens, (n + 1) * tokens)
        left_ref[:, here] = normed[n][...].astype(jnp.float32).T.astype(jnp.bfloat16)
        grads_ref[here, :] = grads[n][...]
    for half in range(2):
        for n in range(4):
            right_ref[n * step : (n + 1) * step, :] = joined[n][:, half * lanes : (half + 1) * lanes]
        stage_ref[...] = jnp.dot(left_ref[...], right_ref[...], preferred_element_type=jnp.float32)
        for r in range(rows // tile):
            for k in range(8):
                first = k * rows + r * tile
                out_ref[2 * r + half, k * tile : (k + 1) * tile, :] = stage_ref[
                    first : first + tile, :
                ].astype(jnp.bfloat16)
    for part in range(2 * rows // tile, 16):
        out_ref[part] = jnp.zeros((8 * tile, lanes), jnp.bfloat16)
    for n in range(4):
        left_ref[:lanes, n * step : (n + 1) * step] = (
            hidden[n][...].astype(jnp.float32).T.astype(jnp.bfloat16)
        )
    down_stage_ref[...] = jnp.dot(
        left_ref[:lanes, :], grads_ref[...], preferred_element_type=jnp.float32
    )
    down_ref[...] = down_stage_ref[: down_ref.shape[0], :].astype(jnp.bfloat16)


def feed_grads(normed, grads, joined, hidden, slice_width, earlier):
    tokens, width = normed[0].shape
    lanes = hidden[0].shape[1]
    return pl.pallas_call(
        feed_grads_kernel,
        out_shape=(
            jax.ShapeDtypeStruct((16, 8 * 16, lanes), jnp.bfloat16),
            jax.ShapeDtypeStruct((slice_width, width), jnp.bfloat16),
        ),
        in_specs=[in_vmem()] * 24 + [pl.BlockSpec(memory_space=pl.ANY)] * len(earlier),
        out_specs=(in_vmem(), in_vmem()),
        scratch_shapes=[
            pltpu.VMEM((width, 8 * tokens), jnp.bfloat16),
            pltpu.VMEM((8 * tokens, lanes), jnp.bfloat16),
            pltpu.VMEM((8 * tokens, width), jnp.bfloat16),
            pltpu.VMEM((width, lanes), jnp.float32),
            pltpu.VMEM((lanes, width), jnp.float32),
        ],
        compiler_params=pltpu.CompilerParams(vmem_limit_bytes=32 * 2**20),
        cost_estimate=pl.CostEstimate(
            flops=48 * tokens * width * lanes, bytes_accessed=12 * 2**20, transcendentals=0
        ),
        name="feed_grads",
    )(*normed, *grads, *joined, *hidden, *earlier)


def owner_parts_kernel(place_ref, parts_ref, kept_ref, sent_ref):
    z, core = place_ref[0], place_ref[1]
    rows = kept_ref.shape[1]
    for owner in range(8):
        at = lax.rem(owner // 2 - z + 4, 4)
        here = slice(owner * rows, (owner + 1) * rows)
        total = parts_ref[0, here, :].astype(jnp.float32)
        for n in range(1, parts_ref.shape[0]):
            total = total + parts_ref[n, here, :].astype(jnp.float32)
        total = total.astype(jnp.bfloat16)

        @pl.when(core == owner % 2)
        def _(total=total, at=at):
            kept_ref[at] = total

        @pl.when(core != owner % 2)
        def _(total=total, at=at):
            sent_ref[at] = total


def owner_parts(place, parts):
    _, height, width = parts.shape
    out = jax.ShapeDtypeStruct((4, height // 8, width), jnp.bfloat16)
    return pl.pallas_call(
        owner_parts_kernel,
        out_shape=(out, out),
        in_specs=[pl.BlockSpec(memory_space=pltpu.SMEM), in_vmem()],
        out_specs=(in_vmem(), in_vmem()),
        compiler_params=pltpu.CompilerParams(vmem_limit_bytes=12 * 2**20),
        name="owner_parts",
    )(place, parts)


def rows_grads_kernel(place_ref, *refs):
    kept_ref, sent_ref, stage_ref = refs[-3:]
    pairs = (len(refs) - 3) // 2
    rest_ref = refs[2 * pairs] if (len(refs) - 3) % 2 else None
    z, core = place_ref[0], place_ref[1]
    rows = stage_ref.shape[0] // 8
    first = 0
    for n in range(pairs):
        left, right = refs[2 * n], refs[2 * n + 1]
        turned = left[...].astype(jnp.float32).T.astype(jnp.bfloat16)
        stage_ref[:, first : first + right.shape[1]] = jnp.dot(
            turned, right[...], preferred_element_type=jnp.float32
        )
        first += right.shape[1]
    for owner in range(8):
        at = lax.rem(owner // 2 - z + 4, 4)

        @pl.when(core == owner % 2)
        def _(owner=owner, at=at):
            kept_ref[at, :rows, :] = stage_ref[owner * rows : (owner + 1) * rows, :].astype(jnp.bfloat16)
            if rest_ref is not None:
                kept_ref[at, rows:, :] = rest_ref[owner]

        @pl.when(core != owner % 2)
        def _(owner=owner, at=at):
            sent_ref[at, :rows, :] = stage_ref[owner * rows : (owner + 1) * rows, :].astype(jnp.bfloat16)
            if rest_ref is not None:
                sent_ref[at, rows:, :] = rest_ref[owner]


def rows_grads(place, pairs, rest=None):
    height = pairs[0][0].shape[1]
    width = sum(right.shape[1] for _, right in pairs)
    rows = height // 8 + (0 if rest is None else rest.shape[1])
    arrays = [array for pair in pairs for array in pair] + ([] if rest is None else [rest])
    out = jax.ShapeDtypeStruct((4, rows, width), jnp.bfloat16)
    return pl.pallas_call(
        rows_grads_kernel,
        out_shape=(out, out),
        in_specs=[pl.BlockSpec(memory_space=pltpu.SMEM)] + [in_vmem()] * len(arrays),
        out_specs=(in_vmem(), in_vmem()),
        scratch_shapes=[pltpu.VMEM((height, width), jnp.float32)],
        compiler_params=pltpu.CompilerParams(vmem_limit_bytes=16 * 2**20),
        cost_estimate=pl.CostEstimate(
            flops=2 * 128 * height * width, bytes_accessed=4 * 2**20, transcendentals=0
        ),
        name="rows_grads",
    )(place, *arrays)


def join_kernel(parts_ref, gate_up_ref):
    width = gate_up_ref.shape[1] // 16
    tile = 16
    for part in range(2 * gate_up_ref.shape[0] // tile):
        r, half = divmod(part, 2)
        columns = [
            parts_ref[part, k * tile : (k + 1) * tile, :].astype(jnp.float32)[:, :width]
            for k in range(8)
        ]
        gate_up_ref[r * tile : (r + 1) * tile, half * 8 * width : (half + 1) * 8 * width] = (
            jnp.concatenate(columns, axis=1)
        )


def join_columns(parts, rows, width):
    return pl.pallas_call(
        join_kernel,
        out_shape=jax.ShapeDtypeStruct((rows, 16 * width), jnp.float32),
        in_specs=[in_vmem()],
        out_specs=in_vmem(),
        compiler_params=pltpu.CompilerParams(vmem_limit_bytes=20 * 2**20),
        name="join_columns",
    )(parts)


def columns_kernel(*refs):
    early, late, out_ref = refs[:5], refs[5:10], refs[10]
    rows = early[0].shape[0]
    columns = out_ref.shape[2]
    blank = jnp.zeros((out_ref.shape[1] - rows, columns), jnp.float32)
    count = early[0].shape[1] // columns
    for n in range(out_ref.shape[0]):
        refs = early if n < count else late
        first = (n if n < count else n - count) * columns
        total = refs[0][:, first : first + columns].astype(jnp.float32)
        for ref in refs[1:]:
            total = total + ref[:, first : first + columns].astype(jnp.float32)
        if n < count:
            total = jnp.concatenate([total, blank], axis=0)
        out_ref[n] = total.astype(jnp.bfloat16)


def column_parts(early, late):
    height = late[0].shape[0]
    columns = (early[0].shape[1] + late[0].shape[1]) // 16
    return pl.pallas_call(
        columns_kernel,
        out_shape=jax.ShapeDtypeStruct((16, height, columns), jnp.bfloat16),
        in_specs=[in_vmem()] * 10,
        out_specs=in_vmem(),
        compiler_params=pltpu.CompilerParams(vmem_limit_bytes=12 * 2**20),
        name="column_parts",
    )(*early, *late)


def core_swap(value):
    return lax.ppermute(value, "wa", [(i, i ^ 1) for i in range(8)])


def z_shift(value, step):
    return lax.ppermute(value, "wa", [(i, (i + 2 * step) % 8) for i in range(8)])


def ctx_exchange(value):
    return lax.all_to_all(value, "ctx", 0, 0, tiled=True)


def ctx_gather(value):
    return ctx_exchange(jnp.broadcast_to(value[None], (16,) + value.shape))


STEPS = (0, 1, 3, 2)


def gather_tokens(value):
    pieces = [z_shift(value, step) if step else value for step in STEPS]
    return [(piece, core_swap(piece)) for piece in pieces]


def pair_tokens(own, other):
    return [
        (mine + core_swap(theirs).astype(jnp.float32)).astype(jnp.bfloat16)
        for mine, theirs in zip(own, other)
    ]


def reduce_tokens(paired):
    total = 0.0
    for step, mine in zip(STEPS, paired):
        total = total + (z_shift(mine, -step) if step else mine).astype(jnp.float32)
    return total


def reduce_rows(kept, sent):
    other = core_swap(sent)
    pieces = [kept[0], other[0]]
    for step in STEPS[1:]:
        mine = kept[step].astype(jnp.float32) + other[step].astype(jnp.float32)
        pieces.append(z_shift(mine.astype(jnp.bfloat16), step))
    return pieces


def after(value, *others):
    held = sum(other[(0,) * other.ndim].astype(jnp.float32) for other in others) * 0.0
    return value + held.astype(value.dtype)


def spread_kernel(parts_ref, left_ref, right_ref, small_ref):
    columns = parts_ref.shape[2]
    rows = left_ref.shape[0]
    count = left_ref.shape[1] // columns
    for n in range(parts_ref.shape[0]):
        part = parts_ref[n].astype(jnp.float32)
        if n < count:
            left_ref[:, n * columns : (n + 1) * columns] = part[:rows]
        else:
            right_ref[:, (n - count) * columns : (n - count + 1) * columns] = part[:rows]
        last = n - parts_ref.shape[0] + small_ref.shape[1] // columns
        if last >= 0:
            small_ref[:, last * columns : (last + 1) * columns] = part[rows : rows + 8]


def spread_columns(parts, rows, width, small_width):
    count, _, columns = parts.shape
    return pl.pallas_call(
        spread_kernel,
        out_shape=(
            jax.ShapeDtypeStruct((rows, width), jnp.float32),
            jax.ShapeDtypeStruct((rows, count * columns - width), jnp.float32),
            jax.ShapeDtypeStruct((8, small_width), jnp.float32),
        ),
        in_specs=[in_vmem()],
        out_specs=(in_vmem(),) * 3,
        compiler_params=pltpu.CompilerParams(vmem_limit_bytes=12 * 2**20),
        name="spread_columns",
    )(parts)


def on_device(
    layer_input,
    positions,
    attention_gain,
    projection,
    projection_biases,
    output_matrix,
    feed_gain,
    gate_up_matrix,
    down_matrix,
    cotangent,
):
    place = lax.axis_index("wa").astype(jnp.int32)
    z, core = place // 2, place % 2
    ctx = lax.axis_index("ctx").astype(jnp.int32)
    rows = projection.shape[0]
    tokens = layer_input.shape[1]
    query_width = QUERY_HEADS * HEAD_SIZE
    key_width = KEY_VALUE_HEADS * HEAD_SIZE
    width = layer_input.shape[2]
    proj_width = projection.shape[1]
    bias_rows = projection_biases.shape[0]
    slice_width = down_matrix.shape[0]
    lanes = -(-slice_width // 128) * 128
    tile = 16
    sources = [(z + 4 - step) % 4 for step in STEPS]

    small = jnp.concatenate([projection_biases, attention_gain, feed_gain])
    small = jnp.pad(small[None], ((0, tile - 1), (0, proj_width - small.shape[0])))
    packed = jnp.concatenate([projection, small], axis=0)
    own = [z_shift(packed, step) if step else packed for step in STEPS]
    others = [core_swap(piece) for piece in own]
    places = jnp.stack([2 * s + core for s in sources] + [2 * s + 1 - core for s in sources])
    full_proj, vectors = place_rows(places, own + others, rows)
    vectors = vectors[:, 0].astype(jnp.float32)
    full_bias = vectors[:, :bias_rows].reshape(1, proj_width)
    gain_one = vectors[:, bias_rows : bias_rows + rows].reshape(1, width)
    gain_two = vectors[:, bias_rows + rows : bias_rows + 2 * rows].reshape(1, width)
    out_rows = after(output_matrix, own[1])
    out_rows = [z_shift(out_rows, step) if step else out_rows for step in STEPS]
    complete_output, _ = place_rows(places, out_rows + [core_swap(piece) for piece in out_rows], rows)

    spot = jnp.stack([z, core])
    kept, sent = split_columns(spot, gate_up_matrix, lanes)
    other = core_swap(sent)
    pieces = []
    for step in STEPS:
        if step:
            both = jnp.concatenate([kept[step], other[step]], axis=0)
            both = z_shift(after(both, out_rows[1], out_rows[2]), step)
            pieces += [both[:rows], both[rows:]]
        else:
            pieces += [kept[0], other[0]]
    part_places = jnp.stack([p for s in sources for p in (2 * s + core, 2 * s + 1 - core)])
    gate_up, _ = place_rows(part_places, pieces, rows)
    down = jnp.pad(down_matrix, ((0, lanes - slice_width), (0, 0)))

    layer_rows = layer_input[0]
    query_pos = positions[0]
    cosine, sine = angles(query_pos)
    cosine = jnp.tile(cosine, (1, 4))
    sine = jnp.tile(jnp.concatenate([-sine, sine], axis=1), (1, 2))
    first_normed, queries, pair = project(layer_rows, gain_one, full_proj, full_bias, cosine, sine)
    out_grad = cotangent[0]
    grad_pairs = gather_tokens(after(out_grad, pieces[2]))

    pairs = ctx_exchange(pair).reshape(16 * tokens, 2 * key_width)
    low = ctx * tokens + jnp.arange(tokens, dtype=jnp.int32) - query_pos
    block = 4 * tokens
    start = jnp.stack(
        [
            ctx * tokens,
            jnp.maximum(jnp.min(low), 0) // block,
            (ctx * tokens + tokens + block - 1) // block,
        ]
    ).astype(jnp.int32)
    low = low[None]
    mixed, lse, attention_output, middle_state, second_normed = attend(
        start, queries, pairs, low, layer_rows, complete_output, gain_two
    )

    normed_pairs = gather_tokens(second_normed)
    worked = [
        feed(normed, grads, gate_up, down) for normed, grads in zip(normed_pairs, grad_pairs)
    ]
    hidden_pieces, joined_pieces, own, other = zip(*worked)
    paired = pair_tokens(own, other)

    gate_up_parts, down_local = feed_grads(
        [piece for pair in normed_pairs for piece in pair],
        [piece for pair in grad_pairs for piece in pair],
        joined_pieces,
        hidden_pieces,
        slice_width,
        paired,
    )
    down_total = lax.psum(down_local, "ctx").astype(jnp.float32)
    normed_two_grad = after(reduce_tokens(paired), down_local)
    gate_up_parts = ctx_exchange(gate_up_parts)

    _, norm_two_pull = jax.vjp(norm_rows, middle_state, gain_two[0])
    middle_part, gain_two_local = norm_two_pull(normed_two_grad)
    middle_grad = out_grad.astype(jnp.float32) + middle_part
    middle_lower = middle_grad.astype(jnp.bfloat16)
    mix_grad = column_product(middle_lower, complete_output).astype(jnp.bfloat16)
    query_back, pair_grad = attend_back(
        start, queries, pairs, low, mix_grad, mixed, lse, cosine, sine
    )
    early = reduce_rows(
        *rows_grads(spot, [(attention_output, middle_lower), (first_normed, query_back)])
    )

    feed_down = after(down, mix_grad)
    feed_outs = [
        jnp.dot(hidden, feed_down, preferred_element_type=jnp.float32) for hidden in hidden_pieces
    ]
    feed_out = reduce_tokens(
        pair_tokens(
            [part[:tokens] for part in feed_outs],
            [part[tokens:].astype(jnp.bfloat16) for part in feed_outs],
        )
    )
    result = (middle_state + feed_out).astype(jnp.bfloat16)

    pieces = ctx_exchange(pair_grad)
    input_grad, kept, sent = project_back(
        spot,
        layer_rows,
        gain_one,
        full_proj,
        cosine,
        sine,
        first_normed,
        query_back,
        middle_grad,
        gain_two_local[None],
        pieces,
    )
    late = reduce_rows(kept, sent)

    kept, sent = owner_parts(spot, gate_up_parts)
    other = core_swap(sent)
    parts = []
    for step in STEPS:
        if step:
            both = z_shift(jnp.concatenate([kept[step], other[step]], axis=0), step)
            parts += [both[:tile], both[tile:]]
        else:
            parts += [kept[0], other[0]]
    parts, _ = place_rows(part_places, parts, tile)
    parts = ctx_gather(after(parts, pieces))
    gate_up_total = join_columns(parts, rows, slice_width)

    mine = ctx_exchange(column_parts(early, late))
    mine = ctx_gather(jnp.sum(mine.astype(jnp.float32), axis=0).astype(jnp.bfloat16))
    output_total, projection_total, vectors = spread_columns(mine, rows, width, 2 * key_width)
    return (
        result[None],
        input_grad[None],
        vectors[0, bias_rows : bias_rows + rows],
        projection_total,
        vectors[0, :bias_rows],
        output_total,
        vectors[1, :rows],
        gate_up_total,
        down_total,
    )


def solution(mesh):
    placed = (
        P("wa", "ctx", None),
        P("wa", "ctx"),
        P("wa"),
        P("wa", None),
        P("wa"),
        P("wa", None),
        P("wa"),
        P("wa", None),
        P("wa", None),
        P("wa", "ctx", None),
    )
    return jax.shard_map(
        on_device,
        mesh=mesh,
        in_specs=placed,
        out_specs=(
            P("wa", "ctx", None),
            P("wa", "ctx", None),
            P("wa"),
            P("wa", None),
            P("wa"),
            P("wa", None),
            P("wa"),
            P("wa", None),
            P("wa", None),
        ),
        check_vma=False,
    )
```

```python
import functools

import jax
import jax.numpy as jnp
from jax import lax
from jax.experimental import pallas as pl
from jax.experimental.pallas import tpu as pltpu
from jax.sharding import PartitionSpec as P

QUERY_HEADS = 14
KEY_VALUE_HEADS = 2
HEAD_SIZE = 64
FF = 4864


EPS = 1e-06
THETA = 1000000.0
NEG = -1e30


def rows_product(left, right):
    return lax.dot_general(
        left, right, (((0,), (0,)), ((), ())), preferred_element_type=jnp.float32
    )


def column_product(left, right):
    return lax.dot_general(
        left, right, (((1,), (1,)), ((), ())), preferred_element_type=jnp.float32
    )


def norm_rows(value, gain):
    return value * lax.rsqrt(jnp.mean(value * value, axis=-1, keepdims=True) + EPS) * gain


def rotate(tensor, cosine_table, sine_table):
    half = tensor.shape[-1] // 2
    first = tensor[..., :half]
    second = tensor[..., half:]
    return jnp.concatenate(
        [first * cosine_table - second * sine_table, second * cosine_table + first * sine_table],
        axis=-1,
    )


def inverse_rotate(tensor, cosine_table, sine_table):
    half = tensor.shape[-1] // 2
    first = tensor[..., :half]
    second = tensor[..., half:]
    return jnp.concatenate(
        [first * cosine_table + second * sine_table, second * cosine_table - first * sine_table],
        axis=-1,
    )


def angles(positions):
    half = HEAD_SIZE // 2
    inverse = THETA ** (-(jnp.arange(half) * 2.0 / HEAD_SIZE))
    turned = positions.astype(jnp.float32)[:, None] * inverse.astype(jnp.float32)
    return (jnp.cos(turned), jnp.sin(turned))


def turn_heads(value, cosine, sine):
    width = value.shape[1]
    lane = lax.broadcasted_iota(jnp.int32, value.shape, 1)
    half = HEAD_SIZE // 2
    partner = jnp.where(
        lane % HEAD_SIZE < half, pltpu.roll(value, width - half, 1), pltpu.roll(value, half, 1)
    )
    repeats = width // cosine.shape[1]
    return value * jnp.tile(cosine, (1, repeats)) + partner * jnp.tile(sine, (1, repeats))


def project_kernel(x_ref, gain_ref, proj_ref, bias_ref, cos_ref, sin_ref, normed_ref, q_ref, pairs_ref):
    x = x_ref[...].astype(jnp.float32)
    scale = lax.rsqrt(jnp.mean(x * x, axis=-1, keepdims=True) + EPS)
    normed = (x * scale * gain_ref[...]).astype(jnp.bfloat16)
    normed_ref[...] = normed
    width = q_ref.shape[1]
    turned = width + KEY_VALUE_HEADS * HEAD_SIZE
    projected = jnp.dot(normed, proj_ref[...], preferred_element_type=jnp.float32) + bias_ref[...]
    rotated = turn_heads(projected[:, :turned], cos_ref[...], sin_ref[...])
    q_ref[...] = rotated[:, :width].astype(jnp.bfloat16)
    pair = jnp.concatenate([rotated[:, width:], projected[:, turned:]], axis=1).astype(jnp.bfloat16)
    for n in range(pairs_ref.shape[0]):
        pairs_ref[n] = pair


def project(x, gain, proj, bias, cosine, sine):
    tokens, width = x.shape
    return pl.pallas_call(
        project_kernel,
        out_shape=(
            jax.ShapeDtypeStruct((tokens, width), jnp.bfloat16),
            jax.ShapeDtypeStruct((tokens, QUERY_HEADS * HEAD_SIZE), jnp.bfloat16),
            jax.ShapeDtypeStruct((16, tokens, 2 * KEY_VALUE_HEADS * HEAD_SIZE), jnp.bfloat16),
        ),
        in_specs=[in_vmem()] * 6,
        out_specs=(in_vmem(),) * 3,
        compiler_params=pltpu.CompilerParams(vmem_limit_bytes=12 * 2**20),
        name="project",
    )(x, gain, proj, bias, cosine, sine)


def project_back_kernel(
    place_ref, x_ref, gain_ref, proj_ref, cos_ref, sin_ref, normed_ref, dq_ref, grad_ref, gain_two_ref,
    pieces_ref, input_grad_ref, kept_ref, sent_ref, stage_ref,
):
    z, core = place_ref[0], place_ref[1]
    key_width = KEY_VALUE_HEADS * HEAD_SIZE
    pair = pieces_ref[0].astype(jnp.float32)
    for n in range(1, pieces_ref.shape[0]):
        pair = pair + pieces_ref[n].astype(jnp.float32)
    keys = turn_heads(pair[:, :key_width], cos_ref[...], -sin_ref[...])
    pair = jnp.concatenate([keys, pair[:, key_width:]], axis=1).astype(jnp.bfloat16)
    turned = normed_ref[...].astype(jnp.float32).T.astype(jnp.bfloat16)
    stage_ref[...] = jnp.dot(turned, pair, preferred_element_type=jnp.float32)
    bias = jnp.concatenate(
        [
            jnp.sum(dq_ref[...].astype(jnp.float32), axis=0, keepdims=True),
            jnp.sum(pair.astype(jnp.float32), axis=0, keepdims=True),
        ],
        axis=1,
    )
    x = x_ref[...].astype(jnp.float32)
    scale = lax.rsqrt(jnp.mean(x * x, axis=-1, keepdims=True) + EPS)
    grad = lax.dot_general(
        jnp.concatenate([dq_ref[...], pair], axis=1),
        proj_ref[...],
        (((1,), (1,)), ((), ())),
        preferred_element_type=jnp.float32,
    )
    gain_one = jnp.sum(grad * x * scale, axis=0, keepdims=True)
    gained = grad * gain_ref[...]
    mean = jnp.mean(gained * x, axis=-1, keepdims=True)
    input_grad_ref[...] = grad_ref[...] + scale * gained - x * (scale * scale * scale * mean)

    rows = stage_ref.shape[0] // 8
    bias_rows = bias.shape[1] // 8
    blank = jnp.zeros((kept_ref.shape[1] - rows - 2, stage_ref.shape[1]), jnp.float32)
    for owner in range(8):
        at = lax.rem(owner // 2 - z + 4, 4)
        here = slice(owner * rows, (owner + 1) * rows)
        gain_two = gain_two_ref[:, here]
        first = jnp.concatenate(
            [bias[:, owner * bias_rows : (owner + 1) * bias_rows], gain_one[:, here]], axis=1
        )
        second = jnp.concatenate(
            [gain_two, jnp.zeros((1, stage_ref.shape[1] - rows), jnp.float32)], axis=1
        )
        both = jnp.concatenate([stage_ref[here, :], first, second, blank], axis=0).astype(jnp.bfloat16)

        @pl.when(core == owner % 2)
        def _(both=both, at=at):
            kept_ref[at] = both

        @pl.when(core != owner % 2)
        def _(both=both, at=at):
            sent_ref[at] = both


def project_back(place, x, gain, proj, cosine, sine, normed, dq, grad, gain_two, pieces):
    tokens, width = x.shape
    pair_width = pieces.shape[2]
    out = jax.ShapeDtypeStruct((4, width // 8 + 16, pair_width), jnp.bfloat16)
    return pl.pallas_call(
        project_back_kernel,
        out_shape=(jax.ShapeDtypeStruct((tokens, width), jnp.float32), out, out),
        in_specs=[pl.BlockSpec(memory_space=pltpu.SMEM)] + [in_vmem()] * 10,
        out_specs=(in_vmem(),) * 3,
        scratch_shapes=[pltpu.VMEM((width, pair_width), jnp.float32)],
        compiler_params=pltpu.CompilerParams(vmem_limit_bytes=16 * 2**20),
        name="project_back",
    )(place, x, gain, proj, cosine, sine, normed, dq, grad, gain_two, pieces)


def key_bias(low_ref, block_start, block, first_index):
    tokens = low_ref.shape[1]
    keys = block_start + lax.broadcasted_iota(jnp.int32, (block, tokens), 0)
    index = first_index + lax.broadcasted_iota(jnp.int32, (block, tokens), 1)
    return jnp.where((keys <= index) & (keys >= low_ref[...]), 0.0, NEG)


def head_places(tokens):
    group = QUERY_HEADS // KEY_VALUE_HEADS
    for h in range(QUERY_HEADS):
        g, i = divmod(h, group)
        yield g, slice(h * HEAD_SIZE, (h + 1) * HEAD_SIZE), slice(i * tokens, (i + 1) * tokens)


def attend_kernel(
    start_ref, q_ref, kv_ref, low_ref, x_ref, out_ref, gain_ref, *refs
):
    mixed_ref, lse_ref, attended_ref, middle_ref, normed_ref = refs[-12:-7]
    qt, s_ref, p_ref, bias_ref, m_ref, l_ref, acc_ref = refs[-7:]
    tokens = q_ref.shape[0]
    block, rows = s_ref.shape
    turned = (q_ref[...].astype(jnp.float32) * HEAD_SIZE ** (-0.5)).T.astype(jnp.bfloat16)
    for g, lanes, at in head_places(tokens):
        qt[g, :, at] = turned[lanes, :]
    m_ref[...] = jnp.full_like(m_ref, NEG)
    l_ref[...] = jnp.zeros_like(l_ref)
    acc_ref[...] = jnp.zeros_like(acc_ref)

    def visit(which, carry):
        block_start = pl.multiple_of(which * block, block)
        here = pl.ds(block_start, block)
        bias_ref[...] = key_bias(low_ref, block_start, block, start_ref[0])
        key_width = KEY_VALUE_HEADS * HEAD_SIZE
        values = kv_ref[here, key_width:].astype(jnp.float32).T.astype(jnp.bfloat16)
        for g in range(KEY_VALUE_HEADS):
            lanes = slice(g * HEAD_SIZE, (g + 1) * HEAD_SIZE)
            s_ref[...] = jnp.dot(kv_ref[here, lanes], qt[g], preferred_element_type=jnp.float32)
            for i in range(rows // tokens):
                at = slice(i * tokens, (i + 1) * tokens)
                s = s_ref[:, at] + bias_ref[...]
                old = m_ref[g, :, at]
                peak = jnp.maximum(old, jnp.max(s, axis=0, keepdims=True))
                e = jnp.exp(s - peak)
                scale = jnp.exp(old - peak)
                m_ref[g, :, at] = peak
                l_ref[g, :, at] = l_ref[g, :, at] * scale + jnp.sum(e, axis=0, keepdims=True)
                acc_ref[g, :, at] = acc_ref[g, :, at] * scale
                p_ref[:, at] = e.astype(jnp.bfloat16)
            acc_ref[g] += jnp.dot(values[lanes, :], p_ref[...], preferred_element_type=jnp.float32)
        return carry

    lax.fori_loop(start_ref[1], start_ref[2], visit, 0)
    mixed = [acc_ref[g, :, at] / l_ref[g, :, at] for g, _, at in head_places(tokens)]
    mixed = jnp.concatenate(mixed, axis=0).T
    mixed_ref[...] = mixed
    lse_ref[...] = m_ref[...] + jnp.log(l_ref[...])
    attended = mixed.astype(jnp.bfloat16)
    attended_ref[...] = attended
    middle = x_ref[...].astype(jnp.float32) + jnp.dot(
        attended, out_ref[...], preferred_element_type=jnp.float32
    )
    middle_ref[...] = middle
    scale = lax.rsqrt(jnp.mean(middle * middle, axis=-1, keepdims=True) + EPS)
    normed_ref[...] = (middle * scale * gain_ref[...]).astype(jnp.bfloat16)


def attend_back_kernel(
    start_ref, q_ref, kv_ref, low_ref, dmix_ref, mixed_ref, lse_ref, cos_ref, sin_ref, dq_ref, dkv_ref,
    qs, qt, ms, mt, delta_ref, s_ref, dp_ref, p_ref, g_ref, bias_ref, acc_ref,
):
    tokens = q_ref.shape[0]
    block, rows = s_ref.shape
    key_width = KEY_VALUE_HEADS * HEAD_SIZE
    q = q_ref[...].astype(jnp.float32) * HEAD_SIZE ** (-0.5)
    dmix = dmix_ref[...].astype(jnp.float32)
    q_turned = q.T.astype(jnp.bfloat16)
    dmix_turned = dmix.T
    weighed = (dmix * mixed_ref[...]).T
    q = q.astype(jnp.bfloat16)
    for g, lanes, at in head_places(tokens):
        qs[g, at, :] = q[:, lanes]
        ms[g, at, :] = dmix_ref[:, lanes]
        qt[g, :, at] = q_turned[lanes, :]
        mt[g, :, at] = dmix_turned[lanes, :].astype(jnp.bfloat16)
        delta_ref[g, :, at] = jnp.sum(weighed[lanes, :], axis=0, keepdims=True)
    acc_ref[...] = jnp.zeros_like(acc_ref)
    dkv_ref[...] = jnp.zeros_like(dkv_ref)

    def visit(which, carry):
        block_start = pl.multiple_of(which * block, block)
        here = pl.ds(block_start, block)
        bias_ref[...] = key_bias(low_ref, block_start, block, start_ref[0])
        keys_turned = kv_ref[here, :key_width].astype(jnp.float32).T.astype(jnp.bfloat16)
        grads = [None] * (2 * KEY_VALUE_HEADS)
        for g in range(KEY_VALUE_HEADS):
            lanes = slice(g * HEAD_SIZE, (g + 1) * HEAD_SIZE)
            s_ref[...] = jnp.dot(kv_ref[here, lanes], qt[g], preferred_element_type=jnp.float32)
            values = kv_ref[here, key_width + g * HEAD_SIZE : key_width + (g + 1) * HEAD_SIZE]
            dp_ref[...] = jnp.dot(values, mt[g], preferred_element_type=jnp.float32)
            for i in range(rows // tokens):
                at = slice(i * tokens, (i + 1) * tokens)
                p = jnp.exp(s_ref[:, at] + bias_ref[...] - lse_ref[g, :, at])
                p_ref[:, at] = p.astype(jnp.bfloat16)
                g_ref[:, at] = (p * (dp_ref[:, at] - delta_ref[g, :, at])).astype(jnp.bfloat16)
            acc_ref[g] += jnp.dot(keys_turned[lanes, :], g_ref[...], preferred_element_type=jnp.float32)
            grads[g] = jnp.dot(g_ref[...], qs[g], preferred_element_type=jnp.float32)
            grads[KEY_VALUE_HEADS + g] = jnp.dot(
                p_ref[...], ms[g], preferred_element_type=jnp.float32
            )
        grads = jnp.concatenate(grads, axis=1).astype(jnp.bfloat16)
        for n in range(block // tokens):
            dkv_ref[which * (block // tokens) + n] = grads[n * tokens : (n + 1) * tokens, :]
        return carry

    lax.fori_loop(start_ref[1], start_ref[2], visit, 0)
    dq = [acc_ref[g, :, at] for g, _, at in head_places(tokens)]
    dq = jnp.concatenate(dq, axis=0).T * HEAD_SIZE ** (-0.5)
    dq_ref[...] = turn_heads(dq, cos_ref[...], -sin_ref[...]).astype(jnp.bfloat16)


def in_vmem():
    return pl.BlockSpec(memory_space=pltpu.VMEM)


def attend(start, queries, pairs, low, x, out_matrix, gain, earlier):
    tokens, width = queries.shape
    rows = QUERY_HEADS // KEY_VALUE_HEADS * tokens
    block = 4 * tokens
    heads = KEY_VALUE_HEADS
    return pl.pallas_call(
        attend_kernel,
        out_shape=(
            jax.ShapeDtypeStruct((tokens, width), jnp.float32),
            jax.ShapeDtypeStruct((heads, 1, rows), jnp.float32),
            jax.ShapeDtypeStruct((tokens, width), jnp.bfloat16),
            jax.ShapeDtypeStruct(x.shape, jnp.float32),
            jax.ShapeDtypeStruct(x.shape, jnp.bfloat16),
        ),
        in_specs=[pl.BlockSpec(memory_space=pltpu.SMEM)]
        + [in_vmem()] * 6
        + [pl.BlockSpec(memory_space=pl.ANY)] * len(earlier),
        out_specs=(in_vmem(),) * 5,
        scratch_shapes=[
            pltpu.VMEM((heads, HEAD_SIZE, rows), jnp.bfloat16),
            pltpu.VMEM((block, rows), jnp.float32),
            pltpu.VMEM((block, rows), jnp.bfloat16),
            pltpu.VMEM((block, tokens), jnp.float32),
            pltpu.VMEM((heads, 1, rows), jnp.float32),
            pltpu.VMEM((heads, 1, rows), jnp.float32),
            pltpu.VMEM((heads, HEAD_SIZE, rows), jnp.float32),
        ],
        compiler_params=pltpu.CompilerParams(vmem_limit_bytes=16 * 2**20),
        cost_estimate=pl.CostEstimate(
            flops=16 * tokens * width * pairs.shape[0], bytes_accessed=2 * 2**20, transcendentals=0
        ),
        name="attend",
    )(start, queries, pairs, low, x, out_matrix, gain, *earlier)


def attend_back(start, queries, pairs, low, mix_grad, mixed, lse, cosine, sine):
    tokens, width = queries.shape
    rows = QUERY_HEADS // KEY_VALUE_HEADS * tokens
    block = 4 * tokens
    heads = KEY_VALUE_HEADS
    return pl.pallas_call(
        attend_back_kernel,
        out_shape=(
            jax.ShapeDtypeStruct((tokens, width), jnp.bfloat16),
            jax.ShapeDtypeStruct((pairs.shape[0] // tokens, tokens, pairs.shape[1]), jnp.bfloat16),
        ),
        in_specs=[pl.BlockSpec(memory_space=pltpu.SMEM)] + [in_vmem()] * 8,
        out_specs=(in_vmem(), in_vmem()),
        scratch_shapes=[
            pltpu.VMEM((heads, rows, HEAD_SIZE), jnp.bfloat16),
            pltpu.VMEM((heads, HEAD_SIZE, rows), jnp.bfloat16),
            pltpu.VMEM((heads, rows, HEAD_SIZE), jnp.bfloat16),
            pltpu.VMEM((heads, HEAD_SIZE, rows), jnp.bfloat16),
            pltpu.VMEM((heads, 1, rows), jnp.float32),
            pltpu.VMEM((block, rows), jnp.float32),
            pltpu.VMEM((block, rows), jnp.float32),
            pltpu.VMEM((block, rows), jnp.bfloat16),
            pltpu.VMEM((block, rows), jnp.bfloat16),
            pltpu.VMEM((block, tokens), jnp.float32),
            pltpu.VMEM((heads, HEAD_SIZE, rows), jnp.float32),
        ],
        compiler_params=pltpu.CompilerParams(vmem_limit_bytes=24 * 2**20),
        cost_estimate=pl.CostEstimate(
            flops=40 * tokens * width * pairs.shape[0], bytes_accessed=4 * 2**20, transcendentals=0
        ),
        name="attend_back",
    )(start, queries, pairs, low, mix_grad, mixed, lse, cosine, sine)


def split_kernel(place_ref, matrix_ref, kept_ref, sent_ref):
    z, core = place_ref[0], place_ref[1]
    width, lanes = matrix_ref.shape[1] // 16, kept_ref.shape[2] // 2
    for owner in range(8):
        at = lax.rem(owner // 2 - z + 4, 4)
        gate = matrix_ref[:, owner * width : (owner + 1) * width].astype(jnp.float32)
        up = matrix_ref[:, (8 + owner) * width : (9 + owner) * width].astype(jnp.float32)
        blank = jnp.zeros((gate.shape[0], lanes - width), jnp.float32)
        both = jnp.concatenate([gate, blank, up, blank], axis=1).astype(jnp.bfloat16)

        @pl.when(core == owner % 2)
        def _(both=both, at=at):
            kept_ref[at] = both

        @pl.when(core != owner % 2)
        def _(both=both, at=at):
            sent_ref[at] = both


def split_columns(place, matrix, lanes):
    rows = matrix.shape[0]
    out = jax.ShapeDtypeStruct((4, rows, 2 * lanes), matrix.dtype)
    return pl.pallas_call(
        split_kernel,
        out_shape=(out, out),
        in_specs=[pl.BlockSpec(memory_space=pltpu.SMEM), in_vmem()],
        out_specs=(in_vmem(), in_vmem()),
        compiler_params=pltpu.CompilerParams(vmem_limit_bytes=16 * 2**20),
        name="split_columns",
    )(place, matrix)


def place_kernel(cuts, at_ref, *refs):
    pieces, (out_ref, rest_ref, sems, rest_sems) = refs[:-4], refs[-4:]
    rows = out_ref.shape[0] // len(cuts)
    copies = []
    for n, (which, lead, first) in enumerate(cuts):
        piece = pieces[which] if lead is None else pieces[which].at[lead]
        copies.append(
            pltpu.make_async_copy(
                piece.at[first : first + rows, :],
                out_ref.at[pl.ds(pl.multiple_of(at_ref[n] * rows, 16), rows), :],
                sems.at[n],
            )
        )
        if rest_ref.shape[0] == len(cuts):
            copies.append(
                pltpu.make_async_copy(piece.at[rows:, :], rest_ref.at[at_ref[n]], rest_sems.at[n])
            )
    for copy in copies:
        copy.start()
    if rest_ref.shape[0] != len(cuts):
        rest_ref[...] = jnp.zeros_like(rest_ref)
    for copy in copies:
        copy.wait()


def place_rows(at, arrays, cuts, rows, rest=0):
    width, kind = arrays[0].shape[-1], arrays[0].dtype
    count = len(cuts)
    rest_shape = (count, rest, width) if rest else (1, 8, 128)
    return pl.pallas_call(
        functools.partial(place_kernel, tuple(cuts)),
        out_shape=(
            jax.ShapeDtypeStruct((count * rows, width), kind),
            jax.ShapeDtypeStruct(rest_shape, kind if rest else jnp.float32),
        ),
        in_specs=[pl.BlockSpec(memory_space=pltpu.SMEM)]
        + [pl.BlockSpec(memory_space=pl.ANY)] * len(arrays),
        out_specs=(in_vmem(), in_vmem()),
        scratch_shapes=[pltpu.SemaphoreType.DMA((count,)), pltpu.SemaphoreType.DMA((count,))],
        compiler_params=pltpu.CompilerParams(vmem_limit_bytes=8 * 2**20),
        name="place_rows",
    )(at, *arrays)


def feed_kernel(left_ref, right_ref, left_grad_ref, right_grad_ref, gate_up_ref, down_ref, hidden_ref, joined_ref, own_ref, other_ref):
    lanes = hidden_ref.shape[1]
    tokens = left_ref.shape[0]
    normed = jnp.concatenate([left_ref[...], right_ref[...]], axis=0)
    grad = jnp.concatenate([left_grad_ref[...], right_grad_ref[...]], axis=0)
    gate = jnp.dot(normed, gate_up_ref[:, :lanes], preferred_element_type=jnp.float32)
    up = jnp.dot(normed, gate_up_ref[:, lanes:], preferred_element_type=jnp.float32)
    hidden_grad = lax.dot_general(
        grad, down_ref[...], (((1,), (1,)), ((), ())), preferred_element_type=jnp.float32
    )
    sg = 1.0 / (1.0 + jnp.exp(-gate))
    act = gate * sg
    hidden_ref[...] = (act * up).astype(jnp.bfloat16)
    joined_ref[:, :lanes] = (hidden_grad * up * sg * (1.0 + gate * (1.0 - sg))).astype(jnp.bfloat16)
    joined_ref[:, lanes:] = (hidden_grad * act).astype(jnp.bfloat16)
    back = lax.dot_general(
        joined_ref[...], gate_up_ref[...], (((1,), (1,)), ((), ())), preferred_element_type=jnp.float32
    )
    own_ref[...] = back[:tokens]
    other_ref[...] = back[tokens:].astype(jnp.bfloat16)


def feed(normed, grads, gate_up, down):
    tokens, width = normed[0].shape
    lanes = down.shape[0]
    return pl.pallas_call(
        feed_kernel,
        out_shape=(
            jax.ShapeDtypeStruct((2 * tokens, lanes), jnp.bfloat16),
            jax.ShapeDtypeStruct((2 * tokens, 2 * lanes), jnp.bfloat16),
            jax.ShapeDtypeStruct((tokens, width), jnp.float32),
            jax.ShapeDtypeStruct((tokens, width), jnp.bfloat16),
        ),
        in_specs=[in_vmem()] * 6,
        out_specs=(in_vmem(),) * 4,
        compiler_params=pltpu.CompilerParams(vmem_limit_bytes=20 * 2**20),
        cost_estimate=pl.CostEstimate(
            flops=20 * tokens * width * lanes, bytes_accessed=6 * 2**20, transcendentals=0
        ),
        name="feed",
    )(*normed, *grads, gate_up, down)


def feed_grads_kernel(*refs):
    normed, grads, joined, hidden = refs[:8], refs[8:16], refs[16:20], refs[20:24]
    out_ref, down_ref, left_ref, right_ref, grads_ref, stage_ref, down_stage_ref = refs[-7:]
    lanes = hidden[0].shape[1]
    tile = 16
    rows = stage_ref.shape[0] // 8
    tokens = normed[0].shape[0]
    step = 2 * tokens
    for n in range(8):
        here = slice(n * tokens, (n + 1) * tokens)
        left_ref[:, here] = normed[n][...].astype(jnp.float32).T.astype(jnp.bfloat16)
        grads_ref[here, :] = grads[n][...]
    for half in range(2):
        for n in range(4):
            right_ref[n * step : (n + 1) * step, :] = joined[n][:, half * lanes : (half + 1) * lanes]
        stage_ref[...] = jnp.dot(left_ref[...], right_ref[...], preferred_element_type=jnp.float32)
        for r in range(rows // tile):
            for k in range(8):
                first = k * rows + r * tile
                out_ref[2 * r + half, k * tile : (k + 1) * tile, :] = stage_ref[
                    first : first + tile, :
                ].astype(jnp.bfloat16)
    for part in range(2 * rows // tile, 16):
        out_ref[part] = jnp.zeros((8 * tile, lanes), jnp.bfloat16)
    for n in range(4):
        left_ref[:lanes, n * step : (n + 1) * step] = (
            hidden[n][...].astype(jnp.float32).T.astype(jnp.bfloat16)
        )
    down_stage_ref[...] = jnp.dot(
        left_ref[:lanes, :], grads_ref[...], preferred_element_type=jnp.float32
    )
    down_ref[...] = down_stage_ref[: down_ref.shape[0], :].astype(jnp.bfloat16)


def feed_grads(normed, grads, joined, hidden, slice_width, earlier):
    tokens, width = normed[0].shape
    lanes = hidden[0].shape[1]
    return pl.pallas_call(
        feed_grads_kernel,
        out_shape=(
            jax.ShapeDtypeStruct((16, 8 * 16, lanes), jnp.bfloat16),
            jax.ShapeDtypeStruct((slice_width, width), jnp.bfloat16),
        ),
        in_specs=[in_vmem()] * 24 + [pl.BlockSpec(memory_space=pl.ANY)] * len(earlier),
        out_specs=(in_vmem(), in_vmem()),
        scratch_shapes=[
            pltpu.VMEM((width, 8 * tokens), jnp.bfloat16),
            pltpu.VMEM((8 * tokens, lanes), jnp.bfloat16),
            pltpu.VMEM((8 * tokens, width), jnp.bfloat16),
            pltpu.VMEM((width, lanes), jnp.float32),
            pltpu.VMEM((lanes, width), jnp.float32),
        ],
        compiler_params=pltpu.CompilerParams(vmem_limit_bytes=32 * 2**20),
        cost_estimate=pl.CostEstimate(
            flops=48 * tokens * width * lanes, bytes_accessed=12 * 2**20, transcendentals=0
        ),
        name="feed_grads",
    )(*normed, *grads, *joined, *hidden, *earlier)


def owner_parts_kernel(place_ref, parts_ref, kept_ref, sent_ref):
    z, core = place_ref[0], place_ref[1]
    rows = kept_ref.shape[1]
    for owner in range(8):
        at = lax.rem(owner // 2 - z + 4, 4)
        here = slice(owner * rows, (owner + 1) * rows)
        total = parts_ref[0, here, :].astype(jnp.float32)
        for n in range(1, parts_ref.shape[0]):
            total = total + parts_ref[n, here, :].astype(jnp.float32)
        total = total.astype(jnp.bfloat16)

        @pl.when(core == owner % 2)
        def _(total=total, at=at):
            kept_ref[at] = total

        @pl.when(core != owner % 2)
        def _(total=total, at=at):
            sent_ref[at] = total


def owner_parts(place, parts):
    _, height, width = parts.shape
    out = jax.ShapeDtypeStruct((4, height // 8, width), jnp.bfloat16)
    return pl.pallas_call(
        owner_parts_kernel,
        out_shape=(out, out),
        in_specs=[pl.BlockSpec(memory_space=pltpu.SMEM), in_vmem()],
        out_specs=(in_vmem(), in_vmem()),
        compiler_params=pltpu.CompilerParams(vmem_limit_bytes=12 * 2**20),
        name="owner_parts",
    )(place, parts)


def rows_grads_kernel(place_ref, *refs):
    kept_ref, sent_ref, stage_ref = refs[-3:]
    pairs = (len(refs) - 3) // 2
    rest_ref = refs[2 * pairs] if (len(refs) - 3) % 2 else None
    z, core = place_ref[0], place_ref[1]
    rows = stage_ref.shape[0] // 8
    first = 0
    for n in range(pairs):
        left, right = refs[2 * n], refs[2 * n + 1]
        turned = left[...].astype(jnp.float32).T.astype(jnp.bfloat16)
        stage_ref[:, first : first + right.shape[1]] = jnp.dot(
            turned, right[...], preferred_element_type=jnp.float32
        )
        first += right.shape[1]
    for owner in range(8):
        at = lax.rem(owner // 2 - z + 4, 4)

        @pl.when(core == owner % 2)
        def _(owner=owner, at=at):
            kept_ref[at, :rows, :] = stage_ref[owner * rows : (owner + 1) * rows, :].astype(jnp.bfloat16)
            if rest_ref is not None:
                kept_ref[at, rows:, :] = rest_ref[owner]

        @pl.when(core != owner % 2)
        def _(owner=owner, at=at):
            sent_ref[at, :rows, :] = stage_ref[owner * rows : (owner + 1) * rows, :].astype(jnp.bfloat16)
            if rest_ref is not None:
                sent_ref[at, rows:, :] = rest_ref[owner]


def rows_grads(place, pairs, rest=None):
    height = pairs[0][0].shape[1]
    width = sum(right.shape[1] for _, right in pairs)
    rows = height // 8 + (0 if rest is None else rest.shape[1])
    arrays = [array for pair in pairs for array in pair] + ([] if rest is None else [rest])
    out = jax.ShapeDtypeStruct((4, rows, width), jnp.bfloat16)
    return pl.pallas_call(
        rows_grads_kernel,
        out_shape=(out, out),
        in_specs=[pl.BlockSpec(memory_space=pltpu.SMEM)] + [in_vmem()] * len(arrays),
        out_specs=(in_vmem(), in_vmem()),
        scratch_shapes=[pltpu.VMEM((height, width), jnp.float32)],
        compiler_params=pltpu.CompilerParams(vmem_limit_bytes=16 * 2**20),
        cost_estimate=pl.CostEstimate(
            flops=2 * 128 * height * width, bytes_accessed=4 * 2**20, transcendentals=0
        ),
        name="rows_grads",
    )(place, *arrays)


def join_kernel(parts_ref, gate_up_ref):
    width = gate_up_ref.shape[1] // 16
    tile = 16
    for part in range(2 * gate_up_ref.shape[0] // tile):
        r, half = divmod(part, 2)
        columns = [
            parts_ref[part, k * tile : (k + 1) * tile, :].astype(jnp.float32)[:, :width]
            for k in range(8)
        ]
        gate_up_ref[r * tile : (r + 1) * tile, half * 8 * width : (half + 1) * 8 * width] = (
            jnp.concatenate(columns, axis=1)
        )


def join_columns(parts, rows, width):
    return pl.pallas_call(
        join_kernel,
        out_shape=jax.ShapeDtypeStruct((rows, 16 * width), jnp.float32),
        in_specs=[in_vmem()],
        out_specs=in_vmem(),
        compiler_params=pltpu.CompilerParams(vmem_limit_bytes=20 * 2**20),
        name="join_columns",
    )(parts)


def columns_kernel(*refs):
    early, late, out_ref = refs[:5], refs[5:10], refs[-1]
    rows = early[0].shape[0]
    columns = out_ref.shape[2]
    blank = jnp.zeros((out_ref.shape[1] - rows, columns), jnp.float32)
    count = early[0].shape[1] // columns
    for n in range(out_ref.shape[0]):
        refs = early if n < count else late
        first = (n if n < count else n - count) * columns
        total = refs[0][:, first : first + columns].astype(jnp.float32)
        for ref in refs[1:]:
            total = total + ref[:, first : first + columns].astype(jnp.float32)
        if n < count:
            total = jnp.concatenate([total, blank], axis=0)
        out_ref[n] = total.astype(jnp.bfloat16)


def column_parts(early, late, earlier):
    height = late[0].shape[0]
    columns = (early[0].shape[1] + late[0].shape[1]) // 16
    return pl.pallas_call(
        columns_kernel,
        out_shape=jax.ShapeDtypeStruct((16, height, columns), jnp.bfloat16),
        in_specs=[in_vmem()] * 10 + [pl.BlockSpec(memory_space=pl.ANY)] * len(earlier),
        out_specs=in_vmem(),
        compiler_params=pltpu.CompilerParams(vmem_limit_bytes=12 * 2**20),
        name="column_parts",
    )(*early, *late, *earlier)


def core_swap(value):
    return lax.ppermute(value, "wa", [(i, i ^ 1) for i in range(8)])


def z_shift(value, step):
    return lax.ppermute(value, "wa", [(i, (i + 2 * step) % 8) for i in range(8)])


def ctx_exchange(value):
    return lax.all_to_all(value, "ctx", 0, 0, tiled=True)


def ctx_gather(value):
    return ctx_exchange(jnp.broadcast_to(value[None], (16,) + value.shape))


STEPS = (0, 1, 3, 2)


def gather_tokens(value):
    pieces = [z_shift(value, step) if step else value for step in STEPS]
    return [(piece, core_swap(piece)) for piece in pieces]


def pair_tokens(own, other):
    return [
        (mine + core_swap(theirs).astype(jnp.float32)).astype(jnp.bfloat16)
        for mine, theirs in zip(own, other)
    ]


def reduce_tokens(paired):
    total = 0.0
    for step, mine in zip(STEPS, paired):
        total = total + (z_shift(mine, -step) if step else mine).astype(jnp.float32)
    return total


def reduce_rows(kept, sent):
    other = core_swap(sent)
    pieces = [kept[0], other[0]]
    for step in STEPS[1:]:
        mine = kept[step].astype(jnp.float32) + other[step].astype(jnp.float32)
        pieces.append(z_shift(mine.astype(jnp.bfloat16), step))
    return pieces


def after(value, *others):
    held = sum(other[(0,) * other.ndim].astype(jnp.float32) for other in others) * 0.0
    return value + held.astype(value.dtype)


def spread_kernel(parts_ref, left_ref, right_ref, small_ref):
    columns = parts_ref.shape[2]
    rows = left_ref.shape[0]
    count = left_ref.shape[1] // columns
    for n in range(parts_ref.shape[0]):
        part = parts_ref[n].astype(jnp.float32)
        if n < count:
            left_ref[:, n * columns : (n + 1) * columns] = part[:rows]
        else:
            right_ref[:, (n - count) * columns : (n - count + 1) * columns] = part[:rows]
        last = n - parts_ref.shape[0] + small_ref.shape[1] // columns
        if last >= 0:
            small_ref[:, last * columns : (last + 1) * columns] = part[rows : rows + 8]


def spread_columns(parts, rows, width, small_width):
    count, _, columns = parts.shape
    return pl.pallas_call(
        spread_kernel,
        out_shape=(
            jax.ShapeDtypeStruct((rows, width), jnp.float32),
            jax.ShapeDtypeStruct((rows, count * columns - width), jnp.float32),
            jax.ShapeDtypeStruct((8, small_width), jnp.float32),
        ),
        in_specs=[in_vmem()],
        out_specs=(in_vmem(),) * 3,
        compiler_params=pltpu.CompilerParams(vmem_limit_bytes=12 * 2**20),
        name="spread_columns",
    )(parts)


def on_device(
    layer_input,
    positions,
    attention_gain,
    projection,
    projection_biases,
    output_matrix,
    feed_gain,
    gate_up_matrix,
    down_matrix,
    cotangent,
):
    place = lax.axis_index("wa").astype(jnp.int32)
    z, core = place // 2, place % 2
    ctx = lax.axis_index("ctx").astype(jnp.int32)
    rows = projection.shape[0]
    tokens = layer_input.shape[1]
    query_width = QUERY_HEADS * HEAD_SIZE
    key_width = KEY_VALUE_HEADS * HEAD_SIZE
    width = layer_input.shape[2]
    proj_width = projection.shape[1]
    bias_rows = projection_biases.shape[0]
    slice_width = down_matrix.shape[0]
    lanes = -(-slice_width // 128) * 128
    tile = 16
    sources = [(z + 4 - step) % 4 for step in STEPS]

    small = jnp.concatenate([projection_biases, attention_gain, feed_gain])
    small = jnp.pad(small[None], ((0, tile - 1), (0, proj_width - small.shape[0])))
    packed = jnp.concatenate([projection, small], axis=0)
    own = [z_shift(packed, step) if step else packed for step in STEPS]
    others = [core_swap(piece) for piece in own]
    places = jnp.stack([2 * s + core for s in sources] + [2 * s + 1 - core for s in sources])
    whole = [(n, None, 0) for n in range(8)]
    full_proj, vectors = place_rows(places, own + others, whole, rows, tile)
    vectors = vectors[:, 0].astype(jnp.float32)
    full_bias = vectors[:, :bias_rows].reshape(1, proj_width)
    gain_one = vectors[:, bias_rows : bias_rows + rows].reshape(1, width)
    gain_two = vectors[:, bias_rows + rows : bias_rows + 2 * rows].reshape(1, width)
    out_rows = after(output_matrix, own[1])
    out_rows = [z_shift(out_rows, step) if step else out_rows for step in STEPS]
    complete_output, _ = place_rows(
        places, out_rows + [core_swap(piece) for piece in out_rows], whole, rows
    )

    spot = jnp.stack([z, core])
    kept, sent = split_columns(spot, gate_up_matrix, lanes)
    other = core_swap(sent)
    pieces = [
        z_shift(after(jnp.concatenate([kept[step], other[step]], axis=0), out_rows[1]), step)
        for step in STEPS[1:]
    ]
    part_places = jnp.stack([p for s in sources for p in (2 * s + core, 2 * s + 1 - core)])
    cuts = [(0, 0, 0), (1, 0, 0)] + [(n, None, part * rows) for n in (2, 3, 4) for part in (0, 1)]
    gate_up, _ = place_rows(part_places, [kept, other] + pieces, cuts, rows)
    down = jnp.pad(down_matrix, ((0, lanes - slice_width), (0, 0)))

    layer_rows = layer_input[0]
    query_pos = positions[0]
    cosine, sine = angles(query_pos)
    cosine = jnp.tile(cosine, (1, 4))
    sine = jnp.tile(jnp.concatenate([-sine, sine], axis=1), (1, 2))
    first_normed, queries, pair = project(layer_rows, gain_one, full_proj, full_bias, cosine, sine)
    out_grad = cotangent[0]
    grad_pairs = gather_tokens(after(out_grad, pieces[0]))

    pairs = ctx_exchange(pair).reshape(16 * tokens, 2 * key_width)
    low = ctx * tokens + jnp.arange(tokens, dtype=jnp.int32) - query_pos
    block = 4 * tokens
    start = jnp.stack(
        [
            ctx * tokens,
            jnp.maximum(jnp.min(low), 0) // block,
            (ctx * tokens + tokens + block - 1) // block,
        ]
    ).astype(jnp.int32)
    low = low[None]
    mixed, lse, attention_output, middle_state, second_normed = attend(
        start, queries, pairs, low, layer_rows, complete_output, gain_two, pieces
    )

    normed_pairs = gather_tokens(after(second_normed, *[pair[0] for pair in grad_pairs[1:]]))
    worked = [
        feed(normed, grads, gate_up, down) for normed, grads in zip(normed_pairs, grad_pairs)
    ]
    hidden_pieces, joined_pieces, own, other = zip(*worked)
    paired = pair_tokens(own, other)

    gate_up_parts, down_local = feed_grads(
        [piece for pair in normed_pairs for piece in pair],
        [piece for pair in grad_pairs for piece in pair],
        joined_pieces,
        hidden_pieces,
        slice_width,
        paired,
    )
    down_total = lax.psum(down_local, "ctx")
    normed_two_grad = after(reduce_tokens(paired), down_local)
    gate_up_parts = ctx_exchange(gate_up_parts)

    _, norm_two_pull = jax.vjp(norm_rows, middle_state, gain_two[0])
    middle_part, gain_two_local = norm_two_pull(normed_two_grad)
    middle_grad = out_grad.astype(jnp.float32) + middle_part
    middle_lower = middle_grad.astype(jnp.bfloat16)
    mix_grad = column_product(middle_lower, complete_output).astype(jnp.bfloat16)
    query_back, pair_grad = attend_back(
        start, queries, pairs, low, mix_grad, mixed, lse, cosine, sine
    )
    early = reduce_rows(
        *rows_grads(spot, [(attention_output, middle_lower), (first_normed, query_back)])
    )

    feed_down = after(down, mix_grad)
    feed_outs = [
        jnp.dot(hidden, feed_down, preferred_element_type=jnp.float32) for hidden in hidden_pieces
    ]
    feed_out = reduce_tokens(
        pair_tokens(
            [part[:tokens] for part in feed_outs],
            [part[tokens:].astype(jnp.bfloat16) for part in feed_outs],
        )
    )
    result = (middle_state + feed_out).astype(jnp.bfloat16)

    pieces = ctx_exchange(after(pair_grad, gate_up_parts))
    input_grad, kept, sent = project_back(
        spot,
        layer_rows,
        gain_one,
        full_proj,
        cosine,
        sine,
        first_normed,
        query_back,
        middle_grad,
        gain_two_local[None],
        pieces,
    )
    late = reduce_rows(kept, sent)

    kept, sent = owner_parts(spot, gate_up_parts)
    other = core_swap(sent)
    parts = [
        z_shift(jnp.concatenate([kept[step], other[step]], axis=0), step) for step in STEPS[1:]
    ]
    cuts = [(0, 0, 0), (1, 0, 0)] + [(n, None, part * tile) for n in (2, 3, 4) for part in (0, 1)]
    parts, _ = place_rows(part_places, [kept, other] + parts, cuts, tile)
    parts = ctx_gather(after(parts, pieces))
    gate_up_total = join_columns(parts, rows, slice_width)

    mine = ctx_exchange(column_parts(early, late, [parts]))
    mine = jnp.sum(mine.astype(jnp.float32), axis=0).astype(jnp.bfloat16)
    mine = ctx_gather(after(mine, down_total))
    output_total, projection_total, vectors = spread_columns(mine, rows, width, 2 * key_width)
    return (
        result[None],
        input_grad[None],
        vectors[0, bias_rows : bias_rows + rows],
        projection_total,
        vectors[0, :bias_rows],
        output_total,
        vectors[1, :rows],
        gate_up_total,
        down_total.astype(jnp.float32),
    )


def solution(mesh):
    placed = (
        P("wa", "ctx", None),
        P("wa", "ctx"),
        P("wa"),
        P("wa", None),
        P("wa"),
        P("wa", None),
        P("wa"),
        P("wa", None),
        P("wa", None),
        P("wa", "ctx", None),
    )
    return jax.shard_map(
        on_device,
        mesh=mesh,
        in_specs=placed,
        out_specs=(
            P("wa", "ctx", None),
            P("wa", "ctx", None),
            P("wa"),
            P("wa", None),
            P("wa"),
            P("wa", None),
            P("wa"),
            P("wa", None),
            P("wa", None),
        ),
        check_vma=False,
    )
```

```python
import functools

import jax
import jax.numpy as jnp
from jax import lax
from jax.experimental import pallas as pl
from jax.experimental.pallas import tpu as pltpu
from jax.sharding import PartitionSpec as P

QUERY_HEADS = 14
KEY_VALUE_HEADS = 2
HEAD_SIZE = 64
FF = 4864


EPS = 1e-06
THETA = 1000000.0
NEG = -1e30


def rows_product(left, right):
    return lax.dot_general(
        left, right, (((0,), (0,)), ((), ())), preferred_element_type=jnp.float32
    )


def column_product(left, right):
    return lax.dot_general(
        left, right, (((1,), (1,)), ((), ())), preferred_element_type=jnp.float32
    )


def norm_rows(value, gain):
    return value * lax.rsqrt(jnp.mean(value * value, axis=-1, keepdims=True) + EPS) * gain


def rotate(tensor, cosine_table, sine_table):
    half = tensor.shape[-1] // 2
    first = tensor[..., :half]
    second = tensor[..., half:]
    return jnp.concatenate(
        [first * cosine_table - second * sine_table, second * cosine_table + first * sine_table],
        axis=-1,
    )


def inverse_rotate(tensor, cosine_table, sine_table):
    half = tensor.shape[-1] // 2
    first = tensor[..., :half]
    second = tensor[..., half:]
    return jnp.concatenate(
        [first * cosine_table + second * sine_table, second * cosine_table - first * sine_table],
        axis=-1,
    )


def angles(positions):
    half = HEAD_SIZE // 2
    inverse = THETA ** (-(jnp.arange(half) * 2.0 / HEAD_SIZE))
    turned = positions.astype(jnp.float32)[:, None] * inverse.astype(jnp.float32)
    return (jnp.cos(turned), jnp.sin(turned))


def turn_heads(value, cosine, sine):
    width = value.shape[1]
    lane = lax.broadcasted_iota(jnp.int32, value.shape, 1)
    half = HEAD_SIZE // 2
    partner = jnp.where(
        lane % HEAD_SIZE < half, pltpu.roll(value, width - half, 1), pltpu.roll(value, half, 1)
    )
    repeats = width // cosine.shape[1]
    return value * jnp.tile(cosine, (1, repeats)) + partner * jnp.tile(sine, (1, repeats))


def fetch(pairs, sems):
    copies = [pltpu.make_async_copy(*pair, sems.at[n]) for n, pair in enumerate(pairs)]
    for copy in copies:
        copy.start()
    for copy in copies:
        copy.wait()


def project_kernel(
    packed_ref, x_ref, cos_ref, sin_ref, normed_ref, q_ref, pairs_ref, proj_ref, gains_ref, small_ref, sems
):
    count = packed_ref.shape[0]
    rows = proj_ref.shape[0] // count
    fetch(
        [
            (packed_ref.at[n, :rows, :], proj_ref.at[n * rows : (n + 1) * rows, :])
            for n in range(count)
        ]
        + [(packed_ref.at[n, rows:, :], small_ref.at[n]) for n in range(count)],
        sems,
    )
    small = [small_ref[n].astype(jnp.float32)[:1] for n in range(count)]
    bias_rows = proj_ref.shape[1] // count
    bias = jnp.concatenate([row[:, :bias_rows] for row in small], axis=1)
    gains = [
        jnp.concatenate([row[:, first : first + rows] for row in small], axis=1)
        for first in (bias_rows, bias_rows + rows)
    ]
    for n in range(2):
        gains_ref[n] = gains[n]
    x = x_ref[...].astype(jnp.float32)
    scale = lax.rsqrt(jnp.mean(x * x, axis=-1, keepdims=True) + EPS)
    normed = (x * scale * gains[0]).astype(jnp.bfloat16)
    normed_ref[...] = normed
    width = q_ref.shape[1]
    turned = width + KEY_VALUE_HEADS * HEAD_SIZE
    projected = jnp.dot(normed, proj_ref[...], preferred_element_type=jnp.float32) + bias
    rotated = turn_heads(projected[:, :turned], cos_ref[...], sin_ref[...])
    q_ref[...] = rotated[:, :width].astype(jnp.bfloat16)
    pair = jnp.concatenate([rotated[:, width:], projected[:, turned:]], axis=1).astype(jnp.bfloat16)
    for n in range(pairs_ref.shape[0]):
        pairs_ref[n] = pair


def project(packed, x, cosine, sine):
    tokens, width = x.shape
    count, height, proj_width = packed.shape
    return pl.pallas_call(
        project_kernel,
        out_shape=(
            jax.ShapeDtypeStruct((tokens, width), jnp.bfloat16),
            jax.ShapeDtypeStruct((tokens, QUERY_HEADS * HEAD_SIZE), jnp.bfloat16),
            jax.ShapeDtypeStruct((16, tokens, 2 * KEY_VALUE_HEADS * HEAD_SIZE), jnp.bfloat16),
            jax.ShapeDtypeStruct((width, proj_width), jnp.bfloat16),
            jax.ShapeDtypeStruct((2, 1, width), jnp.float32),
        ),
        in_specs=[pl.BlockSpec(memory_space=pl.ANY)] + [in_vmem()] * 3,
        out_specs=(in_vmem(),) * 5,
        scratch_shapes=[
            pltpu.VMEM((count, height - width // count, proj_width), jnp.bfloat16),
            pltpu.SemaphoreType.DMA((2 * count,)),
        ],
        compiler_params=pltpu.CompilerParams(vmem_limit_bytes=16 * 2**20),
        name="project",
    )(packed, x, cosine, sine)


def project_back_kernel(
    place_ref, x_ref, gain_ref, proj_ref, cos_ref, sin_ref, normed_ref, dq_ref, grad_ref, gain_two_ref,
    pieces_ref, input_grad_ref, kept_ref, sent_ref, stage_ref,
):
    z, core = place_ref[0], place_ref[1]
    key_width = KEY_VALUE_HEADS * HEAD_SIZE
    pair = pieces_ref[0].astype(jnp.float32)
    for n in range(1, pieces_ref.shape[0]):
        pair = pair + pieces_ref[n].astype(jnp.float32)
    keys = turn_heads(pair[:, :key_width], cos_ref[...], -sin_ref[...])
    pair = jnp.concatenate([keys, pair[:, key_width:]], axis=1).astype(jnp.bfloat16)
    turned = normed_ref[...].astype(jnp.float32).T.astype(jnp.bfloat16)
    stage_ref[...] = jnp.dot(turned, pair, preferred_element_type=jnp.float32)
    bias = jnp.concatenate(
        [
            jnp.sum(dq_ref[...].astype(jnp.float32), axis=0, keepdims=True),
            jnp.sum(pair.astype(jnp.float32), axis=0, keepdims=True),
        ],
        axis=1,
    )
    x = x_ref[...].astype(jnp.float32)
    scale = lax.rsqrt(jnp.mean(x * x, axis=-1, keepdims=True) + EPS)
    grad = lax.dot_general(
        jnp.concatenate([dq_ref[...], pair], axis=1),
        proj_ref[...],
        (((1,), (1,)), ((), ())),
        preferred_element_type=jnp.float32,
    )
    gain_one = jnp.sum(grad * x * scale, axis=0, keepdims=True)
    gained = grad * gain_ref[...]
    mean = jnp.mean(gained * x, axis=-1, keepdims=True)
    input_grad_ref[...] = grad_ref[...] + scale * gained - x * (scale * scale * scale * mean)

    rows = stage_ref.shape[0] // 8
    bias_rows = bias.shape[1] // 8
    blank = jnp.zeros((kept_ref.shape[1] - rows - 2, stage_ref.shape[1]), jnp.float32)
    for owner in range(8):
        at = lax.rem(owner // 2 - z + 4, 4)
        here = slice(owner * rows, (owner + 1) * rows)
        gain_two = gain_two_ref[:, here]
        first = jnp.concatenate(
            [bias[:, owner * bias_rows : (owner + 1) * bias_rows], gain_one[:, here]], axis=1
        )
        second = jnp.concatenate(
            [gain_two, jnp.zeros((1, stage_ref.shape[1] - rows), jnp.float32)], axis=1
        )
        both = jnp.concatenate([stage_ref[here, :], first, second, blank], axis=0).astype(jnp.bfloat16)

        @pl.when(core == owner % 2)
        def _(both=both, at=at):
            kept_ref[at] = both

        @pl.when(core != owner % 2)
        def _(both=both, at=at):
            sent_ref[at] = both


def project_back(place, x, gain, proj, cosine, sine, normed, dq, grad, gain_two, pieces):
    tokens, width = x.shape
    pair_width = pieces.shape[2]
    out = jax.ShapeDtypeStruct((4, width // 8 + 16, pair_width), jnp.bfloat16)
    return pl.pallas_call(
        project_back_kernel,
        out_shape=(jax.ShapeDtypeStruct((tokens, width), jnp.float32), out, out),
        in_specs=[pl.BlockSpec(memory_space=pltpu.SMEM)] + [in_vmem()] * 10,
        out_specs=(in_vmem(),) * 3,
        scratch_shapes=[pltpu.VMEM((width, pair_width), jnp.float32)],
        compiler_params=pltpu.CompilerParams(vmem_limit_bytes=16 * 2**20),
        name="project_back",
    )(place, x, gain, proj, cosine, sine, normed, dq, grad, gain_two, pieces)


def key_bias(low_ref, block_start, block, first_index):
    tokens = low_ref.shape[1]
    keys = block_start + lax.broadcasted_iota(jnp.int32, (block, tokens), 0)
    index = first_index + lax.broadcasted_iota(jnp.int32, (block, tokens), 1)
    return jnp.where((keys <= index) & (keys >= low_ref[...]), 0.0, NEG)


def head_places(tokens):
    group = QUERY_HEADS // KEY_VALUE_HEADS
    for h in range(QUERY_HEADS):
        g, i = divmod(h, group)
        yield g, slice(h * HEAD_SIZE, (h + 1) * HEAD_SIZE), slice(i * tokens, (i + 1) * tokens)


def attend_kernel(
    start_ref, q_ref, kv_ref, low_ref, x_ref, out_ref, gain_ref, *refs
):
    mixed_ref, lse_ref, attended_ref, middle_ref, normed_ref = refs[-12:-7]
    qt, s_ref, p_ref, bias_ref, m_ref, l_ref, acc_ref = refs[-7:]
    tokens = q_ref.shape[0]
    block, rows = s_ref.shape
    turned = (q_ref[...].astype(jnp.float32) * HEAD_SIZE ** (-0.5)).T.astype(jnp.bfloat16)
    for g, lanes, at in head_places(tokens):
        qt[g, :, at] = turned[lanes, :]
    m_ref[...] = jnp.full_like(m_ref, NEG)
    l_ref[...] = jnp.zeros_like(l_ref)
    acc_ref[...] = jnp.zeros_like(acc_ref)

    def visit(which, carry):
        block_start = pl.multiple_of(which * block, block)
        here = pl.ds(block_start, block)
        bias_ref[...] = key_bias(low_ref, block_start, block, start_ref[0])
        key_width = KEY_VALUE_HEADS * HEAD_SIZE
        values = kv_ref[here, key_width:].astype(jnp.float32).T.astype(jnp.bfloat16)
        for g in range(KEY_VALUE_HEADS):
            lanes = slice(g * HEAD_SIZE, (g + 1) * HEAD_SIZE)
            s_ref[...] = jnp.dot(kv_ref[here, lanes], qt[g], preferred_element_type=jnp.float32)
            for i in range(rows // tokens):
                at = slice(i * tokens, (i + 1) * tokens)
                s = s_ref[:, at] + bias_ref[...]
                old = m_ref[g, :, at]
                peak = jnp.maximum(old, jnp.max(s, axis=0, keepdims=True))
                e = jnp.exp(s - peak)
                scale = jnp.exp(old - peak)
                m_ref[g, :, at] = peak
                l_ref[g, :, at] = l_ref[g, :, at] * scale + jnp.sum(e, axis=0, keepdims=True)
                acc_ref[g, :, at] = acc_ref[g, :, at] * scale
                p_ref[:, at] = e.astype(jnp.bfloat16)
            acc_ref[g] += jnp.dot(values[lanes, :], p_ref[...], preferred_element_type=jnp.float32)
        return carry

    lax.fori_loop(start_ref[1], start_ref[2], visit, 0)
    mixed = [acc_ref[g, :, at] / l_ref[g, :, at] for g, _, at in head_places(tokens)]
    mixed = jnp.concatenate(mixed, axis=0).T
    mixed_ref[...] = mixed
    lse_ref[...] = m_ref[...] + jnp.log(l_ref[...])
    attended = mixed.astype(jnp.bfloat16)
    attended_ref[...] = attended
    middle = x_ref[...].astype(jnp.float32) + jnp.dot(
        attended, out_ref[...], preferred_element_type=jnp.float32
    )
    middle_ref[...] = middle
    scale = lax.rsqrt(jnp.mean(middle * middle, axis=-1, keepdims=True) + EPS)
    normed_ref[...] = (middle * scale * gain_ref[...]).astype(jnp.bfloat16)


def attend_back_kernel(
    start_ref, q_ref, kv_ref, low_ref, dmix_ref, mixed_ref, lse_ref, cos_ref, sin_ref, dq_ref, dkv_ref,
    qs, qt, ms, mt, delta_ref, s_ref, dp_ref, p_ref, g_ref, bias_ref, acc_ref,
):
    tokens = q_ref.shape[0]
    block, rows = s_ref.shape
    key_width = KEY_VALUE_HEADS * HEAD_SIZE
    q = q_ref[...].astype(jnp.float32) * HEAD_SIZE ** (-0.5)
    dmix = dmix_ref[...].astype(jnp.float32)
    q_turned = q.T.astype(jnp.bfloat16)
    dmix_turned = dmix.T
    weighed = (dmix * mixed_ref[...]).T
    q = q.astype(jnp.bfloat16)
    for g, lanes, at in head_places(tokens):
        qs[g, at, :] = q[:, lanes]
        ms[g, at, :] = dmix_ref[:, lanes]
        qt[g, :, at] = q_turned[lanes, :]
        mt[g, :, at] = dmix_turned[lanes, :].astype(jnp.bfloat16)
        delta_ref[g, :, at] = jnp.sum(weighed[lanes, :], axis=0, keepdims=True)
    acc_ref[...] = jnp.zeros_like(acc_ref)
    dkv_ref[...] = jnp.zeros_like(dkv_ref)

    def visit(which, carry):
        block_start = pl.multiple_of(which * block, block)
        here = pl.ds(block_start, block)
        bias_ref[...] = key_bias(low_ref, block_start, block, start_ref[0])
        keys_turned = kv_ref[here, :key_width].astype(jnp.float32).T.astype(jnp.bfloat16)
        grads = [None] * (2 * KEY_VALUE_HEADS)
        for g in range(KEY_VALUE_HEADS):
            lanes = slice(g * HEAD_SIZE, (g + 1) * HEAD_SIZE)
            s_ref[...] = jnp.dot(kv_ref[here, lanes], qt[g], preferred_element_type=jnp.float32)
            values = kv_ref[here, key_width + g * HEAD_SIZE : key_width + (g + 1) * HEAD_SIZE]
            dp_ref[...] = jnp.dot(values, mt[g], preferred_element_type=jnp.float32)
            for i in range(rows // tokens):
                at = slice(i * tokens, (i + 1) * tokens)
                p = jnp.exp(s_ref[:, at] + bias_ref[...] - lse_ref[g, :, at])
                p_ref[:, at] = p.astype(jnp.bfloat16)
                g_ref[:, at] = (p * (dp_ref[:, at] - delta_ref[g, :, at])).astype(jnp.bfloat16)
            acc_ref[g] += jnp.dot(keys_turned[lanes, :], g_ref[...], preferred_element_type=jnp.float32)
            grads[g] = jnp.dot(g_ref[...], qs[g], preferred_element_type=jnp.float32)
            grads[KEY_VALUE_HEADS + g] = jnp.dot(
                p_ref[...], ms[g], preferred_element_type=jnp.float32
            )
        grads = jnp.concatenate(grads, axis=1).astype(jnp.bfloat16)
        for n in range(block // tokens):
            dkv_ref[which * (block // tokens) + n] = grads[n * tokens : (n + 1) * tokens, :]
        return carry

    lax.fori_loop(start_ref[1], start_ref[2], visit, 0)
    dq = [acc_ref[g, :, at] for g, _, at in head_places(tokens)]
    dq = jnp.concatenate(dq, axis=0).T * HEAD_SIZE ** (-0.5)
    dq_ref[...] = turn_heads(dq, cos_ref[...], -sin_ref[...]).astype(jnp.bfloat16)


def in_vmem():
    return pl.BlockSpec(memory_space=pltpu.VMEM)


def attend(start, queries, pairs, low, x, out_matrix, gain):
    tokens, width = queries.shape
    rows = QUERY_HEADS // KEY_VALUE_HEADS * tokens
    block = 4 * tokens
    heads = KEY_VALUE_HEADS
    return pl.pallas_call(
        attend_kernel,
        out_shape=(
            jax.ShapeDtypeStruct((tokens, width), jnp.float32),
            jax.ShapeDtypeStruct((heads, 1, rows), jnp.float32),
            jax.ShapeDtypeStruct((tokens, width), jnp.bfloat16),
            jax.ShapeDtypeStruct(x.shape, jnp.float32),
            jax.ShapeDtypeStruct(x.shape, jnp.bfloat16),
        ),
        in_specs=[pl.BlockSpec(memory_space=pltpu.SMEM)] + [in_vmem()] * 6,
        out_specs=(in_vmem(),) * 5,
        scratch_shapes=[
            pltpu.VMEM((heads, HEAD_SIZE, rows), jnp.bfloat16),
            pltpu.VMEM((block, rows), jnp.float32),
            pltpu.VMEM((block, rows), jnp.bfloat16),
            pltpu.VMEM((block, tokens), jnp.float32),
            pltpu.VMEM((heads, 1, rows), jnp.float32),
            pltpu.VMEM((heads, 1, rows), jnp.float32),
            pltpu.VMEM((heads, HEAD_SIZE, rows), jnp.float32),
        ],
        compiler_params=pltpu.CompilerParams(vmem_limit_bytes=16 * 2**20),
        cost_estimate=pl.CostEstimate(
            flops=16 * tokens * width * pairs.shape[0], bytes_accessed=2 * 2**20, transcendentals=0
        ),
        name="attend",
    )(start, queries, pairs, low, x, out_matrix, gain)


def attend_back(start, queries, pairs, low, mix_grad, mixed, lse, cosine, sine):
    tokens, width = queries.shape
    rows = QUERY_HEADS // KEY_VALUE_HEADS * tokens
    block = 4 * tokens
    heads = KEY_VALUE_HEADS
    return pl.pallas_call(
        attend_back_kernel,
        out_shape=(
            jax.ShapeDtypeStruct((tokens, width), jnp.bfloat16),
            jax.ShapeDtypeStruct((pairs.shape[0] // tokens, tokens, pairs.shape[1]), jnp.bfloat16),
        ),
        in_specs=[pl.BlockSpec(memory_space=pltpu.SMEM)] + [in_vmem()] * 8,
        out_specs=(in_vmem(), in_vmem()),
        scratch_shapes=[
            pltpu.VMEM((heads, rows, HEAD_SIZE), jnp.bfloat16),
            pltpu.VMEM((heads, HEAD_SIZE, rows), jnp.bfloat16),
            pltpu.VMEM((heads, rows, HEAD_SIZE), jnp.bfloat16),
            pltpu.VMEM((heads, HEAD_SIZE, rows), jnp.bfloat16),
            pltpu.VMEM((heads, 1, rows), jnp.float32),
            pltpu.VMEM((block, rows), jnp.float32),
            pltpu.VMEM((block, rows), jnp.float32),
            pltpu.VMEM((block, rows), jnp.bfloat16),
            pltpu.VMEM((block, rows), jnp.bfloat16),
            pltpu.VMEM((block, tokens), jnp.float32),
            pltpu.VMEM((heads, HEAD_SIZE, rows), jnp.float32),
        ],
        compiler_params=pltpu.CompilerParams(vmem_limit_bytes=24 * 2**20),
        cost_estimate=pl.CostEstimate(
            flops=40 * tokens * width * pairs.shape[0], bytes_accessed=4 * 2**20, transcendentals=0
        ),
        name="attend_back",
    )(start, queries, pairs, low, mix_grad, mixed, lse, cosine, sine)


def split_kernel(matrix_ref, out_ref):
    width, lanes = matrix_ref.shape[1] // 16, out_ref.shape[2] // 2
    for owner in range(8):
        gate = matrix_ref[:, owner * width : (owner + 1) * width].astype(jnp.float32)
        up = matrix_ref[:, (8 + owner) * width : (9 + owner) * width].astype(jnp.float32)
        blank = jnp.zeros((gate.shape[0], lanes - width), jnp.float32)
        out_ref[owner] = jnp.concatenate([gate, blank, up, blank], axis=1).astype(jnp.bfloat16)


def split_columns(matrix, lanes):
    rows = matrix.shape[0]
    return pl.pallas_call(
        split_kernel,
        out_shape=jax.ShapeDtypeStruct((8, rows, 2 * lanes), matrix.dtype),
        in_specs=[in_vmem()],
        out_specs=in_vmem(),
        compiler_params=pltpu.CompilerParams(vmem_limit_bytes=16 * 2**20),
        name="split_columns",
    )(matrix)


def place_kernel(cuts, at_ref, *refs):
    pieces, (out_ref, rest_ref, sems, rest_sems) = refs[:-4], refs[-4:]
    rows = out_ref.shape[0] // len(cuts)
    copies = []
    for n, (which, lead, first) in enumerate(cuts):
        piece = pieces[which] if lead is None else pieces[which].at[lead]
        copies.append(
            pltpu.make_async_copy(
                piece.at[first : first + rows, :],
                out_ref.at[pl.ds(pl.multiple_of(at_ref[n] * rows, 16), rows), :],
                sems.at[n],
            )
        )
        if rest_ref.shape[0] == len(cuts):
            copies.append(
                pltpu.make_async_copy(piece.at[rows:, :], rest_ref.at[at_ref[n]], rest_sems.at[n])
            )
    for copy in copies:
        copy.start()
    if rest_ref.shape[0] != len(cuts):
        rest_ref[...] = jnp.zeros_like(rest_ref)
    for copy in copies:
        copy.wait()


def place_rows(at, arrays, cuts, rows, rest=0):
    width, kind = arrays[0].shape[-1], arrays[0].dtype
    count = len(cuts)
    rest_shape = (count, rest, width) if rest else (1, 8, 128)
    return pl.pallas_call(
        functools.partial(place_kernel, tuple(cuts)),
        out_shape=(
            jax.ShapeDtypeStruct((count * rows, width), kind),
            jax.ShapeDtypeStruct(rest_shape, kind if rest else jnp.float32),
        ),
        in_specs=[pl.BlockSpec(memory_space=pltpu.SMEM)]
        + [pl.BlockSpec(memory_space=pl.ANY)] * len(arrays),
        out_specs=(in_vmem(), in_vmem()),
        scratch_shapes=[pltpu.SemaphoreType.DMA((count,)), pltpu.SemaphoreType.DMA((count,))],
        compiler_params=pltpu.CompilerParams(vmem_limit_bytes=8 * 2**20),
        name="place_rows",
    )(at, *arrays)


def feed_kernel(
    at_ref, left_ref, right_ref, grads_ref, gate_up_ref, down_ref, hidden_ref, joined_ref, own_ref, other_ref
):
    lanes = hidden_ref.shape[1]
    tokens = left_ref.shape[0]
    normed = jnp.concatenate([left_ref[...], right_ref[...]], axis=0)
    grad = jnp.concatenate([grads_ref[at_ref[0]], grads_ref[at_ref[1]]], axis=0)
    gate = jnp.dot(normed, gate_up_ref[:, :lanes], preferred_element_type=jnp.float32)
    up = jnp.dot(normed, gate_up_ref[:, lanes:], preferred_element_type=jnp.float32)
    hidden_grad = lax.dot_general(
        grad, down_ref[...], (((1,), (1,)), ((), ())), preferred_element_type=jnp.float32
    )
    sg = 1.0 / (1.0 + jnp.exp(-gate))
    act = gate * sg
    hidden_ref[...] = (act * up).astype(jnp.bfloat16)
    joined_ref[:, :lanes] = (hidden_grad * up * sg * (1.0 + gate * (1.0 - sg))).astype(jnp.bfloat16)
    joined_ref[:, lanes:] = (hidden_grad * act).astype(jnp.bfloat16)
    back = lax.dot_general(
        joined_ref[...], gate_up_ref[...], (((1,), (1,)), ((), ())), preferred_element_type=jnp.float32
    )
    own_ref[...] = back[:tokens]
    other_ref[...] = back[tokens:].astype(jnp.bfloat16)


def feed(at, normed, grads, gate_up, down):
    tokens, width = normed[0].shape
    lanes = down.shape[0]
    return pl.pallas_call(
        feed_kernel,
        out_shape=(
            jax.ShapeDtypeStruct((2 * tokens, lanes), jnp.bfloat16),
            jax.ShapeDtypeStruct((2 * tokens, 2 * lanes), jnp.bfloat16),
            jax.ShapeDtypeStruct((tokens, width), jnp.float32),
            jax.ShapeDtypeStruct((tokens, width), jnp.bfloat16),
        ),
        in_specs=[pl.BlockSpec(memory_space=pltpu.SMEM)] + [in_vmem()] * 5,
        out_specs=(in_vmem(),) * 4,
        compiler_params=pltpu.CompilerParams(vmem_limit_bytes=20 * 2**20),
        cost_estimate=pl.CostEstimate(
            flops=20 * tokens * width * lanes, bytes_accessed=6 * 2**20, transcendentals=0
        ),
        name="feed",
    )(at, *normed, grads, gate_up, down)


def feed_grads_kernel(at_ref, *refs):
    normed, grads_in, joined, hidden = refs[:8], refs[8], refs[9:13], refs[13:17]
    out_ref, left_ref, right_ref, stage_ref = refs[-4:]
    lanes = hidden[0].shape[1]
    tile = 16
    rows = stage_ref.shape[0] // 8
    tokens = normed[0].shape[0]
    step = 2 * tokens

    def turned(value, n):
        left_ref[:, n * tokens : (n + 1) * tokens] = value.astype(jnp.float32).T.astype(jnp.bfloat16)

    def multiply(right, at):
        for n in range(4):
            right_ref[n * step : (n + 1) * step, :] = right[n][:, at]
        stage_ref[...] = jnp.dot(left_ref[...], right_ref[...], preferred_element_type=jnp.float32)

    for n in range(8):
        turned(normed[n][...], n)
    for half in range(2):
        multiply(joined, slice(half * lanes, (half + 1) * lanes))
        for r in range(rows // tile):
            for k in range(8):
                first = k * rows + r * tile
                out_ref[2 * r + half, k * tile : (k + 1) * tile, :] = stage_ref[
                    first : first + tile, :
                ].astype(jnp.bfloat16)
    for part in range(2 * rows // tile, 16):
        out_ref[part, : 8 * tile, :] = jnp.zeros((8 * tile, lanes), jnp.bfloat16)
    for n in range(8):
        turned(grads_in[at_ref[n]], n)
    multiply(hidden, slice(0, lanes))
    rows = stage_ref.shape[0] // 16
    blank = jnp.zeros((out_ref.shape[1] - 8 * tile - rows, lanes), jnp.float32)
    for part in range(16):
        piece = jnp.concatenate([stage_ref[part * rows : (part + 1) * rows, :], blank], axis=0)
        out_ref[part, 8 * tile :, :] = piece.astype(jnp.bfloat16)


def feed_grads(at, normed, grads, joined, hidden, earlier):
    tokens, width = normed[0].shape
    lanes = hidden[0].shape[1]
    part = 8 * 16 + -(-width // 16 // 16) * 16
    return pl.pallas_call(
        feed_grads_kernel,
        out_shape=jax.ShapeDtypeStruct((16, part, lanes), jnp.bfloat16),
        in_specs=[pl.BlockSpec(memory_space=pltpu.SMEM)]
        + [in_vmem()] * 17
        + [pl.BlockSpec(memory_space=pl.ANY)] * len(earlier),
        out_specs=in_vmem(),
        scratch_shapes=[
            pltpu.VMEM((width, 8 * tokens), jnp.bfloat16),
            pltpu.VMEM((8 * tokens, lanes), jnp.bfloat16),
            pltpu.VMEM((width, lanes), jnp.float32),
        ],
        compiler_params=pltpu.CompilerParams(vmem_limit_bytes=32 * 2**20),
        cost_estimate=pl.CostEstimate(
            flops=48 * tokens * width * lanes, bytes_accessed=12 * 2**20, transcendentals=0
        ),
        name="feed_grads",
    )(at, *normed, grads, *joined, *hidden, *earlier)


def feed_out_kernel(at_ref, down_ref, *refs):
    hidden, out_ref = refs[:4], refs[-1]
    tokens = out_ref.shape[1]
    for n in range(4):
        out = jnp.dot(hidden[n][...], down_ref[...], preferred_element_type=jnp.float32)
        for part in range(2):
            out_ref[at_ref[2 * n + part]] = out[part * tokens : (part + 1) * tokens].astype(
                jnp.bfloat16
            )


def feed_out(at, down, hidden, earlier):
    tokens = hidden[0].shape[0] // 2
    return pl.pallas_call(
        feed_out_kernel,
        out_shape=jax.ShapeDtypeStruct((8, tokens, down.shape[1]), jnp.bfloat16),
        in_specs=[pl.BlockSpec(memory_space=pltpu.SMEM)]
        + [in_vmem()] * 5
        + [pl.BlockSpec(memory_space=pl.ANY)] * len(earlier),
        out_specs=in_vmem(),
        compiler_params=pltpu.CompilerParams(vmem_limit_bytes=16 * 2**20),
        name="feed_out",
    )(at, down, *hidden, *earlier)


def owner_parts_kernel(place_ref, parts_ref, kept_ref, sent_ref, rest_ref):
    z, core = place_ref[0], place_ref[1]
    rows = kept_ref.shape[1]

    def total(here):
        value = parts_ref[0, here, :].astype(jnp.float32)
        for n in range(1, parts_ref.shape[0]):
            value = value + parts_ref[n, here, :].astype(jnp.float32)
        return value.astype(jnp.bfloat16)

    for owner in range(8):
        at = lax.rem(owner // 2 - z + 4, 4)
        part = total(slice(owner * rows, (owner + 1) * rows))

        @pl.when(core == owner % 2)
        def _(part=part, at=at):
            kept_ref[at] = part

        @pl.when(core != owner % 2)
        def _(part=part, at=at):
            sent_ref[at] = part

    for first in range(0, rest_ref.shape[0], rows):
        rest_ref[first : first + rows, :] = total(slice(8 * rows + first, 9 * rows + first))


def owner_parts(place, parts, rows):
    _, height, width = parts.shape
    out = jax.ShapeDtypeStruct((4, rows, width), jnp.bfloat16)
    return pl.pallas_call(
        owner_parts_kernel,
        out_shape=(out, out, jax.ShapeDtypeStruct((height - 8 * rows, width), jnp.bfloat16)),
        in_specs=[pl.BlockSpec(memory_space=pltpu.SMEM), in_vmem()],
        out_specs=(in_vmem(),) * 3,
        compiler_params=pltpu.CompilerParams(vmem_limit_bytes=12 * 2**20),
        name="owner_parts",
    )(place, parts)


def rows_grads_kernel(place_ref, *refs):
    kept_ref, sent_ref, stage_ref = refs[-3:]
    pairs = (len(refs) - 3) // 2
    rest_ref = refs[2 * pairs] if (len(refs) - 3) % 2 else None
    z, core = place_ref[0], place_ref[1]
    rows = stage_ref.shape[0] // 8
    first = 0
    for n in range(pairs):
        left, right = refs[2 * n], refs[2 * n + 1]
        turned = left[...].astype(jnp.float32).T.astype(jnp.bfloat16)
        stage_ref[:, first : first + right.shape[1]] = jnp.dot(
            turned, right[...], preferred_element_type=jnp.float32
        )
        first += right.shape[1]
    for owner in range(8):
        at = lax.rem(owner // 2 - z + 4, 4)

        @pl.when(core == owner % 2)
        def _(owner=owner, at=at):
            kept_ref[at, :rows, :] = stage_ref[owner * rows : (owner + 1) * rows, :].astype(jnp.bfloat16)
            if rest_ref is not None:
                kept_ref[at, rows:, :] = rest_ref[owner]

        @pl.when(core != owner % 2)
        def _(owner=owner, at=at):
            sent_ref[at, :rows, :] = stage_ref[owner * rows : (owner + 1) * rows, :].astype(jnp.bfloat16)
            if rest_ref is not None:
                sent_ref[at, rows:, :] = rest_ref[owner]


def rows_grads(place, pairs, rest=None):
    height = pairs[0][0].shape[1]
    width = sum(right.shape[1] for _, right in pairs)
    rows = height // 8 + (0 if rest is None else rest.shape[1])
    arrays = [array for pair in pairs for array in pair] + ([] if rest is None else [rest])
    out = jax.ShapeDtypeStruct((4, rows, width), jnp.bfloat16)
    return pl.pallas_call(
        rows_grads_kernel,
        out_shape=(out, out),
        in_specs=[pl.BlockSpec(memory_space=pltpu.SMEM)] + [in_vmem()] * len(arrays),
        out_specs=(in_vmem(), in_vmem()),
        scratch_shapes=[pltpu.VMEM((height, width), jnp.float32)],
        compiler_params=pltpu.CompilerParams(vmem_limit_bytes=16 * 2**20),
        cost_estimate=pl.CostEstimate(
            flops=2 * 128 * height * width, bytes_accessed=4 * 2**20, transcendentals=0
        ),
        name="rows_grads",
    )(place, *arrays)


def join_kernel(parts_ref, gate_up_ref, down_ref, stage_ref):
    width = gate_up_ref.shape[1] // 16
    tile = 16
    for part in range(2 * gate_up_ref.shape[0] // tile):
        r, half = divmod(part, 2)
        columns = [
            parts_ref[part, k * tile : (k + 1) * tile, :].astype(jnp.float32)[:, :width]
            for k in range(8)
        ]
        gate_up_ref[r * tile : (r + 1) * tile, half * 8 * width : (half + 1) * 8 * width] = (
            jnp.concatenate(columns, axis=1)
        )
    rows = stage_ref.shape[0] // 16
    for part in range(16):
        stage_ref[part * rows : (part + 1) * rows, :] = parts_ref[part, 8 * tile :, :].astype(
            jnp.float32
        )[:rows]
    for block in range(stage_ref.shape[0] // 128):
        at = slice(block * 128, (block + 1) * 128)
        down_ref[:, at] = stage_ref[at, :].T[:width]


def join_columns(parts, rows, width, model_width):
    return pl.pallas_call(
        join_kernel,
        out_shape=(
            jax.ShapeDtypeStruct((rows, 16 * width), jnp.float32),
            jax.ShapeDtypeStruct((width, model_width), jnp.float32),
        ),
        in_specs=[in_vmem()],
        out_specs=(in_vmem(), in_vmem()),
        scratch_shapes=[pltpu.VMEM((model_width, parts.shape[2]), jnp.float32)],
        compiler_params=pltpu.CompilerParams(vmem_limit_bytes=24 * 2**20),
        name="join_columns",
    )(parts)


def columns_kernel(*refs):
    ins, out_ref, early_ref, late_ref, sems = refs[:10], refs[-4], refs[-3], refs[-2], refs[-1]
    lead_early = [ref.at[0] if len(ref.shape) == 3 else ref for ref in ins[:5]]
    lead_late = [ref.at[0] if len(ref.shape) == 3 else ref for ref in ins[5:]]
    fetch(
        [(ref, early_ref.at[n]) for n, ref in enumerate(lead_early)]
        + [(ref, late_ref.at[n]) for n, ref in enumerate(lead_late)],
        sems,
    )
    _, rows, width = early_ref.shape
    columns = out_ref.shape[2]
    blank = jnp.zeros((out_ref.shape[1] - rows, columns), jnp.float32)
    count = width // columns
    for n in range(out_ref.shape[0]):
        ref = early_ref if n < count else late_ref
        first = (n if n < count else n - count) * columns
        total = ref[0, :, first : first + columns].astype(jnp.float32)
        for m in range(1, 5):
            total = total + ref[m, :, first : first + columns].astype(jnp.float32)
        if n < count:
            total = jnp.concatenate([total, blank], axis=0)
        out_ref[n] = total.astype(jnp.bfloat16)


def column_parts(early, late):
    early_shape, late_shape = early[-1].shape, late[-1].shape
    columns = (early_shape[1] + late_shape[1]) // 16
    return pl.pallas_call(
        columns_kernel,
        out_shape=jax.ShapeDtypeStruct((16, late_shape[0], columns), jnp.bfloat16),
        in_specs=[pl.BlockSpec(memory_space=pl.ANY)] * 10,
        out_specs=in_vmem(),
        scratch_shapes=[
            pltpu.VMEM((5,) + early_shape, jnp.bfloat16),
            pltpu.VMEM((5,) + late_shape, jnp.bfloat16),
            pltpu.SemaphoreType.DMA((10,)),
        ],
        compiler_params=pltpu.CompilerParams(vmem_limit_bytes=8 * 2**20),
        name="column_parts",
    )(*early, *late)


def core_swap(value):
    return lax.ppermute(value, "wa", [(i, i ^ 1) for i in range(8)])


def z_shift(value, step):
    return lax.ppermute(value, "wa", [(i, (i + 2 * step) % 8) for i in range(8)])


def ctx_exchange(value):
    return lax.all_to_all(value, "ctx", 0, 0, tiled=True)


def ctx_gather(value):
    return ctx_exchange(jnp.broadcast_to(value[None], (16,) + value.shape))


STEPS = (0, 1, 3, 2)


def gather_tokens(value):
    pieces = [z_shift(value, step) if step else value for step in STEPS]
    return [(piece, core_swap(piece)) for piece in pieces]


def pair_tokens(own, other):
    return [
        (mine + core_swap(theirs).astype(jnp.float32)).astype(jnp.bfloat16)
        for mine, theirs in zip(own, other)
    ]


def reduce_tokens(paired):
    total = 0.0
    for step, mine in zip(STEPS, paired):
        total = total + (z_shift(mine, -step) if step else mine).astype(jnp.float32)
    return total


def reduce_rows(kept, sent):
    other = core_swap(sent)
    pieces = [kept, other]
    for step in STEPS[1:]:
        mine = kept[step].astype(jnp.float32) + other[step].astype(jnp.float32)
        pieces.append(z_shift(mine.astype(jnp.bfloat16), step))
    return pieces


def after(value, *others):
    held = sum(other[(0,) * other.ndim].astype(jnp.float32) for other in others) * 0.0
    return value + held.astype(value.dtype)


def spread_kernel(parts_ref, left_ref, right_ref, small_ref):
    columns = parts_ref.shape[2]
    rows = left_ref.shape[0]
    count = left_ref.shape[1] // columns
    for n in range(parts_ref.shape[0]):
        part = parts_ref[n].astype(jnp.float32)
        if n < count:
            left_ref[:, n * columns : (n + 1) * columns] = part[:rows]
        else:
            right_ref[:, (n - count) * columns : (n - count + 1) * columns] = part[:rows]
        last = n - parts_ref.shape[0] + small_ref.shape[1] // columns
        if last >= 0:
            small_ref[:, last * columns : (last + 1) * columns] = part[rows : rows + 8]


def spread_columns(parts, rows, width, small_width):
    count, _, columns = parts.shape
    return pl.pallas_call(
        spread_kernel,
        out_shape=(
            jax.ShapeDtypeStruct((rows, width), jnp.float32),
            jax.ShapeDtypeStruct((rows, count * columns - width), jnp.float32),
            jax.ShapeDtypeStruct((8, small_width), jnp.float32),
        ),
        in_specs=[in_vmem()],
        out_specs=(in_vmem(),) * 3,
        compiler_params=pltpu.CompilerParams(vmem_limit_bytes=12 * 2**20),
        name="spread_columns",
    )(parts)


def on_device(
    layer_input,
    positions,
    attention_gain,
    projection,
    projection_biases,
    output_matrix,
    feed_gain,
    gate_up_matrix,
    down_matrix,
    cotangent,
):
    place = lax.axis_index("wa").astype(jnp.int32)
    z, core = place // 2, place % 2
    ctx = lax.axis_index("ctx").astype(jnp.int32)
    rows = projection.shape[0]
    tokens = layer_input.shape[1]
    query_width = QUERY_HEADS * HEAD_SIZE
    key_width = KEY_VALUE_HEADS * HEAD_SIZE
    width = layer_input.shape[2]
    proj_width = projection.shape[1]
    bias_rows = projection_biases.shape[0]
    slice_width = down_matrix.shape[0]
    lanes = -(-slice_width // 128) * 128
    tile = 16
    sources = [(z + 4 - step) % 4 for step in STEPS]

    small = jnp.concatenate([projection_biases, attention_gain, feed_gain])
    small = jnp.pad(small[None], ((0, tile - 1), (0, proj_width - small.shape[0])))
    packed = lax.all_gather(jnp.concatenate([projection, small], axis=0), "wa", axis=0)

    spot = jnp.stack([z, core])
    local_places = jnp.stack([p for s in sources for p in (2 * s + core, 2 * s + 1 - core)])
    gate_up = lax.all_to_all(split_columns(gate_up_matrix, lanes), "wa", 0, 0, tiled=True)
    gate_up = gate_up.reshape(width, 2 * lanes)
    down = jnp.pad(down_matrix, ((0, lanes - slice_width), (0, 0)))

    layer_rows = layer_input[0]
    query_pos = positions[0]
    cosine, sine = angles(query_pos)
    cosine = jnp.tile(cosine, (1, 4))
    sine = jnp.tile(jnp.concatenate([-sine, sine], axis=1), (1, 2))
    first_normed, queries, pair, full_proj, gains = project(packed, layer_rows, cosine, sine)
    gain_one, gain_two = gains[0], gains[1]
    complete_output = lax.all_gather(after(output_matrix, packed), "wa", axis=0, tiled=True)
    out_grad = cotangent[0]
    all_grads = lax.all_gather(after(out_grad, complete_output), "wa", axis=0)

    pairs = ctx_exchange(pair).reshape(16 * tokens, 2 * key_width)
    low = ctx * tokens + jnp.arange(tokens, dtype=jnp.int32) - query_pos
    block = 4 * tokens
    start = jnp.stack(
        [
            ctx * tokens,
            jnp.maximum(jnp.min(low), 0) // block,
            (ctx * tokens + tokens + block - 1) // block,
        ]
    ).astype(jnp.int32)
    low = low[None]
    mixed, lse, attention_output, middle_state, second_normed = attend(
        start, queries, pairs, low, layer_rows, complete_output, gain_two
    )

    normed_pairs = gather_tokens(second_normed)
    worked = [
        feed(local_places[2 * n : 2 * n + 2], normed, all_grads, gate_up, down)
        for n, normed in enumerate(normed_pairs)
    ]
    hidden_pieces, joined_pieces, own, other = zip(*worked)
    paired = pair_tokens(own, other)

    parts = feed_grads(
        local_places,
        [piece for pair in normed_pairs for piece in pair],
        all_grads,
        joined_pieces,
        hidden_pieces,
        paired,
    )
    normed_two_grad = after(reduce_tokens(paired), parts)
    result = feed_out(local_places, down, hidden_pieces, [parts])
    result = lax.psum_scatter(result, "wa", scatter_dimension=0)
    result = (middle_state + result.astype(jnp.float32)).astype(jnp.bfloat16)
    parts = ctx_exchange(parts)

    _, norm_two_pull = jax.vjp(norm_rows, middle_state, gain_two[0])
    middle_part, gain_two_local = norm_two_pull(normed_two_grad)
    middle_grad = out_grad.astype(jnp.float32) + middle_part
    middle_lower = middle_grad.astype(jnp.bfloat16)
    mix_grad = column_product(middle_lower, complete_output).astype(jnp.bfloat16)
    query_back, pair_grad = attend_back(
        start, queries, pairs, low, mix_grad, mixed, lse, cosine, sine
    )
    early = reduce_rows(
        *rows_grads(spot, [(attention_output, middle_lower), (first_normed, query_back)])
    )

    pieces = ctx_exchange(after(pair_grad, parts))
    input_grad, kept, sent = project_back(
        spot,
        layer_rows,
        gain_one,
        full_proj,
        cosine,
        sine,
        first_normed,
        query_back,
        middle_grad,
        gain_two_local[None],
        pieces,
    )
    late = reduce_rows(kept, sent)

    kept, sent, down_part = owner_parts(spot, parts, tile)
    other = core_swap(sent)
    parts = [
        z_shift(jnp.concatenate([kept[step], other[step]], axis=0), step) for step in STEPS[1:]
    ]
    cuts = [(0, 0, 0), (1, 0, 0)] + [(n, None, part * tile) for n in (2, 3, 4) for part in (0, 1)]
    parts, _ = place_rows(local_places, [kept, other] + parts, cuts, tile)
    parts = lax.all_gather(jnp.concatenate([parts, down_part], axis=0), "ctx", axis=0)
    gate_up_total, down_total = join_columns(parts, rows, slice_width, width)

    mine = ctx_exchange(column_parts(early, late))
    mine = ctx_gather(jnp.sum(mine.astype(jnp.float32), axis=0).astype(jnp.bfloat16))
    output_total, projection_total, vectors = spread_columns(mine, rows, width, 2 * key_width)
    return (
        result[None],
        input_grad[None],
        vectors[0, bias_rows : bias_rows + rows],
        projection_total,
        vectors[0, :bias_rows],
        output_total,
        vectors[1, :rows],
        gate_up_total,
        down_total,
    )


def solution(mesh):
    placed = (
        P("wa", "ctx", None),
        P("wa", "ctx"),
        P("wa"),
        P("wa", None),
        P("wa"),
        P("wa", None),
        P("wa"),
        P("wa", None),
        P("wa", None),
        P("wa", "ctx", None),
    )
    return jax.shard_map(
        on_device,
        mesh=mesh,
        in_specs=placed,
        out_specs=(
            P("wa", "ctx", None),
            P("wa", "ctx", None),
            P("wa"),
            P("wa", None),
            P("wa"),
            P("wa", None),
            P("wa"),
            P("wa", None),
            P("wa", None),
        ),
        check_vma=False,
    )
```

```python
import functools

import jax
import jax.numpy as jnp
from jax import lax
from jax.experimental import pallas as pl
from jax.experimental.pallas import tpu as pltpu
from jax.sharding import PartitionSpec as P

QUERY_HEADS = 14
KEY_VALUE_HEADS = 2
HEAD_SIZE = 64
FF = 4864


EPS = 1e-06
THETA = 1000000.0
NEG = -1e30
VMEM = 56 * 2**20


def rows_product(left, right):
    return lax.dot_general(
        left, right, (((0,), (0,)), ((), ())), preferred_element_type=jnp.float32
    )


def column_product(left, right):
    return lax.dot_general(
        left, right, (((1,), (1,)), ((), ())), preferred_element_type=jnp.float32
    )


def norm_rows(value, gain):
    return value * lax.rsqrt(jnp.mean(value * value, axis=-1, keepdims=True) + EPS) * gain


def rotate(tensor, cosine_table, sine_table):
    half = tensor.shape[-1] // 2
    first = tensor[..., :half]
    second = tensor[..., half:]
    return jnp.concatenate(
        [first * cosine_table - second * sine_table, second * cosine_table + first * sine_table],
        axis=-1,
    )


def inverse_rotate(tensor, cosine_table, sine_table):
    half = tensor.shape[-1] // 2
    first = tensor[..., :half]
    second = tensor[..., half:]
    return jnp.concatenate(
        [first * cosine_table + second * sine_table, second * cosine_table - first * sine_table],
        axis=-1,
    )


def angles(positions):
    half = HEAD_SIZE // 2
    inverse = THETA ** (-(jnp.arange(half) * 2.0 / HEAD_SIZE))
    turned = positions.astype(jnp.float32)[:, None] * inverse.astype(jnp.float32)
    return (jnp.cos(turned), jnp.sin(turned))


def busy(microseconds):
    return pl.CostEstimate(
        flops=microseconds * 1150 * 10**6, bytes_accessed=microseconds * 10**6, transcendentals=0
    )


def turn_heads(value, cosine, sine):
    width = value.shape[1]
    lane = lax.broadcasted_iota(jnp.int32, value.shape, 1)
    half = HEAD_SIZE // 2
    partner = jnp.where(
        lane % HEAD_SIZE < half, pltpu.roll(value, width - half, 1), pltpu.roll(value, half, 1)
    )
    repeats = width // cosine.shape[1]
    return value * jnp.tile(cosine, (1, repeats)) + partner * jnp.tile(sine, (1, repeats))


def fetch(pairs, sems):
    copies = [pltpu.make_async_copy(*pair, sems.at[n]) for n, pair in enumerate(pairs)]
    for copy in copies:
        copy.start()
    for copy in copies:
        copy.wait()


def project_kernel(
    packed_ref, x_ref, cos_ref, sin_ref, normed_ref, q_ref, pair_ref, proj_ref, gains_ref, small_ref, sems
):
    count = packed_ref.shape[0]
    rows = proj_ref.shape[0] // count
    fetch(
        [
            (packed_ref.at[n, :rows, :], proj_ref.at[n * rows : (n + 1) * rows, :])
            for n in range(count)
        ]
        + [(packed_ref.at[n, rows:, :], small_ref.at[n]) for n in range(count)],
        sems,
    )
    small = [small_ref[n].astype(jnp.float32)[:1] for n in range(count)]
    bias_rows = proj_ref.shape[1] // count
    bias = jnp.concatenate([row[:, :bias_rows] for row in small], axis=1)
    gains = [
        jnp.concatenate([row[:, first : first + rows] for row in small], axis=1)
        for first in (bias_rows, bias_rows + rows)
    ]
    for n in range(2):
        gains_ref[n] = gains[n]
    x = x_ref[...].astype(jnp.float32)
    scale = lax.rsqrt(jnp.mean(x * x, axis=-1, keepdims=True) + EPS)
    normed = (x * scale * gains[0]).astype(jnp.bfloat16)
    normed_ref[...] = normed
    width = q_ref.shape[1]
    turned = width + KEY_VALUE_HEADS * HEAD_SIZE
    projected = jnp.dot(normed, proj_ref[...], preferred_element_type=jnp.float32) + bias
    rotated = turn_heads(projected[:, :turned], cos_ref[...], sin_ref[...])
    q_ref[...] = rotated[:, :width].astype(jnp.bfloat16)
    pair = jnp.concatenate([rotated[:, width:], projected[:, turned:]], axis=1).astype(jnp.bfloat16)
    pair_ref[...] = pair


def project(packed, x, cosine, sine):
    tokens, width = x.shape
    count, height, proj_width = packed.shape
    return pl.pallas_call(
        project_kernel,
        out_shape=(
            jax.ShapeDtypeStruct((tokens, width), jnp.bfloat16),
            jax.ShapeDtypeStruct((tokens, QUERY_HEADS * HEAD_SIZE), jnp.bfloat16),
            jax.ShapeDtypeStruct((tokens, 2 * KEY_VALUE_HEADS * HEAD_SIZE), jnp.bfloat16),
            jax.ShapeDtypeStruct((width, proj_width), jnp.bfloat16),
            jax.ShapeDtypeStruct((2, 1, width), jnp.float32),
        ),
        in_specs=[pl.BlockSpec(memory_space=pl.ANY)] + [in_vmem()] * 3,
        out_specs=(in_vmem(),) * 5,
        scratch_shapes=[
            pltpu.VMEM((count, height - width // count, proj_width), jnp.bfloat16),
            pltpu.SemaphoreType.DMA((2 * count,)),
        ],
        compiler_params=pltpu.CompilerParams(vmem_limit_bytes=VMEM),
        cost_estimate=busy(4),
        name="project",
    )(packed, x, cosine, sine)


def copies_kernel(value_ref, *refs):
    out_ref, sems = refs[-2:]
    fetch([(value_ref, out_ref.at[n]) for n in range(out_ref.shape[0])], sems)


def copies(value, count, earlier):
    return pl.pallas_call(
        copies_kernel,
        out_shape=jax.ShapeDtypeStruct((count,) + value.shape, value.dtype),
        in_specs=[in_vmem()] + [pl.BlockSpec(memory_space=pl.ANY)] * len(earlier),
        out_specs=pl.BlockSpec(memory_space=pl.ANY),
        scratch_shapes=[pltpu.SemaphoreType.DMA((count,))],
        compiler_params=pltpu.CompilerParams(vmem_limit_bytes=VMEM),
        cost_estimate=busy(2),
        name="copies",
    )(value, *earlier)


def project_back_kernel(
    place_ref, x_in, gain_ref, proj_in, cos_ref, sin_ref, normed_in, dq_in, grad_in, gain_two_ref, pieces_in, *refs
):
    input_grad_ref, kept_ref, sent_ref, stage_ref = refs[-11:-7]
    x_ref, proj_ref, normed_ref, dq_ref, grad_ref, pieces_ref, sems = refs[-7:]
    ins = (x_in, proj_in, normed_in, dq_in, grad_in, pieces_in)
    fetch(list(zip(ins, (x_ref, proj_ref, normed_ref, dq_ref, grad_ref, pieces_ref))), sems)
    z, core = place_ref[0], place_ref[1]
    key_width = KEY_VALUE_HEADS * HEAD_SIZE
    pair = pieces_ref[0].astype(jnp.float32)
    for n in range(1, pieces_ref.shape[0]):
        pair = pair + pieces_ref[n].astype(jnp.float32)
    keys = turn_heads(pair[:, :key_width], cos_ref[...], -sin_ref[...])
    pair = jnp.concatenate([keys, pair[:, key_width:]], axis=1).astype(jnp.bfloat16)
    turned = normed_ref[...].astype(jnp.float32).T.astype(jnp.bfloat16)
    stage_ref[...] = jnp.dot(turned, pair, preferred_element_type=jnp.float32)
    bias = jnp.concatenate(
        [
            jnp.sum(dq_ref[...].astype(jnp.float32), axis=0, keepdims=True),
            jnp.sum(pair.astype(jnp.float32), axis=0, keepdims=True),
        ],
        axis=1,
    )
    x = x_ref[...].astype(jnp.float32)
    scale = lax.rsqrt(jnp.mean(x * x, axis=-1, keepdims=True) + EPS)
    grad = lax.dot_general(
        jnp.concatenate([dq_ref[...], pair], axis=1),
        proj_ref[...],
        (((1,), (1,)), ((), ())),
        preferred_element_type=jnp.float32,
    )
    gain_one = jnp.sum(grad * x * scale, axis=0, keepdims=True)
    gained = grad * gain_ref[...]
    mean = jnp.mean(gained * x, axis=-1, keepdims=True)
    input_grad_ref[...] = grad_ref[...] + scale * gained - x * (scale * scale * scale * mean)

    rows = stage_ref.shape[0] // 8
    bias_rows = bias.shape[1] // 8
    blank = jnp.zeros((kept_ref.shape[1] - rows - 2, stage_ref.shape[1]), jnp.float32)
    for owner in range(8):
        at = lax.rem(owner // 2 - z + 4, 4)
        here = slice(owner * rows, (owner + 1) * rows)
        gain_two = gain_two_ref[:, here]
        first = jnp.concatenate(
            [bias[:, owner * bias_rows : (owner + 1) * bias_rows], gain_one[:, here]], axis=1
        )
        second = jnp.concatenate(
            [gain_two, jnp.zeros((1, stage_ref.shape[1] - rows), jnp.float32)], axis=1
        )
        both = jnp.concatenate([stage_ref[here, :], first, second, blank], axis=0).astype(jnp.bfloat16)

        @pl.when(core == owner % 2)
        def _(both=both, at=at):
            kept_ref[at] = both

        @pl.when(core != owner % 2)
        def _(both=both, at=at):
            sent_ref[at] = both


def project_back(place, x, gain, proj, cosine, sine, normed, dq, grad, gain_two, pieces, earlier):
    tokens, width = x.shape
    pair_width = pieces.shape[2]
    anywhere = pl.BlockSpec(memory_space=pl.ANY)
    out = jax.ShapeDtypeStruct((4, width // 8 + 16, pair_width), jnp.bfloat16)
    return pl.pallas_call(
        project_back_kernel,
        out_shape=(jax.ShapeDtypeStruct((tokens, width), jnp.float32), out, out),
        in_specs=[
            pl.BlockSpec(memory_space=pltpu.SMEM),
            anywhere,
            in_vmem(),
            anywhere,
            in_vmem(),
            in_vmem(),
            anywhere,
            anywhere,
            anywhere,
            in_vmem(),
            anywhere,
        ]
        + [anywhere] * len(earlier),
        out_specs=(in_vmem(),) * 3,
        scratch_shapes=[pltpu.VMEM((width, pair_width), jnp.float32)]
        + [pltpu.VMEM(a.shape, a.dtype) for a in (x, proj, normed, dq, grad, pieces)]
        + [pltpu.SemaphoreType.DMA((6,))],
        compiler_params=pltpu.CompilerParams(vmem_limit_bytes=VMEM),
        cost_estimate=busy(40),
        name="project_back",
    )(place, x, gain, proj, cosine, sine, normed, dq, grad, gain_two, pieces, *earlier)


def key_bias(low_ref, block_start, block, first_index):
    tokens = low_ref.shape[1]
    keys = block_start + lax.broadcasted_iota(jnp.int32, (block, tokens), 0)
    index = first_index + lax.broadcasted_iota(jnp.int32, (block, tokens), 1)
    return jnp.where((keys <= index) & (keys >= low_ref[...]), 0.0, NEG)


def head_places(tokens):
    group = QUERY_HEADS // KEY_VALUE_HEADS
    for h in range(QUERY_HEADS):
        g, i = divmod(h, group)
        yield g, slice(h * HEAD_SIZE, (h + 1) * HEAD_SIZE), slice(i * tokens, (i + 1) * tokens)


def attend_kernel(
    start_ref, q_in, kv_in, low_ref, x_in, out_in, gain_ref, *refs
):
    mixed_ref, lse_ref, attended_ref, middle_ref, normed_ref = refs[-17:-12]
    qt, s_ref, p_ref, bias_ref, m_ref, l_ref, acc_ref = refs[-12:-5]
    q_ref, kv_ref, x_ref, out_ref, sems = refs[-5:]
    pairs = [(q_in, q_ref), (kv_in, kv_ref), (x_in, x_ref), (out_in, out_ref)]
    loads = [pltpu.make_async_copy(*pair, sems.at[n]) for n, pair in enumerate(pairs)]
    for load in loads:
        load.start()
    for load in loads[:2]:
        load.wait()
    tokens = q_ref.shape[0]
    block, rows = s_ref.shape
    turned = (q_ref[...].astype(jnp.float32) * HEAD_SIZE ** (-0.5)).T.astype(jnp.bfloat16)
    for g, lanes, at in head_places(tokens):
        qt[g, :, at] = turned[lanes, :]
    m_ref[...] = jnp.full_like(m_ref, NEG)
    l_ref[...] = jnp.zeros_like(l_ref)
    acc_ref[...] = jnp.zeros_like(acc_ref)

    def visit(which, carry):
        block_start = pl.multiple_of(which * block, block)
        here = pl.ds(block_start, block)
        bias_ref[...] = key_bias(low_ref, block_start, block, start_ref[0])
        key_width = KEY_VALUE_HEADS * HEAD_SIZE
        values = kv_ref[here, key_width:].astype(jnp.float32).T.astype(jnp.bfloat16)
        for g in range(KEY_VALUE_HEADS):
            lanes = slice(g * HEAD_SIZE, (g + 1) * HEAD_SIZE)
            s_ref[...] = jnp.dot(kv_ref[here, lanes], qt[g], preferred_element_type=jnp.float32)
            for i in range(rows // tokens):
                at = slice(i * tokens, (i + 1) * tokens)
                s = s_ref[:, at] + bias_ref[...]
                old = m_ref[g, :, at]
                peak = jnp.maximum(old, jnp.max(s, axis=0, keepdims=True))
                e = jnp.exp(s - peak)
                scale = jnp.exp(old - peak)
                m_ref[g, :, at] = peak
                l_ref[g, :, at] = l_ref[g, :, at] * scale + jnp.sum(e, axis=0, keepdims=True)
                acc_ref[g, :, at] = acc_ref[g, :, at] * scale
                p_ref[:, at] = e.astype(jnp.bfloat16)
            acc_ref[g] += jnp.dot(values[lanes, :], p_ref[...], preferred_element_type=jnp.float32)
        return carry

    lax.fori_loop(start_ref[1], start_ref[2], visit, 0)
    mixed = [acc_ref[g, :, at] / l_ref[g, :, at] for g, _, at in head_places(tokens)]
    mixed = jnp.concatenate(mixed, axis=0).T
    mixed_ref[...] = mixed
    lse_ref[...] = m_ref[...] + jnp.log(l_ref[...])
    attended = mixed.astype(jnp.bfloat16)
    attended_ref[...] = attended
    for load in loads[2:]:
        load.wait()
    middle = x_ref[...].astype(jnp.float32) + jnp.dot(
        attended, out_ref[...], preferred_element_type=jnp.float32
    )
    middle_ref[...] = middle
    scale = lax.rsqrt(jnp.mean(middle * middle, axis=-1, keepdims=True) + EPS)
    normed_ref[...] = (middle * scale * gain_ref[...]).astype(jnp.bfloat16)


def attend_back_kernel(
    start_ref, q_ref, kv_ref, low_ref, dmix_ref, mixed_ref, lse_ref, cos_ref, sin_ref, dq_ref, dkv_ref,
    qs, qt, ms, mt, delta_ref, s_ref, dp_ref, p_ref, g_ref, bias_ref, acc_ref,
):
    tokens = q_ref.shape[0]
    block, rows = s_ref.shape
    key_width = KEY_VALUE_HEADS * HEAD_SIZE
    q = q_ref[...].astype(jnp.float32) * HEAD_SIZE ** (-0.5)
    dmix = dmix_ref[...].astype(jnp.float32)
    q_turned = q.T.astype(jnp.bfloat16)
    dmix_turned = dmix.T
    weighed = (dmix * mixed_ref[...]).T
    q = q.astype(jnp.bfloat16)
    for g, lanes, at in head_places(tokens):
        qs[g, at, :] = q[:, lanes]
        ms[g, at, :] = dmix_ref[:, lanes]
        qt[g, :, at] = q_turned[lanes, :]
        mt[g, :, at] = dmix_turned[lanes, :].astype(jnp.bfloat16)
        delta_ref[g, :, at] = jnp.sum(weighed[lanes, :], axis=0, keepdims=True)
    acc_ref[...] = jnp.zeros_like(acc_ref)
    dkv_ref[...] = jnp.zeros_like(dkv_ref)

    def visit(which, carry):
        block_start = pl.multiple_of(which * block, block)
        here = pl.ds(block_start, block)
        bias_ref[...] = key_bias(low_ref, block_start, block, start_ref[0])
        keys_turned = kv_ref[here, :key_width].astype(jnp.float32).T.astype(jnp.bfloat16)
        grads = [None] * (2 * KEY_VALUE_HEADS)
        for g in range(KEY_VALUE_HEADS):
            lanes = slice(g * HEAD_SIZE, (g + 1) * HEAD_SIZE)
            s_ref[...] = jnp.dot(kv_ref[here, lanes], qt[g], preferred_element_type=jnp.float32)
            values = kv_ref[here, key_width + g * HEAD_SIZE : key_width + (g + 1) * HEAD_SIZE]
            dp_ref[...] = jnp.dot(values, mt[g], preferred_element_type=jnp.float32)
            for i in range(rows // tokens):
                at = slice(i * tokens, (i + 1) * tokens)
                p = jnp.exp(s_ref[:, at] + bias_ref[...] - lse_ref[g, :, at])
                p_ref[:, at] = p.astype(jnp.bfloat16)
                g_ref[:, at] = (p * (dp_ref[:, at] - delta_ref[g, :, at])).astype(jnp.bfloat16)
            acc_ref[g] += jnp.dot(keys_turned[lanes, :], g_ref[...], preferred_element_type=jnp.float32)
            grads[g] = jnp.dot(g_ref[...], qs[g], preferred_element_type=jnp.float32)
            grads[KEY_VALUE_HEADS + g] = jnp.dot(
                p_ref[...], ms[g], preferred_element_type=jnp.float32
            )
        grads = jnp.concatenate(grads, axis=1).astype(jnp.bfloat16)
        for n in range(block // tokens):
            dkv_ref[which * (block // tokens) + n] = grads[n * tokens : (n + 1) * tokens, :]
        return carry

    lax.fori_loop(start_ref[1], start_ref[2], visit, 0)
    dq = [acc_ref[g, :, at] for g, _, at in head_places(tokens)]
    dq = jnp.concatenate(dq, axis=0).T * HEAD_SIZE ** (-0.5)
    dq_ref[...] = turn_heads(dq, cos_ref[...], -sin_ref[...]).astype(jnp.bfloat16)


def in_vmem():
    return pl.BlockSpec(memory_space=pltpu.VMEM)


def attend(start, queries, pairs, low, x, out_matrix, gain, earlier):
    tokens, width = queries.shape
    rows = QUERY_HEADS // KEY_VALUE_HEADS * tokens
    block = 4 * tokens
    heads = KEY_VALUE_HEADS
    return pl.pallas_call(
        attend_kernel,
        out_shape=(
            jax.ShapeDtypeStruct((tokens, width), jnp.float32),
            jax.ShapeDtypeStruct((heads, 1, rows), jnp.float32),
            jax.ShapeDtypeStruct((tokens, width), jnp.bfloat16),
            jax.ShapeDtypeStruct(x.shape, jnp.float32),
            jax.ShapeDtypeStruct(x.shape, jnp.bfloat16),
        ),
        in_specs=[
            pl.BlockSpec(memory_space=pltpu.SMEM),
            pl.BlockSpec(memory_space=pl.ANY),
            pl.BlockSpec(memory_space=pl.ANY),
            in_vmem(),
            pl.BlockSpec(memory_space=pl.ANY),
            pl.BlockSpec(memory_space=pl.ANY),
            in_vmem(),
        ]
        + [pl.BlockSpec(memory_space=pl.ANY)] * len(earlier),
        out_specs=(in_vmem(),) * 5,
        scratch_shapes=[
            pltpu.VMEM((heads, HEAD_SIZE, rows), jnp.bfloat16),
            pltpu.VMEM((block, rows), jnp.float32),
            pltpu.VMEM((block, rows), jnp.bfloat16),
            pltpu.VMEM((block, tokens), jnp.float32),
            pltpu.VMEM((heads, 1, rows), jnp.float32),
            pltpu.VMEM((heads, 1, rows), jnp.float32),
            pltpu.VMEM((heads, HEAD_SIZE, rows), jnp.float32),
            pltpu.VMEM(queries.shape, queries.dtype),
            pltpu.VMEM(pairs.shape, pairs.dtype),
            pltpu.VMEM(x.shape, x.dtype),
            pltpu.VMEM(out_matrix.shape, out_matrix.dtype),
            pltpu.SemaphoreType.DMA((4,)),
        ],
        compiler_params=pltpu.CompilerParams(vmem_limit_bytes=VMEM),
        cost_estimate=busy(9),
        name="attend",
    )(start, queries, pairs, low, x, out_matrix, gain, *earlier)


def attend_back(start, queries, pairs, low, mix_grad, mixed, lse, cosine, sine):
    tokens, width = queries.shape
    rows = QUERY_HEADS // KEY_VALUE_HEADS * tokens
    block = 4 * tokens
    heads = KEY_VALUE_HEADS
    return pl.pallas_call(
        attend_back_kernel,
        out_shape=(
            jax.ShapeDtypeStruct((tokens, width), jnp.bfloat16),
            jax.ShapeDtypeStruct((pairs.shape[0] // tokens, tokens, pairs.shape[1]), jnp.bfloat16),
        ),
        in_specs=[pl.BlockSpec(memory_space=pltpu.SMEM)] + [in_vmem()] * 8,
        out_specs=(in_vmem(), in_vmem()),
        scratch_shapes=[
            pltpu.VMEM((heads, rows, HEAD_SIZE), jnp.bfloat16),
            pltpu.VMEM((heads, HEAD_SIZE, rows), jnp.bfloat16),
            pltpu.VMEM((heads, rows, HEAD_SIZE), jnp.bfloat16),
            pltpu.VMEM((heads, HEAD_SIZE, rows), jnp.bfloat16),
            pltpu.VMEM((heads, 1, rows), jnp.float32),
            pltpu.VMEM((block, rows), jnp.float32),
            pltpu.VMEM((block, rows), jnp.float32),
            pltpu.VMEM((block, rows), jnp.bfloat16),
            pltpu.VMEM((block, rows), jnp.bfloat16),
            pltpu.VMEM((block, tokens), jnp.float32),
            pltpu.VMEM((heads, HEAD_SIZE, rows), jnp.float32),
        ],
        compiler_params=pltpu.CompilerParams(vmem_limit_bytes=VMEM),
        cost_estimate=busy(25),
        name="attend_back",
    )(start, queries, pairs, low, mix_grad, mixed, lse, cosine, sine)


def split_kernel(place_ref, matrix_ref, down_ref, kept_ref, sent_ref, padded_ref):
    padded_ref[: down_ref.shape[0], :] = down_ref[...]
    padded_ref[down_ref.shape[0] :, :] = jnp.zeros(
        (padded_ref.shape[0] - down_ref.shape[0], down_ref.shape[1]), down_ref.dtype
    )
    z, core = place_ref[0], place_ref[1]
    width, lanes = matrix_ref.shape[1] // 16, kept_ref.shape[2] // 2
    for owner in range(8):
        at = lax.rem(owner // 2 - z + 4, 4)
        gate = matrix_ref[:, owner * width : (owner + 1) * width].astype(jnp.float32)
        up = matrix_ref[:, (8 + owner) * width : (9 + owner) * width].astype(jnp.float32)
        blank = jnp.zeros((gate.shape[0], lanes - width), jnp.float32)
        both = jnp.concatenate([gate, blank, up, blank], axis=1).astype(jnp.bfloat16)

        @pl.when(core == owner % 2)
        def _(both=both, at=at):
            kept_ref[at] = both

        @pl.when(core != owner % 2)
        def _(both=both, at=at):
            sent_ref[at] = both


def split_columns(place, matrix, down, lanes):
    rows = matrix.shape[0]
    out = jax.ShapeDtypeStruct((4, rows, 2 * lanes), matrix.dtype)
    return pl.pallas_call(
        split_kernel,
        out_shape=(out, out, jax.ShapeDtypeStruct((lanes, down.shape[1]), down.dtype)),
        in_specs=[pl.BlockSpec(memory_space=pltpu.SMEM), in_vmem(), in_vmem()],
        out_specs=(in_vmem(),) * 3,
        compiler_params=pltpu.CompilerParams(vmem_limit_bytes=VMEM),
        cost_estimate=busy(4),
        name="split_columns",
    )(place, matrix, down)


def place_kernel(cuts, at_ref, *refs):
    pieces, (out_ref, rest_ref, sems, rest_sems) = refs[:-4], refs[-4:]
    rows = out_ref.shape[0] // len(cuts)
    copies = []
    for n, (which, lead, first) in enumerate(cuts):
        piece = pieces[which] if lead is None else pieces[which].at[lead]
        copies.append(
            pltpu.make_async_copy(
                piece.at[first : first + rows, :],
                out_ref.at[pl.ds(pl.multiple_of(at_ref[n] * rows, 16), rows), :],
                sems.at[n],
            )
        )
        if rest_ref.shape[0] == len(cuts):
            copies.append(
                pltpu.make_async_copy(piece.at[rows:, :], rest_ref.at[at_ref[n]], rest_sems.at[n])
            )
    for copy in copies:
        copy.start()
    if rest_ref.shape[0] != len(cuts):
        rest_ref[...] = jnp.zeros_like(rest_ref)
    for copy in copies:
        copy.wait()


def place_rows(at, arrays, cuts, rows, rest=0):
    width, kind = arrays[0].shape[-1], arrays[0].dtype
    count = len(cuts)
    rest_shape = (count, rest, width) if rest else (1, 8, 128)
    return pl.pallas_call(
        functools.partial(place_kernel, tuple(cuts)),
        out_shape=(
            jax.ShapeDtypeStruct((count * rows, width), kind),
            jax.ShapeDtypeStruct(rest_shape, kind if rest else jnp.float32),
        ),
        in_specs=[pl.BlockSpec(memory_space=pltpu.SMEM)]
        + [pl.BlockSpec(memory_space=pl.ANY)] * len(arrays),
        out_specs=(in_vmem(), in_vmem()),
        scratch_shapes=[pltpu.SemaphoreType.DMA((count,)), pltpu.SemaphoreType.DMA((count,))],
        compiler_params=pltpu.CompilerParams(vmem_limit_bytes=VMEM),
        cost_estimate=busy(2),
        name="place_rows",
    )(at, *arrays)


def feed_kernel(at_ref, *refs):
    normed_in, (grads_in, down_in), gate_up_in = refs[:8], refs[8:10], refs[10:16]
    hidden_ref, own_ref, other_ref, out_ref = refs[16:20]
    normed_ref, grads_ref, gate_up_ref, down_ref, joined_ref, turned_ref, stage_ref, sems = refs[20:]
    tokens = normed_in[0].shape[0]
    lanes = hidden_ref.shape[1]
    step = 2 * tokens
    tile = 16
    pairs = [(down_in, down_ref)]
    rows = gate_up_ref.shape[0] // 8
    pieces = [gate_up_in[0].at[0], gate_up_in[1].at[0]]
    pieces += [ref.at[part * rows : (part + 1) * rows, :] for ref in gate_up_in[2:4] for part in range(2)]
    pieces += gate_up_in[4:]
    for n, piece in enumerate(pieces):
        start = pl.multiple_of(at_ref[n] * rows, 16)
        pairs.append((piece, gate_up_ref.at[pl.ds(start, rows), :]))
    for n in range(8):
        here = slice(n * tokens, (n + 1) * tokens)
        pairs.append((normed_in[n], normed_ref.at[here, :]))
        pairs.append((grads_in.at[at_ref[n]], grads_ref.at[here, :]))
    loads = [pltpu.make_async_copy(*pair, sems.at[n]) for n, pair in enumerate(pairs)]
    for load in loads:
        load.start()
    for load in loads[:9]:
        load.wait()
    for part in range(4):
        for load in loads[9 + 4 * part : 13 + 4 * part]:
            load.wait()
        here = slice(part * step, (part + 1) * step)
        gate = jnp.dot(normed_ref[here, :], gate_up_ref[:, :lanes], preferred_element_type=jnp.float32)
        up = jnp.dot(normed_ref[here, :], gate_up_ref[:, lanes:], preferred_element_type=jnp.float32)
        hidden_grad = lax.dot_general(
            grads_ref[here, :], down_ref[...], (((1,), (1,)), ((), ())), preferred_element_type=jnp.float32
        )
        sg = 1.0 / (1.0 + jnp.exp(-gate))
        act = gate * sg
        hidden_ref[here, :] = (act * up).astype(jnp.bfloat16)
        joined_ref[here, :lanes] = (hidden_grad * up * sg * (1.0 + gate * (1.0 - sg))).astype(
            jnp.bfloat16
        )
        joined_ref[here, lanes:] = (hidden_grad * act).astype(jnp.bfloat16)
        back = lax.dot_general(
            joined_ref[here, :], gate_up_ref[...], (((1,), (1,)), ((), ())), preferred_element_type=jnp.float32
        )
        own_ref[part] = back[:tokens]
        other_ref[part] = back[tokens:].astype(jnp.bfloat16)
        turned_ref[:, here] = normed_ref[here, :].astype(jnp.float32).T.astype(jnp.bfloat16)

    rows = stage_ref.shape[0] // 8
    for half in range(2):
        stage_ref[...] = jnp.dot(
            turned_ref[...],
            joined_ref[:, half * lanes : (half + 1) * lanes],
            preferred_element_type=jnp.float32,
        )
        for r in range(rows // tile):
            for k in range(8):
                first = k * rows + r * tile
                out_ref[2 * r + half, k * tile : (k + 1) * tile, :] = stage_ref[
                    first : first + tile, :
                ].astype(jnp.bfloat16)
    for part in range(2 * rows // tile, 16):
        out_ref[part, : 8 * tile, :] = jnp.zeros((8 * tile, lanes), jnp.bfloat16)
    for part in range(4):
        here = slice(part * step, (part + 1) * step)
        turned_ref[:, here] = grads_ref[here, :].astype(jnp.float32).T.astype(jnp.bfloat16)
    stage_ref[...] = jnp.dot(turned_ref[...], hidden_ref[...], preferred_element_type=jnp.float32)
    rows = stage_ref.shape[0] // 16
    blank = jnp.zeros((out_ref.shape[1] - 8 * tile - rows, lanes), jnp.float32)
    for part in range(16):
        piece = jnp.concatenate([stage_ref[part * rows : (part + 1) * rows, :], blank], axis=0)
        out_ref[part, 8 * tile :, :] = piece.astype(jnp.bfloat16)


def feed(at, normed, grads, gate_up, down):
    tokens, width = normed[0].shape
    lanes = down.shape[0]
    part = 8 * 16 + -(-width // 16 // 16) * 16
    return pl.pallas_call(
        feed_kernel,
        out_shape=(
            jax.ShapeDtypeStruct((8 * tokens, lanes), jnp.bfloat16),
            jax.ShapeDtypeStruct((4, tokens, width), jnp.float32),
            jax.ShapeDtypeStruct((4, tokens, width), jnp.bfloat16),
            jax.ShapeDtypeStruct((16, part, lanes), jnp.bfloat16),
        ),
        in_specs=[pl.BlockSpec(memory_space=pltpu.SMEM)] + [pl.BlockSpec(memory_space=pl.ANY)] * 16,
        out_specs=(in_vmem(),) * 4,
        scratch_shapes=[
            pltpu.VMEM((8 * tokens, width), jnp.bfloat16),
            pltpu.VMEM((8 * tokens, width), jnp.bfloat16),
            pltpu.VMEM((width, 2 * lanes), jnp.bfloat16),
            pltpu.VMEM(down.shape, down.dtype),
            pltpu.VMEM((8 * tokens, 2 * lanes), jnp.bfloat16),
            pltpu.VMEM((width, 8 * tokens), jnp.bfloat16),
            pltpu.VMEM((width, lanes), jnp.float32),
            pltpu.SemaphoreType.DMA((25,)),
        ],
        compiler_params=pltpu.CompilerParams(vmem_limit_bytes=VMEM),
        cost_estimate=busy(18),
        name="feed",
    )(at, *normed, grads, down, *gate_up)


def feed_out_kernel(at_ref, down_ref, *refs):
    hidden, out_ref = refs[0], refs[-1]
    tokens = out_ref.shape[1]
    for n in range(4):
        here = slice(2 * n * tokens, 2 * (n + 1) * tokens)
        out = jnp.dot(hidden[here, :], down_ref[...], preferred_element_type=jnp.float32)
        for part in range(2):
            out_ref[at_ref[2 * n + part]] = out[part * tokens : (part + 1) * tokens].astype(
                jnp.bfloat16
            )


def feed_out(at, down, hidden, earlier):
    tokens = hidden.shape[0] // 8
    return pl.pallas_call(
        feed_out_kernel,
        out_shape=jax.ShapeDtypeStruct((8, tokens, down.shape[1]), jnp.bfloat16),
        in_specs=[pl.BlockSpec(memory_space=pltpu.SMEM)]
        + [in_vmem()] * 2
        + [pl.BlockSpec(memory_space=pl.ANY)] * len(earlier),
        out_specs=in_vmem(),
        compiler_params=pltpu.CompilerParams(vmem_limit_bytes=VMEM),
        cost_estimate=busy(4),
        name="feed_out",
    )(at, down, hidden, *earlier)


def owner_parts_kernel(place_ref, parts_ref, earlier_ref, kept_ref, sent_ref, rest_ref):
    del earlier_ref
    z, core = place_ref[0], place_ref[1]
    rows = kept_ref.shape[1]

    def total(here):
        value = parts_ref[0, here, :].astype(jnp.float32)
        for n in range(1, parts_ref.shape[0]):
            value = value + parts_ref[n, here, :].astype(jnp.float32)
        return value.astype(jnp.bfloat16)

    for owner in range(8):
        at = lax.rem(owner // 2 - z + 4, 4)
        part = total(slice(owner * rows, (owner + 1) * rows))

        @pl.when(core == owner % 2)
        def _(part=part, at=at):
            kept_ref[at] = part

        @pl.when(core != owner % 2)
        def _(part=part, at=at):
            sent_ref[at] = part

    for first in range(0, rest_ref.shape[0], rows):
        rest_ref[first : first + rows, :] = total(slice(8 * rows + first, 9 * rows + first))


def owner_parts(place, parts, rows, earlier):
    _, height, width = parts.shape
    out = jax.ShapeDtypeStruct((4, rows, width), jnp.bfloat16)
    return pl.pallas_call(
        owner_parts_kernel,
        out_shape=(out, out, jax.ShapeDtypeStruct((height - 8 * rows, width), jnp.bfloat16)),
        in_specs=[pl.BlockSpec(memory_space=pltpu.SMEM), in_vmem(), pl.BlockSpec(memory_space=pl.ANY)],
        out_specs=(in_vmem(),) * 3,
        compiler_params=pltpu.CompilerParams(vmem_limit_bytes=VMEM),
        cost_estimate=busy(3),
        name="owner_parts",
    )(place, parts, earlier)


def rows_grads_kernel(place_ref, *refs):
    kept_ref, sent_ref, stage_ref = refs[-3:]
    pairs = (len(refs) - 3) // 2
    rest_ref = refs[2 * pairs] if (len(refs) - 3) % 2 else None
    z, core = place_ref[0], place_ref[1]
    rows = stage_ref.shape[0] // 8
    first = 0
    for n in range(pairs):
        left, right = refs[2 * n], refs[2 * n + 1]
        turned = left[...].astype(jnp.float32).T.astype(jnp.bfloat16)
        stage_ref[:, first : first + right.shape[1]] = jnp.dot(
            turned, right[...], preferred_element_type=jnp.float32
        )
        first += right.shape[1]
    for owner in range(8):
        at = lax.rem(owner // 2 - z + 4, 4)

        @pl.when(core == owner % 2)
        def _(owner=owner, at=at):
            kept_ref[at, :rows, :] = stage_ref[owner * rows : (owner + 1) * rows, :].astype(jnp.bfloat16)
            if rest_ref is not None:
                kept_ref[at, rows:, :] = rest_ref[owner]

        @pl.when(core != owner % 2)
        def _(owner=owner, at=at):
            sent_ref[at, :rows, :] = stage_ref[owner * rows : (owner + 1) * rows, :].astype(jnp.bfloat16)
            if rest_ref is not None:
                sent_ref[at, rows:, :] = rest_ref[owner]


def rows_grads(place, pairs, rest=None):
    height = pairs[0][0].shape[1]
    width = sum(right.shape[1] for _, right in pairs)
    rows = height // 8 + (0 if rest is None else rest.shape[1])
    arrays = [array for pair in pairs for array in pair] + ([] if rest is None else [rest])
    out = jax.ShapeDtypeStruct((4, rows, width), jnp.bfloat16)
    return pl.pallas_call(
        rows_grads_kernel,
        out_shape=(out, out),
        in_specs=[pl.BlockSpec(memory_space=pltpu.SMEM)] + [in_vmem()] * len(arrays),
        out_specs=(in_vmem(), in_vmem()),
        scratch_shapes=[pltpu.VMEM((height, width), jnp.float32)],
        compiler_params=pltpu.CompilerParams(vmem_limit_bytes=VMEM),
        cost_estimate=busy(3),
        name="rows_grads",
    )(place, *arrays)


def join_kernel(parts_ref, gate_up_ref, down_ref, stage_ref):
    width = gate_up_ref.shape[1] // 16
    tile = 16
    for part in range(2 * gate_up_ref.shape[0] // tile):
        r, half = divmod(part, 2)
        columns = [
            parts_ref[part, k * tile : (k + 1) * tile, :].astype(jnp.float32)[:, :width]
            for k in range(8)
        ]
        gate_up_ref[r * tile : (r + 1) * tile, half * 8 * width : (half + 1) * 8 * width] = (
            jnp.concatenate(columns, axis=1)
        )
    rows = stage_ref.shape[0] // 16
    for part in range(16):
        stage_ref[part * rows : (part + 1) * rows, :] = parts_ref[part, 8 * tile :, :].astype(
            jnp.float32
        )[:rows]
    for block in range(stage_ref.shape[0] // 128):
        at = slice(block * 128, (block + 1) * 128)
        down_ref[:, at] = stage_ref[at, :].T[:width]


def join_columns(parts, rows, width, model_width):
    return pl.pallas_call(
        join_kernel,
        out_shape=(
            jax.ShapeDtypeStruct((rows, 16 * width), jnp.float32),
            jax.ShapeDtypeStruct((width, model_width), jnp.float32),
        ),
        in_specs=[in_vmem()],
        out_specs=(in_vmem(), in_vmem()),
        scratch_shapes=[pltpu.VMEM((model_width, parts.shape[2]), jnp.float32)],
        compiler_params=pltpu.CompilerParams(vmem_limit_bytes=VMEM),
        cost_estimate=busy(4),
        name="join_columns",
    )(parts)


def columns_kernel(*refs):
    ins, out_ref, early_ref, late_ref, sems = refs[:10], refs[-4], refs[-3], refs[-2], refs[-1]
    lead_early = [ref.at[0] if len(ref.shape) == 3 else ref for ref in ins[:5]]
    lead_late = [ref.at[0] if len(ref.shape) == 3 else ref for ref in ins[5:]]
    fetch(
        [(ref, early_ref.at[n]) for n, ref in enumerate(lead_early)]
        + [(ref, late_ref.at[n]) for n, ref in enumerate(lead_late)],
        sems,
    )
    _, rows, width = early_ref.shape
    columns = out_ref.shape[2]
    blank = jnp.zeros((out_ref.shape[1] - rows, columns), jnp.float32)
    count = width // columns
    for n in range(out_ref.shape[0]):
        ref = early_ref if n < count else late_ref
        first = (n if n < count else n - count) * columns
        total = ref[0, :, first : first + columns].astype(jnp.float32)
        for m in range(1, 5):
            total = total + ref[m, :, first : first + columns].astype(jnp.float32)
        if n < count:
            total = jnp.concatenate([total, blank], axis=0)
        out_ref[n] = total.astype(jnp.bfloat16)


def column_parts(early, late):
    early_shape, late_shape = early[-1].shape, late[-1].shape
    columns = (early_shape[1] + late_shape[1]) // 16
    return pl.pallas_call(
        columns_kernel,
        out_shape=jax.ShapeDtypeStruct((16, late_shape[0], columns), jnp.bfloat16),
        in_specs=[pl.BlockSpec(memory_space=pl.ANY)] * 10,
        out_specs=in_vmem(),
        scratch_shapes=[
            pltpu.VMEM((5,) + early_shape, jnp.bfloat16),
            pltpu.VMEM((5,) + late_shape, jnp.bfloat16),
            pltpu.SemaphoreType.DMA((10,)),
        ],
        compiler_params=pltpu.CompilerParams(vmem_limit_bytes=VMEM),
        cost_estimate=busy(30),
        name="column_parts",
    )(*early, *late)


def core_swap(value):
    return lax.ppermute(value, "wa", [(i, i ^ 1) for i in range(8)])


def z_shift(value, step):
    return lax.ppermute(value, "wa", [(i, (i + 2 * step) % 8) for i in range(8)])


def ctx_exchange(value):
    return lax.all_to_all(value, "ctx", 0, 0, tiled=True)


def ctx_gather(value):
    return ctx_exchange(jnp.broadcast_to(value[None], (16,) + value.shape))


STEPS = (0, 1, 3, 2)


def gather_tokens(value):
    pieces = [z_shift(value, step) if step else value for step in STEPS]
    return [(piece, core_swap(piece)) for piece in pieces]


def return_tokens(paired):
    return [z_shift(mine, -step) if step else mine for step, mine in zip(STEPS, paired)]


def reduce_rows(kept, sent):
    other = core_swap(sent)
    pieces = [kept, other]
    for step in STEPS[1:]:
        mine = kept[step].astype(jnp.float32) + other[step].astype(jnp.float32)
        pieces.append(z_shift(mine.astype(jnp.bfloat16), step))
    return pieces


def after(value, *others):
    held = sum(other[(0,) * other.ndim].astype(jnp.float32) for other in others) * 0.0
    return value + held.astype(value.dtype)


def spread_kernel(parts_ref, left_ref, right_ref, bias_ref, gain_one_ref, gain_two_ref):
    columns = parts_ref.shape[2]
    rows = left_ref.shape[0]
    count = left_ref.shape[1] // columns
    small = []
    for n in range(parts_ref.shape[0]):
        part = parts_ref[n].astype(jnp.float32)
        if n < count:
            left_ref[:, n * columns : (n + 1) * columns] = part[:rows]
        else:
            right_ref[:, (n - count) * columns : (n - count + 1) * columns] = part[:rows]
        small.append(part[rows : rows + 8])
    small = jnp.concatenate(small[-2:], axis=1)
    bias_rows = bias_ref.shape[1]
    bias_ref[...] = small[:1, :bias_rows]
    gain_one_ref[...] = small[:1, bias_rows : bias_rows + rows]
    gain_two_ref[...] = small[1:2, :rows]


def spread_columns(parts, rows, width, bias_rows):
    count, _, columns = parts.shape
    shapes = [(rows, width), (rows, count * columns - width), (1, bias_rows), (1, rows), (1, rows)]
    return pl.pallas_call(
        spread_kernel,
        out_shape=tuple(jax.ShapeDtypeStruct(shape, jnp.float32) for shape in shapes),
        in_specs=[in_vmem()],
        out_specs=(in_vmem(),) * 5,
        compiler_params=pltpu.CompilerParams(vmem_limit_bytes=VMEM),
        cost_estimate=busy(1),
        name="spread_columns",
    )(parts)


def on_device(
    layer_input,
    positions,
    attention_gain,
    projection,
    projection_biases,
    output_matrix,
    feed_gain,
    gate_up_matrix,
    down_matrix,
    cotangent,
):
    place = lax.axis_index("wa").astype(jnp.int32)
    z, core = place // 2, place % 2
    ctx = lax.axis_index("ctx").astype(jnp.int32)
    rows = projection.shape[0]
    tokens = layer_input.shape[1]
    query_width = QUERY_HEADS * HEAD_SIZE
    key_width = KEY_VALUE_HEADS * HEAD_SIZE
    width = layer_input.shape[2]
    proj_width = projection.shape[1]
    bias_rows = projection_biases.shape[0]
    slice_width = down_matrix.shape[0]
    lanes = -(-slice_width // 128) * 128
    tile = 16
    sources = [(z + 4 - step) % 4 for step in STEPS]

    small = jnp.concatenate([projection_biases, attention_gain, feed_gain])
    small = jnp.pad(small[None], ((0, tile - 1), (0, proj_width - small.shape[0])))
    packed = lax.all_gather(jnp.concatenate([projection, small], axis=0), "wa", axis=0)

    spot = jnp.stack([z, core])
    local_places = jnp.stack([p for s in sources for p in (2 * s + core, 2 * s + 1 - core)])
    kept, sent, down = split_columns(spot, gate_up_matrix, down_matrix, lanes)
    other = core_swap(sent)
    gate_up = [jnp.concatenate([kept[step], other[step]], axis=0) for step in STEPS[1:3]]
    gate_up += [kept[2], other[2]]

    layer_rows = layer_input[0]
    query_pos = positions[0]
    cosine, sine = angles(query_pos)
    cosine = jnp.tile(cosine, (1, 4))
    sine = jnp.tile(jnp.concatenate([-sine, sine], axis=1), (1, 2))
    first_normed, queries, pair, full_proj, gains = project(packed, layer_rows, cosine, sine)
    gain_one, gain_two = gains[0], gains[1]
    complete_output = lax.all_gather(output_matrix, "wa", axis=0, tiled=True)
    out_grad = cotangent[0]
    all_grads = lax.all_gather(out_grad, "wa", axis=0)

    pairs_sent = copies(pair, 16, gate_up)
    gate_up = [z_shift(piece, step) for step, piece in zip((1, 3, 2, 3), gate_up)]
    gate_up[3] = z_shift(gate_up[3], 3)
    pairs = ctx_exchange(pairs_sent).reshape(16 * tokens, 2 * key_width)
    low = ctx * tokens + jnp.arange(tokens, dtype=jnp.int32) - query_pos
    block = 4 * tokens
    start = jnp.stack(
        [
            ctx * tokens,
            jnp.maximum(jnp.min(low), 0) // block,
            (ctx * tokens + tokens + block - 1) // block,
        ]
    ).astype(jnp.int32)
    low = low[None]
    mixed, lse, attention_output, middle_state, second_normed = attend(
        start, queries, pairs, low, layer_rows, complete_output, gain_two, gate_up
    )

    normed_pairs = gather_tokens(second_normed)
    flat_normed = [piece for pair in normed_pairs for piece in pair]
    hidden, own, other, parts = feed(
        local_places, flat_normed, all_grads, [kept, other] + gate_up, down
    )
    other = core_swap(other)
    paired = [
        (own[n] + other[n].astype(jnp.float32)).astype(jnp.bfloat16) for n in range(len(STEPS))
    ]
    returned = return_tokens(paired)

    normed_two_grad = sum(piece.astype(jnp.float32) for piece in returned)
    parts = ctx_exchange(parts)

    _, norm_two_pull = jax.vjp(norm_rows, middle_state, gain_two[0])
    middle_part, gain_two_local = norm_two_pull(normed_two_grad)
    middle_grad = out_grad.astype(jnp.float32) + middle_part
    middle_lower = middle_grad.astype(jnp.bfloat16)
    mix_grad = column_product(middle_lower, complete_output).astype(jnp.bfloat16)
    query_back, pair_grad = attend_back(
        start, queries, pairs, low, mix_grad, mixed, lse, cosine, sine
    )
    early = reduce_rows(
        *rows_grads(spot, [(attention_output, middle_lower), (first_normed, query_back)])
    )

    result = feed_out(local_places, down, hidden, [pair_grad])
    result = lax.psum_scatter(result, "wa", scatter_dimension=0)
    pieces = ctx_exchange(pair_grad)
    input_grad, kept, sent = project_back(
        spot,
        layer_rows,
        gain_one,
        full_proj,
        cosine,
        sine,
        first_normed,
        query_back,
        middle_grad,
        gain_two_local[None],
        pieces,
        early[2:],
    )
    late = reduce_rows(kept, sent)

    kept, sent, down_part = owner_parts(spot, parts, tile, pair_grad)
    other = core_swap(sent)
    parts = [
        z_shift(jnp.concatenate([kept[step], other[step]], axis=0), step) for step in STEPS[1:]
    ]
    cuts = [(0, 0, 0), (1, 0, 0)] + [(n, None, part * tile) for n in (2, 3, 4) for part in (0, 1)]
    parts, _ = place_rows(local_places, [kept, other] + parts, cuts, tile)
    parts = lax.all_gather(jnp.concatenate([parts, down_part], axis=0), "ctx", axis=0)
    gate_up_total, down_total = join_columns(parts, rows, slice_width, width)

    mine = ctx_exchange(column_parts(early, late))
    mine = ctx_gather(jnp.sum(mine.astype(jnp.float32), axis=0).astype(jnp.bfloat16))
    result = (middle_state + after(result.astype(jnp.float32), input_grad)).astype(jnp.bfloat16)
    output_total, projection_total, bias, gain_one, gain_two = spread_columns(
        mine, rows, width, bias_rows
    )
    return (
        result[None],
        input_grad[None],
        gain_one.reshape(rows),
        projection_total,
        bias.reshape(bias_rows),
        output_total,
        gain_two.reshape(rows),
        gate_up_total,
        down_total,
    )


def solution(mesh):
    placed = (
        P("wa", "ctx", None),
        P("wa", "ctx"),
        P("wa"),
        P("wa", None),
        P("wa"),
        P("wa", None),
        P("wa"),
        P("wa", None),
        P("wa", None),
        P("wa", "ctx", None),
    )
    return jax.shard_map(
        on_device,
        mesh=mesh,
        in_specs=placed,
        out_specs=(
            P("wa", "ctx", None),
            P("wa", "ctx", None),
            P("wa"),
            P("wa", None),
            P("wa"),
            P("wa", None),
            P("wa"),
            P("wa", None),
            P("wa", None),
        ),
        check_vma=False,
    )
```

```python
import functools

import jax
import jax.numpy as jnp
from jax import lax
from jax.experimental import pallas as pl
from jax.experimental.pallas import tpu as pltpu
from jax.sharding import PartitionSpec as P

QUERY_HEADS = 14
KEY_VALUE_HEADS = 2
HEAD_SIZE = 64
FF = 4864


EPS = 1e-06
THETA = 1000000.0
NEG = -1e30
VMEM = 56 * 2**20


def rows_product(left, right):
    return lax.dot_general(
        left, right, (((0,), (0,)), ((), ())), preferred_element_type=jnp.float32
    )


def column_product(left, right):
    return lax.dot_general(
        left, right, (((1,), (1,)), ((), ())), preferred_element_type=jnp.float32
    )


def norm_rows(value, gain):
    return value * lax.rsqrt(jnp.mean(value * value, axis=-1, keepdims=True) + EPS) * gain


def rotate(tensor, cosine_table, sine_table):
    half = tensor.shape[-1] // 2
    first = tensor[..., :half]
    second = tensor[..., half:]
    return jnp.concatenate(
        [first * cosine_table - second * sine_table, second * cosine_table + first * sine_table],
        axis=-1,
    )


def inverse_rotate(tensor, cosine_table, sine_table):
    half = tensor.shape[-1] // 2
    first = tensor[..., :half]
    second = tensor[..., half:]
    return jnp.concatenate(
        [first * cosine_table + second * sine_table, second * cosine_table - first * sine_table],
        axis=-1,
    )


def angles(positions):
    half = HEAD_SIZE // 2
    inverse = THETA ** (-(jnp.arange(half) * 2.0 / HEAD_SIZE))
    turned = positions.astype(jnp.float32)[:, None] * inverse.astype(jnp.float32)
    return (jnp.cos(turned), jnp.sin(turned))


def busy(microseconds):
    return pl.CostEstimate(
        flops=microseconds * 1150 * 10**6, bytes_accessed=microseconds * 10**6, transcendentals=0
    )


def turn_heads(value, cosine, sine):
    width = value.shape[1]
    lane = lax.broadcasted_iota(jnp.int32, value.shape, 1)
    half = HEAD_SIZE // 2
    partner = jnp.where(
        lane % HEAD_SIZE < half, pltpu.roll(value, width - half, 1), pltpu.roll(value, half, 1)
    )
    repeats = width // cosine.shape[1]
    return value * jnp.tile(cosine, (1, repeats)) + partner * jnp.tile(sine, (1, repeats))


def fetch(pairs, sems):
    copies = [pltpu.make_async_copy(*pair, sems.at[n]) for n, pair in enumerate(pairs)]
    for copy in copies:
        copy.start()
    for copy in copies:
        copy.wait()


def project_kernel(
    packed_ref, x_ref, cos_ref, sin_ref, normed_ref, q_ref, pair_ref, proj_ref, gains_ref, small_ref, sems
):
    count = packed_ref.shape[0]
    rows = proj_ref.shape[0] // count
    fetch(
        [
            (packed_ref.at[n, :rows, :], proj_ref.at[n * rows : (n + 1) * rows, :])
            for n in range(count)
        ]
        + [(packed_ref.at[n, rows:, :], small_ref.at[n]) for n in range(count)],
        sems,
    )
    small = [small_ref[n].astype(jnp.float32)[:1] for n in range(count)]
    bias_rows = proj_ref.shape[1] // count
    bias = jnp.concatenate([row[:, :bias_rows] for row in small], axis=1)
    gains = [
        jnp.concatenate([row[:, first : first + rows] for row in small], axis=1)
        for first in (bias_rows, bias_rows + rows)
    ]
    for n in range(2):
        gains_ref[n] = gains[n]
    x = x_ref[...].astype(jnp.float32)
    scale = lax.rsqrt(jnp.mean(x * x, axis=-1, keepdims=True) + EPS)
    normed = (x * scale * gains[0]).astype(jnp.bfloat16)
    normed_ref[...] = normed
    width = q_ref.shape[1]
    turned = width + KEY_VALUE_HEADS * HEAD_SIZE
    projected = jnp.dot(normed, proj_ref[...], preferred_element_type=jnp.float32) + bias
    rotated = turn_heads(projected[:, :turned], cos_ref[...], sin_ref[...])
    q_ref[...] = rotated[:, :width].astype(jnp.bfloat16)
    pair = jnp.concatenate([rotated[:, width:], projected[:, turned:]], axis=1).astype(jnp.bfloat16)
    pair_ref[...] = pair


def project(packed, x, cosine, sine):
    tokens, width = x.shape
    count, height, proj_width = packed.shape
    return pl.pallas_call(
        project_kernel,
        out_shape=(
            jax.ShapeDtypeStruct((tokens, width), jnp.bfloat16),
            jax.ShapeDtypeStruct((tokens, QUERY_HEADS * HEAD_SIZE), jnp.bfloat16),
            jax.ShapeDtypeStruct((tokens, 2 * KEY_VALUE_HEADS * HEAD_SIZE), jnp.bfloat16),
            jax.ShapeDtypeStruct((width, proj_width), jnp.bfloat16),
            jax.ShapeDtypeStruct((2, 1, width), jnp.float32),
        ),
        in_specs=[pl.BlockSpec(memory_space=pl.ANY)] + [in_vmem()] * 3,
        out_specs=(in_vmem(),) * 5,
        scratch_shapes=[
            pltpu.VMEM((count, height - width // count, proj_width), jnp.bfloat16),
            pltpu.SemaphoreType.DMA((2 * count,)),
        ],
        compiler_params=pltpu.CompilerParams(vmem_limit_bytes=VMEM),
        cost_estimate=busy(4),
        name="project",
    )(packed, x, cosine, sine)


def copies_kernel(value_ref, *refs):
    out_ref, sems = refs[-2:]
    fetch([(value_ref, out_ref.at[n]) for n in range(out_ref.shape[0])], sems)


def copies(value, count, earlier):
    return pl.pallas_call(
        copies_kernel,
        out_shape=jax.ShapeDtypeStruct((count,) + value.shape, value.dtype),
        in_specs=[in_vmem()] + [pl.BlockSpec(memory_space=pl.ANY)] * len(earlier),
        out_specs=pl.BlockSpec(memory_space=pl.ANY),
        scratch_shapes=[pltpu.SemaphoreType.DMA((count,))],
        compiler_params=pltpu.CompilerParams(vmem_limit_bytes=VMEM),
        cost_estimate=busy(2),
        name="copies",
    )(value, *earlier)


def project_back_kernel(
    place_ref, x_in, gain_ref, proj_in, cos_ref, sin_ref, normed_in, dq_in, grad_in, gain_two_ref, pieces_in, *refs
):
    input_grad_ref, kept_ref, sent_ref, stage_ref = refs[-11:-7]
    x_ref, proj_ref, normed_ref, dq_ref, grad_ref, pieces_ref, sems = refs[-7:]
    ins = (x_in, proj_in, normed_in, dq_in, grad_in, pieces_in)
    fetch(list(zip(ins, (x_ref, proj_ref, normed_ref, dq_ref, grad_ref, pieces_ref))), sems)
    z, core = place_ref[0], place_ref[1]
    key_width = KEY_VALUE_HEADS * HEAD_SIZE
    pair = pieces_ref[0].astype(jnp.float32)
    for n in range(1, pieces_ref.shape[0]):
        pair = pair + pieces_ref[n].astype(jnp.float32)
    keys = turn_heads(pair[:, :key_width], cos_ref[...], -sin_ref[...])
    pair = jnp.concatenate([keys, pair[:, key_width:]], axis=1).astype(jnp.bfloat16)
    turned = normed_ref[...].astype(jnp.float32).T.astype(jnp.bfloat16)
    stage_ref[...] = jnp.dot(turned, pair, preferred_element_type=jnp.float32)
    bias = jnp.concatenate(
        [
            jnp.sum(dq_ref[...].astype(jnp.float32), axis=0, keepdims=True),
            jnp.sum(pair.astype(jnp.float32), axis=0, keepdims=True),
        ],
        axis=1,
    )
    x = x_ref[...].astype(jnp.float32)
    scale = lax.rsqrt(jnp.mean(x * x, axis=-1, keepdims=True) + EPS)
    grad = lax.dot_general(
        jnp.concatenate([dq_ref[...], pair], axis=1),
        proj_ref[...],
        (((1,), (1,)), ((), ())),
        preferred_element_type=jnp.float32,
    )
    gain_one = jnp.sum(grad * x * scale, axis=0, keepdims=True)
    gained = grad * gain_ref[...]
    mean = jnp.mean(gained * x, axis=-1, keepdims=True)
    input_grad_ref[...] = grad_ref[...] + scale * gained - x * (scale * scale * scale * mean)

    rows = stage_ref.shape[0] // 8
    bias_rows = bias.shape[1] // 8
    blank = jnp.zeros((kept_ref.shape[1] - rows - 2, stage_ref.shape[1]), jnp.float32)
    for owner in range(8):
        at = lax.rem(owner // 2 - z + 4, 4)
        here = slice(owner * rows, (owner + 1) * rows)
        gain_two = gain_two_ref[:, here]
        first = jnp.concatenate(
            [bias[:, owner * bias_rows : (owner + 1) * bias_rows], gain_one[:, here]], axis=1
        )
        second = jnp.concatenate(
            [gain_two, jnp.zeros((1, stage_ref.shape[1] - rows), jnp.float32)], axis=1
        )
        both = jnp.concatenate([stage_ref[here, :], first, second, blank], axis=0).astype(jnp.bfloat16)

        @pl.when(core == owner % 2)
        def _(both=both, at=at):
            kept_ref[at] = both

        @pl.when(core != owner % 2)
        def _(both=both, at=at):
            sent_ref[at] = both


def project_back(place, x, gain, proj, cosine, sine, normed, dq, grad, gain_two, pieces, earlier):
    tokens, width = x.shape
    pair_width = pieces.shape[2]
    anywhere = pl.BlockSpec(memory_space=pl.ANY)
    out = jax.ShapeDtypeStruct((4, width // 8 + 16, pair_width), jnp.bfloat16)
    return pl.pallas_call(
        project_back_kernel,
        out_shape=(jax.ShapeDtypeStruct((tokens, width), jnp.float32), out, out),
        in_specs=[
            pl.BlockSpec(memory_space=pltpu.SMEM),
            anywhere,
            in_vmem(),
            anywhere,
            in_vmem(),
            in_vmem(),
            anywhere,
            anywhere,
            anywhere,
            in_vmem(),
            anywhere,
        ]
        + [anywhere] * len(earlier),
        out_specs=(in_vmem(),) * 3,
        scratch_shapes=[pltpu.VMEM((width, pair_width), jnp.float32)]
        + [pltpu.VMEM(a.shape, a.dtype) for a in (x, proj, normed, dq, grad, pieces)]
        + [pltpu.SemaphoreType.DMA((6,))],
        compiler_params=pltpu.CompilerParams(vmem_limit_bytes=VMEM),
        cost_estimate=busy(40),
        name="project_back",
    )(place, x, gain, proj, cosine, sine, normed, dq, grad, gain_two, pieces, *earlier)


def key_bias(low_ref, block_start, block, first_index):
    tokens = low_ref.shape[1]
    keys = block_start + lax.broadcasted_iota(jnp.int32, (block, tokens), 0)
    index = first_index + lax.broadcasted_iota(jnp.int32, (block, tokens), 1)
    return jnp.where((keys <= index) & (keys >= low_ref[...]), 0.0, NEG)


def head_places(tokens):
    group = QUERY_HEADS // KEY_VALUE_HEADS
    for h in range(QUERY_HEADS):
        g, i = divmod(h, group)
        yield g, slice(h * HEAD_SIZE, (h + 1) * HEAD_SIZE), slice(i * tokens, (i + 1) * tokens)


def attend_kernel(
    start_ref, q_in, kv_in, low_ref, x_in, out_in, gain_ref, *refs
):
    mixed_ref, lse_ref, attended_ref, middle_ref, normed_ref = refs[-17:-12]
    qt, s_ref, p_ref, bias_ref, m_ref, l_ref, acc_ref = refs[-12:-5]
    q_ref, kv_ref, x_ref, out_ref, sems = refs[-5:]
    pairs = [(q_in, q_ref), (kv_in, kv_ref), (x_in, x_ref), (out_in, out_ref)]
    loads = [pltpu.make_async_copy(*pair, sems.at[n]) for n, pair in enumerate(pairs)]
    for load in loads:
        load.start()
    for load in loads[:2]:
        load.wait()
    tokens = q_ref.shape[0]
    block, rows = s_ref.shape
    turned = (q_ref[...].astype(jnp.float32) * HEAD_SIZE ** (-0.5)).T.astype(jnp.bfloat16)
    for g, lanes, at in head_places(tokens):
        qt[g, :, at] = turned[lanes, :]
    m_ref[...] = jnp.full_like(m_ref, NEG)
    l_ref[...] = jnp.zeros_like(l_ref)
    acc_ref[...] = jnp.zeros_like(acc_ref)

    def visit(which, carry):
        block_start = pl.multiple_of(which * block, block)
        here = pl.ds(block_start, block)
        bias_ref[...] = key_bias(low_ref, block_start, block, start_ref[0])
        key_width = KEY_VALUE_HEADS * HEAD_SIZE
        values = kv_ref[here, key_width:].astype(jnp.float32).T.astype(jnp.bfloat16)
        for g in range(KEY_VALUE_HEADS):
            lanes = slice(g * HEAD_SIZE, (g + 1) * HEAD_SIZE)
            s_ref[...] = jnp.dot(kv_ref[here, lanes], qt[g], preferred_element_type=jnp.float32)
            for i in range(rows // tokens):
                at = slice(i * tokens, (i + 1) * tokens)
                s = s_ref[:, at] + bias_ref[...]
                old = m_ref[g, :, at]
                peak = jnp.maximum(old, jnp.max(s, axis=0, keepdims=True))
                e = jnp.exp(s - peak)
                scale = jnp.exp(old - peak)
                m_ref[g, :, at] = peak
                l_ref[g, :, at] = l_ref[g, :, at] * scale + jnp.sum(e, axis=0, keepdims=True)
                acc_ref[g, :, at] = acc_ref[g, :, at] * scale
                p_ref[:, at] = e.astype(jnp.bfloat16)
            acc_ref[g] += jnp.dot(values[lanes, :], p_ref[...], preferred_element_type=jnp.float32)
        return carry

    lax.fori_loop(start_ref[1], start_ref[2], visit, 0)
    mixed = [acc_ref[g, :, at] / l_ref[g, :, at] for g, _, at in head_places(tokens)]
    mixed = jnp.concatenate(mixed, axis=0).T
    mixed_ref[...] = mixed
    lse_ref[...] = m_ref[...] + jnp.log(l_ref[...])
    attended = mixed.astype(jnp.bfloat16)
    attended_ref[...] = attended
    for load in loads[2:]:
        load.wait()
    middle = x_ref[...].astype(jnp.float32) + jnp.dot(
        attended, out_ref[...], preferred_element_type=jnp.float32
    )
    middle_ref[...] = middle
    scale = lax.rsqrt(jnp.mean(middle * middle, axis=-1, keepdims=True) + EPS)
    normed_ref[...] = (middle * scale * gain_ref[...]).astype(jnp.bfloat16)


def attend_back_kernel(
    start_ref, q_ref, kv_ref, low_ref, dmix_ref, mixed_ref, lse_ref, cos_ref, sin_ref, dq_ref, dkv_ref,
    qs, qt, ms, mt, delta_ref, s_ref, dp_ref, p_ref, g_ref, bias_ref, acc_ref,
):
    tokens = q_ref.shape[0]
    block, rows = s_ref.shape
    key_width = KEY_VALUE_HEADS * HEAD_SIZE
    q = q_ref[...].astype(jnp.float32) * HEAD_SIZE ** (-0.5)
    dmix = dmix_ref[...].astype(jnp.float32)
    q_turned = q.T.astype(jnp.bfloat16)
    dmix_turned = dmix.T
    weighed = (dmix * mixed_ref[...]).T
    q = q.astype(jnp.bfloat16)
    for g, lanes, at in head_places(tokens):
        qs[g, at, :] = q[:, lanes]
        ms[g, at, :] = dmix_ref[:, lanes]
        qt[g, :, at] = q_turned[lanes, :]
        mt[g, :, at] = dmix_turned[lanes, :].astype(jnp.bfloat16)
        delta_ref[g, :, at] = jnp.sum(weighed[lanes, :], axis=0, keepdims=True)
    acc_ref[...] = jnp.zeros_like(acc_ref)
    dkv_ref[...] = jnp.zeros_like(dkv_ref)

    def visit(which, carry):
        block_start = pl.multiple_of(which * block, block)
        here = pl.ds(block_start, block)
        bias_ref[...] = key_bias(low_ref, block_start, block, start_ref[0])
        keys_turned = kv_ref[here, :key_width].astype(jnp.float32).T.astype(jnp.bfloat16)
        grads = [None] * (2 * KEY_VALUE_HEADS)
        for g in range(KEY_VALUE_HEADS):
            lanes = slice(g * HEAD_SIZE, (g + 1) * HEAD_SIZE)
            s_ref[...] = jnp.dot(kv_ref[here, lanes], qt[g], preferred_element_type=jnp.float32)
            values = kv_ref[here, key_width + g * HEAD_SIZE : key_width + (g + 1) * HEAD_SIZE]
            dp_ref[...] = jnp.dot(values, mt[g], preferred_element_type=jnp.float32)
            for i in range(rows // tokens):
                at = slice(i * tokens, (i + 1) * tokens)
                p = jnp.exp(s_ref[:, at] + bias_ref[...] - lse_ref[g, :, at])
                p_ref[:, at] = p.astype(jnp.bfloat16)
                g_ref[:, at] = (p * (dp_ref[:, at] - delta_ref[g, :, at])).astype(jnp.bfloat16)
            acc_ref[g] += jnp.dot(keys_turned[lanes, :], g_ref[...], preferred_element_type=jnp.float32)
            grads[g] = jnp.dot(g_ref[...], qs[g], preferred_element_type=jnp.float32)
            grads[KEY_VALUE_HEADS + g] = jnp.dot(
                p_ref[...], ms[g], preferred_element_type=jnp.float32
            )
        grads = jnp.concatenate(grads, axis=1).astype(jnp.bfloat16)
        for n in range(block // tokens):
            dkv_ref[which * (block // tokens) + n] = grads[n * tokens : (n + 1) * tokens, :]
        return carry

    lax.fori_loop(start_ref[1], start_ref[2], visit, 0)
    dq = [acc_ref[g, :, at] for g, _, at in head_places(tokens)]
    dq = jnp.concatenate(dq, axis=0).T * HEAD_SIZE ** (-0.5)
    dq_ref[...] = turn_heads(dq, cos_ref[...], -sin_ref[...]).astype(jnp.bfloat16)


def in_vmem():
    return pl.BlockSpec(memory_space=pltpu.VMEM)


def attend(start, queries, pairs, low, x, out_matrix, gain, earlier):
    tokens, width = queries.shape
    rows = QUERY_HEADS // KEY_VALUE_HEADS * tokens
    block = 4 * tokens
    heads = KEY_VALUE_HEADS
    return pl.pallas_call(
        attend_kernel,
        out_shape=(
            jax.ShapeDtypeStruct((tokens, width), jnp.float32),
            jax.ShapeDtypeStruct((heads, 1, rows), jnp.float32),
            jax.ShapeDtypeStruct((tokens, width), jnp.bfloat16),
            jax.ShapeDtypeStruct(x.shape, jnp.float32),
            jax.ShapeDtypeStruct(x.shape, jnp.bfloat16),
        ),
        in_specs=[
            pl.BlockSpec(memory_space=pltpu.SMEM),
            pl.BlockSpec(memory_space=pl.ANY),
            pl.BlockSpec(memory_space=pl.ANY),
            in_vmem(),
            pl.BlockSpec(memory_space=pl.ANY),
            pl.BlockSpec(memory_space=pl.ANY),
            in_vmem(),
        ]
        + [pl.BlockSpec(memory_space=pl.ANY)] * len(earlier),
        out_specs=(in_vmem(),) * 5,
        scratch_shapes=[
            pltpu.VMEM((heads, HEAD_SIZE, rows), jnp.bfloat16),
            pltpu.VMEM((block, rows), jnp.float32),
            pltpu.VMEM((block, rows), jnp.bfloat16),
            pltpu.VMEM((block, tokens), jnp.float32),
            pltpu.VMEM((heads, 1, rows), jnp.float32),
            pltpu.VMEM((heads, 1, rows), jnp.float32),
            pltpu.VMEM((heads, HEAD_SIZE, rows), jnp.float32),
            pltpu.VMEM(queries.shape, queries.dtype),
            pltpu.VMEM(pairs.shape, pairs.dtype),
            pltpu.VMEM(x.shape, x.dtype),
            pltpu.VMEM(out_matrix.shape, out_matrix.dtype),
            pltpu.SemaphoreType.DMA((4,)),
        ],
        compiler_params=pltpu.CompilerParams(vmem_limit_bytes=VMEM),
        cost_estimate=busy(9),
        name="attend",
    )(start, queries, pairs, low, x, out_matrix, gain, *earlier)


def attend_back(start, queries, pairs, low, mix_grad, mixed, lse, cosine, sine):
    tokens, width = queries.shape
    rows = QUERY_HEADS // KEY_VALUE_HEADS * tokens
    block = 4 * tokens
    heads = KEY_VALUE_HEADS
    return pl.pallas_call(
        attend_back_kernel,
        out_shape=(
            jax.ShapeDtypeStruct((tokens, width), jnp.bfloat16),
            jax.ShapeDtypeStruct((pairs.shape[0] // tokens, tokens, pairs.shape[1]), jnp.bfloat16),
        ),
        in_specs=[pl.BlockSpec(memory_space=pltpu.SMEM)] + [in_vmem()] * 8,
        out_specs=(in_vmem(), in_vmem()),
        scratch_shapes=[
            pltpu.VMEM((heads, rows, HEAD_SIZE), jnp.bfloat16),
            pltpu.VMEM((heads, HEAD_SIZE, rows), jnp.bfloat16),
            pltpu.VMEM((heads, rows, HEAD_SIZE), jnp.bfloat16),
            pltpu.VMEM((heads, HEAD_SIZE, rows), jnp.bfloat16),
            pltpu.VMEM((heads, 1, rows), jnp.float32),
            pltpu.VMEM((block, rows), jnp.float32),
            pltpu.VMEM((block, rows), jnp.float32),
            pltpu.VMEM((block, rows), jnp.bfloat16),
            pltpu.VMEM((block, rows), jnp.bfloat16),
            pltpu.VMEM((block, tokens), jnp.float32),
            pltpu.VMEM((heads, HEAD_SIZE, rows), jnp.float32),
        ],
        compiler_params=pltpu.CompilerParams(vmem_limit_bytes=VMEM),
        cost_estimate=busy(25),
        name="attend_back",
    )(start, queries, pairs, low, mix_grad, mixed, lse, cosine, sine)


def split_kernel(place_ref, matrix_ref, down_ref, kept_ref, sent_ref, padded_ref):
    padded_ref[: down_ref.shape[0], :] = down_ref[...]
    padded_ref[down_ref.shape[0] :, :] = jnp.zeros(
        (padded_ref.shape[0] - down_ref.shape[0], down_ref.shape[1]), down_ref.dtype
    )
    z, core = place_ref[0], place_ref[1]
    width, lanes = matrix_ref.shape[1] // 16, kept_ref.shape[2] // 2
    for owner in range(8):
        at = lax.rem(owner // 2 - z + 4, 4)
        gate = matrix_ref[:, owner * width : (owner + 1) * width].astype(jnp.float32)
        up = matrix_ref[:, (8 + owner) * width : (9 + owner) * width].astype(jnp.float32)
        blank = jnp.zeros((gate.shape[0], lanes - width), jnp.float32)
        both = jnp.concatenate([gate, blank, up, blank], axis=1).astype(jnp.bfloat16)

        @pl.when(core == owner % 2)
        def _(both=both, at=at):
            kept_ref[at] = both

        @pl.when(core != owner % 2)
        def _(both=both, at=at):
            sent_ref[at] = both


def split_columns(place, matrix, down, lanes):
    rows = matrix.shape[0]
    out = jax.ShapeDtypeStruct((4, rows, 2 * lanes), matrix.dtype)
    return pl.pallas_call(
        split_kernel,
        out_shape=(out, out, jax.ShapeDtypeStruct((lanes, down.shape[1]), down.dtype)),
        in_specs=[pl.BlockSpec(memory_space=pltpu.SMEM), in_vmem(), in_vmem()],
        out_specs=(in_vmem(),) * 3,
        compiler_params=pltpu.CompilerParams(vmem_limit_bytes=VMEM),
        cost_estimate=busy(4),
        name="split_columns",
    )(place, matrix, down)


def place_kernel(cuts, at_ref, *refs):
    pieces, (out_ref, rest_ref, sems, rest_sems) = refs[:-4], refs[-4:]
    rows = out_ref.shape[0] // len(cuts)
    copies = []
    for n, (which, lead, first) in enumerate(cuts):
        piece = pieces[which] if lead is None else pieces[which].at[lead]
        copies.append(
            pltpu.make_async_copy(
                piece.at[first : first + rows, :],
                out_ref.at[pl.ds(pl.multiple_of(at_ref[n] * rows, 16), rows), :],
                sems.at[n],
            )
        )
        if rest_ref.shape[0] == len(cuts):
            copies.append(
                pltpu.make_async_copy(piece.at[rows:, :], rest_ref.at[at_ref[n]], rest_sems.at[n])
            )
    for copy in copies:
        copy.start()
    if rest_ref.shape[0] != len(cuts):
        rest_ref[...] = jnp.zeros_like(rest_ref)
    for copy in copies:
        copy.wait()


def place_rows(at, arrays, cuts, rows, rest=0):
    width, kind = arrays[0].shape[-1], arrays[0].dtype
    count = len(cuts)
    rest_shape = (count, rest, width) if rest else (1, 8, 128)
    return pl.pallas_call(
        functools.partial(place_kernel, tuple(cuts)),
        out_shape=(
            jax.ShapeDtypeStruct((count * rows, width), kind),
            jax.ShapeDtypeStruct(rest_shape, kind if rest else jnp.float32),
        ),
        in_specs=[pl.BlockSpec(memory_space=pltpu.SMEM)]
        + [pl.BlockSpec(memory_space=pl.ANY)] * len(arrays),
        out_specs=(in_vmem(), in_vmem()),
        scratch_shapes=[pltpu.SemaphoreType.DMA((count,)), pltpu.SemaphoreType.DMA((count,))],
        compiler_params=pltpu.CompilerParams(vmem_limit_bytes=VMEM),
        cost_estimate=busy(2),
        name="place_rows",
    )(at, *arrays)


def feed_kernel(at_ref, *refs):
    normed_in, (grads_in, down_in), gate_up_in = refs[:8], refs[8:10], refs[10:15]
    hidden_ref, own_ref, other_ref, out_ref = refs[15:19]
    normed_ref, grads_ref, gate_up_ref, down_ref, joined_ref, turned_ref, stage_ref, sems = refs[19:]
    tokens = normed_in[0].shape[0]
    lanes = hidden_ref.shape[1]
    step = 2 * tokens
    tile = 16
    pairs = [(down_in, down_ref)]
    rows = gate_up_ref.shape[0] // 8
    pieces = [gate_up_in[0].at[0], gate_up_in[1].at[0]]
    pieces += [ref.at[part * rows : (part + 1) * rows, :] for ref in gate_up_in[2:] for part in range(2)]
    for n, piece in enumerate(pieces):
        start = pl.multiple_of(at_ref[n] * rows, 16)
        pairs.append((piece, gate_up_ref.at[pl.ds(start, rows), :]))
    for n in range(8):
        here = slice(n * tokens, (n + 1) * tokens)
        pairs.append((normed_in[n], normed_ref.at[here, :]))
        pairs.append((grads_in.at[at_ref[n]], grads_ref.at[here, :]))
    loads = [pltpu.make_async_copy(*pair, sems.at[n]) for n, pair in enumerate(pairs)]
    for load in loads:
        load.start()
    for load in loads[:9]:
        load.wait()
    for part in range(4):
        for load in loads[9 + 4 * part : 13 + 4 * part]:
            load.wait()
        here = slice(part * step, (part + 1) * step)
        gate = jnp.dot(normed_ref[here, :], gate_up_ref[:, :lanes], preferred_element_type=jnp.float32)
        up = jnp.dot(normed_ref[here, :], gate_up_ref[:, lanes:], preferred_element_type=jnp.float32)
        hidden_grad = lax.dot_general(
            grads_ref[here, :], down_ref[...], (((1,), (1,)), ((), ())), preferred_element_type=jnp.float32
        )
        sg = 1.0 / (1.0 + jnp.exp(-gate))
        act = gate * sg
        hidden_ref[here, :] = (act * up).astype(jnp.bfloat16)
        joined_ref[here, :lanes] = (hidden_grad * up * sg * (1.0 + gate * (1.0 - sg))).astype(
            jnp.bfloat16
        )
        joined_ref[here, lanes:] = (hidden_grad * act).astype(jnp.bfloat16)
        back = lax.dot_general(
            joined_ref[here, :], gate_up_ref[...], (((1,), (1,)), ((), ())), preferred_element_type=jnp.float32
        )
        own_ref[part] = back[:tokens]
        other_ref[part] = back[tokens:].astype(jnp.bfloat16)
        turned_ref[:, here] = normed_ref[here, :].astype(jnp.float32).T.astype(jnp.bfloat16)

    rows = stage_ref.shape[0] // 8
    for half in range(2):
        stage_ref[...] = jnp.dot(
            turned_ref[...],
            joined_ref[:, half * lanes : (half + 1) * lanes],
            preferred_element_type=jnp.float32,
        )
        for r in range(rows // tile):
            for k in range(8):
                first = k * rows + r * tile
                out_ref[2 * r + half, k * tile : (k + 1) * tile, :] = stage_ref[
                    first : first + tile, :
                ].astype(jnp.bfloat16)
    for part in range(2 * rows // tile, 16):
        out_ref[part, : 8 * tile, :] = jnp.zeros((8 * tile, lanes), jnp.bfloat16)
    for part in range(4):
        here = slice(part * step, (part + 1) * step)
        turned_ref[:, here] = grads_ref[here, :].astype(jnp.float32).T.astype(jnp.bfloat16)
    stage_ref[...] = jnp.dot(turned_ref[...], hidden_ref[...], preferred_element_type=jnp.float32)
    rows = stage_ref.shape[0] // 16
    blank = jnp.zeros((out_ref.shape[1] - 8 * tile - rows, lanes), jnp.float32)
    for part in range(16):
        piece = jnp.concatenate([stage_ref[part * rows : (part + 1) * rows, :], blank], axis=0)
        out_ref[part, 8 * tile :, :] = piece.astype(jnp.bfloat16)


def feed(at, normed, grads, gate_up, down):
    tokens, width = normed[0].shape
    lanes = down.shape[0]
    part = 8 * 16 + -(-width // 16 // 16) * 16
    return pl.pallas_call(
        feed_kernel,
        out_shape=(
            jax.ShapeDtypeStruct((8 * tokens, lanes), jnp.bfloat16),
            jax.ShapeDtypeStruct((4, tokens, width), jnp.float32),
            jax.ShapeDtypeStruct((4, tokens, width), jnp.bfloat16),
            jax.ShapeDtypeStruct((16, part, lanes), jnp.bfloat16),
        ),
        in_specs=[pl.BlockSpec(memory_space=pltpu.SMEM)] + [pl.BlockSpec(memory_space=pl.ANY)] * 15,
        out_specs=(in_vmem(),) * 4,
        scratch_shapes=[
            pltpu.VMEM((8 * tokens, width), jnp.bfloat16),
            pltpu.VMEM((8 * tokens, width), jnp.bfloat16),
            pltpu.VMEM((width, 2 * lanes), jnp.bfloat16),
            pltpu.VMEM(down.shape, down.dtype),
            pltpu.VMEM((8 * tokens, 2 * lanes), jnp.bfloat16),
            pltpu.VMEM((width, 8 * tokens), jnp.bfloat16),
            pltpu.VMEM((width, lanes), jnp.float32),
            pltpu.SemaphoreType.DMA((25,)),
        ],
        compiler_params=pltpu.CompilerParams(vmem_limit_bytes=VMEM),
        cost_estimate=busy(18),
        name="feed",
    )(at, *normed, grads, down, *gate_up)


def feed_out_kernel(at_ref, down_ref, *refs):
    hidden, out_ref = refs[0], refs[-1]
    tokens = out_ref.shape[1]
    for n in range(4):
        here = slice(2 * n * tokens, 2 * (n + 1) * tokens)
        out = jnp.dot(hidden[here, :], down_ref[...], preferred_element_type=jnp.float32)
        for part in range(2):
            out_ref[at_ref[2 * n + part]] = out[part * tokens : (part + 1) * tokens].astype(
                jnp.bfloat16
            )


def feed_out(at, down, hidden, earlier):
    tokens = hidden.shape[0] // 8
    return pl.pallas_call(
        feed_out_kernel,
        out_shape=jax.ShapeDtypeStruct((8, tokens, down.shape[1]), jnp.bfloat16),
        in_specs=[pl.BlockSpec(memory_space=pltpu.SMEM)]
        + [in_vmem()] * 2
        + [pl.BlockSpec(memory_space=pl.ANY)] * len(earlier),
        out_specs=in_vmem(),
        compiler_params=pltpu.CompilerParams(vmem_limit_bytes=VMEM),
        cost_estimate=busy(4),
        name="feed_out",
    )(at, down, hidden, *earlier)


def owner_parts_kernel(place_ref, parts_ref, earlier_ref, kept_ref, sent_ref, rest_ref):
    del earlier_ref
    z, core = place_ref[0], place_ref[1]
    rows = kept_ref.shape[1]

    def total(here):
        value = parts_ref[0, here, :].astype(jnp.float32)
        for n in range(1, parts_ref.shape[0]):
            value = value + parts_ref[n, here, :].astype(jnp.float32)
        return value.astype(jnp.bfloat16)

    for owner in range(8):
        at = lax.rem(owner // 2 - z + 4, 4)
        part = total(slice(owner * rows, (owner + 1) * rows))

        @pl.when(core == owner % 2)
        def _(part=part, at=at):
            kept_ref[at] = part

        @pl.when(core != owner % 2)
        def _(part=part, at=at):
            sent_ref[at] = part

    for first in range(0, rest_ref.shape[0], rows):
        rest_ref[first : first + rows, :] = total(slice(8 * rows + first, 9 * rows + first))


def owner_parts(place, parts, rows, earlier):
    _, height, width = parts.shape
    out = jax.ShapeDtypeStruct((4, rows, width), jnp.bfloat16)
    return pl.pallas_call(
        owner_parts_kernel,
        out_shape=(out, out, jax.ShapeDtypeStruct((height - 8 * rows, width), jnp.bfloat16)),
        in_specs=[pl.BlockSpec(memory_space=pltpu.SMEM), in_vmem(), pl.BlockSpec(memory_space=pl.ANY)],
        out_specs=(in_vmem(),) * 3,
        compiler_params=pltpu.CompilerParams(vmem_limit_bytes=VMEM),
        cost_estimate=busy(3),
        name="owner_parts",
    )(place, parts, earlier)


def rows_grads_kernel(place_ref, *refs):
    kept_ref, sent_ref, stage_ref = refs[-3:]
    pairs = (len(refs) - 3) // 2
    rest_ref = refs[2 * pairs] if (len(refs) - 3) % 2 else None
    z, core = place_ref[0], place_ref[1]
    rows = stage_ref.shape[0] // 8
    first = 0
    for n in range(pairs):
        left, right = refs[2 * n], refs[2 * n + 1]
        turned = left[...].astype(jnp.float32).T.astype(jnp.bfloat16)
        stage_ref[:, first : first + right.shape[1]] = jnp.dot(
            turned, right[...], preferred_element_type=jnp.float32
        )
        first += right.shape[1]
    for owner in range(8):
        at = lax.rem(owner // 2 - z + 4, 4)

        @pl.when(core == owner % 2)
        def _(owner=owner, at=at):
            kept_ref[at, :rows, :] = stage_ref[owner * rows : (owner + 1) * rows, :].astype(jnp.bfloat16)
            if rest_ref is not None:
                kept_ref[at, rows:, :] = rest_ref[owner]

        @pl.when(core != owner % 2)
        def _(owner=owner, at=at):
            sent_ref[at, :rows, :] = stage_ref[owner * rows : (owner + 1) * rows, :].astype(jnp.bfloat16)
            if rest_ref is not None:
                sent_ref[at, rows:, :] = rest_ref[owner]


def rows_grads(place, pairs, rest=None):
    height = pairs[0][0].shape[1]
    width = sum(right.shape[1] for _, right in pairs)
    rows = height // 8 + (0 if rest is None else rest.shape[1])
    arrays = [array for pair in pairs for array in pair] + ([] if rest is None else [rest])
    out = jax.ShapeDtypeStruct((4, rows, width), jnp.bfloat16)
    return pl.pallas_call(
        rows_grads_kernel,
        out_shape=(out, out),
        in_specs=[pl.BlockSpec(memory_space=pltpu.SMEM)] + [in_vmem()] * len(arrays),
        out_specs=(in_vmem(), in_vmem()),
        scratch_shapes=[pltpu.VMEM((height, width), jnp.float32)],
        compiler_params=pltpu.CompilerParams(vmem_limit_bytes=VMEM),
        cost_estimate=busy(3),
        name="rows_grads",
    )(place, *arrays)


def join_kernel(parts_ref, gate_up_ref, down_ref, stage_ref):
    width = gate_up_ref.shape[1] // 16
    tile = 16
    for part in range(2 * gate_up_ref.shape[0] // tile):
        r, half = divmod(part, 2)
        columns = [
            parts_ref[part, k * tile : (k + 1) * tile, :].astype(jnp.float32)[:, :width]
            for k in range(8)
        ]
        gate_up_ref[r * tile : (r + 1) * tile, half * 8 * width : (half + 1) * 8 * width] = (
            jnp.concatenate(columns, axis=1)
        )
    rows = stage_ref.shape[0] // 16
    for part in range(16):
        stage_ref[part * rows : (part + 1) * rows, :] = parts_ref[part, 8 * tile :, :].astype(
            jnp.float32
        )[:rows]
    for block in range(stage_ref.shape[0] // 128):
        at = slice(block * 128, (block + 1) * 128)
        down_ref[:, at] = stage_ref[at, :].T[:width]


def join_columns(parts, rows, width, model_width):
    return pl.pallas_call(
        join_kernel,
        out_shape=(
            jax.ShapeDtypeStruct((rows, 16 * width), jnp.float32),
            jax.ShapeDtypeStruct((width, model_width), jnp.float32),
        ),
        in_specs=[in_vmem()],
        out_specs=(in_vmem(), in_vmem()),
        scratch_shapes=[pltpu.VMEM((model_width, parts.shape[2]), jnp.float32)],
        compiler_params=pltpu.CompilerParams(vmem_limit_bytes=VMEM),
        cost_estimate=busy(4),
        name="join_columns",
    )(parts)


def columns_kernel(*refs):
    ins, out_ref, early_ref, late_ref, sems = refs[:10], refs[-4], refs[-3], refs[-2], refs[-1]
    lead_early = [ref.at[0] if len(ref.shape) == 3 else ref for ref in ins[:5]]
    lead_late = [ref.at[0] if len(ref.shape) == 3 else ref for ref in ins[5:]]
    fetch(
        [(ref, early_ref.at[n]) for n, ref in enumerate(lead_early)]
        + [(ref, late_ref.at[n]) for n, ref in enumerate(lead_late)],
        sems,
    )
    _, rows, width = early_ref.shape
    columns = out_ref.shape[2]
    blank = jnp.zeros((out_ref.shape[1] - rows, columns), jnp.float32)
    count = width // columns
    for n in range(out_ref.shape[0]):
        ref = early_ref if n < count else late_ref
        first = (n if n < count else n - count) * columns
        total = ref[0, :, first : first + columns].astype(jnp.float32)
        for m in range(1, 5):
            total = total + ref[m, :, first : first + columns].astype(jnp.float32)
        if n < count:
            total = jnp.concatenate([total, blank], axis=0)
        out_ref[n] = total.astype(jnp.bfloat16)


def column_parts(early, late):
    early_shape, late_shape = early[-1].shape, late[-1].shape
    columns = (early_shape[1] + late_shape[1]) // 16
    return pl.pallas_call(
        columns_kernel,
        out_shape=jax.ShapeDtypeStruct((16, late_shape[0], columns), jnp.bfloat16),
        in_specs=[pl.BlockSpec(memory_space=pl.ANY)] * 10,
        out_specs=in_vmem(),
        scratch_shapes=[
            pltpu.VMEM((5,) + early_shape, jnp.bfloat16),
            pltpu.VMEM((5,) + late_shape, jnp.bfloat16),
            pltpu.SemaphoreType.DMA((10,)),
        ],
        compiler_params=pltpu.CompilerParams(vmem_limit_bytes=VMEM),
        cost_estimate=busy(30),
        name="column_parts",
    )(*early, *late)


def core_swap(value):
    return lax.ppermute(value, "wa", [(i, i ^ 1) for i in range(8)])


def z_shift(value, step):
    return lax.ppermute(value, "wa", [(i, (i + 2 * step) % 8) for i in range(8)])


def ctx_exchange(value):
    return lax.all_to_all(value, "ctx", 0, 0, tiled=True)


def ctx_gather(value):
    return ctx_exchange(jnp.broadcast_to(value[None], (16,) + value.shape))


STEPS = (0, 1, 3, 2)


def gather_tokens(value):
    pieces = [z_shift(value, step) if step else value for step in STEPS]
    return [(piece, core_swap(piece)) for piece in pieces]


def return_tokens(paired):
    return [z_shift(mine, -step) if step else mine for step, mine in zip(STEPS, paired)]


def reduce_rows(kept, sent):
    other = core_swap(sent)
    pieces = [kept, other]
    for step in STEPS[1:]:
        mine = kept[step].astype(jnp.float32) + other[step].astype(jnp.float32)
        pieces.append(z_shift(mine.astype(jnp.bfloat16), step))
    return pieces


def after(value, *others):
    held = sum(other[(0,) * other.ndim].astype(jnp.float32) for other in others) * 0.0
    return value + held.astype(value.dtype)


def spread_kernel(parts_ref, left_ref, right_ref, bias_ref, gain_one_ref, gain_two_ref):
    columns = parts_ref.shape[2]
    rows = left_ref.shape[0]
    count = left_ref.shape[1] // columns
    small = []
    for n in range(parts_ref.shape[0]):
        part = parts_ref[n].astype(jnp.float32)
        if n < count:
            left_ref[:, n * columns : (n + 1) * columns] = part[:rows]
        else:
            right_ref[:, (n - count) * columns : (n - count + 1) * columns] = part[:rows]
        small.append(part[rows : rows + 8])
    small = jnp.concatenate(small[-2:], axis=1)
    bias_rows = bias_ref.shape[1]
    bias_ref[...] = small[:1, :bias_rows]
    gain_one_ref[...] = small[:1, bias_rows : bias_rows + rows]
    gain_two_ref[...] = small[1:2, :rows]


def spread_columns(parts, rows, width, bias_rows):
    count, _, columns = parts.shape
    shapes = [(rows, width), (rows, count * columns - width), (1, bias_rows), (1, rows), (1, rows)]
    return pl.pallas_call(
        spread_kernel,
        out_shape=tuple(jax.ShapeDtypeStruct(shape, jnp.float32) for shape in shapes),
        in_specs=[in_vmem()],
        out_specs=(in_vmem(),) * 5,
        compiler_params=pltpu.CompilerParams(vmem_limit_bytes=VMEM),
        cost_estimate=busy(1),
        name="spread_columns",
    )(parts)


def on_device(
    layer_input,
    positions,
    attention_gain,
    projection,
    projection_biases,
    output_matrix,
    feed_gain,
    gate_up_matrix,
    down_matrix,
    cotangent,
):
    place = lax.axis_index("wa").astype(jnp.int32)
    z, core = place // 2, place % 2
    ctx = lax.axis_index("ctx").astype(jnp.int32)
    rows = projection.shape[0]
    tokens = layer_input.shape[1]
    query_width = QUERY_HEADS * HEAD_SIZE
    key_width = KEY_VALUE_HEADS * HEAD_SIZE
    width = layer_input.shape[2]
    proj_width = projection.shape[1]
    bias_rows = projection_biases.shape[0]
    slice_width = down_matrix.shape[0]
    lanes = -(-slice_width // 128) * 128
    tile = 16
    sources = [(z + 4 - step) % 4 for step in STEPS]

    small = jnp.concatenate([projection_biases, attention_gain, feed_gain])
    small = jnp.pad(small[None], ((0, tile - 1), (0, proj_width - small.shape[0])))
    packed = lax.all_gather(jnp.concatenate([projection, small], axis=0), "wa", axis=0)

    spot = jnp.stack([z, core])
    local_places = jnp.stack([p for s in sources for p in (2 * s + core, 2 * s + 1 - core)])
    kept, sent, down = split_columns(spot, gate_up_matrix, down_matrix, lanes)
    other = core_swap(sent)
    gate_up = [jnp.concatenate([kept[step], other[step]], axis=0) for step in STEPS[1:]]

    layer_rows = layer_input[0]
    query_pos = positions[0]
    cosine, sine = angles(query_pos)
    cosine = jnp.tile(cosine, (1, 4))
    sine = jnp.tile(jnp.concatenate([-sine, sine], axis=1), (1, 2))
    first_normed, queries, pair, full_proj, gains = project(packed, layer_rows, cosine, sine)
    gain_one, gain_two = gains[0], gains[1]
    complete_output = lax.all_gather(output_matrix, "wa", axis=0, tiled=True)
    out_grad = cotangent[0]
    all_grads = lax.all_gather(out_grad, "wa", axis=0)

    pairs_sent = copies(pair, 16, gate_up)
    gate_up = [z_shift(piece, step) for step, piece in zip(STEPS[1:], gate_up)]
    pairs = ctx_exchange(pairs_sent).reshape(16 * tokens, 2 * key_width)
    low = ctx * tokens + jnp.arange(tokens, dtype=jnp.int32) - query_pos
    block = 4 * tokens
    start = jnp.stack(
        [
            ctx * tokens,
            jnp.maximum(jnp.min(low), 0) // block,
            (ctx * tokens + tokens + block - 1) // block,
        ]
    ).astype(jnp.int32)
    low = low[None]
    mixed, lse, attention_output, middle_state, second_normed = attend(
        start, queries, pairs, low, layer_rows, complete_output, gain_two, gate_up[:2]
    )

    normed_pairs = gather_tokens(second_normed)
    flat_normed = [piece for pair in normed_pairs for piece in pair]
    hidden, own, other, parts = feed(
        local_places, flat_normed, all_grads, [kept, other] + gate_up, down
    )
    other = core_swap(other)
    paired = [
        (own[n] + other[n].astype(jnp.float32)).astype(jnp.bfloat16) for n in range(len(STEPS))
    ]
    returned = return_tokens(paired)

    normed_two_grad = sum(piece.astype(jnp.float32) for piece in returned)
    parts = ctx_exchange(parts)

    _, norm_two_pull = jax.vjp(norm_rows, middle_state, gain_two[0])
    middle_part, gain_two_local = norm_two_pull(normed_two_grad)
    middle_grad = out_grad.astype(jnp.float32) + middle_part
    middle_lower = middle_grad.astype(jnp.bfloat16)
    mix_grad = column_product(middle_lower, complete_output).astype(jnp.bfloat16)
    query_back, pair_grad = attend_back(
        start, queries, pairs, low, mix_grad, mixed, lse, cosine, sine
    )
    early = reduce_rows(
        *rows_grads(spot, [(attention_output, middle_lower), (first_normed, query_back)])
    )

    result = feed_out(local_places, down, hidden, [pair_grad])
    result = lax.psum_scatter(result, "wa", scatter_dimension=0)
    pieces = ctx_exchange(pair_grad)
    input_grad, kept, sent = project_back(
        spot,
        layer_rows,
        gain_one,
        full_proj,
        cosine,
        sine,
        first_normed,
        query_back,
        middle_grad,
        gain_two_local[None],
        pieces,
        early[2:],
    )
    late = reduce_rows(kept, sent)

    kept, sent, down_part = owner_parts(spot, parts, tile, pair_grad)
    other = core_swap(sent)
    parts = [
        z_shift(jnp.concatenate([kept[step], other[step]], axis=0), step) for step in STEPS[1:]
    ]
    cuts = [(0, 0, 0), (1, 0, 0)] + [(n, None, part * tile) for n in (2, 3, 4) for part in (0, 1)]
    parts, _ = place_rows(local_places, [kept, other] + parts, cuts, tile)
    parts = lax.all_gather(jnp.concatenate([parts, down_part], axis=0), "ctx", axis=0)
    gate_up_total, down_total = join_columns(parts, rows, slice_width, width)

    mine = ctx_exchange(column_parts(early, late))
    mine = ctx_gather(jnp.sum(mine.astype(jnp.float32), axis=0).astype(jnp.bfloat16))
    result = (middle_state + after(result.astype(jnp.float32), input_grad)).astype(jnp.bfloat16)
    output_total, projection_total, bias, gain_one, gain_two = spread_columns(
        mine, rows, width, bias_rows
    )
    return (
        result[None],
        input_grad[None],
        gain_one.reshape(rows),
        projection_total,
        bias.reshape(bias_rows),
        output_total,
        gain_two.reshape(rows),
        gate_up_total,
        down_total,
    )


def solution(mesh):
    placed = (
        P("wa", "ctx", None),
        P("wa", "ctx"),
        P("wa"),
        P("wa", None),
        P("wa"),
        P("wa", None),
        P("wa"),
        P("wa", None),
        P("wa", None),
        P("wa", "ctx", None),
    )
    return jax.shard_map(
        on_device,
        mesh=mesh,
        in_specs=placed,
        out_specs=(
            P("wa", "ctx", None),
            P("wa", "ctx", None),
            P("wa"),
            P("wa", None),
            P("wa"),
            P("wa", None),
            P("wa"),
            P("wa", None),
            P("wa", None),
        ),
        check_vma=False,
    )
```

```python
import functools

import jax
import jax.numpy as jnp
from jax import lax
from jax.experimental import pallas as pl
from jax.experimental.pallas import tpu as pltpu
from jax.sharding import PartitionSpec as P

QUERY_HEADS = 14
KEY_VALUE_HEADS = 2
HEAD_SIZE = 64
FF = 4864


EPS = 1e-06
THETA = 1000000.0
NEG = -1e30
VMEM = 56 * 2**20


def rows_product(left, right):
    return lax.dot_general(
        left, right, (((0,), (0,)), ((), ())), preferred_element_type=jnp.float32
    )


def column_product(left, right):
    return lax.dot_general(
        left, right, (((1,), (1,)), ((), ())), preferred_element_type=jnp.float32
    )


def norm_rows(value, gain):
    return value * lax.rsqrt(jnp.mean(value * value, axis=-1, keepdims=True) + EPS) * gain


def rotate(tensor, cosine_table, sine_table):
    half = tensor.shape[-1] // 2
    first = tensor[..., :half]
    second = tensor[..., half:]
    return jnp.concatenate(
        [first * cosine_table - second * sine_table, second * cosine_table + first * sine_table],
        axis=-1,
    )


def inverse_rotate(tensor, cosine_table, sine_table):
    half = tensor.shape[-1] // 2
    first = tensor[..., :half]
    second = tensor[..., half:]
    return jnp.concatenate(
        [first * cosine_table + second * sine_table, second * cosine_table - first * sine_table],
        axis=-1,
    )


def angles(positions):
    half = HEAD_SIZE // 2
    inverse = THETA ** (-(jnp.arange(half) * 2.0 / HEAD_SIZE))
    turned = positions.astype(jnp.float32)[:, None] * inverse.astype(jnp.float32)
    return (jnp.cos(turned), jnp.sin(turned))


def busy(microseconds):
    return pl.CostEstimate(
        flops=microseconds * 1150 * 10**6, bytes_accessed=microseconds * 10**6, transcendentals=0
    )


def turn_heads(value, cosine, sine):
    width = value.shape[1]
    lane = lax.broadcasted_iota(jnp.int32, value.shape, 1)
    half = HEAD_SIZE // 2
    partner = jnp.where(
        lane % HEAD_SIZE < half, pltpu.roll(value, width - half, 1), pltpu.roll(value, half, 1)
    )
    repeats = width // cosine.shape[1]
    return value * jnp.tile(cosine, (1, repeats)) + partner * jnp.tile(sine, (1, repeats))


def fetch(pairs, sems):
    copies = [pltpu.make_async_copy(*pair, sems.at[n]) for n, pair in enumerate(pairs)]
    for copy in copies:
        copy.start()
    for copy in copies:
        copy.wait()


def project_kernel(
    packed_ref, x_ref, cos_ref, sin_ref, normed_ref, q_ref, pair_ref, proj_ref, gains_ref, small_ref, sems
):
    count = packed_ref.shape[0]
    rows = proj_ref.shape[0] // count
    fetch(
        [
            (packed_ref.at[n, :rows, :], proj_ref.at[n * rows : (n + 1) * rows, :])
            for n in range(count)
        ]
        + [(packed_ref.at[n, rows:, :], small_ref.at[n]) for n in range(count)],
        sems,
    )
    small = [small_ref[n].astype(jnp.float32)[:1] for n in range(count)]
    bias_rows = proj_ref.shape[1] // count
    bias = jnp.concatenate([row[:, :bias_rows] for row in small], axis=1)
    gains = [
        jnp.concatenate([row[:, first : first + rows] for row in small], axis=1)
        for first in (bias_rows, bias_rows + rows)
    ]
    for n in range(2):
        gains_ref[n] = gains[n]
    x = x_ref[...].astype(jnp.float32)
    scale = lax.rsqrt(jnp.mean(x * x, axis=-1, keepdims=True) + EPS)
    normed = (x * scale * gains[0]).astype(jnp.bfloat16)
    normed_ref[...] = normed
    width = q_ref.shape[1]
    turned = width + KEY_VALUE_HEADS * HEAD_SIZE
    projected = jnp.dot(normed, proj_ref[...], preferred_element_type=jnp.float32) + bias
    rotated = turn_heads(projected[:, :turned], cos_ref[...], sin_ref[...])
    q_ref[...] = rotated[:, :width].astype(jnp.bfloat16)
    pair = jnp.concatenate([rotated[:, width:], projected[:, turned:]], axis=1).astype(jnp.bfloat16)
    pair_ref[...] = pair


def project(packed, x, cosine, sine):
    tokens, width = x.shape
    count, height, proj_width = packed.shape
    return pl.pallas_call(
        project_kernel,
        out_shape=(
            jax.ShapeDtypeStruct((tokens, width), jnp.bfloat16),
            jax.ShapeDtypeStruct((tokens, QUERY_HEADS * HEAD_SIZE), jnp.bfloat16),
            jax.ShapeDtypeStruct((tokens, 2 * KEY_VALUE_HEADS * HEAD_SIZE), jnp.bfloat16),
            jax.ShapeDtypeStruct((width, proj_width), jnp.bfloat16),
            jax.ShapeDtypeStruct((2, 1, width), jnp.float32),
        ),
        in_specs=[pl.BlockSpec(memory_space=pl.ANY)] + [in_vmem()] * 3,
        out_specs=(in_vmem(),) * 5,
        scratch_shapes=[
            pltpu.VMEM((count, height - width // count, proj_width), jnp.bfloat16),
            pltpu.SemaphoreType.DMA((2 * count,)),
        ],
        compiler_params=pltpu.CompilerParams(vmem_limit_bytes=VMEM),
        cost_estimate=busy(4),
        name="project",
    )(packed, x, cosine, sine)


def copies_kernel(value_ref, *refs):
    out_ref, sems = refs[-2:]
    fetch([(value_ref, out_ref.at[n]) for n in range(out_ref.shape[0])], sems)


def copies(value, count, earlier):
    return pl.pallas_call(
        copies_kernel,
        out_shape=jax.ShapeDtypeStruct((count,) + value.shape, value.dtype),
        in_specs=[in_vmem()] + [pl.BlockSpec(memory_space=pl.ANY)] * len(earlier),
        out_specs=pl.BlockSpec(memory_space=pl.ANY),
        scratch_shapes=[pltpu.SemaphoreType.DMA((count,))],
        compiler_params=pltpu.CompilerParams(vmem_limit_bytes=VMEM),
        cost_estimate=busy(2),
        name="copies",
    )(value, *earlier)


def project_back_kernel(
    place_ref, x_in, gain_ref, proj_in, cos_ref, sin_ref, normed_in, dq_in, grad_in, gain_two_ref, pieces_in, *refs
):
    input_grad_ref, kept_ref, sent_ref, stage_ref = refs[-11:-7]
    x_ref, proj_ref, normed_ref, dq_ref, grad_ref, pieces_ref, sems = refs[-7:]
    ins = (x_in, proj_in, normed_in, dq_in, grad_in, pieces_in)
    fetch(list(zip(ins, (x_ref, proj_ref, normed_ref, dq_ref, grad_ref, pieces_ref))), sems)
    z, core = place_ref[0], place_ref[1]
    key_width = KEY_VALUE_HEADS * HEAD_SIZE
    pair = pieces_ref[0].astype(jnp.float32)
    for n in range(1, pieces_ref.shape[0]):
        pair = pair + pieces_ref[n].astype(jnp.float32)
    keys = turn_heads(pair[:, :key_width], cos_ref[...], -sin_ref[...])
    pair = jnp.concatenate([keys, pair[:, key_width:]], axis=1).astype(jnp.bfloat16)
    turned = normed_ref[...].astype(jnp.float32).T.astype(jnp.bfloat16)
    stage_ref[...] = jnp.dot(turned, pair, preferred_element_type=jnp.float32)
    bias = jnp.concatenate(
        [
            jnp.sum(dq_ref[...].astype(jnp.float32), axis=0, keepdims=True),
            jnp.sum(pair.astype(jnp.float32), axis=0, keepdims=True),
        ],
        axis=1,
    )
    x = x_ref[...].astype(jnp.float32)
    scale = lax.rsqrt(jnp.mean(x * x, axis=-1, keepdims=True) + EPS)
    grad = lax.dot_general(
        jnp.concatenate([dq_ref[...], pair], axis=1),
        proj_ref[...],
        (((1,), (1,)), ((), ())),
        preferred_element_type=jnp.float32,
    )
    gain_one = jnp.sum(grad * x * scale, axis=0, keepdims=True)
    gained = grad * gain_ref[...]
    mean = jnp.mean(gained * x, axis=-1, keepdims=True)
    input_grad_ref[...] = grad_ref[...] + scale * gained - x * (scale * scale * scale * mean)

    rows = stage_ref.shape[0] // 8
    bias_rows = bias.shape[1] // 8
    blank = jnp.zeros((kept_ref.shape[1] - rows - 2, stage_ref.shape[1]), jnp.float32)
    for owner in range(8):
        at = lax.rem(owner // 2 - z + 4, 4)
        here = slice(owner * rows, (owner + 1) * rows)
        gain_two = gain_two_ref[:, here]
        first = jnp.concatenate(
            [bias[:, owner * bias_rows : (owner + 1) * bias_rows], gain_one[:, here]], axis=1
        )
        second = jnp.concatenate(
            [gain_two, jnp.zeros((1, stage_ref.shape[1] - rows), jnp.float32)], axis=1
        )
        both = jnp.concatenate([stage_ref[here, :], first, second, blank], axis=0).astype(jnp.bfloat16)

        @pl.when(core == owner % 2)
        def _(both=both, at=at):
            kept_ref[at] = both

        @pl.when(core != owner % 2)
        def _(both=both, at=at):
            sent_ref[at] = both


def project_back(place, x, gain, proj, cosine, sine, normed, dq, grad, gain_two, pieces, earlier):
    tokens, width = x.shape
    pair_width = pieces.shape[2]
    anywhere = pl.BlockSpec(memory_space=pl.ANY)
    out = jax.ShapeDtypeStruct((4, width // 8 + 16, pair_width), jnp.bfloat16)
    return pl.pallas_call(
        project_back_kernel,
        out_shape=(jax.ShapeDtypeStruct((tokens, width), jnp.float32), out, out),
        in_specs=[
            pl.BlockSpec(memory_space=pltpu.SMEM),
            anywhere,
            in_vmem(),
            anywhere,
            in_vmem(),
            in_vmem(),
            anywhere,
            anywhere,
            anywhere,
            in_vmem(),
            anywhere,
        ]
        + [anywhere] * len(earlier),
        out_specs=(in_vmem(),) * 3,
        scratch_shapes=[pltpu.VMEM((width, pair_width), jnp.float32)]
        + [pltpu.VMEM(a.shape, a.dtype) for a in (x, proj, normed, dq, grad, pieces)]
        + [pltpu.SemaphoreType.DMA((6,))],
        compiler_params=pltpu.CompilerParams(vmem_limit_bytes=VMEM),
        cost_estimate=busy(40),
        name="project_back",
    )(place, x, gain, proj, cosine, sine, normed, dq, grad, gain_two, pieces, *earlier)


def key_bias(low_ref, block_start, block, first_index):
    tokens = low_ref.shape[1]
    keys = block_start + lax.broadcasted_iota(jnp.int32, (block, tokens), 0)
    index = first_index + lax.broadcasted_iota(jnp.int32, (block, tokens), 1)
    return jnp.where((keys <= index) & (keys >= low_ref[...]), 0.0, NEG)


def head_places(tokens):
    group = QUERY_HEADS // KEY_VALUE_HEADS
    for h in range(QUERY_HEADS):
        g, i = divmod(h, group)
        yield g, slice(h * HEAD_SIZE, (h + 1) * HEAD_SIZE), slice(i * tokens, (i + 1) * tokens)


def attend_kernel(
    start_ref, q_in, kv_in, low_ref, x_in, out_in, gain_ref, *refs
):
    mixed_ref, lse_ref, attended_ref, middle_ref, normed_ref = refs[-17:-12]
    qt, s_ref, p_ref, bias_ref, m_ref, l_ref, acc_ref = refs[-12:-5]
    q_ref, kv_ref, x_ref, out_ref, sems = refs[-5:]
    pairs = [(q_in, q_ref), (kv_in, kv_ref), (x_in, x_ref), (out_in, out_ref)]
    loads = [pltpu.make_async_copy(*pair, sems.at[n]) for n, pair in enumerate(pairs)]
    for load in loads:
        load.start()
    for load in loads[:2]:
        load.wait()
    tokens = q_ref.shape[0]
    block, rows = s_ref.shape
    turned = (q_ref[...].astype(jnp.float32) * HEAD_SIZE ** (-0.5)).T.astype(jnp.bfloat16)
    for g, lanes, at in head_places(tokens):
        qt[g, :, at] = turned[lanes, :]
    m_ref[...] = jnp.full_like(m_ref, NEG)
    l_ref[...] = jnp.zeros_like(l_ref)
    acc_ref[...] = jnp.zeros_like(acc_ref)

    def visit(which, carry):
        block_start = pl.multiple_of(which * block, block)
        here = pl.ds(block_start, block)
        bias_ref[...] = key_bias(low_ref, block_start, block, start_ref[0])
        key_width = KEY_VALUE_HEADS * HEAD_SIZE
        values = kv_ref[here, key_width:].astype(jnp.float32).T.astype(jnp.bfloat16)
        for g in range(KEY_VALUE_HEADS):
            lanes = slice(g * HEAD_SIZE, (g + 1) * HEAD_SIZE)
            s_ref[...] = jnp.dot(kv_ref[here, lanes], qt[g], preferred_element_type=jnp.float32)
            for i in range(rows // tokens):
                at = slice(i * tokens, (i + 1) * tokens)
                s = s_ref[:, at] + bias_ref[...]
                old = m_ref[g, :, at]
                peak = jnp.maximum(old, jnp.max(s, axis=0, keepdims=True))
                e = jnp.exp(s - peak)
                scale = jnp.exp(old - peak)
                m_ref[g, :, at] = peak
                l_ref[g, :, at] = l_ref[g, :, at] * scale + jnp.sum(e, axis=0, keepdims=True)
                acc_ref[g, :, at] = acc_ref[g, :, at] * scale
                p_ref[:, at] = e.astype(jnp.bfloat16)
            acc_ref[g] += jnp.dot(values[lanes, :], p_ref[...], preferred_element_type=jnp.float32)
        return carry

    lax.fori_loop(start_ref[1], start_ref[2], visit, 0)
    mixed = [acc_ref[g, :, at] / l_ref[g, :, at] for g, _, at in head_places(tokens)]
    mixed = jnp.concatenate(mixed, axis=0).T
    mixed_ref[...] = mixed
    lse_ref[...] = m_ref[...] + jnp.log(l_ref[...])
    attended = mixed.astype(jnp.bfloat16)
    attended_ref[...] = attended
    for load in loads[2:]:
        load.wait()
    middle = x_ref[...].astype(jnp.float32) + jnp.dot(
        attended, out_ref[...], preferred_element_type=jnp.float32
    )
    middle_ref[...] = middle
    scale = lax.rsqrt(jnp.mean(middle * middle, axis=-1, keepdims=True) + EPS)
    normed_ref[...] = (middle * scale * gain_ref[...]).astype(jnp.bfloat16)


def attend_back_kernel(
    start_ref, q_ref, kv_ref, low_ref, dmix_ref, mixed_ref, lse_ref, cos_ref, sin_ref, dq_ref, dkv_ref,
    qs, qt, ms, mt, delta_ref, s_ref, dp_ref, p_ref, g_ref, bias_ref, acc_ref,
):
    tokens = q_ref.shape[0]
    block, rows = s_ref.shape
    key_width = KEY_VALUE_HEADS * HEAD_SIZE
    q = q_ref[...].astype(jnp.float32) * HEAD_SIZE ** (-0.5)
    dmix = dmix_ref[...].astype(jnp.float32)
    q_turned = q.T.astype(jnp.bfloat16)
    dmix_turned = dmix.T
    weighed = (dmix * mixed_ref[...]).T
    q = q.astype(jnp.bfloat16)
    for g, lanes, at in head_places(tokens):
        qs[g, at, :] = q[:, lanes]
        ms[g, at, :] = dmix_ref[:, lanes]
        qt[g, :, at] = q_turned[lanes, :]
        mt[g, :, at] = dmix_turned[lanes, :].astype(jnp.bfloat16)
        delta_ref[g, :, at] = jnp.sum(weighed[lanes, :], axis=0, keepdims=True)
    acc_ref[...] = jnp.zeros_like(acc_ref)
    dkv_ref[...] = jnp.zeros_like(dkv_ref)

    def visit(which, carry):
        block_start = pl.multiple_of(which * block, block)
        here = pl.ds(block_start, block)
        bias_ref[...] = key_bias(low_ref, block_start, block, start_ref[0])
        keys_turned = kv_ref[here, :key_width].astype(jnp.float32).T.astype(jnp.bfloat16)
        grads = [None] * (2 * KEY_VALUE_HEADS)
        for g in range(KEY_VALUE_HEADS):
            lanes = slice(g * HEAD_SIZE, (g + 1) * HEAD_SIZE)
            s_ref[...] = jnp.dot(kv_ref[here, lanes], qt[g], preferred_element_type=jnp.float32)
            values = kv_ref[here, key_width + g * HEAD_SIZE : key_width + (g + 1) * HEAD_SIZE]
            dp_ref[...] = jnp.dot(values, mt[g], preferred_element_type=jnp.float32)
            for i in range(rows // tokens):
                at = slice(i * tokens, (i + 1) * tokens)
                p = jnp.exp(s_ref[:, at] + bias_ref[...] - lse_ref[g, :, at])
                p_ref[:, at] = p.astype(jnp.bfloat16)
                g_ref[:, at] = (p * (dp_ref[:, at] - delta_ref[g, :, at])).astype(jnp.bfloat16)
            acc_ref[g] += jnp.dot(keys_turned[lanes, :], g_ref[...], preferred_element_type=jnp.float32)
            grads[g] = jnp.dot(g_ref[...], qs[g], preferred_element_type=jnp.float32)
            grads[KEY_VALUE_HEADS + g] = jnp.dot(
                p_ref[...], ms[g], preferred_element_type=jnp.float32
            )
        grads = jnp.concatenate(grads, axis=1).astype(jnp.bfloat16)
        for n in range(block // tokens):
            dkv_ref[which * (block // tokens) + n] = grads[n * tokens : (n + 1) * tokens, :]
        return carry

    lax.fori_loop(start_ref[1], start_ref[2], visit, 0)
    dq = [acc_ref[g, :, at] for g, _, at in head_places(tokens)]
    dq = jnp.concatenate(dq, axis=0).T * HEAD_SIZE ** (-0.5)
    dq_ref[...] = turn_heads(dq, cos_ref[...], -sin_ref[...]).astype(jnp.bfloat16)


def in_vmem():
    return pl.BlockSpec(memory_space=pltpu.VMEM)


def attend(start, queries, pairs, low, x, out_matrix, gain, earlier):
    tokens, width = queries.shape
    rows = QUERY_HEADS // KEY_VALUE_HEADS * tokens
    block = 4 * tokens
    heads = KEY_VALUE_HEADS
    return pl.pallas_call(
        attend_kernel,
        out_shape=(
            jax.ShapeDtypeStruct((tokens, width), jnp.float32),
            jax.ShapeDtypeStruct((heads, 1, rows), jnp.float32),
            jax.ShapeDtypeStruct((tokens, width), jnp.bfloat16),
            jax.ShapeDtypeStruct(x.shape, jnp.float32),
            jax.ShapeDtypeStruct(x.shape, jnp.bfloat16),
        ),
        in_specs=[
            pl.BlockSpec(memory_space=pltpu.SMEM),
            pl.BlockSpec(memory_space=pl.ANY),
            pl.BlockSpec(memory_space=pl.ANY),
            in_vmem(),
            pl.BlockSpec(memory_space=pl.ANY),
            pl.BlockSpec(memory_space=pl.ANY),
            in_vmem(),
        ]
        + [pl.BlockSpec(memory_space=pl.ANY)] * len(earlier),
        out_specs=(in_vmem(),) * 5,
        scratch_shapes=[
            pltpu.VMEM((heads, HEAD_SIZE, rows), jnp.bfloat16),
            pltpu.VMEM((block, rows), jnp.float32),
            pltpu.VMEM((block, rows), jnp.bfloat16),
            pltpu.VMEM((block, tokens), jnp.float32),
            pltpu.VMEM((heads, 1, rows), jnp.float32),
            pltpu.VMEM((heads, 1, rows), jnp.float32),
            pltpu.VMEM((heads, HEAD_SIZE, rows), jnp.float32),
            pltpu.VMEM(queries.shape, queries.dtype),
            pltpu.VMEM(pairs.shape, pairs.dtype),
            pltpu.VMEM(x.shape, x.dtype),
            pltpu.VMEM(out_matrix.shape, out_matrix.dtype),
            pltpu.SemaphoreType.DMA((4,)),
        ],
        compiler_params=pltpu.CompilerParams(vmem_limit_bytes=VMEM),
        cost_estimate=busy(9),
        name="attend",
    )(start, queries, pairs, low, x, out_matrix, gain, *earlier)


def attend_back(start, queries, pairs, low, mix_grad, mixed, lse, cosine, sine):
    tokens, width = queries.shape
    rows = QUERY_HEADS // KEY_VALUE_HEADS * tokens
    block = 4 * tokens
    heads = KEY_VALUE_HEADS
    return pl.pallas_call(
        attend_back_kernel,
        out_shape=(
            jax.ShapeDtypeStruct((tokens, width), jnp.bfloat16),
            jax.ShapeDtypeStruct((pairs.shape[0] // tokens, tokens, pairs.shape[1]), jnp.bfloat16),
        ),
        in_specs=[pl.BlockSpec(memory_space=pltpu.SMEM)] + [in_vmem()] * 8,
        out_specs=(in_vmem(), in_vmem()),
        scratch_shapes=[
            pltpu.VMEM((heads, rows, HEAD_SIZE), jnp.bfloat16),
            pltpu.VMEM((heads, HEAD_SIZE, rows), jnp.bfloat16),
            pltpu.VMEM((heads, rows, HEAD_SIZE), jnp.bfloat16),
            pltpu.VMEM((heads, HEAD_SIZE, rows), jnp.bfloat16),
            pltpu.VMEM((heads, 1, rows), jnp.float32),
            pltpu.VMEM((block, rows), jnp.float32),
            pltpu.VMEM((block, rows), jnp.float32),
            pltpu.VMEM((block, rows), jnp.bfloat16),
            pltpu.VMEM((block, rows), jnp.bfloat16),
            pltpu.VMEM((block, tokens), jnp.float32),
            pltpu.VMEM((heads, HEAD_SIZE, rows), jnp.float32),
        ],
        compiler_params=pltpu.CompilerParams(vmem_limit_bytes=VMEM),
        cost_estimate=busy(25),
        name="attend_back",
    )(start, queries, pairs, low, mix_grad, mixed, lse, cosine, sine)


def split_kernel(place_ref, matrix_ref, down_ref, kept_ref, sent_ref, padded_ref):
    padded_ref[: down_ref.shape[0], :] = down_ref[...]
    padded_ref[down_ref.shape[0] :, :] = jnp.zeros(
        (padded_ref.shape[0] - down_ref.shape[0], down_ref.shape[1]), down_ref.dtype
    )
    z, core = place_ref[0], place_ref[1]
    width, lanes = matrix_ref.shape[1] // 16, kept_ref.shape[2] // 2
    for owner in range(8):
        at = lax.rem(owner // 2 - z + 4, 4)
        gate = matrix_ref[:, owner * width : (owner + 1) * width].astype(jnp.float32)
        up = matrix_ref[:, (8 + owner) * width : (9 + owner) * width].astype(jnp.float32)
        blank = jnp.zeros((gate.shape[0], lanes - width), jnp.float32)
        both = jnp.concatenate([gate, blank, up, blank], axis=1).astype(jnp.bfloat16)

        @pl.when(core == owner % 2)
        def _(both=both, at=at):
            kept_ref[at] = both

        @pl.when(core != owner % 2)
        def _(both=both, at=at):
            sent_ref[at] = both


def split_columns(place, matrix, down, lanes):
    rows = matrix.shape[0]
    out = jax.ShapeDtypeStruct((4, rows, 2 * lanes), matrix.dtype)
    return pl.pallas_call(
        split_kernel,
        out_shape=(out, out, jax.ShapeDtypeStruct((lanes, down.shape[1]), down.dtype)),
        in_specs=[pl.BlockSpec(memory_space=pltpu.SMEM), in_vmem(), in_vmem()],
        out_specs=(in_vmem(),) * 3,
        compiler_params=pltpu.CompilerParams(vmem_limit_bytes=VMEM),
        cost_estimate=busy(4),
        name="split_columns",
    )(place, matrix, down)


def place_kernel(cuts, at_ref, *refs):
    pieces, (out_ref, rest_ref, sems, rest_sems) = refs[:-4], refs[-4:]
    rows = out_ref.shape[0] // len(cuts)
    copies = []
    for n, (which, lead, first) in enumerate(cuts):
        piece = pieces[which] if lead is None else pieces[which].at[lead]
        copies.append(
            pltpu.make_async_copy(
                piece.at[first : first + rows, :],
                out_ref.at[pl.ds(pl.multiple_of(at_ref[n] * rows, 16), rows), :],
                sems.at[n],
            )
        )
        if rest_ref.shape[0] == len(cuts):
            copies.append(
                pltpu.make_async_copy(piece.at[rows:, :], rest_ref.at[at_ref[n]], rest_sems.at[n])
            )
    for copy in copies:
        copy.start()
    if rest_ref.shape[0] != len(cuts):
        rest_ref[...] = jnp.zeros_like(rest_ref)
    for copy in copies:
        copy.wait()


def place_rows(at, arrays, cuts, rows, rest=0):
    width, kind = arrays[0].shape[-1], arrays[0].dtype
    count = len(cuts)
    rest_shape = (count, rest, width) if rest else (1, 8, 128)
    return pl.pallas_call(
        functools.partial(place_kernel, tuple(cuts)),
        out_shape=(
            jax.ShapeDtypeStruct((count * rows, width), kind),
            jax.ShapeDtypeStruct(rest_shape, kind if rest else jnp.float32),
        ),
        in_specs=[pl.BlockSpec(memory_space=pltpu.SMEM)]
        + [pl.BlockSpec(memory_space=pl.ANY)] * len(arrays),
        out_specs=(in_vmem(), in_vmem()),
        scratch_shapes=[pltpu.SemaphoreType.DMA((count,)), pltpu.SemaphoreType.DMA((count,))],
        compiler_params=pltpu.CompilerParams(vmem_limit_bytes=VMEM),
        cost_estimate=busy(2),
        name="place_rows",
    )(at, *arrays)


def down_places(width, row_tiles):
    full, tile = 2 * row_tiles, 16
    extra = -(-width // 16 // tile) * tile - tile
    rest = (width - full * extra) // (16 - full)
    for part in range(full):
        yield part, 8 * tile, extra, part * extra
    for part in range(full, 16):
        yield part, 0, rest, full * extra + (part - full) * rest


def feed_kernel(at_ref, *refs):
    normed_in, (grads_in, down_in), gate_up_in = refs[:8], refs[8:10], refs[10:15]
    hidden_ref, own_ref, other_ref, out_ref = refs[15:19]
    normed_ref, grads_ref, gate_up_ref, down_ref, joined_ref, turned_ref, stage_ref, sems = refs[19:]
    tokens = normed_in[0].shape[0]
    lanes = hidden_ref.shape[1]
    step = 2 * tokens
    tile = 16
    pairs = [(down_in, down_ref)]
    rows = gate_up_ref.shape[0] // 8
    pieces = [gate_up_in[0].at[0], gate_up_in[1].at[0]]
    pieces += [ref.at[part * rows : (part + 1) * rows, :] for ref in gate_up_in[2:] for part in range(2)]
    for n, piece in enumerate(pieces):
        start = pl.multiple_of(at_ref[n] * rows, 16)
        pairs.append((piece, gate_up_ref.at[pl.ds(start, rows), :]))
    for n in range(8):
        here = slice(n * tokens, (n + 1) * tokens)
        pairs.append((normed_in[n], normed_ref.at[here, :]))
        pairs.append((grads_in.at[at_ref[n]], grads_ref.at[here, :]))
    loads = [pltpu.make_async_copy(*pair, sems.at[n]) for n, pair in enumerate(pairs)]
    for load in loads:
        load.start()
    for load in loads[:9]:
        load.wait()
    for part in range(4):
        for load in loads[9 + 4 * part : 13 + 4 * part]:
            load.wait()
        here = slice(part * step, (part + 1) * step)
        gate = jnp.dot(normed_ref[here, :], gate_up_ref[:, :lanes], preferred_element_type=jnp.float32)
        up = jnp.dot(normed_ref[here, :], gate_up_ref[:, lanes:], preferred_element_type=jnp.float32)
        hidden_grad = lax.dot_general(
            grads_ref[here, :], down_ref[...], (((1,), (1,)), ((), ())), preferred_element_type=jnp.float32
        )
        sg = 1.0 / (1.0 + jnp.exp(-gate))
        act = gate * sg
        hidden_ref[here, :] = (act * up).astype(jnp.bfloat16)
        joined_ref[here, :lanes] = (hidden_grad * up * sg * (1.0 + gate * (1.0 - sg))).astype(
            jnp.bfloat16
        )
        joined_ref[here, lanes:] = (hidden_grad * act).astype(jnp.bfloat16)
        back = lax.dot_general(
            joined_ref[here, :], gate_up_ref[...], (((1,), (1,)), ((), ())), preferred_element_type=jnp.float32
        )
        own_ref[part] = back[:tokens]
        other_ref[part] = back[tokens:].astype(jnp.bfloat16)
        turned_ref[:, here] = normed_ref[here, :].astype(jnp.float32).T.astype(jnp.bfloat16)

    rows = stage_ref.shape[0] // 8
    for half in range(2):
        stage_ref[...] = jnp.dot(
            turned_ref[...],
            joined_ref[:, half * lanes : (half + 1) * lanes],
            preferred_element_type=jnp.float32,
        )
        for r in range(rows // tile):
            for k in range(8):
                first = k * rows + r * tile
                out_ref[2 * r + half, k * tile : (k + 1) * tile, :] = stage_ref[
                    first : first + tile, :
                ].astype(jnp.bfloat16)
    for part in range(4):
        here = slice(part * step, (part + 1) * step)
        turned_ref[:, here] = grads_ref[here, :].astype(jnp.float32).T.astype(jnp.bfloat16)
    stage_ref[...] = jnp.dot(turned_ref[...], hidden_ref[...], preferred_element_type=jnp.float32)
    for part, first, height, source in down_places(stage_ref.shape[0], rows // tile):
        out_ref[part, first : first + height, :] = stage_ref[source : source + height, :].astype(
            jnp.bfloat16
        )
        if first == 0:
            out_ref[part, height:, :] = jnp.zeros((out_ref.shape[1] - height, lanes), jnp.bfloat16)


def feed(at, normed, grads, gate_up, down):
    tokens, width = normed[0].shape
    lanes = down.shape[0]
    part = 8 * 16 + -(-width // 16 // 16) * 16 - 16
    return pl.pallas_call(
        feed_kernel,
        out_shape=(
            jax.ShapeDtypeStruct((8 * tokens, lanes), jnp.bfloat16),
            jax.ShapeDtypeStruct((4, tokens, width), jnp.float32),
            jax.ShapeDtypeStruct((4, tokens, width), jnp.bfloat16),
            jax.ShapeDtypeStruct((16, part, lanes), jnp.bfloat16),
        ),
        in_specs=[pl.BlockSpec(memory_space=pltpu.SMEM)] + [pl.BlockSpec(memory_space=pl.ANY)] * 15,
        out_specs=(in_vmem(),) * 4,
        scratch_shapes=[
            pltpu.VMEM((8 * tokens, width), jnp.bfloat16),
            pltpu.VMEM((8 * tokens, width), jnp.bfloat16),
            pltpu.VMEM((width, 2 * lanes), jnp.bfloat16),
            pltpu.VMEM(down.shape, down.dtype),
            pltpu.VMEM((8 * tokens, 2 * lanes), jnp.bfloat16),
            pltpu.VMEM((width, 8 * tokens), jnp.bfloat16),
            pltpu.VMEM((width, lanes), jnp.float32),
            pltpu.SemaphoreType.DMA((25,)),
        ],
        compiler_params=pltpu.CompilerParams(vmem_limit_bytes=VMEM),
        cost_estimate=busy(18),
        name="feed",
    )(at, *normed, grads, down, *gate_up)


def feed_out_kernel(at_ref, down_ref, *refs):
    hidden, out_ref = refs[0], refs[-1]
    tokens = out_ref.shape[1]
    for n in range(4):
        here = slice(2 * n * tokens, 2 * (n + 1) * tokens)
        out = jnp.dot(hidden[here, :], down_ref[...], preferred_element_type=jnp.float32)
        for part in range(2):
            out_ref[at_ref[2 * n + part]] = out[part * tokens : (part + 1) * tokens].astype(
                jnp.bfloat16
            )


def feed_out(at, down, hidden, earlier):
    tokens = hidden.shape[0] // 8
    return pl.pallas_call(
        feed_out_kernel,
        out_shape=jax.ShapeDtypeStruct((8, tokens, down.shape[1]), jnp.bfloat16),
        in_specs=[pl.BlockSpec(memory_space=pltpu.SMEM)]
        + [in_vmem()] * 2
        + [pl.BlockSpec(memory_space=pl.ANY)] * len(earlier),
        out_specs=in_vmem(),
        compiler_params=pltpu.CompilerParams(vmem_limit_bytes=VMEM),
        cost_estimate=busy(4),
        name="feed_out",
    )(at, down, hidden, *earlier)


def owner_parts_kernel(place_ref, parts_ref, earlier_ref, kept_ref, sent_ref, whole_ref):
    del earlier_ref
    z, core = place_ref[0], place_ref[1]
    rows = kept_ref.shape[1]

    def total(here):
        value = parts_ref[0, here, :].astype(jnp.float32)
        for n in range(1, parts_ref.shape[0]):
            value = value + parts_ref[n, here, :].astype(jnp.float32)
        return value.astype(jnp.bfloat16)

    for owner in range(8):
        at = lax.rem(owner // 2 - z + 4, 4)
        part = total(slice(owner * rows, (owner + 1) * rows))
        whole_ref[owner * rows : (owner + 1) * rows, :] = part

        @pl.when(core == owner % 2)
        def _(part=part, at=at):
            kept_ref[at] = part

        @pl.when(core != owner % 2)
        def _(part=part, at=at):
            sent_ref[at] = part

    for first in range(8 * rows, whole_ref.shape[0], rows):
        whole_ref[first : first + rows, :] = total(slice(first, first + rows))


def owner_parts(place, parts, rows, earlier):
    _, height, width = parts.shape
    out = jax.ShapeDtypeStruct((4, rows, width), jnp.bfloat16)
    return pl.pallas_call(
        owner_parts_kernel,
        out_shape=(out, out, jax.ShapeDtypeStruct((height, width), jnp.bfloat16)),
        in_specs=[pl.BlockSpec(memory_space=pltpu.SMEM), in_vmem(), pl.BlockSpec(memory_space=pl.ANY)],
        out_specs=(in_vmem(),) * 3,
        compiler_params=pltpu.CompilerParams(vmem_limit_bytes=VMEM),
        cost_estimate=busy(3),
        name="owner_parts",
    )(place, parts, earlier)


def rows_grads_kernel(place_ref, *refs):
    kept_ref, sent_ref, stage_ref = refs[-3:]
    pairs = (len(refs) - 3) // 2
    rest_ref = refs[2 * pairs] if (len(refs) - 3) % 2 else None
    z, core = place_ref[0], place_ref[1]
    rows = stage_ref.shape[0] // 8
    first = 0
    for n in range(pairs):
        left, right = refs[2 * n], refs[2 * n + 1]
        turned = left[...].astype(jnp.float32).T.astype(jnp.bfloat16)
        stage_ref[:, first : first + right.shape[1]] = jnp.dot(
            turned, right[...], preferred_element_type=jnp.float32
        )
        first += right.shape[1]
    for owner in range(8):
        at = lax.rem(owner // 2 - z + 4, 4)

        @pl.when(core == owner % 2)
        def _(owner=owner, at=at):
            kept_ref[at, :rows, :] = stage_ref[owner * rows : (owner + 1) * rows, :].astype(jnp.bfloat16)
            if rest_ref is not None:
                kept_ref[at, rows:, :] = rest_ref[owner]

        @pl.when(core != owner % 2)
        def _(owner=owner, at=at):
            sent_ref[at, :rows, :] = stage_ref[owner * rows : (owner + 1) * rows, :].astype(jnp.bfloat16)
            if rest_ref is not None:
                sent_ref[at, rows:, :] = rest_ref[owner]


def rows_grads(place, pairs, rest=None):
    height = pairs[0][0].shape[1]
    width = sum(right.shape[1] for _, right in pairs)
    rows = height // 8 + (0 if rest is None else rest.shape[1])
    arrays = [array for pair in pairs for array in pair] + ([] if rest is None else [rest])
    out = jax.ShapeDtypeStruct((4, rows, width), jnp.bfloat16)
    return pl.pallas_call(
        rows_grads_kernel,
        out_shape=(out, out),
        in_specs=[pl.BlockSpec(memory_space=pltpu.SMEM)] + [in_vmem()] * len(arrays),
        out_specs=(in_vmem(), in_vmem()),
        scratch_shapes=[pltpu.VMEM((height, width), jnp.float32)],
        compiler_params=pltpu.CompilerParams(vmem_limit_bytes=VMEM),
        cost_estimate=busy(3),
        name="rows_grads",
    )(place, *arrays)


def join_kernel(parts_in, gate_up_out, down_ref, parts_ref, gate_up_ref, stage_ref, in_sems, out_sems):
    width = gate_up_ref.shape[1] // 16
    tile = 16
    loads = [
        pltpu.make_async_copy(parts_in.at[n], parts_ref.at[n], in_sems.at[n])
        for n in range(parts_in.shape[0])
    ]
    for load in loads:
        load.start()
    stores = []
    for r in range(gate_up_ref.shape[0] // tile):
        here = slice(r * tile, (r + 1) * tile)
        for half in range(2):
            part = 2 * r + half
            loads[part].wait()
            columns = [
                parts_ref[part, k * tile : (k + 1) * tile, :].astype(jnp.float32)[:, :width]
                for k in range(8)
            ]
            gate_up_ref[here, half * 8 * width : (half + 1) * 8 * width] = jnp.concatenate(
                columns, axis=1
            )
        stores.append(
            pltpu.make_async_copy(gate_up_ref.at[here, :], gate_up_out.at[here, :], out_sems.at[r])
        )
        stores[-1].start()
    for load in loads[2 * len(stores) :]:
        load.wait()
    for part, first, height, source in down_places(stage_ref.shape[0], len(stores)):
        stage_ref[source : source + height, :] = parts_ref[part, first : first + height, :].astype(
            jnp.float32
        )
    for block in range(stage_ref.shape[0] // 128):
        at = slice(block * 128, (block + 1) * 128)
        down_ref[:, at] = stage_ref[at, :].T[:width]
    for store in stores:
        store.wait()


def join_columns(parts, rows, width, model_width):
    anywhere = pl.BlockSpec(memory_space=pl.ANY)
    return pl.pallas_call(
        join_kernel,
        out_shape=(
            jax.ShapeDtypeStruct((rows, 16 * width), jnp.float32),
            jax.ShapeDtypeStruct((width, model_width), jnp.float32),
        ),
        in_specs=[anywhere],
        out_specs=(anywhere, in_vmem()),
        scratch_shapes=[
            pltpu.VMEM(parts.shape, parts.dtype),
            pltpu.VMEM((rows, 16 * width), jnp.float32),
            pltpu.VMEM((model_width, parts.shape[2]), jnp.float32),
            pltpu.SemaphoreType.DMA((16,)),
            pltpu.SemaphoreType.DMA((rows // 16,)),
        ],
        compiler_params=pltpu.CompilerParams(vmem_limit_bytes=VMEM),
        cost_estimate=busy(4),
        name="join_columns",
    )(parts)


def columns_kernel(*refs):
    ins, out_ref, early_ref, late_ref, sems = refs[:10], refs[-4], refs[-3], refs[-2], refs[-1]
    lead_early = [ref.at[0] if len(ref.shape) == 3 else ref for ref in ins[:5]]
    lead_late = [ref.at[0] if len(ref.shape) == 3 else ref for ref in ins[5:]]
    fetch(
        [(ref, early_ref.at[n]) for n, ref in enumerate(lead_early)]
        + [(ref, late_ref.at[n]) for n, ref in enumerate(lead_late)],
        sems,
    )
    _, rows, width = early_ref.shape
    columns = out_ref.shape[2]
    blank = jnp.zeros((out_ref.shape[1] - rows, columns), jnp.float32)
    count = width // columns
    for n in range(out_ref.shape[0]):
        ref = early_ref if n < count else late_ref
        first = (n if n < count else n - count) * columns
        total = ref[0, :, first : first + columns].astype(jnp.float32)
        for m in range(1, 5):
            total = total + ref[m, :, first : first + columns].astype(jnp.float32)
        if n < count:
            total = jnp.concatenate([total, blank], axis=0)
        out_ref[n] = total.astype(jnp.bfloat16)


def column_parts(early, late):
    early_shape, late_shape = early[-1].shape, late[-1].shape
    columns = (early_shape[1] + late_shape[1]) // 16
    return pl.pallas_call(
        columns_kernel,
        out_shape=jax.ShapeDtypeStruct((16, late_shape[0], columns), jnp.bfloat16),
        in_specs=[pl.BlockSpec(memory_space=pl.ANY)] * 10,
        out_specs=in_vmem(),
        scratch_shapes=[
            pltpu.VMEM((5,) + early_shape, jnp.bfloat16),
            pltpu.VMEM((5,) + late_shape, jnp.bfloat16),
            pltpu.SemaphoreType.DMA((10,)),
        ],
        compiler_params=pltpu.CompilerParams(vmem_limit_bytes=VMEM),
        cost_estimate=busy(30),
        name="column_parts",
    )(*early, *late)


def core_swap(value):
    return lax.ppermute(value, "wa", [(i, i ^ 1) for i in range(8)])


def z_shift(value, step):
    return lax.ppermute(value, "wa", [(i, (i + 2 * step) % 8) for i in range(8)])


def ctx_exchange(value):
    return lax.all_to_all(value, "ctx", 0, 0, tiled=True)


def ctx_gather(value):
    return ctx_exchange(jnp.broadcast_to(value[None], (16,) + value.shape))


STEPS = (0, 1, 3, 2)


def gather_tokens(value):
    pieces = [z_shift(value, step) if step else value for step in STEPS]
    return [(piece, core_swap(piece)) for piece in pieces]


def return_tokens(paired):
    return [z_shift(mine, -step) if step else mine for step, mine in zip(STEPS, paired)]


def reduce_rows(kept, sent):
    other = core_swap(sent)
    pieces = [kept, other]
    for step in STEPS[1:]:
        mine = kept[step].astype(jnp.float32) + other[step].astype(jnp.float32)
        pieces.append(z_shift(mine.astype(jnp.bfloat16), step))
    return pieces


def after(value, *others):
    held = sum(other[(0,) * other.ndim].astype(jnp.float32) for other in others) * 0.0
    return value + held.astype(value.dtype)


def spread_kernel(parts_ref, left_ref, right_ref, bias_ref, gain_one_ref, gain_two_ref):
    columns = parts_ref.shape[2]
    rows = left_ref.shape[0]
    count = left_ref.shape[1] // columns
    small = []
    for n in range(parts_ref.shape[0]):
        part = parts_ref[n].astype(jnp.float32)
        if n < count:
            left_ref[:, n * columns : (n + 1) * columns] = part[:rows]
        else:
            right_ref[:, (n - count) * columns : (n - count + 1) * columns] = part[:rows]
        small.append(part[rows : rows + 8])
    small = jnp.concatenate(small[-2:], axis=1)
    bias_rows = bias_ref.shape[1]
    bias_ref[...] = small[:1, :bias_rows]
    gain_one_ref[...] = small[:1, bias_rows : bias_rows + rows]
    gain_two_ref[...] = small[1:2, :rows]


def spread_columns(parts, rows, width, bias_rows):
    count, _, columns = parts.shape
    shapes = [(rows, width), (rows, count * columns - width), (1, bias_rows), (1, rows), (1, rows)]
    return pl.pallas_call(
        spread_kernel,
        out_shape=tuple(jax.ShapeDtypeStruct(shape, jnp.float32) for shape in shapes),
        in_specs=[in_vmem()],
        out_specs=(in_vmem(),) * 5,
        compiler_params=pltpu.CompilerParams(vmem_limit_bytes=VMEM),
        cost_estimate=busy(1),
        name="spread_columns",
    )(parts)


def on_device(
    layer_input,
    positions,
    attention_gain,
    projection,
    projection_biases,
    output_matrix,
    feed_gain,
    gate_up_matrix,
    down_matrix,
    cotangent,
):
    place = lax.axis_index("wa").astype(jnp.int32)
    z, core = place // 2, place % 2
    ctx = lax.axis_index("ctx").astype(jnp.int32)
    rows = projection.shape[0]
    tokens = layer_input.shape[1]
    query_width = QUERY_HEADS * HEAD_SIZE
    key_width = KEY_VALUE_HEADS * HEAD_SIZE
    width = layer_input.shape[2]
    proj_width = projection.shape[1]
    bias_rows = projection_biases.shape[0]
    slice_width = down_matrix.shape[0]
    lanes = -(-slice_width // 128) * 128
    tile = 16
    sources = [(z + 4 - step) % 4 for step in STEPS]

    small = jnp.concatenate([projection_biases, attention_gain, feed_gain])
    small = jnp.pad(small[None], ((0, tile - 1), (0, proj_width - small.shape[0])))
    packed = lax.all_gather(jnp.concatenate([projection, small], axis=0), "wa", axis=0)

    spot = jnp.stack([z, core])
    local_places = jnp.stack([p for s in sources for p in (2 * s + core, 2 * s + 1 - core)])
    kept, sent, down = split_columns(spot, gate_up_matrix, down_matrix, lanes)
    other = core_swap(sent)
    gate_up = [jnp.concatenate([kept[step], other[step]], axis=0) for step in STEPS[1:]]

    layer_rows = layer_input[0]
    query_pos = positions[0]
    cosine, sine = angles(query_pos)
    cosine = jnp.tile(cosine, (1, 4))
    sine = jnp.tile(jnp.concatenate([-sine, sine], axis=1), (1, 2))
    first_normed, queries, pair, full_proj, gains = project(packed, layer_rows, cosine, sine)
    gain_one, gain_two = gains[0], gains[1]
    complete_output = lax.all_gather(output_matrix, "wa", axis=0, tiled=True)
    out_grad = cotangent[0]
    all_grads = lax.all_gather(out_grad, "wa", axis=0)

    pairs_sent = copies(pair, 16, gate_up)
    gate_up = [z_shift(piece, step) for step, piece in zip(STEPS[1:], gate_up)]
    pairs = ctx_exchange(pairs_sent).reshape(16 * tokens, 2 * key_width)
    low = ctx * tokens + jnp.arange(tokens, dtype=jnp.int32) - query_pos
    block = 4 * tokens
    start = jnp.stack(
        [
            ctx * tokens,
            jnp.maximum(jnp.min(low), 0) // block,
            (ctx * tokens + tokens + block - 1) // block,
        ]
    ).astype(jnp.int32)
    low = low[None]
    mixed, lse, attention_output, middle_state, second_normed = attend(
        start, queries, pairs, low, layer_rows, complete_output, gain_two, gate_up[:2]
    )

    normed_pairs = gather_tokens(second_normed)
    flat_normed = [piece for pair in normed_pairs for piece in pair]
    hidden, own, other, parts = feed(
        local_places, flat_normed, all_grads, [kept, other] + gate_up, down
    )
    other = core_swap(other)
    paired = [
        (own[n] + other[n].astype(jnp.float32)).astype(jnp.bfloat16) for n in range(len(STEPS))
    ]
    returned = return_tokens(paired)

    normed_two_grad = sum(piece.astype(jnp.float32) for piece in returned)
    parts = ctx_exchange(parts)

    _, norm_two_pull = jax.vjp(norm_rows, middle_state, gain_two[0])
    middle_part, gain_two_local = norm_two_pull(normed_two_grad)
    middle_grad = out_grad.astype(jnp.float32) + middle_part
    middle_lower = middle_grad.astype(jnp.bfloat16)
    mix_grad = column_product(middle_lower, complete_output).astype(jnp.bfloat16)
    query_back, pair_grad = attend_back(
        start, queries, pairs, low, mix_grad, mixed, lse, cosine, sine
    )
    early = reduce_rows(
        *rows_grads(spot, [(attention_output, middle_lower), (first_normed, query_back)])
    )

    result = feed_out(local_places, down, hidden, [pair_grad])
    result = lax.psum_scatter(result, "wa", scatter_dimension=0)
    pieces = ctx_exchange(pair_grad)
    input_grad, kept, sent = project_back(
        spot,
        layer_rows,
        gain_one,
        full_proj,
        cosine,
        sine,
        first_normed,
        query_back,
        middle_grad,
        gain_two_local[None],
        pieces,
        early[2:],
    )
    late = reduce_rows(kept, sent)

    kept, sent, whole = owner_parts(spot, parts, tile, pair_grad)
    other = core_swap(sent)
    parts = [
        z_shift(jnp.concatenate([kept[step], other[step]], axis=0), step) for step in STEPS[1:]
    ]
    cuts = [(0, 0, 0), (1, 0, 0)] + [(n, None, part * tile) for n in (2, 3, 4) for part in (0, 1)]
    parts, _ = place_rows(local_places, [kept, other] + parts, cuts, tile)
    parts = jnp.where(ctx < 2 * rows // tile, parts, whole[: 8 * tile])
    parts = lax.all_gather(jnp.concatenate([parts, whole[8 * tile :]], axis=0), "ctx", axis=0)
    gate_up_total, down_total = join_columns(parts, rows, slice_width, width)

    mine = ctx_exchange(column_parts(early, late))
    mine = ctx_gather(jnp.sum(mine.astype(jnp.float32), axis=0).astype(jnp.bfloat16))
    result = (middle_state + after(result.astype(jnp.float32), input_grad)).astype(jnp.bfloat16)
    output_total, projection_total, bias, gain_one, gain_two = spread_columns(
        mine, rows, width, bias_rows
    )
    return (
        result[None],
        input_grad[None],
        gain_one.reshape(rows),
        projection_total,
        bias.reshape(bias_rows),
        output_total,
        gain_two.reshape(rows),
        gate_up_total,
        down_total,
    )


def solution(mesh):
    placed = (
        P("wa", "ctx", None),
        P("wa", "ctx"),
        P("wa"),
        P("wa", None),
        P("wa"),
        P("wa", None),
        P("wa"),
        P("wa", None),
        P("wa", None),
        P("wa", "ctx", None),
    )
    return jax.shard_map(
        on_device,
        mesh=mesh,
        in_specs=placed,
        out_specs=(
            P("wa", "ctx", None),
            P("wa", "ctx", None),
            P("wa"),
            P("wa", None),
            P("wa"),
            P("wa", None),
            P("wa"),
            P("wa", None),
            P("wa", None),
        ),
        check_vma=False,
    )
```

```python
import functools

import jax
import jax.numpy as jnp
from jax import lax
from jax.experimental import pallas as pl
from jax.experimental.pallas import tpu as pltpu
from jax.sharding import PartitionSpec as P

QUERY_HEADS = 14
KEY_VALUE_HEADS = 2
HEAD_SIZE = 64
FF = 4864


EPS = 1e-06
THETA = 1000000.0
NEG = -1e30
VMEM = 56 * 2**20


def rows_product(left, right):
    return lax.dot_general(
        left, right, (((0,), (0,)), ((), ())), preferred_element_type=jnp.float32
    )


def column_product(left, right):
    return lax.dot_general(
        left, right, (((1,), (1,)), ((), ())), preferred_element_type=jnp.float32
    )


def norm_rows(value, gain):
    return value * lax.rsqrt(jnp.mean(value * value, axis=-1, keepdims=True) + EPS) * gain


def rotate(tensor, cosine_table, sine_table):
    half = tensor.shape[-1] // 2
    first = tensor[..., :half]
    second = tensor[..., half:]
    return jnp.concatenate(
        [first * cosine_table - second * sine_table, second * cosine_table + first * sine_table],
        axis=-1,
    )


def inverse_rotate(tensor, cosine_table, sine_table):
    half = tensor.shape[-1] // 2
    first = tensor[..., :half]
    second = tensor[..., half:]
    return jnp.concatenate(
        [first * cosine_table + second * sine_table, second * cosine_table - first * sine_table],
        axis=-1,
    )


def angles(positions):
    half = HEAD_SIZE // 2
    inverse = THETA ** (-(jnp.arange(half) * 2.0 / HEAD_SIZE))
    turned = positions.astype(jnp.float32)[:, None] * inverse.astype(jnp.float32)
    return (jnp.cos(turned), jnp.sin(turned))


def busy(microseconds):
    return pl.CostEstimate(
        flops=microseconds * 1150 * 10**6, bytes_accessed=microseconds * 10**6, transcendentals=0
    )


def turn_heads(value, cosine, sine):
    width = value.shape[1]
    lane = lax.broadcasted_iota(jnp.int32, value.shape, 1)
    half = HEAD_SIZE // 2
    partner = jnp.where(
        lane % HEAD_SIZE < half, pltpu.roll(value, width - half, 1), pltpu.roll(value, half, 1)
    )
    repeats = width // cosine.shape[1]
    return value * jnp.tile(cosine, (1, repeats)) + partner * jnp.tile(sine, (1, repeats))


def fetch(pairs, sems):
    copies = [pltpu.make_async_copy(*pair, sems.at[n]) for n, pair in enumerate(pairs)]
    for copy in copies:
        copy.start()
    for copy in copies:
        copy.wait()


def project_kernel(
    packed_ref, x_ref, cos_ref, sin_ref, normed_ref, q_ref, pair_ref, proj_ref, gains_ref, small_ref, sems
):
    count = packed_ref.shape[0]
    rows = proj_ref.shape[0] // count
    fetch(
        [
            (packed_ref.at[n, :rows, :], proj_ref.at[n * rows : (n + 1) * rows, :])
            for n in range(count)
        ]
        + [(packed_ref.at[n, rows:, :], small_ref.at[n]) for n in range(count)],
        sems,
    )
    small = [small_ref[n].astype(jnp.float32)[:1] for n in range(count)]
    bias_rows = proj_ref.shape[1] // count
    bias = jnp.concatenate([row[:, :bias_rows] for row in small], axis=1)
    gains = [
        jnp.concatenate([row[:, first : first + rows] for row in small], axis=1)
        for first in (bias_rows, bias_rows + rows)
    ]
    for n in range(2):
        gains_ref[n] = gains[n]
    x = x_ref[...].astype(jnp.float32)
    scale = lax.rsqrt(jnp.mean(x * x, axis=-1, keepdims=True) + EPS)
    normed = (x * scale * gains[0]).astype(jnp.bfloat16)
    normed_ref[...] = normed
    width = q_ref.shape[1]
    turned = width + KEY_VALUE_HEADS * HEAD_SIZE
    projected = jnp.dot(normed, proj_ref[...], preferred_element_type=jnp.float32) + bias
    rotated = turn_heads(projected[:, :turned], cos_ref[...], sin_ref[...])
    q_ref[...] = rotated[:, :width].astype(jnp.bfloat16)
    pair = jnp.concatenate([rotated[:, width:], projected[:, turned:]], axis=1).astype(jnp.bfloat16)
    pair_ref[...] = pair


def project(packed, x, cosine, sine):
    tokens, width = x.shape
    count, height, proj_width = packed.shape
    return pl.pallas_call(
        project_kernel,
        out_shape=(
            jax.ShapeDtypeStruct((tokens, width), jnp.bfloat16),
            jax.ShapeDtypeStruct((tokens, QUERY_HEADS * HEAD_SIZE), jnp.bfloat16),
            jax.ShapeDtypeStruct((tokens, 2 * KEY_VALUE_HEADS * HEAD_SIZE), jnp.bfloat16),
            jax.ShapeDtypeStruct((width, proj_width), jnp.bfloat16),
            jax.ShapeDtypeStruct((2, 1, width), jnp.float32),
        ),
        in_specs=[pl.BlockSpec(memory_space=pl.ANY)] + [in_vmem()] * 3,
        out_specs=(in_vmem(),) * 5,
        scratch_shapes=[
            pltpu.VMEM((count, height - width // count, proj_width), jnp.bfloat16),
            pltpu.SemaphoreType.DMA((2 * count,)),
        ],
        compiler_params=pltpu.CompilerParams(vmem_limit_bytes=VMEM),
        cost_estimate=busy(4),
        name="project",
    )(packed, x, cosine, sine)


def copies_kernel(value_ref, *refs):
    out_ref, sems = refs[-2:]
    fetch([(value_ref, out_ref.at[n]) for n in range(out_ref.shape[0])], sems)


def copies(value, count, earlier):
    return pl.pallas_call(
        copies_kernel,
        out_shape=jax.ShapeDtypeStruct((count,) + value.shape, value.dtype),
        in_specs=[in_vmem()] + [pl.BlockSpec(memory_space=pl.ANY)] * len(earlier),
        out_specs=pl.BlockSpec(memory_space=pl.ANY),
        scratch_shapes=[pltpu.SemaphoreType.DMA((count,))],
        compiler_params=pltpu.CompilerParams(vmem_limit_bytes=VMEM),
        cost_estimate=busy(2),
        name="copies",
    )(value, *earlier)


def project_back_kernel(
    place_ref, x_in, gain_ref, proj_in, cos_ref, sin_ref, normed_in, dq_in, grad_in, gain_two_ref, pieces_in, *refs
):
    input_grad_ref, kept_ref, sent_ref, stage_ref = refs[-11:-7]
    x_ref, proj_ref, normed_ref, dq_ref, grad_ref, pieces_ref, sems = refs[-7:]
    ins = (x_in, proj_in, normed_in, dq_in, grad_in, pieces_in)
    fetch(list(zip(ins, (x_ref, proj_ref, normed_ref, dq_ref, grad_ref, pieces_ref))), sems)
    z, core = place_ref[0], place_ref[1]
    key_width = KEY_VALUE_HEADS * HEAD_SIZE
    pair = pieces_ref[0].astype(jnp.float32)
    for n in range(1, pieces_ref.shape[0]):
        pair = pair + pieces_ref[n].astype(jnp.float32)
    keys = turn_heads(pair[:, :key_width], cos_ref[...], -sin_ref[...])
    pair = jnp.concatenate([keys, pair[:, key_width:]], axis=1).astype(jnp.bfloat16)
    turned = normed_ref[...].astype(jnp.float32).T.astype(jnp.bfloat16)
    stage_ref[...] = jnp.dot(turned, pair, preferred_element_type=jnp.float32)
    bias = jnp.concatenate(
        [
            jnp.sum(dq_ref[...].astype(jnp.float32), axis=0, keepdims=True),
            jnp.sum(pair.astype(jnp.float32), axis=0, keepdims=True),
        ],
        axis=1,
    )
    x = x_ref[...].astype(jnp.float32)
    scale = lax.rsqrt(jnp.mean(x * x, axis=-1, keepdims=True) + EPS)
    grad = lax.dot_general(
        jnp.concatenate([dq_ref[...], pair], axis=1),
        proj_ref[...],
        (((1,), (1,)), ((), ())),
        preferred_element_type=jnp.float32,
    )
    gain_one = jnp.sum(grad * x * scale, axis=0, keepdims=True)
    gained = grad * gain_ref[...]
    mean = jnp.mean(gained * x, axis=-1, keepdims=True)
    input_grad_ref[...] = grad_ref[...] + scale * gained - x * (scale * scale * scale * mean)

    rows = stage_ref.shape[0] // 8
    bias_rows = bias.shape[1] // 8
    blank = jnp.zeros((kept_ref.shape[1] - rows - 2, stage_ref.shape[1]), jnp.float32)
    for owner in range(8):
        at = lax.rem(owner // 2 - z + 4, 4)
        here = slice(owner * rows, (owner + 1) * rows)
        gain_two = gain_two_ref[:, here]
        first = jnp.concatenate(
            [bias[:, owner * bias_rows : (owner + 1) * bias_rows], gain_one[:, here]], axis=1
        )
        second = jnp.concatenate(
            [gain_two, jnp.zeros((1, stage_ref.shape[1] - rows), jnp.float32)], axis=1
        )
        both = jnp.concatenate([stage_ref[here, :], first, second, blank], axis=0).astype(jnp.bfloat16)

        @pl.when(core == owner % 2)
        def _(both=both, at=at):
            kept_ref[at] = both

        @pl.when(core != owner % 2)
        def _(both=both, at=at):
            sent_ref[at] = both


def project_back(place, x, gain, proj, cosine, sine, normed, dq, grad, gain_two, pieces, earlier):
    tokens, width = x.shape
    pair_width = pieces.shape[2]
    anywhere = pl.BlockSpec(memory_space=pl.ANY)
    out = jax.ShapeDtypeStruct((4, width // 8 + 16, pair_width), jnp.bfloat16)
    return pl.pallas_call(
        project_back_kernel,
        out_shape=(jax.ShapeDtypeStruct((tokens, width), jnp.float32), out, out),
        in_specs=[
            pl.BlockSpec(memory_space=pltpu.SMEM),
            anywhere,
            in_vmem(),
            anywhere,
            in_vmem(),
            in_vmem(),
            anywhere,
            anywhere,
            anywhere,
            in_vmem(),
            anywhere,
        ]
        + [anywhere] * len(earlier),
        out_specs=(in_vmem(),) * 3,
        scratch_shapes=[pltpu.VMEM((width, pair_width), jnp.float32)]
        + [pltpu.VMEM(a.shape, a.dtype) for a in (x, proj, normed, dq, grad, pieces)]
        + [pltpu.SemaphoreType.DMA((6,))],
        compiler_params=pltpu.CompilerParams(vmem_limit_bytes=VMEM),
        cost_estimate=busy(40),
        name="project_back",
    )(place, x, gain, proj, cosine, sine, normed, dq, grad, gain_two, pieces, *earlier)


def key_bias(low_ref, block_start, block, first_index):
    tokens = low_ref.shape[1]
    keys = block_start + lax.broadcasted_iota(jnp.int32, (block, tokens), 0)
    index = first_index + lax.broadcasted_iota(jnp.int32, (block, tokens), 1)
    return jnp.where((keys <= index) & (keys >= low_ref[...]), 0.0, NEG)


def head_places(tokens):
    group = QUERY_HEADS // KEY_VALUE_HEADS
    for h in range(QUERY_HEADS):
        g, i = divmod(h, group)
        yield g, slice(h * HEAD_SIZE, (h + 1) * HEAD_SIZE), slice(i * tokens, (i + 1) * tokens)


def attend_kernel(
    start_ref, q_in, kv_in, low_ref, x_in, out_in, gain_ref, *refs
):
    mixed_ref, lse_ref, attended_ref, middle_ref, normed_ref = refs[-17:-12]
    qt, s_ref, p_ref, bias_ref, m_ref, l_ref, acc_ref = refs[-12:-5]
    q_ref, kv_ref, x_ref, out_ref, sems = refs[-5:]
    pairs = [(q_in, q_ref), (kv_in, kv_ref), (x_in, x_ref), (out_in, out_ref)]
    loads = [pltpu.make_async_copy(*pair, sems.at[n]) for n, pair in enumerate(pairs)]
    for load in loads:
        load.start()
    for load in loads[:2]:
        load.wait()
    tokens = q_ref.shape[0]
    block, rows = s_ref.shape
    turned = (q_ref[...].astype(jnp.float32) * HEAD_SIZE ** (-0.5)).T.astype(jnp.bfloat16)
    for g, lanes, at in head_places(tokens):
        qt[g, :, at] = turned[lanes, :]
    m_ref[...] = jnp.full_like(m_ref, NEG)
    l_ref[...] = jnp.zeros_like(l_ref)
    acc_ref[...] = jnp.zeros_like(acc_ref)

    def visit(which, carry):
        block_start = pl.multiple_of(which * block, block)
        here = pl.ds(block_start, block)
        bias_ref[...] = key_bias(low_ref, block_start, block, start_ref[0])
        key_width = KEY_VALUE_HEADS * HEAD_SIZE
        values = kv_ref[here, key_width:].astype(jnp.float32).T.astype(jnp.bfloat16)
        for g in range(KEY_VALUE_HEADS):
            lanes = slice(g * HEAD_SIZE, (g + 1) * HEAD_SIZE)
            s_ref[...] = jnp.dot(kv_ref[here, lanes], qt[g], preferred_element_type=jnp.float32)
            for i in range(rows // tokens):
                at = slice(i * tokens, (i + 1) * tokens)
                s = s_ref[:, at] + bias_ref[...]
                old = m_ref[g, :, at]
                peak = jnp.maximum(old, jnp.max(s, axis=0, keepdims=True))
                e = jnp.exp(s - peak)
                scale = jnp.exp(old - peak)
                m_ref[g, :, at] = peak
                l_ref[g, :, at] = l_ref[g, :, at] * scale + jnp.sum(e, axis=0, keepdims=True)
                acc_ref[g, :, at] = acc_ref[g, :, at] * scale
                p_ref[:, at] = e.astype(jnp.bfloat16)
            acc_ref[g] += jnp.dot(values[lanes, :], p_ref[...], preferred_element_type=jnp.float32)
        return carry

    lax.fori_loop(start_ref[1], start_ref[2], visit, 0)
    mixed = [acc_ref[g, :, at] / l_ref[g, :, at] for g, _, at in head_places(tokens)]
    mixed = jnp.concatenate(mixed, axis=0).T
    mixed_ref[...] = mixed
    lse_ref[...] = m_ref[...] + jnp.log(l_ref[...])
    attended = mixed.astype(jnp.bfloat16)
    attended_ref[...] = attended
    for load in loads[2:]:
        load.wait()
    middle = x_ref[...].astype(jnp.float32) + jnp.dot(
        attended, out_ref[...], preferred_element_type=jnp.float32
    )
    middle_ref[...] = middle
    scale = lax.rsqrt(jnp.mean(middle * middle, axis=-1, keepdims=True) + EPS)
    normed_ref[...] = (middle * scale * gain_ref[...]).astype(jnp.bfloat16)


def attend_back_kernel(
    start_ref, q_ref, kv_ref, low_ref, dmix_ref, mixed_ref, lse_ref, cos_ref, sin_ref, dq_ref, dkv_ref,
    qs, qt, ms, mt, delta_ref, s_ref, dp_ref, p_ref, g_ref, bias_ref, acc_ref,
):
    tokens = q_ref.shape[0]
    block, rows = s_ref.shape
    key_width = KEY_VALUE_HEADS * HEAD_SIZE
    q = q_ref[...].astype(jnp.float32) * HEAD_SIZE ** (-0.5)
    dmix = dmix_ref[...].astype(jnp.float32)
    q_turned = q.T.astype(jnp.bfloat16)
    dmix_turned = dmix.T
    weighed = (dmix * mixed_ref[...]).T
    q = q.astype(jnp.bfloat16)
    for g, lanes, at in head_places(tokens):
        qs[g, at, :] = q[:, lanes]
        ms[g, at, :] = dmix_ref[:, lanes]
        qt[g, :, at] = q_turned[lanes, :]
        mt[g, :, at] = dmix_turned[lanes, :].astype(jnp.bfloat16)
        delta_ref[g, :, at] = jnp.sum(weighed[lanes, :], axis=0, keepdims=True)
    acc_ref[...] = jnp.zeros_like(acc_ref)
    dkv_ref[...] = jnp.zeros_like(dkv_ref)

    def visit(which, carry):
        block_start = pl.multiple_of(which * block, block)
        here = pl.ds(block_start, block)
        bias_ref[...] = key_bias(low_ref, block_start, block, start_ref[0])
        keys_turned = kv_ref[here, :key_width].astype(jnp.float32).T.astype(jnp.bfloat16)
        grads = [None] * (2 * KEY_VALUE_HEADS)
        for g in range(KEY_VALUE_HEADS):
            lanes = slice(g * HEAD_SIZE, (g + 1) * HEAD_SIZE)
            s_ref[...] = jnp.dot(kv_ref[here, lanes], qt[g], preferred_element_type=jnp.float32)
            values = kv_ref[here, key_width + g * HEAD_SIZE : key_width + (g + 1) * HEAD_SIZE]
            dp_ref[...] = jnp.dot(values, mt[g], preferred_element_type=jnp.float32)
            for i in range(rows // tokens):
                at = slice(i * tokens, (i + 1) * tokens)
                p = jnp.exp(s_ref[:, at] + bias_ref[...] - lse_ref[g, :, at])
                p_ref[:, at] = p.astype(jnp.bfloat16)
                g_ref[:, at] = (p * (dp_ref[:, at] - delta_ref[g, :, at])).astype(jnp.bfloat16)
            acc_ref[g] += jnp.dot(keys_turned[lanes, :], g_ref[...], preferred_element_type=jnp.float32)
            grads[g] = jnp.dot(g_ref[...], qs[g], preferred_element_type=jnp.float32)
            grads[KEY_VALUE_HEADS + g] = jnp.dot(
                p_ref[...], ms[g], preferred_element_type=jnp.float32
            )
        grads = jnp.concatenate(grads, axis=1).astype(jnp.bfloat16)
        for n in range(block // tokens):
            dkv_ref[which * (block // tokens) + n] = grads[n * tokens : (n + 1) * tokens, :]
        return carry

    lax.fori_loop(start_ref[1], start_ref[2], visit, 0)
    dq = [acc_ref[g, :, at] for g, _, at in head_places(tokens)]
    dq = jnp.concatenate(dq, axis=0).T * HEAD_SIZE ** (-0.5)
    dq_ref[...] = turn_heads(dq, cos_ref[...], -sin_ref[...]).astype(jnp.bfloat16)


def in_vmem():
    return pl.BlockSpec(memory_space=pltpu.VMEM)


def attend(start, queries, pairs, low, x, out_matrix, gain, earlier):
    tokens, width = queries.shape
    rows = QUERY_HEADS // KEY_VALUE_HEADS * tokens
    block = 4 * tokens
    heads = KEY_VALUE_HEADS
    return pl.pallas_call(
        attend_kernel,
        out_shape=(
            jax.ShapeDtypeStruct((tokens, width), jnp.float32),
            jax.ShapeDtypeStruct((heads, 1, rows), jnp.float32),
            jax.ShapeDtypeStruct((tokens, width), jnp.bfloat16),
            jax.ShapeDtypeStruct(x.shape, jnp.float32),
            jax.ShapeDtypeStruct(x.shape, jnp.bfloat16),
        ),
        in_specs=[
            pl.BlockSpec(memory_space=pltpu.SMEM),
            pl.BlockSpec(memory_space=pl.ANY),
            pl.BlockSpec(memory_space=pl.ANY),
            in_vmem(),
            pl.BlockSpec(memory_space=pl.ANY),
            pl.BlockSpec(memory_space=pl.ANY),
            in_vmem(),
        ]
        + [pl.BlockSpec(memory_space=pl.ANY)] * len(earlier),
        out_specs=(in_vmem(),) * 5,
        scratch_shapes=[
            pltpu.VMEM((heads, HEAD_SIZE, rows), jnp.bfloat16),
            pltpu.VMEM((block, rows), jnp.float32),
            pltpu.VMEM((block, rows), jnp.bfloat16),
            pltpu.VMEM((block, tokens), jnp.float32),
            pltpu.VMEM((heads, 1, rows), jnp.float32),
            pltpu.VMEM((heads, 1, rows), jnp.float32),
            pltpu.VMEM((heads, HEAD_SIZE, rows), jnp.float32),
            pltpu.VMEM(queries.shape, queries.dtype),
            pltpu.VMEM(pairs.shape, pairs.dtype),
            pltpu.VMEM(x.shape, x.dtype),
            pltpu.VMEM(out_matrix.shape, out_matrix.dtype),
            pltpu.SemaphoreType.DMA((4,)),
        ],
        compiler_params=pltpu.CompilerParams(vmem_limit_bytes=VMEM),
        cost_estimate=busy(9),
        name="attend",
    )(start, queries, pairs, low, x, out_matrix, gain, *earlier)


def attend_back(start, queries, pairs, low, mix_grad, mixed, lse, cosine, sine):
    tokens, width = queries.shape
    rows = QUERY_HEADS // KEY_VALUE_HEADS * tokens
    block = 4 * tokens
    heads = KEY_VALUE_HEADS
    return pl.pallas_call(
        attend_back_kernel,
        out_shape=(
            jax.ShapeDtypeStruct((tokens, width), jnp.bfloat16),
            jax.ShapeDtypeStruct((pairs.shape[0] // tokens, tokens, pairs.shape[1]), jnp.bfloat16),
        ),
        in_specs=[pl.BlockSpec(memory_space=pltpu.SMEM)] + [in_vmem()] * 8,
        out_specs=(in_vmem(), in_vmem()),
        scratch_shapes=[
            pltpu.VMEM((heads, rows, HEAD_SIZE), jnp.bfloat16),
            pltpu.VMEM((heads, HEAD_SIZE, rows), jnp.bfloat16),
            pltpu.VMEM((heads, rows, HEAD_SIZE), jnp.bfloat16),
            pltpu.VMEM((heads, HEAD_SIZE, rows), jnp.bfloat16),
            pltpu.VMEM((heads, 1, rows), jnp.float32),
            pltpu.VMEM((block, rows), jnp.float32),
            pltpu.VMEM((block, rows), jnp.float32),
            pltpu.VMEM((block, rows), jnp.bfloat16),
            pltpu.VMEM((block, rows), jnp.bfloat16),
            pltpu.VMEM((block, tokens), jnp.float32),
            pltpu.VMEM((heads, HEAD_SIZE, rows), jnp.float32),
        ],
        compiler_params=pltpu.CompilerParams(vmem_limit_bytes=VMEM),
        cost_estimate=busy(25),
        name="attend_back",
    )(start, queries, pairs, low, mix_grad, mixed, lse, cosine, sine)


def split_kernel(place_ref, matrix_ref, down_ref, kept_ref, sent_ref, padded_ref):
    padded_ref[: down_ref.shape[0], :] = down_ref[...]
    padded_ref[down_ref.shape[0] :, :] = jnp.zeros(
        (padded_ref.shape[0] - down_ref.shape[0], down_ref.shape[1]), down_ref.dtype
    )
    z, core = place_ref[0], place_ref[1]
    width, lanes = matrix_ref.shape[1] // 16, kept_ref.shape[2] // 2
    for owner in range(8):
        at = lax.rem(owner // 2 - z + 4, 4)
        gate = matrix_ref[:, owner * width : (owner + 1) * width].astype(jnp.float32)
        up = matrix_ref[:, (8 + owner) * width : (9 + owner) * width].astype(jnp.float32)
        blank = jnp.zeros((gate.shape[0], lanes - width), jnp.float32)
        both = jnp.concatenate([gate, blank, up, blank], axis=1).astype(jnp.bfloat16)

        @pl.when(core == owner % 2)
        def _(both=both, at=at):
            kept_ref[at] = both

        @pl.when(core != owner % 2)
        def _(both=both, at=at):
            sent_ref[at] = both


def split_columns(place, matrix, down, lanes):
    rows = matrix.shape[0]
    out = jax.ShapeDtypeStruct((4, rows, 2 * lanes), matrix.dtype)
    return pl.pallas_call(
        split_kernel,
        out_shape=(out, out, jax.ShapeDtypeStruct((lanes, down.shape[1]), down.dtype)),
        in_specs=[pl.BlockSpec(memory_space=pltpu.SMEM), in_vmem(), in_vmem()],
        out_specs=(in_vmem(),) * 3,
        compiler_params=pltpu.CompilerParams(vmem_limit_bytes=VMEM),
        cost_estimate=busy(4),
        name="split_columns",
    )(place, matrix, down)


def place_kernel(cuts, at_ref, *refs):
    pieces, (out_ref, rest_ref, sems, rest_sems) = refs[:-4], refs[-4:]
    rows = out_ref.shape[0] // len(cuts)
    copies = []
    for n, (which, lead, first) in enumerate(cuts):
        piece = pieces[which] if lead is None else pieces[which].at[lead]
        copies.append(
            pltpu.make_async_copy(
                piece.at[first : first + rows, :],
                out_ref.at[pl.ds(pl.multiple_of(at_ref[n] * rows, 16), rows), :],
                sems.at[n],
            )
        )
        if rest_ref.shape[0] == len(cuts):
            copies.append(
                pltpu.make_async_copy(piece.at[rows:, :], rest_ref.at[at_ref[n]], rest_sems.at[n])
            )
    for copy in copies:
        copy.start()
    if rest_ref.shape[0] != len(cuts):
        rest_ref[...] = jnp.zeros_like(rest_ref)
    for copy in copies:
        copy.wait()


def place_rows(at, arrays, cuts, rows, rest=0):
    width, kind = arrays[0].shape[-1], arrays[0].dtype
    count = len(cuts)
    rest_shape = (count, rest, width) if rest else (1, 8, 128)
    return pl.pallas_call(
        functools.partial(place_kernel, tuple(cuts)),
        out_shape=(
            jax.ShapeDtypeStruct((count * rows, width), kind),
            jax.ShapeDtypeStruct(rest_shape, kind if rest else jnp.float32),
        ),
        in_specs=[pl.BlockSpec(memory_space=pltpu.SMEM)]
        + [pl.BlockSpec(memory_space=pl.ANY)] * len(arrays),
        out_specs=(in_vmem(), in_vmem()),
        scratch_shapes=[pltpu.SemaphoreType.DMA((count,)), pltpu.SemaphoreType.DMA((count,))],
        compiler_params=pltpu.CompilerParams(vmem_limit_bytes=VMEM),
        cost_estimate=busy(2),
        name="place_rows",
    )(at, *arrays)


def down_places(width, row_tiles):
    full, tile = 2 * row_tiles, 16
    extra = -(-width // 16 // tile) * tile - tile
    rest = (width - full * extra) // (16 - full)
    for part in range(full):
        yield part, 8 * tile, extra, part * extra
    for part in range(full, 16):
        yield part, 0, rest, full * extra + (part - full) * rest


def feed_kernel(at_ref, *refs):
    normed_in, (grads_in, down_in), gate_up_in = refs[:8], refs[8:10], refs[10:15]
    hidden_ref, own_ref, other_ref, out_ref = refs[15:19]
    normed_ref, grads_ref, gate_up_ref, down_ref, joined_ref, turned_ref, stage_ref, sems = refs[19:]
    tokens = normed_in[0].shape[0]
    lanes = hidden_ref.shape[1]
    step = 2 * tokens
    tile = 16
    pairs = [(down_in, down_ref)]
    rows = gate_up_ref.shape[0] // 8
    pieces = [gate_up_in[0].at[0], gate_up_in[1].at[0]]
    pieces += [ref.at[part * rows : (part + 1) * rows, :] for ref in gate_up_in[2:] for part in range(2)]
    for n, piece in enumerate(pieces):
        start = pl.multiple_of(at_ref[n] * rows, 16)
        pairs.append((piece, gate_up_ref.at[pl.ds(start, rows), :]))
    for n in range(8):
        here = slice(n * tokens, (n + 1) * tokens)
        pairs.append((normed_in[n], normed_ref.at[here, :]))
        pairs.append((grads_in.at[at_ref[n]], grads_ref.at[here, :]))
    loads = [pltpu.make_async_copy(*pair, sems.at[n]) for n, pair in enumerate(pairs)]
    for load in loads:
        load.start()
    for load in loads[:9]:
        load.wait()
    for part in range(4):
        for load in loads[9 + 4 * part : 13 + 4 * part]:
            load.wait()
        here = slice(part * step, (part + 1) * step)
        gate = jnp.dot(normed_ref[here, :], gate_up_ref[:, :lanes], preferred_element_type=jnp.float32)
        up = jnp.dot(normed_ref[here, :], gate_up_ref[:, lanes:], preferred_element_type=jnp.float32)
        hidden_grad = lax.dot_general(
            grads_ref[here, :], down_ref[...], (((1,), (1,)), ((), ())), preferred_element_type=jnp.float32
        )
        sg = 1.0 / (1.0 + jnp.exp(-gate))
        act = gate * sg
        hidden_ref[here, :] = (act * up).astype(jnp.bfloat16)
        joined_ref[here, :lanes] = (hidden_grad * up * sg * (1.0 + gate * (1.0 - sg))).astype(
            jnp.bfloat16
        )
        joined_ref[here, lanes:] = (hidden_grad * act).astype(jnp.bfloat16)
        back = lax.dot_general(
            joined_ref[here, :], gate_up_ref[...], (((1,), (1,)), ((), ())), preferred_element_type=jnp.float32
        )
        own_ref[part] = back[:tokens]
        other_ref[part] = back[tokens:].astype(jnp.bfloat16)
        turned_ref[:, here] = normed_ref[here, :].astype(jnp.float32).T.astype(jnp.bfloat16)

    rows = stage_ref.shape[0] // 8
    for half in range(2):
        stage_ref[...] = jnp.dot(
            turned_ref[...],
            joined_ref[:, half * lanes : (half + 1) * lanes],
            preferred_element_type=jnp.float32,
        )
        for r in range(rows // tile):
            for k in range(8):
                first = k * rows + r * tile
                out_ref[2 * r + half, k * tile : (k + 1) * tile, :] = stage_ref[
                    first : first + tile, :
                ].astype(jnp.bfloat16)
    for part in range(4):
        here = slice(part * step, (part + 1) * step)
        turned_ref[:, here] = grads_ref[here, :].astype(jnp.float32).T.astype(jnp.bfloat16)
    stage_ref[...] = jnp.dot(turned_ref[...], hidden_ref[...], preferred_element_type=jnp.float32)
    for part, first, height, source in down_places(stage_ref.shape[0], rows // tile):
        out_ref[part, first : first + height, :] = stage_ref[source : source + height, :].astype(
            jnp.bfloat16
        )
        if first == 0:
            out_ref[part, height:, :] = jnp.zeros((out_ref.shape[1] - height, lanes), jnp.bfloat16)


def feed(at, normed, grads, gate_up, down):
    tokens, width = normed[0].shape
    lanes = down.shape[0]
    part = 8 * 16 + -(-width // 16 // 16) * 16 - 16
    return pl.pallas_call(
        feed_kernel,
        out_shape=(
            jax.ShapeDtypeStruct((8 * tokens, lanes), jnp.bfloat16),
            jax.ShapeDtypeStruct((4, tokens, width), jnp.float32),
            jax.ShapeDtypeStruct((4, tokens, width), jnp.bfloat16),
            jax.ShapeDtypeStruct((16, part, lanes), jnp.bfloat16),
        ),
        in_specs=[pl.BlockSpec(memory_space=pltpu.SMEM)] + [pl.BlockSpec(memory_space=pl.ANY)] * 15,
        out_specs=(in_vmem(),) * 4,
        scratch_shapes=[
            pltpu.VMEM((8 * tokens, width), jnp.bfloat16),
            pltpu.VMEM((8 * tokens, width), jnp.bfloat16),
            pltpu.VMEM((width, 2 * lanes), jnp.bfloat16),
            pltpu.VMEM(down.shape, down.dtype),
            pltpu.VMEM((8 * tokens, 2 * lanes), jnp.bfloat16),
            pltpu.VMEM((width, 8 * tokens), jnp.bfloat16),
            pltpu.VMEM((width, lanes), jnp.float32),
            pltpu.SemaphoreType.DMA((25,)),
        ],
        compiler_params=pltpu.CompilerParams(vmem_limit_bytes=VMEM),
        cost_estimate=busy(18),
        name="feed",
    )(at, *normed, grads, down, *gate_up)


def feed_out_kernel(at_ref, down_ref, *refs):
    hidden, out_ref = refs[0], refs[-1]
    tokens = out_ref.shape[1]
    for n in range(4):
        here = slice(2 * n * tokens, 2 * (n + 1) * tokens)
        out = jnp.dot(hidden[here, :], down_ref[...], preferred_element_type=jnp.float32)
        for part in range(2):
            out_ref[at_ref[2 * n + part]] = out[part * tokens : (part + 1) * tokens].astype(
                jnp.bfloat16
            )


def feed_out(at, down, hidden, earlier):
    tokens = hidden.shape[0] // 8
    return pl.pallas_call(
        feed_out_kernel,
        out_shape=jax.ShapeDtypeStruct((8, tokens, down.shape[1]), jnp.bfloat16),
        in_specs=[pl.BlockSpec(memory_space=pltpu.SMEM)]
        + [in_vmem()] * 2
        + [pl.BlockSpec(memory_space=pl.ANY)] * len(earlier),
        out_specs=in_vmem(),
        compiler_params=pltpu.CompilerParams(vmem_limit_bytes=VMEM),
        cost_estimate=busy(4),
        name="feed_out",
    )(at, down, hidden, *earlier)


def owner_parts_kernel(place_ref, parts_ref, *refs):
    kept_ref, sent_ref, whole_ref = refs[-3:]
    z, core = place_ref[0], place_ref[1]
    rows = kept_ref.shape[1]

    def total(here):
        value = parts_ref[0, here, :].astype(jnp.float32)
        for n in range(1, parts_ref.shape[0]):
            value = value + parts_ref[n, here, :].astype(jnp.float32)
        return value.astype(jnp.bfloat16)

    for owner in range(8):
        at = lax.rem(owner // 2 - z + 4, 4)
        part = total(slice(owner * rows, (owner + 1) * rows))
        whole_ref[owner * rows : (owner + 1) * rows, :] = part

        @pl.when(core == owner % 2)
        def _(part=part, at=at):
            kept_ref[at] = part

        @pl.when(core != owner % 2)
        def _(part=part, at=at):
            sent_ref[at] = part

    for first in range(8 * rows, whole_ref.shape[0], rows):
        whole_ref[first : first + rows, :] = total(slice(first, first + rows))


def owner_parts(place, parts, rows, earlier):
    _, height, width = parts.shape
    out = jax.ShapeDtypeStruct((4, rows, width), jnp.bfloat16)
    return pl.pallas_call(
        owner_parts_kernel,
        out_shape=(out, out, jax.ShapeDtypeStruct((height, width), jnp.bfloat16)),
        in_specs=[pl.BlockSpec(memory_space=pltpu.SMEM), in_vmem()]
        + [pl.BlockSpec(memory_space=pl.ANY)] * len(earlier),
        out_specs=(in_vmem(),) * 3,
        compiler_params=pltpu.CompilerParams(vmem_limit_bytes=VMEM),
        cost_estimate=busy(3),
        name="owner_parts",
    )(place, parts, *earlier)


def rows_grads_kernel(place_ref, *refs):
    kept_ref, sent_ref, stage_ref = refs[-3:]
    pairs = (len(refs) - 3) // 2
    rest_ref = refs[2 * pairs] if (len(refs) - 3) % 2 else None
    z, core = place_ref[0], place_ref[1]
    rows = stage_ref.shape[0] // 8
    first = 0
    for n in range(pairs):
        left, right = refs[2 * n], refs[2 * n + 1]
        turned = left[...].astype(jnp.float32).T.astype(jnp.bfloat16)
        stage_ref[:, first : first + right.shape[1]] = jnp.dot(
            turned, right[...], preferred_element_type=jnp.float32
        )
        first += right.shape[1]
    for owner in range(8):
        at = lax.rem(owner // 2 - z + 4, 4)

        @pl.when(core == owner % 2)
        def _(owner=owner, at=at):
            kept_ref[at, :rows, :] = stage_ref[owner * rows : (owner + 1) * rows, :].astype(jnp.bfloat16)
            if rest_ref is not None:
                kept_ref[at, rows:, :] = rest_ref[owner]

        @pl.when(core != owner % 2)
        def _(owner=owner, at=at):
            sent_ref[at, :rows, :] = stage_ref[owner * rows : (owner + 1) * rows, :].astype(jnp.bfloat16)
            if rest_ref is not None:
                sent_ref[at, rows:, :] = rest_ref[owner]


def rows_grads(place, pairs, rest=None):
    height = pairs[0][0].shape[1]
    width = sum(right.shape[1] for _, right in pairs)
    rows = height // 8 + (0 if rest is None else rest.shape[1])
    arrays = [array for pair in pairs for array in pair] + ([] if rest is None else [rest])
    out = jax.ShapeDtypeStruct((4, rows, width), jnp.bfloat16)
    return pl.pallas_call(
        rows_grads_kernel,
        out_shape=(out, out),
        in_specs=[pl.BlockSpec(memory_space=pltpu.SMEM)] + [in_vmem()] * len(arrays),
        out_specs=(in_vmem(), in_vmem()),
        scratch_shapes=[pltpu.VMEM((height, width), jnp.float32)],
        compiler_params=pltpu.CompilerParams(vmem_limit_bytes=VMEM),
        cost_estimate=busy(3),
        name="rows_grads",
    )(place, *arrays)


def join_kernel(parts_in, gate_up_out, down_ref, parts_ref, gate_up_ref, stage_ref, in_sems, out_sems):
    width = gate_up_ref.shape[1] // 16
    tile = 16
    loads = [
        pltpu.make_async_copy(parts_in.at[n], parts_ref.at[n], in_sems.at[n])
        for n in range(parts_in.shape[0])
    ]
    for load in loads:
        load.start()
    stores = []
    for r in range(gate_up_ref.shape[0] // tile):
        here = slice(r * tile, (r + 1) * tile)
        for half in range(2):
            part = 2 * r + half
            loads[part].wait()
            columns = [
                parts_ref[part, k * tile : (k + 1) * tile, :].astype(jnp.float32)[:, :width]
                for k in range(8)
            ]
            gate_up_ref[here, half * 8 * width : (half + 1) * 8 * width] = jnp.concatenate(
                columns, axis=1
            )
        stores.append(
            pltpu.make_async_copy(gate_up_ref.at[here, :], gate_up_out.at[here, :], out_sems.at[r])
        )
        stores[-1].start()
    for load in loads[2 * len(stores) :]:
        load.wait()
    for part, first, height, source in down_places(stage_ref.shape[0], len(stores)):
        stage_ref[source : source + height, :] = parts_ref[part, first : first + height, :].astype(
            jnp.float32
        )
    for block in range(stage_ref.shape[0] // 128):
        at = slice(block * 128, (block + 1) * 128)
        down_ref[:, at] = stage_ref[at, :].T[:width]
    for store in stores:
        store.wait()


def join_columns(parts, rows, width, model_width):
    anywhere = pl.BlockSpec(memory_space=pl.ANY)
    return pl.pallas_call(
        join_kernel,
        out_shape=(
            jax.ShapeDtypeStruct((rows, 16 * width), jnp.float32),
            jax.ShapeDtypeStruct((width, model_width), jnp.float32),
        ),
        in_specs=[anywhere],
        out_specs=(anywhere, in_vmem()),
        scratch_shapes=[
            pltpu.VMEM(parts.shape, parts.dtype),
            pltpu.VMEM((rows, 16 * width), jnp.float32),
            pltpu.VMEM((model_width, parts.shape[2]), jnp.float32),
            pltpu.SemaphoreType.DMA((16,)),
            pltpu.SemaphoreType.DMA((rows // 16,)),
        ],
        compiler_params=pltpu.CompilerParams(vmem_limit_bytes=VMEM),
        cost_estimate=busy(4),
        name="join_columns",
    )(parts)


def columns_kernel(*refs):
    ins, out_ref, early_ref, late_ref, sems = refs[:10], refs[-4], refs[-3], refs[-2], refs[-1]
    lead_early = [ref.at[0] if len(ref.shape) == 3 else ref for ref in ins[:5]]
    lead_late = [ref.at[0] if len(ref.shape) == 3 else ref for ref in ins[5:]]
    fetch(
        [(ref, early_ref.at[n]) for n, ref in enumerate(lead_early)]
        + [(ref, late_ref.at[n]) for n, ref in enumerate(lead_late)],
        sems,
    )
    _, rows, width = early_ref.shape
    columns = out_ref.shape[2]
    blank = jnp.zeros((out_ref.shape[1] - rows, columns), jnp.float32)
    count = width // columns
    for n in range(out_ref.shape[0]):
        ref = early_ref if n < count else late_ref
        first = (n if n < count else n - count) * columns
        total = ref[0, :, first : first + columns].astype(jnp.float32)
        for m in range(1, 5):
            total = total + ref[m, :, first : first + columns].astype(jnp.float32)
        if n < count:
            total = jnp.concatenate([total, blank], axis=0)
        out_ref[n] = total.astype(jnp.bfloat16)


def column_parts(early, late):
    early_shape, late_shape = early[-1].shape, late[-1].shape
    columns = (early_shape[1] + late_shape[1]) // 16
    return pl.pallas_call(
        columns_kernel,
        out_shape=jax.ShapeDtypeStruct((16, late_shape[0], columns), jnp.bfloat16),
        in_specs=[pl.BlockSpec(memory_space=pl.ANY)] * 10,
        out_specs=in_vmem(),
        scratch_shapes=[
            pltpu.VMEM((5,) + early_shape, jnp.bfloat16),
            pltpu.VMEM((5,) + late_shape, jnp.bfloat16),
            pltpu.SemaphoreType.DMA((10,)),
        ],
        compiler_params=pltpu.CompilerParams(vmem_limit_bytes=VMEM),
        cost_estimate=busy(30),
        name="column_parts",
    )(*early, *late)


def core_swap(value):
    return lax.ppermute(value, "wa", [(i, i ^ 1) for i in range(8)])


def z_shift(value, step):
    return lax.ppermute(value, "wa", [(i, (i + 2 * step) % 8) for i in range(8)])


def ctx_exchange(value):
    return lax.all_to_all(value, "ctx", 0, 0, tiled=True)


def ctx_gather(value):
    return ctx_exchange(jnp.broadcast_to(value[None], (16,) + value.shape))


STEPS = (0, 1, 3, 2)


def gather_tokens(value):
    pieces = [z_shift(value, step) if step else value for step in STEPS]
    return [(piece, core_swap(piece)) for piece in pieces]


def return_tokens(paired):
    return [z_shift(mine, -step) if step else mine for step, mine in zip(STEPS, paired)]


def reduce_rows(kept, sent):
    other = core_swap(sent)
    pieces = [kept, other]
    for step in STEPS[1:]:
        mine = kept[step].astype(jnp.float32) + other[step].astype(jnp.float32)
        pieces.append(z_shift(mine.astype(jnp.bfloat16), step))
    return pieces


def after(value, *others):
    held = sum(other[(0,) * other.ndim].astype(jnp.float32) for other in others) * 0.0
    return value + held.astype(value.dtype)


def spread_kernel(parts_ref, left_ref, right_ref, bias_ref, gain_one_ref, gain_two_ref):
    columns = parts_ref.shape[2]
    rows = left_ref.shape[0]
    count = left_ref.shape[1] // columns
    small = []
    for n in range(parts_ref.shape[0]):
        part = parts_ref[n].astype(jnp.float32)
        if n < count:
            left_ref[:, n * columns : (n + 1) * columns] = part[:rows]
        else:
            right_ref[:, (n - count) * columns : (n - count + 1) * columns] = part[:rows]
        small.append(part[rows : rows + 8])
    small = jnp.concatenate(small[-2:], axis=1)
    bias_rows = bias_ref.shape[1]
    bias_ref[...] = small[:1, :bias_rows]
    gain_one_ref[...] = small[:1, bias_rows : bias_rows + rows]
    gain_two_ref[...] = small[1:2, :rows]


def spread_columns(parts, rows, width, bias_rows):
    count, _, columns = parts.shape
    shapes = [(rows, width), (rows, count * columns - width), (1, bias_rows), (1, rows), (1, rows)]
    return pl.pallas_call(
        spread_kernel,
        out_shape=tuple(jax.ShapeDtypeStruct(shape, jnp.float32) for shape in shapes),
        in_specs=[in_vmem()],
        out_specs=(in_vmem(),) * 5,
        compiler_params=pltpu.CompilerParams(vmem_limit_bytes=VMEM),
        cost_estimate=busy(1),
        name="spread_columns",
    )(parts)


def on_device(
    layer_input,
    positions,
    attention_gain,
    projection,
    projection_biases,
    output_matrix,
    feed_gain,
    gate_up_matrix,
    down_matrix,
    cotangent,
):
    place = lax.axis_index("wa").astype(jnp.int32)
    z, core = place // 2, place % 2
    ctx = lax.axis_index("ctx").astype(jnp.int32)
    rows = projection.shape[0]
    tokens = layer_input.shape[1]
    query_width = QUERY_HEADS * HEAD_SIZE
    key_width = KEY_VALUE_HEADS * HEAD_SIZE
    width = layer_input.shape[2]
    proj_width = projection.shape[1]
    bias_rows = projection_biases.shape[0]
    slice_width = down_matrix.shape[0]
    lanes = -(-slice_width // 128) * 128
    tile = 16
    sources = [(z + 4 - step) % 4 for step in STEPS]

    small = jnp.concatenate([projection_biases, attention_gain, feed_gain])
    small = jnp.pad(small[None], ((0, tile - 1), (0, proj_width - small.shape[0])))
    packed = lax.all_gather(jnp.concatenate([projection, small], axis=0), "wa", axis=0)

    spot = jnp.stack([z, core])
    local_places = jnp.stack([p for s in sources for p in (2 * s + core, 2 * s + 1 - core)])
    kept, sent, down = split_columns(spot, gate_up_matrix, down_matrix, lanes)
    other = core_swap(sent)
    gate_up = [jnp.concatenate([kept[step], other[step]], axis=0) for step in STEPS[1:]]

    layer_rows = layer_input[0]
    query_pos = positions[0]
    cosine, sine = angles(query_pos)
    cosine = jnp.tile(cosine, (1, 4))
    sine = jnp.tile(jnp.concatenate([-sine, sine], axis=1), (1, 2))
    first_normed, queries, pair, full_proj, gains = project(packed, layer_rows, cosine, sine)
    gain_one, gain_two = gains[0], gains[1]
    complete_output = lax.all_gather(output_matrix, "wa", axis=0, tiled=True)
    out_grad = cotangent[0]
    all_grads = lax.all_gather(out_grad, "wa", axis=0)

    pairs_sent = copies(pair, 16, gate_up)
    gate_up = [z_shift(piece, step) for step, piece in zip(STEPS[1:], gate_up)]
    pairs = ctx_exchange(pairs_sent).reshape(16 * tokens, 2 * key_width)
    low = ctx * tokens + jnp.arange(tokens, dtype=jnp.int32) - query_pos
    block = 4 * tokens
    start = jnp.stack(
        [
            ctx * tokens,
            jnp.maximum(jnp.min(low), 0) // block,
            (ctx * tokens + tokens + block - 1) // block,
        ]
    ).astype(jnp.int32)
    low = low[None]
    mixed, lse, attention_output, middle_state, second_normed = attend(
        start, queries, pairs, low, layer_rows, complete_output, gain_two, gate_up[:2]
    )

    normed_pairs = gather_tokens(second_normed)
    flat_normed = [piece for pair in normed_pairs for piece in pair]
    hidden, own, other, parts = feed(
        local_places, flat_normed, all_grads, [kept, other] + gate_up, down
    )
    other = core_swap(other)
    paired = [
        (own[n] + other[n].astype(jnp.float32)).astype(jnp.bfloat16) for n in range(len(STEPS))
    ]
    returned = return_tokens(paired)

    normed_two_grad = sum(piece.astype(jnp.float32) for piece in returned)
    parts = ctx_exchange(parts)

    _, norm_two_pull = jax.vjp(norm_rows, middle_state, gain_two[0])
    middle_part, gain_two_local = norm_two_pull(normed_two_grad)
    middle_grad = out_grad.astype(jnp.float32) + middle_part
    middle_lower = middle_grad.astype(jnp.bfloat16)
    mix_grad = column_product(middle_lower, complete_output).astype(jnp.bfloat16)
    query_back, pair_grad = attend_back(
        start, queries, pairs, low, mix_grad, mixed, lse, cosine, sine
    )
    early = reduce_rows(
        *rows_grads(spot, [(attention_output, middle_lower), (first_normed, query_back)])
    )

    result = feed_out(local_places, down, hidden, [pair_grad])
    result = lax.psum_scatter(result, "wa", scatter_dimension=0)
    pieces = ctx_exchange(pair_grad)
    input_grad, kept, sent = project_back(
        spot,
        layer_rows,
        gain_one,
        full_proj,
        cosine,
        sine,
        first_normed,
        query_back,
        middle_grad,
        gain_two_local[None],
        pieces,
        [],
    )
    late = reduce_rows(kept, sent)

    kept, sent, whole = owner_parts(spot, parts, tile, [pair_grad] + early[2:])
    other = core_swap(sent)
    parts = [
        z_shift(jnp.concatenate([kept[step], other[step]], axis=0), step) for step in STEPS[1:]
    ]
    cuts = [(0, 0, 0), (1, 0, 0)] + [(n, None, part * tile) for n in (2, 3, 4) for part in (0, 1)]
    parts, _ = place_rows(local_places, [kept, other] + parts, cuts, tile)
    parts = jnp.where(ctx < 2 * rows // tile, parts, whole[: 8 * tile])
    parts = lax.all_gather(jnp.concatenate([parts, whole[8 * tile :]], axis=0), "ctx", axis=0)
    gate_up_total, down_total = join_columns(parts, rows, slice_width, width)

    mine = ctx_exchange(column_parts(early, late))
    mine = ctx_gather(jnp.sum(mine.astype(jnp.float32), axis=0).astype(jnp.bfloat16))
    result = (middle_state + after(result.astype(jnp.float32), input_grad)).astype(jnp.bfloat16)
    output_total, projection_total, bias, gain_one, gain_two = spread_columns(
        mine, rows, width, bias_rows
    )
    return (
        result[None],
        input_grad[None],
        gain_one.reshape(rows),
        projection_total,
        bias.reshape(bias_rows),
        output_total,
        gain_two.reshape(rows),
        gate_up_total,
        down_total,
    )


def solution(mesh):
    placed = (
        P("wa", "ctx", None),
        P("wa", "ctx"),
        P("wa"),
        P("wa", None),
        P("wa"),
        P("wa", None),
        P("wa"),
        P("wa", None),
        P("wa", None),
        P("wa", "ctx", None),
    )
    return jax.shard_map(
        on_device,
        mesh=mesh,
        in_specs=placed,
        out_specs=(
            P("wa", "ctx", None),
            P("wa", "ctx", None),
            P("wa"),
            P("wa", None),
            P("wa"),
            P("wa", None),
            P("wa"),
            P("wa", None),
            P("wa", None),
        ),
        check_vma=False,
    )
```

```python
import functools

import jax
import jax.numpy as jnp
from jax import lax
from jax.experimental import pallas as pl
from jax.experimental.pallas import tpu as pltpu
from jax.sharding import PartitionSpec as P

QUERY_HEADS = 14
KEY_VALUE_HEADS = 2
HEAD_SIZE = 64
FF = 4864


EPS = 1e-06
THETA = 1000000.0
NEG = -1e30
VMEM = 56 * 2**20


def rows_product(left, right):
    return lax.dot_general(
        left, right, (((0,), (0,)), ((), ())), preferred_element_type=jnp.float32
    )


def column_product(left, right):
    return lax.dot_general(
        left, right, (((1,), (1,)), ((), ())), preferred_element_type=jnp.float32
    )


def norm_rows(value, gain):
    return value * lax.rsqrt(jnp.mean(value * value, axis=-1, keepdims=True) + EPS) * gain


def rotate(tensor, cosine_table, sine_table):
    half = tensor.shape[-1] // 2
    first = tensor[..., :half]
    second = tensor[..., half:]
    return jnp.concatenate(
        [first * cosine_table - second * sine_table, second * cosine_table + first * sine_table],
        axis=-1,
    )


def inverse_rotate(tensor, cosine_table, sine_table):
    half = tensor.shape[-1] // 2
    first = tensor[..., :half]
    second = tensor[..., half:]
    return jnp.concatenate(
        [first * cosine_table + second * sine_table, second * cosine_table - first * sine_table],
        axis=-1,
    )


def angles(positions):
    half = HEAD_SIZE // 2
    inverse = THETA ** (-(jnp.arange(half) * 2.0 / HEAD_SIZE))
    turned = positions.astype(jnp.float32)[:, None] * inverse.astype(jnp.float32)
    return (jnp.cos(turned), jnp.sin(turned))


def busy(microseconds):
    return pl.CostEstimate(
        flops=microseconds * 1150 * 10**6, bytes_accessed=microseconds * 10**6, transcendentals=0
    )


def turn_heads(value, cosine, sine):
    width = value.shape[1]
    lane = lax.broadcasted_iota(jnp.int32, value.shape, 1)
    half = HEAD_SIZE // 2
    partner = jnp.where(
        lane % HEAD_SIZE < half, pltpu.roll(value, width - half, 1), pltpu.roll(value, half, 1)
    )
    repeats = width // cosine.shape[1]
    return value * jnp.tile(cosine, (1, repeats)) + partner * jnp.tile(sine, (1, repeats))


def fetch(pairs, sems):
    copies = [pltpu.make_async_copy(*pair, sems.at[n]) for n, pair in enumerate(pairs)]
    for copy in copies:
        copy.start()
    for copy in copies:
        copy.wait()


def project_kernel(
    packed_ref, x_ref, cos_ref, sin_ref, normed_ref, q_ref, pair_ref, proj_ref, gains_ref, small_ref, sems
):
    count = packed_ref.shape[0]
    rows = proj_ref.shape[0] // count
    fetch(
        [
            (packed_ref.at[n, :rows, :], proj_ref.at[n * rows : (n + 1) * rows, :])
            for n in range(count)
        ]
        + [(packed_ref.at[n, rows:, :], small_ref.at[n]) for n in range(count)],
        sems,
    )
    small = [small_ref[n].astype(jnp.float32)[:1] for n in range(count)]
    bias_rows = proj_ref.shape[1] // count
    bias = jnp.concatenate([row[:, :bias_rows] for row in small], axis=1)
    gains = [
        jnp.concatenate([row[:, first : first + rows] for row in small], axis=1)
        for first in (bias_rows, bias_rows + rows)
    ]
    for n in range(2):
        gains_ref[n] = gains[n]
    x = x_ref[...].astype(jnp.float32)
    scale = lax.rsqrt(jnp.mean(x * x, axis=-1, keepdims=True) + EPS)
    normed = (x * scale * gains[0]).astype(jnp.bfloat16)
    normed_ref[...] = normed
    width = q_ref.shape[1]
    turned = width + KEY_VALUE_HEADS * HEAD_SIZE
    projected = jnp.dot(normed, proj_ref[...], preferred_element_type=jnp.float32) + bias
    rotated = turn_heads(projected[:, :turned], cos_ref[...], sin_ref[...])
    q_ref[...] = rotated[:, :width].astype(jnp.bfloat16)
    pair = jnp.concatenate([rotated[:, width:], projected[:, turned:]], axis=1).astype(jnp.bfloat16)
    pair_ref[...] = pair


def project(packed, x, cosine, sine):
    tokens, width = x.shape
    count, height, proj_width = packed.shape
    return pl.pallas_call(
        project_kernel,
        out_shape=(
            jax.ShapeDtypeStruct((tokens, width), jnp.bfloat16),
            jax.ShapeDtypeStruct((tokens, QUERY_HEADS * HEAD_SIZE), jnp.bfloat16),
            jax.ShapeDtypeStruct((tokens, 2 * KEY_VALUE_HEADS * HEAD_SIZE), jnp.bfloat16),
            jax.ShapeDtypeStruct((width, proj_width), jnp.bfloat16),
            jax.ShapeDtypeStruct((2, 1, width), jnp.float32),
        ),
        in_specs=[pl.BlockSpec(memory_space=pl.ANY)] + [in_vmem()] * 3,
        out_specs=(in_vmem(),) * 5,
        scratch_shapes=[
            pltpu.VMEM((count, height - width // count, proj_width), jnp.bfloat16),
            pltpu.SemaphoreType.DMA((2 * count,)),
        ],
        compiler_params=pltpu.CompilerParams(vmem_limit_bytes=VMEM),
        cost_estimate=busy(4),
        name="project",
    )(packed, x, cosine, sine)


def copies_kernel(value_ref, *refs):
    out_ref, sems = refs[-2:]
    fetch([(value_ref, out_ref.at[n]) for n in range(out_ref.shape[0])], sems)


def copies(value, count, earlier):
    return pl.pallas_call(
        copies_kernel,
        out_shape=jax.ShapeDtypeStruct((count,) + value.shape, value.dtype),
        in_specs=[in_vmem()] + [pl.BlockSpec(memory_space=pl.ANY)] * len(earlier),
        out_specs=pl.BlockSpec(memory_space=pl.ANY),
        scratch_shapes=[pltpu.SemaphoreType.DMA((count,))],
        compiler_params=pltpu.CompilerParams(vmem_limit_bytes=VMEM),
        cost_estimate=busy(2),
        name="copies",
    )(value, *earlier)


def project_back_kernel(
    place_ref, x_in, gain_ref, proj_in, cos_ref, sin_ref, normed_in, dq_in, grad_in, gain_two_ref, pieces_in, *refs
):
    input_grad_ref, kept_ref, sent_ref, stage_ref = refs[-11:-7]
    x_ref, proj_ref, normed_ref, dq_ref, grad_ref, pieces_ref, sems = refs[-7:]
    ins = (x_in, proj_in, normed_in, dq_in, grad_in, pieces_in)
    fetch(list(zip(ins, (x_ref, proj_ref, normed_ref, dq_ref, grad_ref, pieces_ref))), sems)
    z, core = place_ref[0], place_ref[1]
    key_width = KEY_VALUE_HEADS * HEAD_SIZE
    pair = pieces_ref[0].astype(jnp.float32)
    for n in range(1, pieces_ref.shape[0]):
        pair = pair + pieces_ref[n].astype(jnp.float32)
    keys = turn_heads(pair[:, :key_width], cos_ref[...], -sin_ref[...])
    pair = jnp.concatenate([keys, pair[:, key_width:]], axis=1).astype(jnp.bfloat16)
    turned = normed_ref[...].astype(jnp.float32).T.astype(jnp.bfloat16)
    stage_ref[...] = jnp.dot(turned, pair, preferred_element_type=jnp.float32)
    bias = jnp.concatenate(
        [
            jnp.sum(dq_ref[...].astype(jnp.float32), axis=0, keepdims=True),
            jnp.sum(pair.astype(jnp.float32), axis=0, keepdims=True),
        ],
        axis=1,
    )
    x = x_ref[...].astype(jnp.float32)
    scale = lax.rsqrt(jnp.mean(x * x, axis=-1, keepdims=True) + EPS)
    grad = lax.dot_general(
        jnp.concatenate([dq_ref[...], pair], axis=1),
        proj_ref[...],
        (((1,), (1,)), ((), ())),
        preferred_element_type=jnp.float32,
    )
    gain_one = jnp.sum(grad * x * scale, axis=0, keepdims=True)
    gained = grad * gain_ref[...]
    mean = jnp.mean(gained * x, axis=-1, keepdims=True)
    input_grad_ref[...] = grad_ref[...] + scale * gained - x * (scale * scale * scale * mean)

    rows = stage_ref.shape[0] // 8
    bias_rows = bias.shape[1] // 8
    blank = jnp.zeros((kept_ref.shape[1] - rows - 2, stage_ref.shape[1]), jnp.float32)
    for owner in range(8):
        at = lax.rem(owner // 2 - z + 4, 4)
        here = slice(owner * rows, (owner + 1) * rows)
        gain_two = gain_two_ref[:, here]
        first = jnp.concatenate(
            [bias[:, owner * bias_rows : (owner + 1) * bias_rows], gain_one[:, here]], axis=1
        )
        second = jnp.concatenate(
            [gain_two, jnp.zeros((1, stage_ref.shape[1] - rows), jnp.float32)], axis=1
        )
        both = jnp.concatenate([stage_ref[here, :], first, second, blank], axis=0).astype(jnp.bfloat16)

        @pl.when(core == owner % 2)
        def _(both=both, at=at):
            kept_ref[at] = both

        @pl.when(core != owner % 2)
        def _(both=both, at=at):
            sent_ref[at] = both


def project_back(place, x, gain, proj, cosine, sine, normed, dq, grad, gain_two, pieces, earlier):
    tokens, width = x.shape
    pair_width = pieces.shape[2]
    anywhere = pl.BlockSpec(memory_space=pl.ANY)
    out = jax.ShapeDtypeStruct((4, width // 8 + 16, pair_width), jnp.bfloat16)
    return pl.pallas_call(
        project_back_kernel,
        out_shape=(jax.ShapeDtypeStruct((tokens, width), jnp.float32), out, out),
        in_specs=[
            pl.BlockSpec(memory_space=pltpu.SMEM),
            anywhere,
            in_vmem(),
            anywhere,
            in_vmem(),
            in_vmem(),
            anywhere,
            anywhere,
            anywhere,
            in_vmem(),
            anywhere,
        ]
        + [anywhere] * len(earlier),
        out_specs=(in_vmem(),) * 3,
        scratch_shapes=[pltpu.VMEM((width, pair_width), jnp.float32)]
        + [pltpu.VMEM(a.shape, a.dtype) for a in (x, proj, normed, dq, grad, pieces)]
        + [pltpu.SemaphoreType.DMA((6,))],
        compiler_params=pltpu.CompilerParams(vmem_limit_bytes=VMEM),
        cost_estimate=busy(40),
        name="project_back",
    )(place, x, gain, proj, cosine, sine, normed, dq, grad, gain_two, pieces, *earlier)


def key_bias(low_ref, block_start, block, first_index):
    tokens = low_ref.shape[1]
    keys = block_start + lax.broadcasted_iota(jnp.int32, (block, tokens), 0)
    index = first_index + lax.broadcasted_iota(jnp.int32, (block, tokens), 1)
    return jnp.where((keys <= index) & (keys >= low_ref[...]), 0.0, NEG)


def head_places(tokens):
    group = QUERY_HEADS // KEY_VALUE_HEADS
    for h in range(QUERY_HEADS):
        g, i = divmod(h, group)
        yield g, slice(h * HEAD_SIZE, (h + 1) * HEAD_SIZE), slice(i * tokens, (i + 1) * tokens)


def attend_kernel(
    start_ref, q_in, kv_in, low_ref, x_in, out_in, gain_ref, *refs
):
    mixed_ref, lse_ref, attended_ref, middle_ref, normed_ref = refs[-17:-12]
    qt, s_ref, p_ref, bias_ref, m_ref, l_ref, acc_ref = refs[-12:-5]
    q_ref, kv_ref, x_ref, out_ref, sems = refs[-5:]
    pairs = [(q_in, q_ref), (kv_in, kv_ref), (x_in, x_ref), (out_in, out_ref)]
    loads = [pltpu.make_async_copy(*pair, sems.at[n]) for n, pair in enumerate(pairs)]
    for load in loads:
        load.start()
    for load in loads[:2]:
        load.wait()
    tokens = q_ref.shape[0]
    block, rows = s_ref.shape
    turned = (q_ref[...].astype(jnp.float32) * HEAD_SIZE ** (-0.5)).T.astype(jnp.bfloat16)
    for g, lanes, at in head_places(tokens):
        qt[g, :, at] = turned[lanes, :]
    m_ref[...] = jnp.full_like(m_ref, NEG)
    l_ref[...] = jnp.zeros_like(l_ref)
    acc_ref[...] = jnp.zeros_like(acc_ref)

    def visit(which, carry):
        block_start = pl.multiple_of(which * block, block)
        here = pl.ds(block_start, block)
        bias_ref[...] = key_bias(low_ref, block_start, block, start_ref[0])
        key_width = KEY_VALUE_HEADS * HEAD_SIZE
        values = kv_ref[here, key_width:].astype(jnp.float32).T.astype(jnp.bfloat16)
        for g in range(KEY_VALUE_HEADS):
            lanes = slice(g * HEAD_SIZE, (g + 1) * HEAD_SIZE)
            s_ref[...] = jnp.dot(kv_ref[here, lanes], qt[g], preferred_element_type=jnp.float32)
            for i in range(rows // tokens):
                at = slice(i * tokens, (i + 1) * tokens)
                s = s_ref[:, at] + bias_ref[...]
                old = m_ref[g, :, at]
                peak = jnp.maximum(old, jnp.max(s, axis=0, keepdims=True))
                e = jnp.exp(s - peak)
                scale = jnp.exp(old - peak)
                m_ref[g, :, at] = peak
                l_ref[g, :, at] = l_ref[g, :, at] * scale + jnp.sum(e, axis=0, keepdims=True)
                acc_ref[g, :, at] = acc_ref[g, :, at] * scale
                p_ref[:, at] = e.astype(jnp.bfloat16)
            acc_ref[g] += jnp.dot(values[lanes, :], p_ref[...], preferred_element_type=jnp.float32)
        return carry

    lax.fori_loop(start_ref[1], start_ref[2], visit, 0)
    mixed = [acc_ref[g, :, at] / l_ref[g, :, at] for g, _, at in head_places(tokens)]
    mixed = jnp.concatenate(mixed, axis=0).T
    mixed_ref[...] = mixed
    lse_ref[...] = m_ref[...] + jnp.log(l_ref[...])
    attended = mixed.astype(jnp.bfloat16)
    attended_ref[...] = attended
    for load in loads[2:]:
        load.wait()
    middle = x_ref[...].astype(jnp.float32) + jnp.dot(
        attended, out_ref[...], preferred_element_type=jnp.float32
    )
    middle_ref[...] = middle
    scale = lax.rsqrt(jnp.mean(middle * middle, axis=-1, keepdims=True) + EPS)
    normed_ref[...] = (middle * scale * gain_ref[...]).astype(jnp.bfloat16)


def attend_back_kernel(
    start_ref, q_ref, kv_ref, low_ref, dmix_ref, mixed_ref, lse_ref, cos_ref, sin_ref, dq_ref, dkv_ref,
    qs, qt, ms, mt, delta_ref, s_ref, dp_ref, p_ref, g_ref, bias_ref, acc_ref,
):
    tokens = q_ref.shape[0]
    block, rows = s_ref.shape
    key_width = KEY_VALUE_HEADS * HEAD_SIZE
    q = q_ref[...].astype(jnp.float32) * HEAD_SIZE ** (-0.5)
    dmix = dmix_ref[...].astype(jnp.float32)
    q_turned = q.T.astype(jnp.bfloat16)
    dmix_turned = dmix.T
    weighed = (dmix * mixed_ref[...]).T
    q = q.astype(jnp.bfloat16)
    for g, lanes, at in head_places(tokens):
        qs[g, at, :] = q[:, lanes]
        ms[g, at, :] = dmix_ref[:, lanes]
        qt[g, :, at] = q_turned[lanes, :]
        mt[g, :, at] = dmix_turned[lanes, :].astype(jnp.bfloat16)
        delta_ref[g, :, at] = jnp.sum(weighed[lanes, :], axis=0, keepdims=True)
    acc_ref[...] = jnp.zeros_like(acc_ref)
    dkv_ref[...] = jnp.zeros_like(dkv_ref)

    def visit(which, carry):
        block_start = pl.multiple_of(which * block, block)
        here = pl.ds(block_start, block)
        bias_ref[...] = key_bias(low_ref, block_start, block, start_ref[0])
        keys_turned = kv_ref[here, :key_width].astype(jnp.float32).T.astype(jnp.bfloat16)
        grads = [None] * (2 * KEY_VALUE_HEADS)
        for g in range(KEY_VALUE_HEADS):
            lanes = slice(g * HEAD_SIZE, (g + 1) * HEAD_SIZE)
            s_ref[...] = jnp.dot(kv_ref[here, lanes], qt[g], preferred_element_type=jnp.float32)
            values = kv_ref[here, key_width + g * HEAD_SIZE : key_width + (g + 1) * HEAD_SIZE]
            dp_ref[...] = jnp.dot(values, mt[g], preferred_element_type=jnp.float32)
            for i in range(rows // tokens):
                at = slice(i * tokens, (i + 1) * tokens)
                p = jnp.exp(s_ref[:, at] + bias_ref[...] - lse_ref[g, :, at])
                p_ref[:, at] = p.astype(jnp.bfloat16)
                g_ref[:, at] = (p * (dp_ref[:, at] - delta_ref[g, :, at])).astype(jnp.bfloat16)
            acc_ref[g] += jnp.dot(keys_turned[lanes, :], g_ref[...], preferred_element_type=jnp.float32)
            grads[g] = jnp.dot(g_ref[...], qs[g], preferred_element_type=jnp.float32)
            grads[KEY_VALUE_HEADS + g] = jnp.dot(
                p_ref[...], ms[g], preferred_element_type=jnp.float32
            )
        grads = jnp.concatenate(grads, axis=1).astype(jnp.bfloat16)
        for n in range(block // tokens):
            dkv_ref[which * (block // tokens) + n] = grads[n * tokens : (n + 1) * tokens, :]
        return carry

    lax.fori_loop(start_ref[1], start_ref[2], visit, 0)
    dq = [acc_ref[g, :, at] for g, _, at in head_places(tokens)]
    dq = jnp.concatenate(dq, axis=0).T * HEAD_SIZE ** (-0.5)
    dq_ref[...] = turn_heads(dq, cos_ref[...], -sin_ref[...]).astype(jnp.bfloat16)


def in_vmem():
    return pl.BlockSpec(memory_space=pltpu.VMEM)


def attend(start, queries, pairs, low, x, out_matrix, gain, earlier):
    tokens, width = queries.shape
    rows = QUERY_HEADS // KEY_VALUE_HEADS * tokens
    block = 4 * tokens
    heads = KEY_VALUE_HEADS
    return pl.pallas_call(
        attend_kernel,
        out_shape=(
            jax.ShapeDtypeStruct((tokens, width), jnp.float32),
            jax.ShapeDtypeStruct((heads, 1, rows), jnp.float32),
            jax.ShapeDtypeStruct((tokens, width), jnp.bfloat16),
            jax.ShapeDtypeStruct(x.shape, jnp.float32),
            jax.ShapeDtypeStruct(x.shape, jnp.bfloat16),
        ),
        in_specs=[
            pl.BlockSpec(memory_space=pltpu.SMEM),
            pl.BlockSpec(memory_space=pl.ANY),
            pl.BlockSpec(memory_space=pl.ANY),
            in_vmem(),
            pl.BlockSpec(memory_space=pl.ANY),
            pl.BlockSpec(memory_space=pl.ANY),
            in_vmem(),
        ]
        + [pl.BlockSpec(memory_space=pl.ANY)] * len(earlier),
        out_specs=(in_vmem(),) * 5,
        scratch_shapes=[
            pltpu.VMEM((heads, HEAD_SIZE, rows), jnp.bfloat16),
            pltpu.VMEM((block, rows), jnp.float32),
            pltpu.VMEM((block, rows), jnp.bfloat16),
            pltpu.VMEM((block, tokens), jnp.float32),
            pltpu.VMEM((heads, 1, rows), jnp.float32),
            pltpu.VMEM((heads, 1, rows), jnp.float32),
            pltpu.VMEM((heads, HEAD_SIZE, rows), jnp.float32),
            pltpu.VMEM(queries.shape, queries.dtype),
            pltpu.VMEM(pairs.shape, pairs.dtype),
            pltpu.VMEM(x.shape, x.dtype),
            pltpu.VMEM(out_matrix.shape, out_matrix.dtype),
            pltpu.SemaphoreType.DMA((4,)),
        ],
        compiler_params=pltpu.CompilerParams(vmem_limit_bytes=VMEM),
        cost_estimate=busy(9),
        name="attend",
    )(start, queries, pairs, low, x, out_matrix, gain, *earlier)


def attend_back(start, queries, pairs, low, mix_grad, mixed, lse, cosine, sine):
    tokens, width = queries.shape
    rows = QUERY_HEADS // KEY_VALUE_HEADS * tokens
    block = 4 * tokens
    heads = KEY_VALUE_HEADS
    return pl.pallas_call(
        attend_back_kernel,
        out_shape=(
            jax.ShapeDtypeStruct((tokens, width), jnp.bfloat16),
            jax.ShapeDtypeStruct((pairs.shape[0] // tokens, tokens, pairs.shape[1]), jnp.bfloat16),
        ),
        in_specs=[pl.BlockSpec(memory_space=pltpu.SMEM)] + [in_vmem()] * 8,
        out_specs=(in_vmem(), in_vmem()),
        scratch_shapes=[
            pltpu.VMEM((heads, rows, HEAD_SIZE), jnp.bfloat16),
            pltpu.VMEM((heads, HEAD_SIZE, rows), jnp.bfloat16),
            pltpu.VMEM((heads, rows, HEAD_SIZE), jnp.bfloat16),
            pltpu.VMEM((heads, HEAD_SIZE, rows), jnp.bfloat16),
            pltpu.VMEM((heads, 1, rows), jnp.float32),
            pltpu.VMEM((block, rows), jnp.float32),
            pltpu.VMEM((block, rows), jnp.float32),
            pltpu.VMEM((block, rows), jnp.bfloat16),
            pltpu.VMEM((block, rows), jnp.bfloat16),
            pltpu.VMEM((block, tokens), jnp.float32),
            pltpu.VMEM((heads, HEAD_SIZE, rows), jnp.float32),
        ],
        compiler_params=pltpu.CompilerParams(vmem_limit_bytes=VMEM),
        cost_estimate=busy(25),
        name="attend_back",
    )(start, queries, pairs, low, mix_grad, mixed, lse, cosine, sine)


def split_kernel(place_ref, matrix_ref, down_ref, kept_ref, sent_ref, padded_ref):
    padded_ref[: down_ref.shape[0], :] = down_ref[...]
    padded_ref[down_ref.shape[0] :, :] = jnp.zeros(
        (padded_ref.shape[0] - down_ref.shape[0], down_ref.shape[1]), down_ref.dtype
    )
    z, core = place_ref[0], place_ref[1]
    width, lanes = matrix_ref.shape[1] // 16, kept_ref.shape[2] // 2
    for owner in range(8):
        at = lax.rem(owner // 2 - z + 4, 4)
        gate = matrix_ref[:, owner * width : (owner + 1) * width].astype(jnp.float32)
        up = matrix_ref[:, (8 + owner) * width : (9 + owner) * width].astype(jnp.float32)
        blank = jnp.zeros((gate.shape[0], lanes - width), jnp.float32)
        both = jnp.concatenate([gate, blank, up, blank], axis=1).astype(jnp.bfloat16)

        @pl.when(core == owner % 2)
        def _(both=both, at=at):
            kept_ref[at] = both

        @pl.when(core != owner % 2)
        def _(both=both, at=at):
            sent_ref[at] = both


def split_columns(place, matrix, down, lanes):
    rows = matrix.shape[0]
    out = jax.ShapeDtypeStruct((4, rows, 2 * lanes), matrix.dtype)
    return pl.pallas_call(
        split_kernel,
        out_shape=(out, out, jax.ShapeDtypeStruct((lanes, down.shape[1]), down.dtype)),
        in_specs=[pl.BlockSpec(memory_space=pltpu.SMEM), in_vmem(), in_vmem()],
        out_specs=(in_vmem(),) * 3,
        compiler_params=pltpu.CompilerParams(vmem_limit_bytes=VMEM),
        cost_estimate=busy(4),
        name="split_columns",
    )(place, matrix, down)


def pack_kernel(cuts, at_ref, *refs):
    pieces, whole, (out_ref, sems) = refs[:-3], refs[-3], refs[-2:]
    rows = 16
    height = len(cuts) * rows
    tail = pltpu.make_async_copy(whole.at[height:, :], out_ref.at[height:, :], sems.at[len(cuts)])
    tail.start()

    @pl.when(at_ref[len(cuts)] == 1)
    def _():
        pairs = []
        for n, (which, lead, first) in enumerate(cuts):
            piece = pieces[which] if lead is None else pieces[which].at[lead]
            start = pl.multiple_of(at_ref[n] * rows, rows)
            pairs.append((piece.at[first : first + rows, :], out_ref.at[pl.ds(start, rows), :]))
        fetch(pairs, sems)

    @pl.when(at_ref[len(cuts)] == 0)
    def _():
        fetch([(whole.at[:height, :], out_ref.at[:height, :])], sems)

    tail.wait()


def pack_parts(at, arrays, cuts, whole):
    return pl.pallas_call(
        functools.partial(pack_kernel, tuple(cuts)),
        out_shape=jax.ShapeDtypeStruct(whole.shape, whole.dtype),
        in_specs=[pl.BlockSpec(memory_space=pltpu.SMEM)]
        + [pl.BlockSpec(memory_space=pl.ANY)] * (len(arrays) + 1),
        out_specs=in_vmem(),
        scratch_shapes=[pltpu.SemaphoreType.DMA((len(cuts) + 1,))],
        compiler_params=pltpu.CompilerParams(vmem_limit_bytes=VMEM),
        cost_estimate=busy(2),
        name="pack_parts",
    )(at, *arrays, whole)


def down_places(width, row_tiles):
    full, tile = 2 * row_tiles, 16
    extra = -(-width // 16 // tile) * tile - tile
    rest = (width - full * extra) // (16 - full)
    for part in range(full):
        yield part, 8 * tile, extra, part * extra
    for part in range(full, 16):
        yield part, 0, rest, full * extra + (part - full) * rest


def feed_kernel(at_ref, *refs):
    normed_in, (grads_in, down_in), gate_up_in = refs[:8], refs[8:10], refs[10:15]
    hidden_ref, own_ref, other_ref, out_ref = refs[15:19]
    normed_ref, grads_ref, gate_up_ref, down_ref, joined_ref, turned_ref, stage_ref, sems = refs[19:]
    tokens = normed_in[0].shape[0]
    lanes = hidden_ref.shape[1]
    step = 2 * tokens
    tile = 16
    pairs = [(down_in, down_ref)]
    rows = gate_up_ref.shape[0] // 8
    pieces = [gate_up_in[0].at[0], gate_up_in[1].at[0]]
    pieces += [ref.at[part * rows : (part + 1) * rows, :] for ref in gate_up_in[2:] for part in range(2)]
    for n, piece in enumerate(pieces):
        start = pl.multiple_of(at_ref[n] * rows, 16)
        pairs.append((piece, gate_up_ref.at[pl.ds(start, rows), :]))
    for n in range(8):
        here = slice(n * tokens, (n + 1) * tokens)
        pairs.append((normed_in[n], normed_ref.at[here, :]))
        pairs.append((grads_in.at[at_ref[n]], grads_ref.at[here, :]))
    loads = [pltpu.make_async_copy(*pair, sems.at[n]) for n, pair in enumerate(pairs)]
    for load in loads:
        load.start()
    for load in loads[:9]:
        load.wait()
    for part in range(4):
        for load in loads[9 + 4 * part : 13 + 4 * part]:
            load.wait()
        here = slice(part * step, (part + 1) * step)
        gate = jnp.dot(normed_ref[here, :], gate_up_ref[:, :lanes], preferred_element_type=jnp.float32)
        up = jnp.dot(normed_ref[here, :], gate_up_ref[:, lanes:], preferred_element_type=jnp.float32)
        hidden_grad = lax.dot_general(
            grads_ref[here, :], down_ref[...], (((1,), (1,)), ((), ())), preferred_element_type=jnp.float32
        )
        sg = 1.0 / (1.0 + jnp.exp(-gate))
        act = gate * sg
        hidden_ref[here, :] = (act * up).astype(jnp.bfloat16)
        joined_ref[here, :lanes] = (hidden_grad * up * sg * (1.0 + gate * (1.0 - sg))).astype(
            jnp.bfloat16
        )
        joined_ref[here, lanes:] = (hidden_grad * act).astype(jnp.bfloat16)
        back = lax.dot_general(
            joined_ref[here, :], gate_up_ref[...], (((1,), (1,)), ((), ())), preferred_element_type=jnp.float32
        )
        own_ref[part] = back[:tokens]
        other_ref[part] = back[tokens:].astype(jnp.bfloat16)
        turned_ref[:, here] = normed_ref[here, :].astype(jnp.float32).T.astype(jnp.bfloat16)

    rows = stage_ref.shape[0] // 8
    for half in range(2):
        stage_ref[...] = jnp.dot(
            turned_ref[...],
            joined_ref[:, half * lanes : (half + 1) * lanes],
            preferred_element_type=jnp.float32,
        )
        for r in range(rows // tile):
            for k in range(8):
                first = k * rows + r * tile
                out_ref[2 * r + half, k * tile : (k + 1) * tile, :] = stage_ref[
                    first : first + tile, :
                ].astype(jnp.bfloat16)
    for part in range(4):
        here = slice(part * step, (part + 1) * step)
        turned_ref[:, here] = grads_ref[here, :].astype(jnp.float32).T.astype(jnp.bfloat16)
    stage_ref[...] = jnp.dot(turned_ref[...], hidden_ref[...], preferred_element_type=jnp.float32)
    for part, first, height, source in down_places(stage_ref.shape[0], rows // tile):
        out_ref[part, first : first + height, :] = stage_ref[source : source + height, :].astype(
            jnp.bfloat16
        )
        if first == 0:
            out_ref[part, height:, :] = jnp.zeros((out_ref.shape[1] - height, lanes), jnp.bfloat16)


def feed(at, normed, grads, gate_up, down):
    tokens, width = normed[0].shape
    lanes = down.shape[0]
    part = 8 * 16 + -(-width // 16 // 16) * 16 - 16
    return pl.pallas_call(
        feed_kernel,
        out_shape=(
            jax.ShapeDtypeStruct((8 * tokens, lanes), jnp.bfloat16),
            jax.ShapeDtypeStruct((4, tokens, width), jnp.float32),
            jax.ShapeDtypeStruct((4, tokens, width), jnp.bfloat16),
            jax.ShapeDtypeStruct((16, part, lanes), jnp.bfloat16),
        ),
        in_specs=[pl.BlockSpec(memory_space=pltpu.SMEM)] + [pl.BlockSpec(memory_space=pl.ANY)] * 15,
        out_specs=(in_vmem(),) * 4,
        scratch_shapes=[
            pltpu.VMEM((8 * tokens, width), jnp.bfloat16),
            pltpu.VMEM((8 * tokens, width), jnp.bfloat16),
            pltpu.VMEM((width, 2 * lanes), jnp.bfloat16),
            pltpu.VMEM(down.shape, down.dtype),
            pltpu.VMEM((8 * tokens, 2 * lanes), jnp.bfloat16),
            pltpu.VMEM((width, 8 * tokens), jnp.bfloat16),
            pltpu.VMEM((width, lanes), jnp.float32),
            pltpu.SemaphoreType.DMA((25,)),
        ],
        compiler_params=pltpu.CompilerParams(vmem_limit_bytes=VMEM),
        cost_estimate=busy(18),
        name="feed",
    )(at, *normed, grads, down, *gate_up)


def feed_out_kernel(at_ref, down_ref, *refs):
    hidden, out_ref = refs[0], refs[-1]
    tokens = out_ref.shape[1]
    for n in range(4):
        here = slice(2 * n * tokens, 2 * (n + 1) * tokens)
        out = jnp.dot(hidden[here, :], down_ref[...], preferred_element_type=jnp.float32)
        for part in range(2):
            out_ref[at_ref[2 * n + part]] = out[part * tokens : (part + 1) * tokens].astype(
                jnp.bfloat16
            )


def feed_out(at, down, hidden, earlier):
    tokens = hidden.shape[0] // 8
    return pl.pallas_call(
        feed_out_kernel,
        out_shape=jax.ShapeDtypeStruct((8, tokens, down.shape[1]), jnp.bfloat16),
        in_specs=[pl.BlockSpec(memory_space=pltpu.SMEM)]
        + [in_vmem()] * 2
        + [pl.BlockSpec(memory_space=pl.ANY)] * len(earlier),
        out_specs=in_vmem(),
        compiler_params=pltpu.CompilerParams(vmem_limit_bytes=VMEM),
        cost_estimate=busy(4),
        name="feed_out",
    )(at, down, hidden, *earlier)


def owner_parts_kernel(place_ref, parts_ref, *refs):
    kept_ref, sent_ref, whole_ref = refs[-3:]
    z, core = place_ref[0], place_ref[1]
    rows = kept_ref.shape[1]

    def total(here):
        value = parts_ref[0, here, :].astype(jnp.float32)
        for n in range(1, parts_ref.shape[0]):
            value = value + parts_ref[n, here, :].astype(jnp.float32)
        return value.astype(jnp.bfloat16)

    for owner in range(8):
        at = lax.rem(owner // 2 - z + 4, 4)
        part = total(slice(owner * rows, (owner + 1) * rows))
        whole_ref[owner * rows : (owner + 1) * rows, :] = part

        @pl.when(core == owner % 2)
        def _(part=part, at=at):
            kept_ref[at] = part

        @pl.when(core != owner % 2)
        def _(part=part, at=at):
            sent_ref[at] = part

    for first in range(8 * rows, whole_ref.shape[0], rows):
        whole_ref[first : first + rows, :] = total(slice(first, first + rows))


def owner_parts(place, parts, rows, earlier):
    _, height, width = parts.shape
    out = jax.ShapeDtypeStruct((4, rows, width), jnp.bfloat16)
    return pl.pallas_call(
        owner_parts_kernel,
        out_shape=(out, out, jax.ShapeDtypeStruct((height, width), jnp.bfloat16)),
        in_specs=[pl.BlockSpec(memory_space=pltpu.SMEM), in_vmem()]
        + [pl.BlockSpec(memory_space=pl.ANY)] * len(earlier),
        out_specs=(in_vmem(),) * 3,
        compiler_params=pltpu.CompilerParams(vmem_limit_bytes=VMEM),
        cost_estimate=busy(3),
        name="owner_parts",
    )(place, parts, *earlier)


def rows_grads_kernel(place_ref, *refs):
    kept_ref, sent_ref, stage_ref = refs[-3:]
    pairs = (len(refs) - 3) // 2
    rest_ref = refs[2 * pairs] if (len(refs) - 3) % 2 else None
    z, core = place_ref[0], place_ref[1]
    rows = stage_ref.shape[0] // 8
    first = 0
    for n in range(pairs):
        left, right = refs[2 * n], refs[2 * n + 1]
        turned = left[...].astype(jnp.float32).T.astype(jnp.bfloat16)
        stage_ref[:, first : first + right.shape[1]] = jnp.dot(
            turned, right[...], preferred_element_type=jnp.float32
        )
        first += right.shape[1]
    for owner in range(8):
        at = lax.rem(owner // 2 - z + 4, 4)

        @pl.when(core == owner % 2)
        def _(owner=owner, at=at):
            kept_ref[at, :rows, :] = stage_ref[owner * rows : (owner + 1) * rows, :].astype(jnp.bfloat16)
            if rest_ref is not None:
                kept_ref[at, rows:, :] = rest_ref[owner]

        @pl.when(core != owner % 2)
        def _(owner=owner, at=at):
            sent_ref[at, :rows, :] = stage_ref[owner * rows : (owner + 1) * rows, :].astype(jnp.bfloat16)
            if rest_ref is not None:
                sent_ref[at, rows:, :] = rest_ref[owner]


def rows_grads(place, pairs, rest=None):
    height = pairs[0][0].shape[1]
    width = sum(right.shape[1] for _, right in pairs)
    rows = height // 8 + (0 if rest is None else rest.shape[1])
    arrays = [array for pair in pairs for array in pair] + ([] if rest is None else [rest])
    out = jax.ShapeDtypeStruct((4, rows, width), jnp.bfloat16)
    return pl.pallas_call(
        rows_grads_kernel,
        out_shape=(out, out),
        in_specs=[pl.BlockSpec(memory_space=pltpu.SMEM)] + [in_vmem()] * len(arrays),
        out_specs=(in_vmem(), in_vmem()),
        scratch_shapes=[pltpu.VMEM((height, width), jnp.float32)],
        compiler_params=pltpu.CompilerParams(vmem_limit_bytes=VMEM),
        cost_estimate=busy(3),
        name="rows_grads",
    )(place, *arrays)


def join_kernel(parts_in, gate_up_out, down_ref, parts_ref, gate_up_ref, stage_ref, in_sems, out_sems):
    width = gate_up_ref.shape[1] // 16
    tile = 16
    loads = [
        pltpu.make_async_copy(parts_in.at[n], parts_ref.at[n], in_sems.at[n])
        for n in range(parts_in.shape[0])
    ]
    for load in loads:
        load.start()
    stores = []
    for r in range(gate_up_ref.shape[0] // tile):
        here = slice(r * tile, (r + 1) * tile)
        for half in range(2):
            part = 2 * r + half
            loads[part].wait()
            columns = [
                parts_ref[part, k * tile : (k + 1) * tile, :].astype(jnp.float32)[:, :width]
                for k in range(8)
            ]
            gate_up_ref[here, half * 8 * width : (half + 1) * 8 * width] = jnp.concatenate(
                columns, axis=1
            )
        stores.append(
            pltpu.make_async_copy(gate_up_ref.at[here, :], gate_up_out.at[here, :], out_sems.at[r])
        )
        stores[-1].start()
    for load in loads[2 * len(stores) :]:
        load.wait()
    for part, first, height, source in down_places(stage_ref.shape[0], len(stores)):
        stage_ref[source : source + height, :] = parts_ref[part, first : first + height, :].astype(
            jnp.float32
        )
    for block in range(stage_ref.shape[0] // 128):
        at = slice(block * 128, (block + 1) * 128)
        down_ref[:, at] = stage_ref[at, :].T[:width]
    for store in stores:
        store.wait()


def join_columns(parts, rows, width, model_width):
    anywhere = pl.BlockSpec(memory_space=pl.ANY)
    return pl.pallas_call(
        join_kernel,
        out_shape=(
            jax.ShapeDtypeStruct((rows, 16 * width), jnp.float32),
            jax.ShapeDtypeStruct((width, model_width), jnp.float32),
        ),
        in_specs=[anywhere],
        out_specs=(anywhere, in_vmem()),
        scratch_shapes=[
            pltpu.VMEM(parts.shape, parts.dtype),
            pltpu.VMEM((rows, 16 * width), jnp.float32),
            pltpu.VMEM((model_width, parts.shape[2]), jnp.float32),
            pltpu.SemaphoreType.DMA((16,)),
            pltpu.SemaphoreType.DMA((rows // 16,)),
        ],
        compiler_params=pltpu.CompilerParams(vmem_limit_bytes=VMEM),
        cost_estimate=busy(4),
        name="join_columns",
    )(parts)


def columns_kernel(*refs):
    ins, out_ref, early_ref, late_ref, sems = refs[:10], refs[-4], refs[-3], refs[-2], refs[-1]
    lead_early = [ref.at[0] if len(ref.shape) == 3 else ref for ref in ins[:5]]
    lead_late = [ref.at[0] if len(ref.shape) == 3 else ref for ref in ins[5:]]
    fetch(
        [(ref, early_ref.at[n]) for n, ref in enumerate(lead_early)]
        + [(ref, late_ref.at[n]) for n, ref in enumerate(lead_late)],
        sems,
    )
    _, rows, width = early_ref.shape
    columns = out_ref.shape[2]
    blank = jnp.zeros((out_ref.shape[1] - rows, columns), jnp.float32)
    count = width // columns
    for n in range(out_ref.shape[0]):
        ref = early_ref if n < count else late_ref
        first = (n if n < count else n - count) * columns
        total = ref[0, :, first : first + columns].astype(jnp.float32)
        for m in range(1, 5):
            total = total + ref[m, :, first : first + columns].astype(jnp.float32)
        if n < count:
            total = jnp.concatenate([total, blank], axis=0)
        out_ref[n] = total.astype(jnp.bfloat16)


def column_parts(early, late):
    early_shape, late_shape = early[-1].shape, late[-1].shape
    columns = (early_shape[1] + late_shape[1]) // 16
    return pl.pallas_call(
        columns_kernel,
        out_shape=jax.ShapeDtypeStruct((16, late_shape[0], columns), jnp.bfloat16),
        in_specs=[pl.BlockSpec(memory_space=pl.ANY)] * 10,
        out_specs=in_vmem(),
        scratch_shapes=[
            pltpu.VMEM((5,) + early_shape, jnp.bfloat16),
            pltpu.VMEM((5,) + late_shape, jnp.bfloat16),
            pltpu.SemaphoreType.DMA((10,)),
        ],
        compiler_params=pltpu.CompilerParams(vmem_limit_bytes=VMEM),
        cost_estimate=busy(30),
        name="column_parts",
    )(*early, *late)


def core_swap(value):
    return lax.ppermute(value, "wa", [(i, i ^ 1) for i in range(8)])


def z_shift(value, step):
    return lax.ppermute(value, "wa", [(i, (i + 2 * step) % 8) for i in range(8)])


def ctx_exchange(value):
    return lax.all_to_all(value, "ctx", 0, 0, tiled=True)


def ctx_gather(value):
    return ctx_exchange(jnp.broadcast_to(value[None], (16,) + value.shape))


STEPS = (0, 1, 3, 2)


def gather_tokens(value):
    pieces = [z_shift(value, step) if step else value for step in STEPS]
    return [(piece, core_swap(piece)) for piece in pieces]


def return_tokens(paired):
    return [z_shift(mine, -step) if step else mine for step, mine in zip(STEPS, paired)]


def reduce_rows(kept, sent):
    other = core_swap(sent)
    pieces = [kept, other]
    for step in STEPS[1:]:
        mine = kept[step].astype(jnp.float32) + other[step].astype(jnp.float32)
        pieces.append(z_shift(mine.astype(jnp.bfloat16), step))
    return pieces


def after(value, *others):
    held = sum(other[(0,) * other.ndim].astype(jnp.float32) for other in others) * 0.0
    return value + held.astype(value.dtype)


def spread_kernel(parts_ref, left_ref, right_ref, bias_ref, gain_one_ref, gain_two_ref):
    columns = parts_ref.shape[2]
    rows = left_ref.shape[0]
    count = left_ref.shape[1] // columns
    small = []
    for n in range(parts_ref.shape[0]):
        part = parts_ref[n].astype(jnp.float32)
        if n < count:
            left_ref[:, n * columns : (n + 1) * columns] = part[:rows]
        else:
            right_ref[:, (n - count) * columns : (n - count + 1) * columns] = part[:rows]
        small.append(part[rows : rows + 8])
    small = jnp.concatenate(small[-2:], axis=1)
    bias_rows = bias_ref.shape[1]
    bias_ref[...] = small[:1, :bias_rows]
    gain_one_ref[...] = small[:1, bias_rows : bias_rows + rows]
    gain_two_ref[...] = small[1:2, :rows]


def spread_columns(parts, rows, width, bias_rows):
    count, _, columns = parts.shape
    shapes = [(rows, width), (rows, count * columns - width), (1, bias_rows), (1, rows), (1, rows)]
    return pl.pallas_call(
        spread_kernel,
        out_shape=tuple(jax.ShapeDtypeStruct(shape, jnp.float32) for shape in shapes),
        in_specs=[in_vmem()],
        out_specs=(in_vmem(),) * 5,
        compiler_params=pltpu.CompilerParams(vmem_limit_bytes=VMEM),
        cost_estimate=busy(1),
        name="spread_columns",
    )(parts)


def on_device(
    layer_input,
    positions,
    attention_gain,
    projection,
    projection_biases,
    output_matrix,
    feed_gain,
    gate_up_matrix,
    down_matrix,
    cotangent,
):
    place = lax.axis_index("wa").astype(jnp.int32)
    z, core = place // 2, place % 2
    ctx = lax.axis_index("ctx").astype(jnp.int32)
    rows = projection.shape[0]
    tokens = layer_input.shape[1]
    query_width = QUERY_HEADS * HEAD_SIZE
    key_width = KEY_VALUE_HEADS * HEAD_SIZE
    width = layer_input.shape[2]
    proj_width = projection.shape[1]
    bias_rows = projection_biases.shape[0]
    slice_width = down_matrix.shape[0]
    lanes = -(-slice_width // 128) * 128
    tile = 16
    sources = [(z + 4 - step) % 4 for step in STEPS]

    small = jnp.concatenate([projection_biases, attention_gain, feed_gain])
    small = jnp.pad(small[None], ((0, tile - 1), (0, proj_width - small.shape[0])))
    packed = lax.all_gather(jnp.concatenate([projection, small], axis=0), "wa", axis=0)

    spot = jnp.stack([z, core])
    local_places = jnp.stack([p for s in sources for p in (2 * s + core, 2 * s + 1 - core)])
    kept, sent, down = split_columns(spot, gate_up_matrix, down_matrix, lanes)
    other = core_swap(sent)
    gate_up = [jnp.concatenate([kept[step], other[step]], axis=0) for step in STEPS[1:]]

    layer_rows = layer_input[0]
    query_pos = positions[0]
    cosine, sine = angles(query_pos)
    cosine = jnp.tile(cosine, (1, 4))
    sine = jnp.tile(jnp.concatenate([-sine, sine], axis=1), (1, 2))
    first_normed, queries, pair, full_proj, gains = project(packed, layer_rows, cosine, sine)
    gain_one, gain_two = gains[0], gains[1]
    complete_output = lax.all_gather(output_matrix, "wa", axis=0, tiled=True)
    out_grad = cotangent[0]
    all_grads = lax.all_gather(out_grad, "wa", axis=0)

    pairs_sent = copies(pair, 16, gate_up)
    gate_up = [z_shift(piece, step) for step, piece in zip(STEPS[1:], gate_up)]
    pairs = ctx_exchange(pairs_sent).reshape(16 * tokens, 2 * key_width)
    low = ctx * tokens + jnp.arange(tokens, dtype=jnp.int32) - query_pos
    block = 4 * tokens
    start = jnp.stack(
        [
            ctx * tokens,
            jnp.maximum(jnp.min(low), 0) // block,
            (ctx * tokens + tokens + block - 1) // block,
        ]
    ).astype(jnp.int32)
    low = low[None]
    mixed, lse, attention_output, middle_state, second_normed = attend(
        start, queries, pairs, low, layer_rows, complete_output, gain_two, gate_up[:2]
    )

    normed_pairs = gather_tokens(second_normed)
    flat_normed = [piece for pair in normed_pairs for piece in pair]
    hidden, own, other, parts = feed(
        local_places, flat_normed, all_grads, [kept, other] + gate_up, down
    )
    other = core_swap(other)
    paired = [
        (own[n] + other[n].astype(jnp.float32)).astype(jnp.bfloat16) for n in range(len(STEPS))
    ]
    returned = return_tokens(paired)

    normed_two_grad = sum(piece.astype(jnp.float32) for piece in returned)
    parts = ctx_exchange(parts)

    _, norm_two_pull = jax.vjp(norm_rows, middle_state, gain_two[0])
    middle_part, gain_two_local = norm_two_pull(normed_two_grad)
    middle_grad = out_grad.astype(jnp.float32) + middle_part
    middle_lower = middle_grad.astype(jnp.bfloat16)
    mix_grad = column_product(middle_lower, complete_output).astype(jnp.bfloat16)
    query_back, pair_grad = attend_back(
        start, queries, pairs, low, mix_grad, mixed, lse, cosine, sine
    )
    early = reduce_rows(
        *rows_grads(spot, [(attention_output, middle_lower), (first_normed, query_back)])
    )

    result = feed_out(local_places, down, hidden, [pair_grad])
    result = lax.psum_scatter(result, "wa", scatter_dimension=0)
    pieces = ctx_exchange(pair_grad)
    input_grad, kept, sent = project_back(
        spot,
        layer_rows,
        gain_one,
        full_proj,
        cosine,
        sine,
        first_normed,
        query_back,
        middle_grad,
        gain_two_local[None],
        pieces,
        [],
    )
    late = reduce_rows(kept, sent)

    kept, sent, whole = owner_parts(spot, parts, tile, [pair_grad] + early[2:])
    other = core_swap(sent)
    parts = [
        z_shift(jnp.concatenate([kept[step], other[step]], axis=0), step) for step in STEPS[1:]
    ]
    cuts = [(0, 0, 0), (1, 0, 0)] + [(n, None, part * tile) for n in (2, 3, 4) for part in (0, 1)]
    exchanged = (ctx < 2 * rows // tile).astype(jnp.int32)
    parts = pack_parts(
        jnp.concatenate([local_places, exchanged[None]]), [kept, other] + parts, cuts, whole
    )
    parts = lax.all_gather(parts, "ctx", axis=0)
    gate_up_total, down_total = join_columns(parts, rows, slice_width, width)

    mine = ctx_exchange(column_parts(early, late))
    mine = ctx_gather(jnp.sum(mine.astype(jnp.float32), axis=0).astype(jnp.bfloat16))
    result = (middle_state + after(result.astype(jnp.float32), input_grad)).astype(jnp.bfloat16)
    output_total, projection_total, bias, gain_one, gain_two = spread_columns(
        mine, rows, width, bias_rows
    )
    return (
        result[None],
        input_grad[None],
        gain_one.reshape(rows),
        projection_total,
        bias.reshape(bias_rows),
        output_total,
        gain_two.reshape(rows),
        gate_up_total,
        down_total,
    )


def solution(mesh):
    placed = (
        P("wa", "ctx", None),
        P("wa", "ctx"),
        P("wa"),
        P("wa", None),
        P("wa"),
        P("wa", None),
        P("wa"),
        P("wa", None),
        P("wa", None),
        P("wa", "ctx", None),
    )
    return jax.shard_map(
        on_device,
        mesh=mesh,
        in_specs=placed,
        out_specs=(
            P("wa", "ctx", None),
            P("wa", "ctx", None),
            P("wa"),
            P("wa", None),
            P("wa"),
            P("wa", None),
            P("wa"),
            P("wa", None),
            P("wa", None),
        ),
        check_vma=False,
    )
```
